32 devices in a mesh: dp: 8 (over z, y), mp: 4 (over x, core).
Axes of the slice: x: 2, y: 2, z: 4, core: 2. Of those that a mesh axis runs over, the one named last changes fastest.
Arguments:
- tokens: bfloat16 [4096, 2048], P('dp'), may hold values from -6 to 6
- gain_first: float32 [2048], replicated, may hold values from 0.25 to 1.75
- w_qkv: bfloat16 [2048, 3, 2048], P(None, None, 'mp'), may hold values from -0.125 to 0.125
- w_out: bfloat16 [2048, 2048], P('mp'), may hold values from -0.5 to 0.5
- gain_second: float32 [2048], replicated, may hold values from 0.25 to 1.75
- router: float32 [2048, 4], replicated, may hold values from -0.09375 to 0.09375
- w_up: bfloat16 [4, 2048, 2048], P(None, None, 'mp'), may hold values from -0.125 to 0.125
- w_down: bfloat16 [4, 2048, 2048], P(None, 'mp'), may hold values from -0.0625 to 0.0625
- slot: int32 [4096], P('dp'), may hold values from 0 to 639, as said below
- cotangent: bfloat16 [4096, 2048], P('dp'), may hold values from -6 to 6
Outputs:
- output: bfloat16 [4096, 2048], P('dp')
- grad_tokens: bfloat16 [4096, 2048], P('dp')
- grad_gain_first: float32 [2048], replicated
- grad_qkv: float32 [2048, 3, 2048], P(None, None, 'mp')
- grad_out: float32 [2048, 2048], P('mp')
- grad_gain_second: float32 [2048], replicated
- grad_router: float32 [2048, 4], replicated
- grad_up: float32 [4, 2048, 2048], P(None, None, 'mp')
- grad_down: float32 [4, 2048, 2048], P(None, 'mp')
The draws below stay inside these ranges and needn't reach their ends.
Inputs may be any that keep to these rules, and one draw needn't show every extreme that they name: Within the 512 tokens of one index of dp all slots differ; a token with slot s goes to index floor(s / 80) of dp, row s mod 80 of that index's block from the sender. One index of dp, drawn from the seed, receives exactly 80 tokens from every index.
All inputs are finite; a program needn't handle non-finite values.
Results may differ from the reference program's by a relative error of at most 0.022.
Values may be sent and summed in bfloat16 or wider, within the bound.
No kernel may reach another device: no remote copies, remote signals or barrier semaphores. Data moves between devices by JAX's collectives and lax.ppermute only.
A program may use at most 192 MiB of HBM per device.

```python
from functools import partial
import jax
import jax.numpy as jnp
from jax import lax

D = 2048
HEADS = 16
HEAD = 128
FF = 8192
BUCKETS = 4
TOK_DEV = 512
FQ = 2048
CAP = 80
TOKENS = 4096
N_DP = 8


def draw_slot(key, part):
    key = jax.random.fold_in(key, 7)
    sources = TOKENS // TOK_DEV
    total = sources * CAP
    first_key, second_key, third_key = jax.random.split(key, 3)
    full_target = jax.random.randint(first_key, (), 0, sources)
    noise = jax.random.randint(second_key, (sources, total), 0, 1 << 20)
    position = jnp.arange(total, dtype=jnp.int32)
    favored = (position // CAP == full_target).astype(jnp.int32)
    score = (noise + favored * (1 << 21)) * total + position[None, :]
    ignored, chosen = lax.top_k(score, TOK_DEV)
    order = jax.random.randint(third_key, (sources, TOK_DEV), 0, 1 << 20) * TOK_DEV + jnp.arange(TOK_DEV, dtype=jnp.int32)[None, :]
    shuffle = jnp.argsort(order, axis=1)
    placed = jnp.take_along_axis(chosen, shuffle, axis=1)
    return placed.reshape(-1).astype(jnp.int32)


def level_of(stream_key, extent, shards, least, largest):
    level = 1.0
    for axis_at, shards_of in shards:
        heights = jax.random.uniform(jax.random.fold_in(jax.random.fold_in(stream_key, 6), axis_at), (shards_of,), jnp.float32, least / len(shards), largest / len(shards))
        level = level * jnp.repeat(jnp.exp(heights), extent[axis_at] // shards_of).reshape((-1,) + (1,) * (len(extent) - 1 - axis_at))
    return level


def gaussian(own_key, shape, width, limit, cuts=(), held_as=jnp.bfloat16):
    level = level_of(own_key, shape, cuts, -0.22, 0.18) if cuts else 1.0
    entries = jax.random.normal(own_key, shape, jnp.float32) * width * level
    return jnp.minimum(jnp.maximum(entries, -limit), limit).astype(held_as)


def setup_inputs(seed: int = 0) -> dict:
    arg_keys = jax.random.split(jax.random.key(seed), 11)
    tokens = gaussian(arg_keys[0], (TOKENS, D), 1.0, 6.0, ((0, 8),))
    gain_first = jnp.clip(1.0 + 0.15 * jax.random.normal(arg_keys[1], (D,), jnp.float32), 0.25, 1.75)
    w_qkv = gaussian(arg_keys[2], (D, 3, D), D ** -0.5, 0.125, ((2, 4),))
    w_out = gaussian(arg_keys[3], (D, D), (D // 16) ** -0.5, 0.5, ((0, 4),))
    gain_second = jnp.clip(1.0 + 0.15 * jax.random.normal(arg_keys[4], (D,), jnp.float32), 0.25, 1.75)
    router = gaussian(arg_keys[5], (D, BUCKETS), (2 * D) ** -0.5, 0.09375, (), jnp.float32)
    w_up = gaussian(arg_keys[6], (BUCKETS, D, FQ), D ** -0.5, 0.125, ((2, 4),))
    w_down = gaussian(arg_keys[7], (BUCKETS, FQ, D), FF ** -0.5, 0.0625, ((1, 4),))
    slot = draw_slot(jax.random.fold_in(arg_keys[10], 71), 0)
    cotangent = gaussian(arg_keys[9], (TOKENS, D), 1.0, 6.0, ((0, 8),))
    return dict(tokens=tokens, gain_first=gain_first, w_qkv=w_qkv, w_out=w_out, gain_second=gain_second, router=router, w_up=w_up, w_down=w_down, slot=slot, cotangent=cotangent)


HIGHEST = lax.Precision.HIGHEST
EPSILON = 1e-05

@jax.custom_vjp
def low(v):
    return lax.optimization_barrier(v.astype(jnp.bfloat16)).astype(jnp.float32)

@jax.custom_vjp
def low_back(v):
    return v

def low_keep(v):
    return (low(v), None)

def low_pass(kept, grad):
    return (grad,)

def back_keep(v):
    return (v, None)

def back_low(kept, grad):
    return (low(grad),)
low.defvjp(low_keep, low_pass)
low_back.defvjp(back_keep, back_low)

def normalize(values, gain):
    return values * lax.rsqrt(lax.optimization_barrier(jnp.mean(values * values, -1, keepdims=True)) + EPSILON) * gain

def rotary_table(length, head_size):
    position = jnp.arange(length, dtype=jnp.float32)
    inverse = 10000.0 ** (-jnp.arange(0, head_size, 2, dtype=jnp.float32) / head_size)
    angles = position[:, None] * inverse[None, :]
    angles = jnp.concatenate([angles, angles], -1)
    return (jnp.cos(angles), jnp.sin(angles))

def rotate(values, cos_table, sin_table):
    middle = values.shape[-1] // 2
    turned = jnp.concatenate([-values[..., middle:], values[..., :middle]], -1)
    return values * cos_table[:, None, :] + turned * sin_table[:, None, :]

def attend_sequence(normed, w_qkv, w_out, cos_table, sin_table):
    length = normed.shape[0]
    projected = low_back(jnp.einsum('td,dch->cth', normed, w_qkv, precision=HIGHEST))
    split_heads = projected.reshape(3, length, HEADS, HEAD)
    query_rows = low(rotate(split_heads[0], cos_table, sin_table))
    key_rows = low(rotate(split_heads[1], cos_table, sin_table))
    value_rows = low(split_heads[2])
    scores = low_back(jnp.einsum('qhe,khe->hqk', query_rows, key_rows, precision=HIGHEST) * HEAD ** (-0.5))
    causal = jnp.arange(length)[:, None] >= jnp.arange(length)[None, :]
    scores = jnp.where(causal[None], scores, -1000000000.0)
    weights = low(jax.nn.softmax(scores, axis=-1))
    mixed = jnp.einsum('hqk,khe->qhe', weights, value_rows, precision=HIGHEST)
    mixed = low_back(low(mixed.reshape(length, D)))
    return jnp.dot(mixed, w_out, precision=HIGHEST)

def forward(source, gain_first, w_qkv, w_out, gain_second, router, w_up, w_down, place, bucket_ids):
    cos_table, sin_table = rotary_table(TOK_DEV, HEAD)
    normed = low(normalize(source, gain_first))
    sequences = normed.reshape(N_DP, TOK_DEV, D)
    attend = partial(attend_sequence, w_qkv=w_qkv, w_out=w_out, cos_table=cos_table, sin_table=sin_table)
    attn = lax.map(jax.checkpoint(attend), sequences)
    attn = low_back(attn.reshape(TOKENS, D))
    resid = source + attn
    normed_second = normalize(resid, gain_second)
    logits = jnp.dot(normed_second, router, precision=HIGHEST)
    prob = jax.nn.softmax(logits, axis=-1)
    onehot = (bucket_ids[:, None] == jnp.arange(BUCKETS, dtype=jnp.int32)[None, :]).astype(jnp.float32)
    gate = BUCKETS * lax.optimization_barrier(jnp.sum(prob * onehot, -1))
    sent = low_back(low(normed_second))
    buffers = jnp.zeros((N_DP * N_DP * CAP, D), jnp.float32).at[place].set(sent)
    grouped = buffers.reshape(BUCKETS, N_DP // BUCKETS * N_DP * CAP, D)
    results = []
    for level in range(BUCKETS):
        pre = low_back(jnp.einsum('rd,qdh->rqh', grouped[level], w_up[:level + 1], precision=HIGHEST))
        act = low(jnp.square(jax.nn.relu(pre)))
        results.append(jnp.einsum('rqh,qhd->rd', act, w_down[:level + 1], precision=HIGHEST))
    combined = low_back(low(jnp.concatenate(results, 0)))
    ffn_rows = combined[place]
    return resid + gate[:, None] * ffn_rows

def reference(tokens, gain_first, w_qkv, w_out, gain_second, router, w_up, w_down, slot, cotangent):
    target = (slot // CAP).astype(jnp.int32)
    source_ids = (jnp.arange(TOKENS, dtype=jnp.int32) // TOK_DEV).astype(jnp.int32)
    place = (target * (N_DP * CAP) + source_ids * CAP + slot % CAP).astype(jnp.int32)
    bucket_ids = (target // (N_DP // BUCKETS)).astype(jnp.int32)
    primal = (tokens.astype(jnp.float32), gain_first, w_qkv.astype(jnp.float32), w_out.astype(jnp.float32), gain_second, router, w_up.astype(jnp.float32), w_down.astype(jnp.float32))
    result, pullback = jax.vjp(partial(forward, place=place, bucket_ids=bucket_ids), *primal)
    grads = pullback(cotangent.astype(jnp.float32))
    return (result.astype(jnp.bfloat16), grads[0].astype(jnp.bfloat16), grads[1], grads[2], grads[3], grads[4], grads[5], grads[6], grads[7])
```

```python
from functools import partial

import jax
import jax.numpy as jnp
from jax import lax
from jax.experimental import pallas as pl
from jax.experimental.pallas import tpu as pltpu
from jax.sharding import PartitionSpec as P

HEAD = 128
HIGHEST = lax.Precision.HIGHEST
EPSILON = 1e-05
F32 = jnp.float32
BF16 = jnp.bfloat16
VMEM_LIMIT = 56 * 1024 * 1024
NN = (((1,), (0,)), ((), ()))
NT = (((1,), (1,)), ((), ()))


def dot(a, b, dims=NN):
    return lax.dot_general(a, b, dims, preferred_element_type=F32)


def low(x):
    return lax.reduce_precision(x, 8, 7).astype(BF16)


def params():
    return pltpu.CompilerParams(vmem_limit_bytes=VMEM_LIMIT)


def cost(flops, nbytes, transcendentals=0):
    return pl.CostEstimate(flops=flops, bytes_accessed=nbytes, transcendentals=transcendentals)


def rotary_table(length, head_size):
    position = jnp.arange(length, dtype=F32)
    inverse = 10000.0 ** (-jnp.arange(0, head_size, 2, dtype=F32) / head_size)
    angles = position[:, None] * inverse[None, :]
    angles = jnp.concatenate([angles, angles], -1)
    sign = jnp.where(jnp.arange(head_size) < head_size // 2, -1.0, 1.0)
    return jnp.cos(angles), jnp.sin(angles) * sign


def attend_kernel(x_ref, gain_ref, w_ref, cos_ref, sin_ref, wout_ref,
                  part_ref, normed_ref, qkv_ref, lse_ref, mixed_ref, *, heads, steps):
    g = pl.program_id(0)
    length = x_ref.shape[0]
    half = length // 2
    scale = HEAD ** -0.5

    @pl.when(g == 0)
    def _():
        values = x_ref[...].astype(F32)
        inv = lax.rsqrt(jnp.mean(values * values, -1, keepdims=True) + EPSILON)
        normed_ref[...] = (values * inv * gain_ref[...]).astype(BF16)

    normed = normed_ref[...]
    cos, sin = cos_ref[...], sin_ref[...]
    projected = [dot(normed, w_ref[c]) for c in range(3)]
    for h in range(heads):
        cols = slice(h * HEAD, (h + 1) * HEAD)
        q, k, v = (p[:, cols] for p in projected)
        q = (q * cos + pltpu.roll(q, HEAD // 2, 1) * sin).astype(BF16)
        k = (k * cos + pltpu.roll(k, HEAD // 2, 1) * sin).astype(BF16)
        v = v.astype(BF16)
        qkv_ref[0, :, cols] = q
        qkv_ref[1, :, cols] = k
        qkv_ref[2, :, cols] = v
        for b in range(2):
            rows = slice(b * half, (b + 1) * half)
            keys = (b + 1) * half
            scores = dot(q[rows], k[:keys], NT) * scale
            at = lax.broadcasted_iota(jnp.int32, scores.shape, 0) + b * half
            to = lax.broadcasted_iota(jnp.int32, scores.shape, 1)
            scores = jnp.where(at >= to, scores, -1000000000.0)
            top = jnp.max(scores, -1, keepdims=True)
            weights = jnp.exp(scores - top)
            total = jnp.sum(weights, -1, keepdims=True)
            lse_ref[h, rows, :] = jnp.broadcast_to(top + jnp.log(total), (half, HEAD))
            low = (weights * (1.0 / total)).astype(BF16)
            mixed_ref[rows, pl.ds(pl.multiple_of((g * heads + h) * HEAD, HEAD), HEAD)] = dot(low, v[:keys]).astype(BF16)

    @pl.when(g == steps - 1)
    def _():
        part_ref[...] = dot(mixed_ref[...], wout_ref[...]).astype(BF16)


def attend(tokens, gain, w3, cos, sin, w_out):
    length, model = tokens.shape
    local = w3.shape[2]
    local_heads = local // HEAD
    heads = 2 if local_heads % 2 == 0 else 1
    steps = local_heads // heads
    wide = heads * HEAD
    full = lambda *shape: pl.BlockSpec(shape, lambda g: (0,) * len(shape))
    return pl.pallas_call(
        partial(attend_kernel, heads=heads, steps=steps),
        grid=(steps,),
        in_specs=[
            full(length, model), full(1, model),
            pl.BlockSpec((3, model, wide), lambda g: (0, 0, g)),
            full(length, HEAD), full(length, HEAD), full(local, model),
        ],
        out_specs=[
            full(length, model), full(length, model),
            pl.BlockSpec((3, length, wide), lambda g: (0, 0, g)),
            pl.BlockSpec((heads, length, HEAD), lambda g: (g, 0, 0)),
            full(length, local),
        ],
        out_shape=[
            jax.ShapeDtypeStruct((length, model), BF16),
            jax.ShapeDtypeStruct((length, model), BF16),
            jax.ShapeDtypeStruct((3, length, local), BF16),
            jax.ShapeDtypeStruct((local_heads, length, HEAD), F32),
            jax.ShapeDtypeStruct((length, local), BF16),
        ],
        compiler_params=params(),
        cost_estimate=cost(2 * length * model * local * 4 + 4 * length * length * local,
                           2 * (2 * length * model + 4 * model * local), length * length * local_heads),
        name="attend",
    )(tokens, gain, w3, cos, sin, w_out)


def attend_back_kernel(ga_ref, normed_t_ref, qkv_ref, lse_ref, mixed_t_ref, wout_ref, w_ref, cos_ref, sin_ref,
                       *rest, heads, steps, deps):
    gqkv_ref, gout_ref, first_ref, acc_ref, gp_ref = rest[deps:]
    g = pl.program_id(0)
    length = ga_ref.shape[0]
    model = ga_ref.shape[1]
    half = length // 2
    scale = HEAD ** -0.5
    cos, sin = cos_ref[...], sin_ref[...]
    ga = ga_ref[...]
    gmixed = dot(ga, wout_ref[...], NT).astype(BF16)
    for h in range(heads):
        cols = slice(h * HEAD, (h + 1) * HEAD)
        q, k, v = (qkv_ref[c, :, cols] for c in range(3))
        gm = gmixed[:, cols]
        gq, gk, gv = [], [None, None], [None, None]
        for b in range(2):
            rows = slice(b * half, (b + 1) * half)
            keys = (b + 1) * half
            scores = dot(q[rows], k[:keys], NT) * scale
            at = lax.broadcasted_iota(jnp.int32, scores.shape, 0) + b * half
            to = lax.broadcasted_iota(jnp.int32, scores.shape, 1)
            probs = jnp.where(at >= to, jnp.exp(scores - lse_ref[h, rows, :1]), 0.0)
            gprobs = dot(gm[rows], v[:keys], NT)
            gscores = probs * (gprobs - jnp.sum(gprobs * probs, -1, keepdims=True))
            gs = gscores.astype(BF16)
            low = probs.astype(BF16)
            gq.append(dot(gs, k[:keys]) * scale)
            gs_t, low_t = gs.T, low.T
            for j in range(b + 1):
                part = slice(j * half, (j + 1) * half)
                a = dot(gs_t[part], q[rows]) * scale
                c = dot(low_t[part], gm[rows])
                gk[j] = a if gk[j] is None else gk[j] + a
                gv[j] = c if gv[j] is None else gv[j] + c
        gq = jnp.concatenate(gq, 0)
        gk = jnp.concatenate(gk, 0)
        gv = jnp.concatenate(gv, 0)
        gp_ref[0, :, cols] = (gq * cos - pltpu.roll(gq, HEAD // 2, 1) * sin).astype(BF16)
        gp_ref[1, :, cols] = (gk * cos - pltpu.roll(gk, HEAD // 2, 1) * sin).astype(BF16)
        gp_ref[2, :, cols] = gv.astype(BF16)

    gout_ref[...] = dot(mixed_t_ref[...], ga).astype(BF16)
    for c in range(3):
        gqkv_ref[c] = dot(normed_t_ref[...], gp_ref[c]).astype(BF16)
    total = dot(gp_ref[0], w_ref[0], NT)
    for c in (1, 2):
        total = total + dot(gp_ref[c], w_ref[c], NT)

    @pl.when(g > 0)
    def _():
        acc_ref[...] += total

    @pl.when(g == 0)
    def _():
        acc_ref[...] = total

    @pl.when(g == steps - 1)
    def _():
        first_ref[...] = acc_ref[...].astype(BF16)


def attend_back(ga, normed_t, qkv, lse, mixed_t, w_out, w3, cos, sin, deps=()):
    length, model = ga.shape
    local = w3.shape[2]
    local_heads = local // HEAD
    heads = 2 if local_heads % 2 == 0 else 1
    steps = local_heads // heads
    wide = heads * HEAD
    full = lambda *shape: pl.BlockSpec(shape, lambda g: (0,) * len(shape))
    return pl.pallas_call(
        partial(attend_back_kernel, heads=heads, steps=steps, deps=len(deps)),
        grid=(steps,),
        in_specs=[
            full(length, model), full(model, length),
            pl.BlockSpec((3, length, wide), lambda g: (0, 0, g)),
            pl.BlockSpec((heads, length, HEAD), lambda g: (g, 0, 0)),
            pl.BlockSpec((wide, length), lambda g: (g, 0)),
            pl.BlockSpec((wide, model), lambda g: (g, 0)),
            pl.BlockSpec((3, model, wide), lambda g: (0, 0, g)),
            full(length, HEAD), full(length, HEAD),
        ] + [pl.BlockSpec(memory_space=pl.ANY)] * len(deps),
        out_specs=[
            pl.BlockSpec((3, model, wide), lambda g: (0, 0, g)),
            pl.BlockSpec((wide, model), lambda g: (g, 0)),
            full(length, model),
        ],
        out_shape=[
            jax.ShapeDtypeStruct((3, model, local), BF16),
            jax.ShapeDtypeStruct((local, model), BF16),
            jax.ShapeDtypeStruct((length, model), BF16),
        ],
        scratch_shapes=[pltpu.VMEM((length, model), F32), pltpu.VMEM((3, length, wide), BF16)],
        compiler_params=params(),
        cost_estimate=cost(2 * length * model * local * 8 + 10 * length * length * local,
                           2 * (4 * length * model + 8 * model * local), length * length * local_heads),
        name="attend_back",
    )(ga, normed_t, qkv, lse, mixed_t, w_out, w3, cos, sin, *deps)


def own_grad_kernel(sent_ref, cot_ref, bucket_ref, gate_ref, unsort_ref, up_ref, down_ref, *rest, row_bounds, deps):
    gsent_ref, act_ref, acc_ref = rest[deps:]
    level = pl.program_id(0)
    for q, rows in enumerate(row_bounds):
        @pl.when(level == q)
        def _(q=q, rows=rows):
            keep = bucket_ref[:rows, :1] >= q
            pre = dot(sent_ref[:rows], up_ref[0])
            active = jnp.where(keep, jnp.maximum(pre, 0.0), 0.0)
            act_ref[0, :rows] = (active * active).astype(BF16)
            gact = dot(cot_ref[:rows], down_ref[0], NT)
            gpre = (gact * (2.0 * gate_ref[:rows, :1]) * active).astype(BF16)
            s = dot(gpre, up_ref[0], NT)
            if q == 0:
                acc_ref[...] = s
            else:
                acc_ref[:rows] += s
            if q == len(row_bounds) - 1:
                gsent_ref[...] = dot(unsort_ref[...], acc_ref[...].astype(BF16)).astype(BF16)


def own_grad(sent, cot, bucket, gate, unsort, w_up, w_down, row_bounds, deps=()):
    length, model = sent.shape
    levels, _, hidden = w_up.shape
    full = lambda *shape: pl.BlockSpec(shape, lambda q: (0,) * len(shape))
    return pl.pallas_call(
        partial(own_grad_kernel, row_bounds=tuple(row_bounds), deps=len(deps)),
        grid=(levels,),
        in_specs=[
            full(length, model), full(length, model), full(length, 128), full(length, 128), full(length, length),
            pl.BlockSpec((1, model, hidden), lambda q: (q, 0, 0)),
            pl.BlockSpec((1, hidden, model), lambda q: (q, 0, 0)),
        ] + [pl.BlockSpec(memory_space=pl.ANY)] * len(deps),
        out_specs=[full(length, model), pl.BlockSpec((1, length, hidden), lambda q: (q, 0, 0))],
        out_shape=[jax.ShapeDtypeStruct((length, model), BF16), jax.ShapeDtypeStruct((levels, length, hidden), BF16)],
        scratch_shapes=[pltpu.VMEM((length, model), F32)],
        compiler_params=params(),
        cost_estimate=cost(6 * sum(row_bounds) * model * hidden, 4 * levels * model * hidden + 6 * length * model),
        name="own_grad",
    )(sent, cot, bucket, gate, unsort, w_up, w_down, *deps)


def own_forward_kernel(act_ref, cot_ref, unsort_ref, down_ref, *rest, row_bounds, deps):
    ffn_ref, ggate_ref, acc_ref = rest[deps:]
    level = pl.program_id(0)
    for q, rows in enumerate(row_bounds):
        @pl.when(level == q)
        def _(q=q, rows=rows):
            f = dot(act_ref[0, :rows], down_ref[0])
            if q == 0:
                acc_ref[...] = f
            else:
                acc_ref[:rows] += f
            if q == len(row_bounds) - 1:
                total = acc_ref[...]
                ggate = jnp.sum(total * cot_ref[...].astype(F32), -1, keepdims=True)
                ggate_ref[...] = jnp.broadcast_to(ggate, ggate_ref.shape)
                ffn_ref[...] = dot(unsort_ref[...], total.astype(BF16)).astype(BF16)


def own_forward(act, cot, unsort, w_down, row_bounds, deps=()):
    length, model = cot.shape
    levels, hidden, _ = w_down.shape
    full = lambda *shape: pl.BlockSpec(shape, lambda q: (0,) * len(shape))
    return pl.pallas_call(
        partial(own_forward_kernel, row_bounds=tuple(row_bounds), deps=len(deps)),
        grid=(levels,),
        in_specs=[
            pl.BlockSpec((1, length, hidden), lambda q: (q, 0, 0)),
            full(length, model), full(length, length),
            pl.BlockSpec((1, hidden, model), lambda q: (q, 0, 0)),
        ] + [pl.BlockSpec(memory_space=pl.ANY)] * len(deps),
        out_specs=[full(length, model), full(length, 128)],
        out_shape=[jax.ShapeDtypeStruct((length, model), BF16), jax.ShapeDtypeStruct((length, 128), F32)],
        scratch_shapes=[pltpu.VMEM((length, model), F32)],
        compiler_params=params(),
        cost_estimate=cost(2 * sum(row_bounds) * model * hidden, 2 * levels * model * hidden + 6 * length * model),
        name="own_forward",
    )(act, cot, unsort, w_down, *deps)


AUX = 16


def block_copies(s_refs, c_refs, s_buf, aux_buf, c_buf, sems, k, slot):
    core = lax.rem(lax.axis_index("mp"), 2)
    part, rows = s_buf.shape[1] // 2, c_buf.shape[1] // 2
    at = lambda c, size: pl.ds(pl.multiple_of(c * size, size), size)
    mine, other = core, 1 - core
    ends = [
        (s_refs[2 * k].at[pl.ds(0, part)], s_buf.at[slot, at(mine, part)]),
        (s_refs[2 * k].at[pl.ds(part, AUX)], aux_buf.at[slot]),
        (s_refs[2 * k + 1].at[pl.ds(0, part)], s_buf.at[slot, at(other, part)]),
        (c_refs[2 * k], c_buf.at[slot, at(mine, rows)]),
        (c_refs[2 * k + 1], c_buf.at[slot, at(other, rows)]),
    ]
    return [pltpu.make_async_copy(src, dst, sems.at[slot, i]) for i, (src, dst) in enumerate(ends)]


def fetch_block(s_refs, c_refs, s_buf, aux_buf, c_buf, sems):
    b = pl.program_id(0)
    count = len(s_refs) // 2
    copies = partial(block_copies, s_refs, c_refs, s_buf, aux_buf, c_buf, sems)
    for k in range(count):
        @pl.when(b == (k if k == 0 else k - 1))
        def _(k=k):
            for c in copies(k, k % 2):
                c.start()
    for k in range(count):
        @pl.when(b == k)
        def _(k=k):
            for c in copies(k, k % 2):
                c.wait()
    return lax.rem(b, 2)


def weight_first_kernel(*refs, level, rows, count, deps):
    s_refs, c_refs = refs[:2 * count], refs[2 * count:4 * count]
    up_t_ref, down_ref = refs[4 * count:4 * count + 2]
    act_ref, gpre_ref, s_buf, aux_buf, c_buf, sems = refs[4 * count + 2 + deps:]
    slot = fetch_block(s_refs, c_refs, s_buf, aux_buf, c_buf, sems)
    aux = aux_buf[slot, :, :rows].astype(F32)
    gate = aux[0:1] + aux[1:2] + aux[2:3]
    keep = aux[3:4] >= level
    pre = dot(up_t_ref[0], s_buf[slot, :, :rows])
    active = jnp.where(keep, jnp.maximum(pre, 0.0), 0.0)
    act_ref[0] = (active * active * gate).astype(BF16)
    gact = dot(down_ref[0], c_buf[slot, :rows], NT)
    gpre_ref[0] = (gact * (2.0 * gate) * active).astype(BF16)


def weight_second_kernel(*refs, rows, count, deps):
    s_refs, c_refs = refs[:2 * count], refs[2 * count:4 * count]
    act_ref, gpre_ref = refs[4 * count:4 * count + 2]
    gup_ref, gdown_ref, s_buf, aux_buf, c_buf, sems = refs[4 * count + 2 + deps:]
    b = pl.program_id(0)
    slot = fetch_block(s_refs, c_refs, s_buf, aux_buf, c_buf, sems)
    u = dot(s_buf[slot, :, :rows], gpre_ref[0], NT)
    d = dot(act_ref[0], c_buf[slot, :rows])

    @pl.when(b == 0)
    def _():
        gup_ref[0] = u
        gdown_ref[0] = d

    @pl.when(b > 0)
    def _():
        gup_ref[0] += u
        gdown_ref[0] += d


def block_scratch(length, model):
    return [
        pltpu.VMEM((2, model, length), BF16), pltpu.VMEM((2, AUX, length), BF16),
        pltpu.VMEM((2, length, model), BF16), pltpu.SemaphoreType.DMA((2, 5)),
    ]


def weight_first(level, rows, sents, cots, up_t, w_down, deps=()):
    count = len(sents) // 2
    levels, hidden, model = up_t.shape
    length = sents[0].shape[1]
    rows = -(-rows // 128) * 128
    anywhere = pl.BlockSpec(memory_space=pl.ANY)
    return pl.pallas_call(
        partial(weight_first_kernel, level=level, rows=rows, count=count, deps=len(deps)),
        grid=(count,),
        in_specs=[anywhere] * (4 * count) + [
            pl.BlockSpec((1, hidden, model), lambda b: (level, 0, 0)),
            pl.BlockSpec((1, hidden, model), lambda b: (level, 0, 0)),
        ] + [anywhere] * len(deps),
        out_specs=[pl.BlockSpec((1, hidden, rows), lambda b: (b, 0, 0))] * 2,
        out_shape=[jax.ShapeDtypeStruct((count, hidden, rows), BF16)] * 2,
        scratch_shapes=block_scratch(length, model),
        compiler_params=params(),
        cost_estimate=cost(4 * count * rows * model * hidden, 4 * count * rows * model),
        name=f"weight_first_{level}",
    )(*sents, *cots, up_t, w_down, *deps)


def weight_second(level, levels, rows, sents, cots, act, gpre, carried, deps=()):
    count = len(sents) // 2
    _, hidden, rows = act.shape
    length, model = sents[0].shape[1], cots[0].shape[1]
    anywhere = pl.BlockSpec(memory_space=pl.ANY)
    first = 4 * count + 2
    return pl.pallas_call(
        partial(weight_second_kernel, rows=rows, count=count, deps=len(carried) + len(deps)),
        grid=(count,),
        in_specs=[anywhere] * (4 * count) + [pl.BlockSpec((1, hidden, rows), lambda b: (b, 0, 0))] * 2
        + [anywhere] * (len(carried) + len(deps)),
        out_specs=[
            pl.BlockSpec((1, model, hidden), lambda b: (level, 0, 0)),
            pl.BlockSpec((1, hidden, model), lambda b: (level, 0, 0)),
        ],
        out_shape=[jax.ShapeDtypeStruct((levels, model, hidden), F32), jax.ShapeDtypeStruct((levels, hidden, model), F32)],
        input_output_aliases={first: 0, first + 1: 1} if carried else {},
        scratch_shapes=block_scratch(length, model),
        compiler_params=params(),
        cost_estimate=cost(4 * count * rows * model * hidden, 4 * count * rows * model + 8 * model * hidden),
        name=f"weight_second_{level}",
    )(*sents, *cots, act, gpre, *carried, *deps)


def ring_order(count):
    nz = 4 if count % 4 == 0 else 1
    ny = count // nz
    if nz == 1 or ny % 2:
        return list(range(count))
    order = [(z, 0) for z in range(nz)]
    for y in range(1, ny):
        line = list(range(1, nz))
        order += [(z, y) for z in (reversed(line) if y % 2 else line)]
    order += [(0, y) for y in range(ny - 1, 0, -1)]
    return [z * ny + y for z, y in order]


class Ring:
    def __init__(self):
        self.log = []
        self.count = lax.axis_size("dp")
        self.order = ring_order(self.count)
        n = self.count
        place = [0] * n
        for p, d in enumerate(self.order):
            place[d] = p
        self.position = jnp.array(place, jnp.int32)[lax.axis_index("dp")]
        self.right = [(self.order[p], self.order[(p + 1) % n]) for p in range(n)]
        self.left = [(self.order[(p + 1) % n], self.order[p]) for p in range(n)]

    def to_right(self, x):
        out = lax.ppermute(x, "dp", self.right)
        self.log.append(out)
        return out

    def to_left(self, x):
        out = lax.ppermute(x, "dp", self.left)
        self.log.append(out)
        return out

    def logged(self, f, *args):
        self.log = []
        out = f(*args)
        pairs = [tuple(self.log[i:i + 2]) for i in range(0, len(self.log), 2)]
        self.log = []
        return out, pairs

    def gather(self, x, axis):
        out = [x]
        r = l = x
        for _ in range(self.count // 2 - 1):
            r, l = self.to_right(r), self.to_left(l)
            out += [r, l]
        cut = x.shape[axis] // 2
        first = self.to_right(lax.slice_in_dim(r, 0, cut, axis=axis))
        second = self.to_left(lax.slice_in_dim(l, cut, 2 * cut, axis=axis))
        out.append(jnp.concatenate([first, second], axis))
        return out

    def offsets(self):
        out = [0]
        for k in range(1, self.count // 2):
            out += [-k, k]
        return out + [self.count // 2]

    def indices(self):
        return [(self.position + k) % self.count for k in self.offsets()]

    def reduce_scatter(self, x, axis):
        n = self.count
        size = x.shape[axis] // n
        cut = size // 2

        def piece(k, start=0, length=size):
            at = ((self.position + k) % n) * size + start
            return lax.dynamic_slice_in_dim(x, at, length, axis=axis)

        def join(a, b):
            return low(a.astype(F32) + b.astype(F32))

        far = n // 2
        r = self.to_right(piece(far, 0, cut))
        l = self.to_left(piece(-far, cut, cut))
        k = far - 1
        r = jnp.concatenate([join(r, piece(k, 0, cut)), piece(k, cut, cut)], axis)
        l = jnp.concatenate([piece(-k, 0, cut), join(l, piece(-k, cut, cut))], axis)
        r, l = self.to_right(r), self.to_left(l)
        for k in range(far - 2, 0, -1):
            r, l = self.to_right(join(r, piece(k))), self.to_left(join(l, piece(-k)))
        return low(r.astype(F32) + l.astype(F32) + piece(0).astype(F32))


def core_swap(x):
    n = lax.axis_size("mp")
    return lax.ppermute(x, "mp", [(i, i ^ 1) for i in range(n)])


def sum_over_x(x):
    n = lax.axis_size("mp") // 2
    index = lax.axis_index("mp")
    parts = [x] + [
        lax.ppermute(x, "mp", [(i, (i + 2 * k) % (2 * n)) for i in range(2 * n)]) for k in range(1, n)
    ]
    if n == 1:
        return x.astype(F32)
    if n == 2:
        return parts[0].astype(F32) + parts[1].astype(F32)
    stacked = jnp.stack(parts)
    total = None
    for j in range(n):
        term = lax.dynamic_index_in_dim(stacked, (index // 2 - j) % n, 0, keepdims=False).astype(F32)
        total = term if total is None else total + term
    return total


def sum_over_all(x):
    x = x + core_swap(x)
    n = lax.axis_size("dp")
    step = 1
    while step < n:
        x = x + lax.ppermute(x, "dp", [(i, i ^ step) for i in range(n)])
        step *= 2
    return x


def on_device(tokens, gain_first, w_qkv, w_out, gain_second, router, w_up, w_down, slot, cotangent):
    length, model = tokens.shape
    buckets = w_up.shape[0]
    devices_dp = lax.axis_size("dp")
    groups = devices_dp // buckets
    capacity = length * 5 // (4 * devices_dp)
    row_bounds = [min(length, (buckets - level) * groups * capacity) for level in range(buckets)]
    ring = Ring()
    core = lax.axis_index("mp") % 2
    half = length // 2

    bucket_ids = slot // capacity // groups
    places = jnp.arange(length, dtype=jnp.int32)
    key = (buckets - 1 - bucket_ids) * length + places
    rank = jnp.sum((key[None, :] < key[:, None]).astype(jnp.int32), 1)
    rank_here = jnp.roll(rank, -core * half)
    sort_rows = places[:, None] == rank[None, :]
    sort_here = places[:, None] == rank_here[None, :]
    sort_low = sort_here.astype(BF16)
    unsort_low = (rank_here[:, None] == places[None, :]).astype(BF16)
    bucket_sorted = jnp.sum(jnp.where(sort_rows, bucket_ids[None, :], 0), 1)

    def part_of(x, c, axis=0):
        size = x.shape[axis] // 2
        return lax.dynamic_slice_in_dim(x, c * size, size, axis=axis)

    def own_rows(x):
        return part_of(x, core)

    def other_rows(x):
        return part_of(x, 1 - core)

    def sum_halves(mine, others):
        return sum_over_x(low(mine.astype(F32) + core_swap(others).astype(F32)))

    def joined(mine, other):
        return jnp.concatenate([jnp.where(core == 0, mine, other), jnp.where(core == 0, other, mine)], 0)

    cot_sorted = dot(sort_rows.astype(BF16), cotangent).astype(BF16)
    cot_halves, cot_steps = ring.logged(ring.gather, own_rows(cot_sorted), 0)

    w3 = jnp.transpose(w_qkv, (1, 0, 2))
    cos, sin = rotary_table(length, HEAD)
    part, normed_low, qkv, lse, mixed = attend(tokens, gain_first[None, :], w3, cos, sin, w_out)
    attn = sum_halves(own_rows(part), other_rows(part))
    normed_t, mixed_t, up_t = normed_low.T, mixed.T, jnp.transpose(w_up, (0, 2, 1))

    resid = own_rows(tokens).astype(F32) + attn
    inv = lax.rsqrt(jnp.mean(resid * resid, -1, keepdims=True) + EPSILON)
    xhat = resid * inv
    normed_second = xhat * gain_second
    logits = jnp.dot(normed_second, router, precision=HIGHEST)
    prob = jax.nn.softmax(logits, axis=-1)
    onehot = (own_rows(bucket_ids)[:, None] == jnp.arange(buckets)[None, :]).astype(F32)
    gate = buckets * jnp.sum(prob * onehot, -1)
    sent_half = normed_second.astype(BF16)
    sent_both = jnp.concatenate([sent_half, core_swap(sent_half)], 0)
    gate_both = jnp.concatenate([gate, core_swap(gate)], 0)
    gate_sorted = jnp.sum(jnp.where(sort_here, gate_both[None, :], 0.0), 1)

    sent_sorted = dot(sort_low, sent_both).astype(BF16)
    sent_sorted_t = lax.dot_general(sent_both, sort_low, (((0,), (1,)), ((), ())), preferred_element_type=F32).astype(BF16)

    gate_1 = low(gate_sorted)
    gate_2 = low(gate_sorted - gate_1.astype(F32))
    gate_3 = low(gate_sorted - gate_1.astype(F32) - gate_2.astype(F32))
    aux = jnp.stack([gate_1, gate_2, gate_3, bucket_sorted.astype(BF16)] + [jnp.zeros_like(gate_1)] * (AUX - 4))
    sent_own = jnp.concatenate([part_of(sent_sorted_t, core), aux], 0)
    sent_halves, sent_steps = ring.logged(ring.gather, sent_own, 1)

    wide = lambda x: jnp.broadcast_to(x[:, None], (length, 128))
    gsent_part, act = own_grad(
        sent_sorted, cot_sorted, wide(bucket_sorted), wide(gate_sorted), unsort_low, w_up, w_down, row_bounds, cot_steps[0])
    grad_sent = sum_halves(gsent_part[:half], gsent_part[half:]).astype(BF16).astype(F32)
    ffn_part, ggate_part = own_forward(act, cot_sorted, unsort_low, w_down, row_bounds, cot_steps[1])
    ffn_rows = sum_halves(ffn_part[:half], ffn_part[half:]).astype(BF16).astype(F32)
    ggate_part = jnp.sum(jnp.where(sort_rows, ggate_part[:, :1], 0.0), 0)
    grad_gate = ggate_part + core_swap(ggate_part)
    grad_gate = sum_over_x(own_rows(grad_gate))

    grad_output = own_rows(cotangent).astype(F32)
    output_half = (resid + gate[:, None] * ffn_rows).astype(BF16)
    grad_prob = buckets * grad_gate[:, None] * onehot
    grad_logits = prob * (grad_prob - jnp.sum(grad_prob * prob, -1, keepdims=True))
    grad_router = jnp.dot(normed_second.T, grad_logits, precision=HIGHEST)
    grad_second = grad_sent + jnp.dot(grad_logits, router.T, precision=HIGHEST)
    grad_gain_second = jnp.sum(grad_second * xhat, 0)
    scaled = grad_second * gain_second
    grad_resid = grad_output + inv * (scaled - xhat * jnp.mean(scaled * xhat, -1, keepdims=True))
    ga_half = low(grad_resid)
    grad_attn = joined(ga_half, core_swap(ga_half))

    gqkv, gout, first_part = attend_back(grad_attn, normed_t, qkv, lse, mixed_t, w_out, w3, cos, sin, cot_steps[2])

    gqkv_chunk, qkv_steps = ring.logged(ring.reduce_scatter, gqkv, 1)
    gout_chunk, out_steps = ring.logged(ring.reduce_scatter, gout, 0)
    gqkv_chunks, qkv_more = ring.logged(ring.gather, gqkv_chunk, 1)
    gout_chunks, out_more = ring.logged(ring.gather, gout_chunk, 0)
    sum_steps = [a + b for a, b in zip(qkv_steps + qkv_more, out_steps + out_more)]
    grad_wout = jnp.zeros(gout.shape, F32)
    grad_wqkv = jnp.zeros(gqkv.shape, F32)
    for at, a, b in zip(ring.indices(), gout_chunks, gqkv_chunks):
        grad_wout = lax.dynamic_update_slice_in_dim(grad_wout, a.astype(F32), at * a.shape[0], 0)
        grad_wqkv = lax.dynamic_update_slice_in_dim(grad_wqkv, b.astype(F32), at * b.shape[1], 1)

    grad_first = sum_halves(own_rows(first_part), other_rows(first_part))
    source = own_rows(tokens).astype(F32)
    inv_first = lax.rsqrt(jnp.mean(source * source, -1, keepdims=True) + EPSILON)
    xhat_first = source * inv_first
    grad_gain_first = jnp.sum(grad_first * xhat_first, 0)
    scaled_first = grad_first * gain_first
    grad_source = inv_first * (scaled_first - xhat_first * jnp.mean(scaled_first * xhat_first, -1, keepdims=True))
    tokens_half = (grad_source + grad_resid).astype(BF16)
    output = joined(output_half, core_swap(output_half))
    grad_tokens = joined(tokens_half, core_swap(tokens_half))
    small = jnp.concatenate([grad_router.T, grad_gain_second[None], grad_gain_first[None]], 0)
    small = sum_over_all(small)

    sents = [sent_own, part_of(sent_sorted_t, 1 - core)]
    cots = [cot_halves[0], other_rows(cot_sorted)]
    for k in range(1, devices_dp):
        sents += [sent_halves[k], core_swap(sent_halves[k])]
        cots += [cot_halves[k], core_swap(cot_halves[k])]
    carried = ()
    for level, rows in enumerate(row_bounds):
        deps = [sum_steps[i] if 0 <= i < len(sum_steps) else () for i in (2 * level - 1, 2 * level)]
        act_all, gpre_all = weight_first(level, rows, sents, cots, up_t, w_down, deps[0])
        carried = weight_second(level, buckets, rows, sents, cots, act_all, gpre_all, carried, deps[1])
    grad_up, grad_down = carried

    return (
        output,
        grad_tokens,
        small[buckets + 1],
        jnp.transpose(grad_wqkv, (1, 0, 2)),
        grad_wout,
        small[buckets],
        small[:buckets].T,
        grad_up,
        grad_down,
    )


def solution(mesh):
    placed = (
        P("dp", None),
        P(),
        P(None, None, "mp"),
        P("mp", None),
        P(),
        P(),
        P(None, None, "mp"),
        P(None, "mp", None),
        P("dp"),
        P("dp", None),
    )
    return jax.shard_map(
        on_device,
        mesh=mesh,
        in_specs=placed,
        out_specs=(
            P("dp", None),
            P("dp", None),
            P(),
            P(None, None, "mp"),
            P("mp", None),
            P(),
            P(),
            P(None, None, "mp"),
            P(None, "mp", None),
        ),
        check_vma=False,
    )
```

```python
from functools import partial

import jax
import jax.numpy as jnp
from jax import lax
from jax.experimental import pallas as pl
from jax.experimental.pallas import tpu as pltpu
from jax.sharding import PartitionSpec as P

HEAD = 128
HIGHEST = lax.Precision.HIGHEST
EPSILON = 1e-05
F32 = jnp.float32
BF16 = jnp.bfloat16
VMEM_LIMIT = 56 * 1024 * 1024
COST = 4
NN = (((1,), (0,)), ((), ()))
NT = (((1,), (1,)), ((), ()))
TN = (((0,), (0,)), ((), ()))


def dot(a, b, dims=NN):
    return lax.dot_general(a, b, dims, preferred_element_type=F32)


def low(x):
    return lax.reduce_precision(x, 8, 7).astype(BF16)


def params():
    return pltpu.CompilerParams(vmem_limit_bytes=VMEM_LIMIT)


def cost(flops, nbytes, transcendentals=0):
    return pl.CostEstimate(flops=flops // COST, bytes_accessed=nbytes // COST, transcendentals=transcendentals // COST)


def rotary_table(length, head_size):
    position = jnp.arange(length, dtype=F32)
    inverse = 10000.0 ** (-jnp.arange(0, head_size, 2, dtype=F32) / head_size)
    angles = position[:, None] * inverse[None, :]
    angles = jnp.concatenate([angles, angles], -1)
    sign = jnp.where(jnp.arange(head_size) < head_size // 2, -1.0, 1.0)
    return jnp.cos(angles), jnp.sin(angles) * sign


def attend_kernel(x_ref, gain_ref, w_ref, cos_ref, sin_ref, wout_ref,
                  mine_ref, other_ref, normed_ref, qkv_ref, lse_ref, mixed_ref, *, heads, steps):
    g = pl.program_id(0)
    length = x_ref.shape[0]
    half = length // 2
    scale = HEAD ** -0.5

    @pl.when(g == 0)
    def _():
        values = x_ref[...].astype(F32)
        inv = lax.rsqrt(jnp.mean(values * values, -1, keepdims=True) + EPSILON)
        normed_ref[...] = (values * inv * gain_ref[...]).astype(BF16)

    normed = normed_ref[...]
    cos, sin = cos_ref[...], sin_ref[...]
    projected = [dot(normed, w_ref[c]) for c in range(3)]
    for h in range(heads):
        cols = slice(h * HEAD, (h + 1) * HEAD)
        q, k, v = (p[:, cols] for p in projected)
        q = (q * cos + pltpu.roll(q, HEAD // 2, 1) * sin).astype(BF16)
        k = (k * cos + pltpu.roll(k, HEAD // 2, 1) * sin).astype(BF16)
        v = v.astype(BF16)
        qkv_ref[0, :, cols] = q
        qkv_ref[1, :, cols] = k
        qkv_ref[2, :, cols] = v
        for b in range(2):
            rows = slice(b * half, (b + 1) * half)
            keys = (b + 1) * half
            scores = dot(q[rows], k[:keys], NT) * scale
            at = lax.broadcasted_iota(jnp.int32, scores.shape, 0) + b * half
            to = lax.broadcasted_iota(jnp.int32, scores.shape, 1)
            scores = jnp.where(at >= to, scores, -1000000000.0)
            top = jnp.max(scores, -1, keepdims=True)
            weights = jnp.exp(scores - top)
            total = jnp.sum(weights, -1, keepdims=True)
            lse_ref[h, rows, :] = jnp.broadcast_to(top + jnp.log(total), (half, HEAD))
            low = (weights * (1.0 / total)).astype(BF16)
            mixed_ref[rows, pl.ds(pl.multiple_of((g * heads + h) * HEAD, HEAD), HEAD)] = dot(low, v[:keys]).astype(BF16)

    @pl.when(g == steps - 1)
    def _():
        core = lax.rem(lax.axis_index("mp"), 2)
        for ref, c in ((other_ref, 1 - core), (mine_ref, core)):
            rows = pl.ds(pl.multiple_of(c * half, half), half)
            ref[...] = dot(mixed_ref[rows, :], wout_ref[...]).astype(BF16)


def attend(tokens, gain, w3, cos, sin, w_out):
    length, model = tokens.shape
    local = w3.shape[2]
    local_heads = local // HEAD
    heads = 2 if local_heads % 2 == 0 else 1
    steps = local_heads // heads
    wide = heads * HEAD
    full = lambda *shape: pl.BlockSpec(shape, lambda g: (0,) * len(shape))
    return pl.pallas_call(
        partial(attend_kernel, heads=heads, steps=steps),
        grid=(steps,),
        in_specs=[
            full(length, model), full(1, model),
            pl.BlockSpec((3, model, wide), lambda g: (0, 0, g)),
            full(length, HEAD), full(length, HEAD), full(local, model),
        ],
        out_specs=[
            full(length // 2, model), full(length // 2, model), full(length, model),
            pl.BlockSpec((3, length, wide), lambda g: (0, 0, g)),
            pl.BlockSpec((heads, length, HEAD), lambda g: (g, 0, 0)),
            full(length, local),
        ],
        out_shape=[
            jax.ShapeDtypeStruct((length // 2, model), BF16),
            jax.ShapeDtypeStruct((length // 2, model), BF16),
            jax.ShapeDtypeStruct((length, model), BF16),
            jax.ShapeDtypeStruct((3, length, local), BF16),
            jax.ShapeDtypeStruct((local_heads, length, HEAD), F32),
            jax.ShapeDtypeStruct((length, local), BF16),
        ],
        compiler_params=params(),
        cost_estimate=cost(2 * length * model * local * 4 + 4 * length * length * local,
                           2 * (2 * length * model + 4 * model * local), length * length * local_heads),
        name="attend",
    )(tokens, gain, w3, cos, sin, w_out)


def attend_back_kernel(ga_ref, normed_ref, qkv_ref, lse_ref, mixed_ref, wout_ref, w_ref, cos_ref, sin_ref,
                       *rest, heads, steps, deps):
    grad_ref, first_ref, acc_ref = rest[deps:]
    g = pl.program_id(0)
    length = ga_ref.shape[0]
    half = length // 2
    scale = HEAD ** -0.5
    cos, sin = cos_ref[...], sin_ref[...]
    ga = ga_ref[...]
    gmixed = dot(ga, wout_ref[...], NT).astype(BF16)
    gproj = [[], [], []]
    for h in range(heads):
        cols = slice(h * HEAD, (h + 1) * HEAD)
        q, k, v = (qkv_ref[c, :, cols] for c in range(3))
        gm = gmixed[:, cols]
        gq, gk, gv = [], [None, None], [None, None]
        for b in range(2):
            rows = slice(b * half, (b + 1) * half)
            keys = (b + 1) * half
            scores = dot(q[rows], k[:keys], NT) * scale
            at = lax.broadcasted_iota(jnp.int32, scores.shape, 0) + b * half
            to = lax.broadcasted_iota(jnp.int32, scores.shape, 1)
            probs = jnp.where(at >= to, jnp.exp(scores - lse_ref[h, rows, :1]), 0.0)
            gprobs = dot(gm[rows], v[:keys], NT)
            gscores = probs * (gprobs - jnp.sum(gprobs * probs, -1, keepdims=True))
            gs = gscores.astype(BF16)
            low_probs = probs.astype(BF16)
            gq.append(dot(gs, k[:keys]) * scale)
            for j in range(b + 1):
                part = slice(j * half, (j + 1) * half)
                a = dot(gs[:, part], q[rows], TN) * scale
                c = dot(low_probs[:, part], gm[rows], TN)
                gk[j] = a if gk[j] is None else gk[j] + a
                gv[j] = c if gv[j] is None else gv[j] + c
        gq = jnp.concatenate(gq, 0)
        gk = jnp.concatenate(gk, 0)
        gv = jnp.concatenate(gv, 0)
        gproj[0].append((gq * cos - pltpu.roll(gq, HEAD // 2, 1) * sin).astype(BF16))
        gproj[1].append((gk * cos - pltpu.roll(gk, HEAD // 2, 1) * sin).astype(BF16))
        gproj[2].append(gv.astype(BF16))
    gproj = [jnp.concatenate(p, 1) for p in gproj]

    @pl.when(g == 0)
    def _():
        acc_ref[...] = jnp.zeros_like(acc_ref)

    grad_ref[3] = dot(ga, mixed_ref[...], TN).astype(BF16)
    for c in range(3):
        grad_ref[c] = dot(normed_ref[...], gproj[c], TN).astype(BF16)
        acc_ref[...] += dot(gproj[c], w_ref[c], NT)

    @pl.when(g == steps - 1)
    def _():
        first_ref[...] = acc_ref[...].astype(BF16)


def attend_back(ga, normed, qkv, lse, mixed, w_out, w3, cos, sin, deps=()):
    length, model = ga.shape
    local = w3.shape[2]
    local_heads = local // HEAD
    heads = 2 if local_heads % 2 == 0 else 1
    steps = local_heads // heads
    wide = heads * HEAD
    full = lambda *shape: pl.BlockSpec(shape, lambda g: (0,) * len(shape))
    return pl.pallas_call(
        partial(attend_back_kernel, heads=heads, steps=steps, deps=len(deps)),
        grid=(steps,),
        in_specs=[
            full(length, model), full(length, model),
            pl.BlockSpec((3, length, wide), lambda g: (0, 0, g)),
            pl.BlockSpec((heads, length, HEAD), lambda g: (g, 0, 0)),
            pl.BlockSpec((length, wide), lambda g: (0, g)),
            pl.BlockSpec((wide, model), lambda g: (g, 0)),
            pl.BlockSpec((3, model, wide), lambda g: (0, 0, g)),
            full(length, HEAD), full(length, HEAD),
        ] + [pl.BlockSpec(memory_space=pl.ANY)] * len(deps),
        out_specs=[pl.BlockSpec((4, model, wide), lambda g: (0, 0, g)), full(length, model)],
        out_shape=[
            jax.ShapeDtypeStruct((4, model, local), BF16),
            jax.ShapeDtypeStruct((length, model), BF16),
        ],
        scratch_shapes=[pltpu.VMEM((length, model), F32)],
        compiler_params=params(),
        cost_estimate=cost(2 * length * model * local * 8 + 10 * length * length * local,
                           2 * (4 * length * model + 8 * model * local), length * length * local_heads),
        name="attend_back",
    )(ga, normed, qkv, lse, mixed, w_out, w3, cos, sin, *deps)


def own_grad_kernel(sent_ref, cot_ref, bucket_ref, gate_ref, unsort_ref, up_ref, down_ref, *rest, row_bounds, deps):
    mine_ref, other_ref, act_ref, acc_ref = rest[deps:]
    level = pl.program_id(0)
    for q, rows in enumerate(row_bounds):
        @pl.when(level == q)
        def _(q=q, rows=rows):
            keep = bucket_ref[:rows, :1] >= q
            pre = dot(sent_ref[:rows], up_ref[0])
            active = jnp.where(keep, jnp.maximum(pre, 0.0), 0.0)
            act_ref[0, :rows] = (active * active).astype(BF16)
            gact = dot(cot_ref[:rows], down_ref[0], NT)
            gpre = (gact * (2.0 * gate_ref[:rows, :1]) * active).astype(BF16)
            s = dot(gpre, up_ref[0], NT)
            if q == 0:
                acc_ref[...] = s
            else:
                acc_ref[:rows] += s
            if q == len(row_bounds) - 1:
                half = mine_ref.shape[0]
                total = acc_ref[...].astype(BF16)
                other_ref[...] = dot(unsort_ref[half:], total).astype(BF16)
                mine_ref[...] = dot(unsort_ref[:half], total).astype(BF16)


def own_grad(sent, cot, bucket, gate, unsort, w_up, w_down, row_bounds, deps=()):
    length, model = sent.shape
    levels, _, hidden = w_up.shape
    full = lambda *shape: pl.BlockSpec(shape, lambda q: (0,) * len(shape))
    return pl.pallas_call(
        partial(own_grad_kernel, row_bounds=tuple(row_bounds), deps=len(deps)),
        grid=(levels,),
        in_specs=[
            full(length, model), full(length, model), full(length, 128), full(length, 128), full(length, length),
            pl.BlockSpec((1, model, hidden), lambda q: (q, 0, 0)),
            pl.BlockSpec((1, hidden, model), lambda q: (q, 0, 0)),
        ] + [pl.BlockSpec(memory_space=pl.ANY)] * len(deps),
        out_specs=[full(length // 2, model)] * 2 + [pl.BlockSpec((1, length, hidden), lambda q: (q, 0, 0))],
        out_shape=[jax.ShapeDtypeStruct((length // 2, model), BF16)] * 2
        + [jax.ShapeDtypeStruct((levels, length, hidden), BF16)],
        scratch_shapes=[pltpu.VMEM((length, model), F32)],
        compiler_params=params(),
        cost_estimate=cost(6 * sum(row_bounds) * model * hidden, 4 * levels * model * hidden + 6 * length * model),
        name="own_grad",
    )(sent, cot, bucket, gate, unsort, w_up, w_down, *deps)


def own_forward_kernel(act_ref, cot_ref, unsort_ref, down_ref, *rest, row_bounds, deps):
    ffn_ref, ggate_ref, acc_ref = rest[deps:]
    level = pl.program_id(0)
    for q, rows in enumerate(row_bounds):
        @pl.when(level == q)
        def _(q=q, rows=rows):
            f = dot(act_ref[0, :rows], down_ref[0])
            if q == 0:
                acc_ref[...] = f
            else:
                acc_ref[:rows] += f
            if q == len(row_bounds) - 1:
                total = acc_ref[...]
                ggate = jnp.sum(total * cot_ref[...].astype(F32), -1, keepdims=True)
                ggate_ref[...] = jnp.broadcast_to(ggate, ggate_ref.shape)
                ffn_ref[...] = dot(unsort_ref[...], total.astype(BF16)).astype(BF16)


def own_forward(act, cot, unsort, w_down, row_bounds, deps=()):
    length, model = cot.shape
    levels, hidden, _ = w_down.shape
    full = lambda *shape: pl.BlockSpec(shape, lambda q: (0,) * len(shape))
    return pl.pallas_call(
        partial(own_forward_kernel, row_bounds=tuple(row_bounds), deps=len(deps)),
        grid=(levels,),
        in_specs=[
            pl.BlockSpec((1, length, hidden), lambda q: (q, 0, 0)),
            full(length, model), full(length, length),
            pl.BlockSpec((1, hidden, model), lambda q: (q, 0, 0)),
        ] + [pl.BlockSpec(memory_space=pl.ANY)] * len(deps),
        out_specs=[full(length, model), full(length, 128)],
        out_shape=[jax.ShapeDtypeStruct((length, model), BF16), jax.ShapeDtypeStruct((length, 128), F32)],
        scratch_shapes=[pltpu.VMEM((length, model), F32)],
        compiler_params=params(),
        cost_estimate=cost(2 * sum(row_bounds) * model * hidden, 2 * levels * model * hidden + 6 * length * model),
        name="own_forward",
    )(act, cot, unsort, w_down, *deps)


AUX = 16


def gates_and_buckets(aux):
    row = lax.broadcasted_iota(jnp.int32, (AUX, 128), 0)
    gates = dot(aux, (row < 3).astype(BF16), TN)
    buckets = dot(aux, (row == 3).astype(BF16), TN)
    return gates, buckets


def weight_kernel(s_ref, c_ref, up_ref, down_ref, *refs, level, rows, group, carried, deps):
    gup_ref, gdown_ref, up_buf, down_buf, s_buf, aux_buf, c_buf, gup, gdown, sems = refs[carried + deps:]
    b = pl.program_id(0)
    steps = pl.num_programs(0)
    slices, piece = s_ref.shape[1], s_ref.shape[3]
    length = c_ref.shape[2]
    span = pl.ds(0, rows)

    def tokens_of(step, slot):
        out = []
        for j in range(group):
            block = step * group + j
            to = pl.ds(j * rows, rows)
            for m in range(slices):
                out.append((s_ref.at[block, m, span], s_buf.at[slot, to, pl.ds(m * piece, piece)]))
            for m in range(length // piece):
                out.append((s_ref.at[block, m, pl.ds(length, AUX)], aux_buf.at[slot, j, pl.ds(0, AUX), pl.ds(m * piece, piece)]))
        return [pltpu.make_async_copy(x, y, sems.at[slot, i]) for i, (x, y) in enumerate(out)]

    def cots_of(step, slot):
        out = []
        for j in range(group):
            block = step * group + j
            to = pl.ds(j * rows, rows)
            for m in range(slices):
                out.append((c_ref.at[block, m, span], c_buf.at[slot, to, pl.ds(m * piece, piece)]))
        return [pltpu.make_async_copy(x, y, sems.at[2 + slot, i]) for i, (x, y) in enumerate(out)]

    up_copy = pltpu.make_async_copy(up_ref.at[level], up_buf, sems.at[4, 0])
    down_copy = pltpu.make_async_copy(down_ref.at[level], down_buf, sems.at[4, 1])
    ends = [pltpu.make_async_copy(gup, gup_ref.at[level], sems.at[4, 2]),
            pltpu.make_async_copy(gdown, gdown_ref.at[level], sems.at[4, 3])]
    slot = lax.rem(b, 2)

    @pl.when(b == 0)
    def _():
        for c in [up_copy] + tokens_of(0, 0) + [down_copy] + cots_of(0, 0):
            c.start()

    @pl.when(b + 1 < steps)
    def _():
        for c in tokens_of(b + 1, 1 - slot) + cots_of(b + 1, 1 - slot):
            c.start()

    @pl.when(b == 0)
    def _():
        up_copy.wait()

    for c in tokens_of(b, slot):
        c.wait()
    columns = [gates_and_buckets(aux_buf[slot, j]) for j in range(group)]
    gate = jnp.concatenate([g[:rows, :1] for g, _ in columns], 0)
    keep = jnp.concatenate([k[:rows, :1] for _, k in columns], 0) >= level
    pre = dot(s_buf[slot], up_buf[...])
    active = jnp.where(keep, jnp.maximum(pre, 0.0), 0.0)
    act = (active * active * gate).astype(BF16)

    @pl.when(b == 0)
    def _():
        down_copy.wait()

    for c in cots_of(b, slot):
        c.wait()
    gact = dot(c_buf[slot], down_buf[...], NT)
    gpre = (gact * (2.0 * gate) * active).astype(BF16)

    @pl.when(b == 0)
    def _():
        gup[...] = dot(s_buf[slot], gpre, TN)
        gdown[...] = dot(act, c_buf[slot], TN)

    @pl.when(jnp.logical_and(b > 0, b < steps - 1))
    def _():
        gup[...] += dot(s_buf[slot], gpre, TN)
        gdown[...] += dot(act, c_buf[slot], TN)

    @pl.when(b == steps - 1)
    def _():
        gup[...] += dot(s_buf[slot], gpre, TN)
        ends[0].start()
        gdown[...] += dot(act, c_buf[slot], TN)
        ends[1].start()
        for c in ends:
            c.wait()


def weight_gradients(level, rows, sents, cots, w_up, w_down, carried, deps=()):
    levels, model, hidden = w_up.shape
    blocks, slices, length, piece = cots.shape
    group = max(1, min(4, 1024 // rows))
    while blocks % group or blocks // group < 2:
        group -= 1
    copies = group * (slices + length // piece)
    anywhere = pl.BlockSpec(memory_space=pl.ANY)
    return pl.pallas_call(
        partial(weight_kernel, level=level, rows=rows, group=group, carried=len(carried), deps=len(deps)),
        grid=(blocks // group,),
        in_specs=[anywhere] * (4 + len(carried) + len(deps)),
        out_specs=[anywhere] * 2,
        out_shape=[jax.ShapeDtypeStruct((levels, model, hidden), F32), jax.ShapeDtypeStruct((levels, hidden, model), F32)],
        input_output_aliases={4: 0, 5: 1} if carried else {},
        scratch_shapes=[
            pltpu.VMEM((model, hidden), BF16), pltpu.VMEM((hidden, model), BF16),
            pltpu.VMEM((2, group * rows, model), BF16), pltpu.VMEM((2, group, AUX, length), BF16),
            pltpu.VMEM((2, group * rows, model), BF16),
            pltpu.VMEM((model, hidden), F32), pltpu.VMEM((hidden, model), F32),
            pltpu.SemaphoreType.DMA((5, max(4, copies))),
        ],
        compiler_params=params(),
        cost_estimate=cost(8 * blocks * rows * model * hidden, 4 * blocks * length * model + 16 * model * hidden),
        name=f"weight_gradients_{level}",
    )(sents, cots, w_up, w_down, *carried, *deps)


def unpack_kernel(order_ref, *refs, count, carried):
    chunk_refs = refs[:count]
    qkv_ref, out_ref = refs[count + carried:]
    size = qkv_ref.shape[1]
    for k in range(count):
        @pl.when(pl.program_id(0) == k)
        def _(k=k):
            for c in range(3):
                qkv_ref[c] = chunk_refs[k][c * size:(c + 1) * size].astype(F32)
            out_ref[...] = chunk_refs[k][3 * size:4 * size].astype(F32).T


def unpack(order, chunks, size, total, carried=()):
    height, local = chunks[0].shape
    anywhere = pl.BlockSpec(memory_space=pl.ANY)
    count = len(chunks)
    return pl.pallas_call(
        partial(unpack_kernel, count=count, carried=len(carried)),
        grid_spec=pltpu.PrefetchScalarGridSpec(
            num_scalar_prefetch=1,
            grid=(count,),
            in_specs=[pl.BlockSpec((height, local), lambda b, o: (0, 0), pipeline_mode=pl.Buffered(1))] * count
            + [anywhere] * len(carried),
            out_specs=[
                pl.BlockSpec((3, size, local), lambda b, o: (0, o[b], 0)),
                pl.BlockSpec((local, size), lambda b, o: (0, o[b])),
            ],
        ),
        out_shape=[
            jax.ShapeDtypeStruct((3, total * size, local), F32),
            jax.ShapeDtypeStruct((local, total * size), F32),
        ],
        input_output_aliases={count + 1: 0, count + 2: 1} if carried else {},
        compiler_params=params(),
        cost_estimate=cost(0, 24 * count * size * local),
        name="unpack_some" if not carried else "unpack_rest",
    )(order, *chunks, *carried)


def add_kernel(*refs, count):
    total = refs[0][...].astype(F32)
    for ref in refs[1:count]:
        total = total + ref[...].astype(F32)
    refs[-1][...] = total.astype(BF16)


def add_rows(parts, deps=()):
    rows, columns = parts[0].shape
    block = pl.BlockSpec((rows // 4, columns), lambda i: (i, 0))
    return pl.pallas_call(
        partial(add_kernel, count=len(parts)),
        grid=(4,),
        in_specs=[block] * len(parts) + [pl.BlockSpec(memory_space=pl.ANY)] * len(deps),
        out_specs=block,
        out_shape=jax.ShapeDtypeStruct((rows, columns), BF16),
        compiler_params=params(),
        cost_estimate=cost(rows * columns, 6 * rows * columns),
        name="add_rows",
    )(*parts, *deps)


def pass_kernel(*refs):
    pass


def after(arrays, deps):
    anywhere = pl.BlockSpec(memory_space=pl.ANY)
    return pl.pallas_call(
        pass_kernel,
        in_specs=[anywhere] * (len(arrays) + len(deps)),
        out_specs=[anywhere] * len(arrays),
        out_shape=[jax.ShapeDtypeStruct(x.shape, x.dtype) for x in arrays],
        input_output_aliases={i: i for i in range(len(arrays))},
        compiler_params=params(),
        cost_estimate=cost(0, 0),
        name="after",
    )(*arrays, *deps)


def join_kernel(index_ref, right_local, left_local, right_ref, left_ref, *rest, cut, deps):
    right_out, left_out = rest[deps:]
    size = right_local.shape[1]
    if right_ref.shape[1] == size:
        right_out[0] = (right_local[0].astype(F32) + right_ref[0].astype(F32)).astype(BF16)
        left_out[0] = (left_local[0].astype(F32) + left_ref[0].astype(F32)).astype(BF16)
    else:
        right_out[0, :cut] = (right_local[0, :cut].astype(F32) + right_ref[0].astype(F32)).astype(BF16)
        right_out[0, cut:] = right_local[0, cut:]
        left_out[0, :cut] = left_local[0, :cut]
        left_out[0, cut:] = (left_local[0, cut:].astype(F32) + left_ref[0].astype(F32)).astype(BF16)


def join(grads, indices, right, left, size, deps=()):
    kinds, _, local = grads.shape
    arrived = right.shape[1]
    out = pl.BlockSpec((1, size, local), lambda i, o: (i, 0, 0))
    return pl.pallas_call(
        partial(join_kernel, cut=size // 2, deps=len(deps)),
        grid_spec=pltpu.PrefetchScalarGridSpec(
            num_scalar_prefetch=1,
            grid=(kinds,),
            in_specs=[
                pl.BlockSpec((1, size, local), lambda i, o: (i, o[0], 0)),
                pl.BlockSpec((1, size, local), lambda i, o: (i, o[1], 0)),
                pl.BlockSpec((1, arrived, local), lambda i, o: (i, 0, 0)),
                pl.BlockSpec((1, arrived, local), lambda i, o: (i, 0, 0)),
            ] + [pl.BlockSpec(memory_space=pl.ANY)] * len(deps),
            out_specs=[out, out],
        ),
        out_shape=[jax.ShapeDtypeStruct((kinds, size, local), BF16)] * 2,
        compiler_params=params(),
        cost_estimate=cost(2 * kinds * size * local, 12 * kinds * size * local),
        name="join",
    )(indices, grads, grads, right, left, *deps)


def join_own_kernel(index_ref, local_ref, right_ref, left_ref, extra_ref, *rest):
    kinds, size, _ = right_ref.shape
    for c in range(kinds):
        total = local_ref[c].astype(F32) + right_ref[c].astype(F32) + left_ref[c].astype(F32)
        rest[-1][c * size:(c + 1) * size] = total.astype(BF16)
    rest[-1][kinds * size:] = extra_ref[...]


def join_own(grads, indices, right, left, extra, deps=()):
    kinds, size, local = right.shape
    block = pl.BlockSpec((kinds, size, local), lambda i, o: (0, 0, 0))
    height = kinds * size + extra.shape[0]
    return pl.pallas_call(
        join_own_kernel,
        grid_spec=pltpu.PrefetchScalarGridSpec(
            num_scalar_prefetch=1,
            grid=(1,),
            in_specs=[pl.BlockSpec((kinds, size, local), lambda i, o: (0, o[0], 0)), block, block,
                      pl.BlockSpec(extra.shape, lambda i, o: (0, 0))]
            + [pl.BlockSpec(memory_space=pl.ANY)] * len(deps),
            out_specs=pl.BlockSpec((height, local), lambda i, o: (0, 0)),
        ),
        out_shape=jax.ShapeDtypeStruct((height, local), BF16),
        compiler_params=params(),
        cost_estimate=cost(2 * kinds * size * local, 8 * kinds * size * local),
        name="join_own",
    )(indices, grads, right, left, extra, *deps)


def ring_order(count):
    nz = 4 if count % 4 == 0 else 1
    ny = count // nz
    if nz == 1 or ny % 2:
        return list(range(count))
    order = [(z, 0) for z in range(nz)]
    for y in range(1, ny):
        line = list(range(1, nz))
        order += [(z, y) for z in (reversed(line) if y % 2 else line)]
    order += [(0, y) for y in range(ny - 1, 0, -1)]
    return [z * ny + y for z, y in order]


class Ring:
    def __init__(self):
        self.log = []
        self.count = lax.axis_size("dp")
        self.order = ring_order(self.count)
        n = self.count
        place = [0] * n
        for p, d in enumerate(self.order):
            place[d] = p
        self.position = jnp.array(place, jnp.int32)[lax.axis_index("dp")]
        self.right = [(self.order[p], self.order[(p + 1) % n]) for p in range(n)]
        self.left = [(self.order[(p + 1) % n], self.order[p]) for p in range(n)]

    def to_right(self, x):
        out = lax.ppermute(x, "dp", self.right)
        self.log.append(out)
        return out

    def to_left(self, x):
        out = lax.ppermute(x, "dp", self.left)
        self.log.append(out)
        return out

    def logged(self, f, *args):
        self.log = []
        out = f(*args)
        pairs = [tuple(self.log[i:i + 2]) for i in range(0, len(self.log), 2)]
        self.log = []
        return out, pairs

    def gather(self, x, axis):
        out = [x]
        r = l = x
        for _ in range(self.count // 2 - 1):
            r, l = self.to_right(r), self.to_left(l)
            out += [r, l]
        size = x.shape[axis]
        cut = size // 32 * 16
        first = self.to_right(lax.slice_in_dim(r, 0, cut, axis=axis))
        second = self.to_left(lax.slice_in_dim(l, cut, size, axis=axis))
        out.append(jnp.concatenate([first, second], axis))
        return out

    def offsets(self):
        out = [0]
        for k in range(1, self.count // 2):
            out += [-k, k]
        return out + [self.count // 2]

    def indices(self):
        return [(self.position + k) % self.count for k in self.offsets()]

    def reduce_start(self, x):
        size = x.shape[1] // self.count
        cut = size // 2
        far = self.count // 2
        at = ((self.position + far) % self.count) * size
        r = lax.dynamic_slice_in_dim(x, at, cut, axis=1)
        l = lax.dynamic_slice_in_dim(x, at + cut, cut, axis=1)
        return (self.to_right(r), self.to_left(l)), (r, l)

    def reduce_step(self, x, arrived, k, deps=()):
        indices = jnp.stack([(self.position + k) % self.count, (self.position - k) % self.count]).astype(jnp.int32)
        r, l = join(x, indices, *arrived, x.shape[1] // self.count, deps)
        return (self.to_right(r), self.to_left(l)), (r, l)

    def reduce_end(self, x, arrived, extra, deps=()):
        return join_own(x, self.position[None].astype(jnp.int32), *arrived, extra, deps)


def core_swap(x):
    n = lax.axis_size("mp")
    return lax.ppermute(x, "mp", [(i, i ^ 1) for i in range(n)])


def sum_over_x(x):
    n = lax.axis_size("mp") // 2
    index = lax.axis_index("mp")
    parts = [x] + [
        lax.ppermute(x, "mp", [(i, (i + 2 * k) % (2 * n)) for i in range(2 * n)]) for k in range(1, n)
    ]
    if n == 1:
        return x.astype(F32)
    if n == 2:
        return parts[0].astype(F32) + parts[1].astype(F32)
    stacked = jnp.stack(parts)
    total = None
    for j in range(n):
        term = lax.dynamic_index_in_dim(stacked, (index // 2 - j) % n, 0, keepdims=False).astype(F32)
        total = term if total is None else total + term
    return total


def on_device(tokens, gain_first, w_qkv, w_out, gain_second, router, w_up, w_down, slot, cotangent):
    length, model = tokens.shape
    buckets = w_up.shape[0]
    devices_dp = lax.axis_size("dp")
    groups = devices_dp // buckets
    capacity = length * 5 // (4 * devices_dp)
    row_bounds = [min(length, (buckets - level) * groups * capacity) for level in range(buckets)]
    ring = Ring()
    core = lax.axis_index("mp") % 2
    half = length // 2

    bucket_ids = slot // capacity // groups
    places = jnp.arange(length, dtype=jnp.int32)
    key = (buckets - 1 - bucket_ids) * length + places
    rank = jnp.sum((key[None, :] < key[:, None]).astype(jnp.int32), 1)
    rank_here = jnp.roll(rank, -core * half)
    sort_rows = places[:, None] == rank[None, :]
    sort_here = places[:, None] == rank_here[None, :]
    sort_low = sort_here.astype(BF16)
    unsort_low = (rank_here[:, None] == places[None, :]).astype(BF16)
    bucket_sorted = jnp.sum(jnp.where(sort_rows, bucket_ids[None, :], 0), 1)

    def part_of(x, c, axis=0):
        size = x.shape[axis] // 2
        return lax.dynamic_slice_in_dim(x, c * size, size, axis=axis)

    def own_rows(x):
        return part_of(x, core)

    def other_rows(x):
        return part_of(x, 1 - core)

    def joined(mine, other):
        return jnp.concatenate([jnp.where(core == 0, mine, other), jnp.where(core == 0, other, mine)], 0)

    cot_sorted = dot(sort_rows.astype(BF16), cotangent).astype(BF16)
    slices = lax.axis_size("mp")
    piece = model // slices
    me = lax.axis_index("mp")
    cot_piece = lax.dynamic_slice_in_dim(cot_sorted, me * piece, piece, axis=1)
    cots = lax.all_gather(cot_piece, ("dp", "mp"), axis=0).reshape(devices_dp, slices, length, piece)

    w3 = jnp.transpose(w_qkv, (1, 0, 2))
    cos, sin = rotary_table(length, HEAD)
    part_mine, part_other, normed_low, qkv, lse, mixed = attend(tokens, gain_first[None, :], w3, cos, sin, w_out)
    attn_rows = add_rows([part_mine, core_swap(part_other)], (cot_piece,))
    attn = sum_over_x(attn_rows)

    resid = own_rows(tokens).astype(F32) + attn
    inv = lax.rsqrt(jnp.mean(resid * resid, -1, keepdims=True) + EPSILON)
    xhat = resid * inv
    normed_second = xhat * gain_second
    logits = jnp.dot(normed_second, router, precision=HIGHEST)
    prob = jax.nn.softmax(logits, axis=-1)
    onehot = (own_rows(bucket_ids)[:, None] == jnp.arange(buckets)[None, :]).astype(F32)
    gate = buckets * jnp.sum(prob * onehot, -1)
    sent_half = normed_second.astype(BF16)
    sent_both = jnp.concatenate([sent_half, core_swap(sent_half)], 0)
    gate_both = jnp.concatenate([gate, core_swap(gate)], 0)
    gate_sorted = jnp.sum(jnp.where(sort_here, gate_both[None, :], 0.0), 1)

    sent_sorted = dot(sort_low, sent_both).astype(BF16)

    gate_1 = low(gate_sorted)
    gate_2 = low(gate_sorted - gate_1.astype(F32))
    gate_3 = low(gate_sorted - gate_1.astype(F32) - gate_2.astype(F32))
    aux = jnp.stack([gate_1, gate_2, gate_3, bucket_sorted.astype(BF16)] + [jnp.zeros_like(gate_1)] * (AUX - 4))
    sent_piece = jnp.concatenate([
        lax.dynamic_slice_in_dim(sent_sorted, me * piece, piece, axis=1),
        lax.dynamic_slice_in_dim(aux, (me % (length // piece)) * piece, piece, axis=1)], 0)
    sents = lax.all_gather(sent_piece, ("dp", "mp"), axis=0).reshape(devices_dp, slices, length + AUX, piece)

    wide = lambda x: jnp.broadcast_to(x[:, None], (length, 128))
    gsent_mine, gsent_other, act = own_grad(
        sent_sorted, cot_sorted, wide(bucket_sorted), wide(gate_sorted), unsort_low, w_up, w_down, row_bounds,
        (sent_piece,))
    gsent_rows = add_rows([gsent_mine, core_swap(gsent_other)])
    grad_sent = sum_over_x(gsent_rows).astype(BF16).astype(F32)
    ffn_part, ggate_part = own_forward(
        act, cot_sorted, sort_rows.astype(BF16).T, w_down, row_bounds, (gsent_rows,))
    ffn_rows = sum_over_x(add_rows([own_rows(ffn_part), core_swap(other_rows(ffn_part))])).astype(BF16).astype(F32)
    ggate_part = jnp.sum(jnp.where(sort_rows, ggate_part[:, :1], 0.0), 0)
    grad_gate = ggate_part + core_swap(ggate_part)
    grad_gate = sum_over_x(own_rows(grad_gate))

    grad_output = own_rows(cotangent).astype(F32)
    output_half = (resid + gate[:, None] * ffn_rows).astype(BF16)
    grad_prob = buckets * grad_gate[:, None] * onehot
    grad_logits = prob * (grad_prob - jnp.sum(grad_prob * prob, -1, keepdims=True))
    grad_router = jnp.dot(normed_second.T, grad_logits, precision=HIGHEST)
    grad_second = grad_sent + jnp.dot(grad_logits, router.T, precision=HIGHEST)
    grad_gain_second = jnp.sum(grad_second * xhat, 0)
    scaled = grad_second * gain_second
    grad_resid = grad_output + inv * (scaled - xhat * jnp.mean(scaled * xhat, -1, keepdims=True))
    ga_half = low(grad_resid)
    grad_attn = joined(ga_half, core_swap(ga_half))

    grads, first_part = attend_back(
        grad_attn, normed_low, qkv, lse, mixed, w_out, w3, cos, sin)

    grad_first = sum_over_x(add_rows([own_rows(first_part), core_swap(other_rows(first_part))])).astype(BF16).astype(F32)
    source = own_rows(tokens).astype(F32)
    inv_first = lax.rsqrt(jnp.mean(source * source, -1, keepdims=True) + EPSILON)
    xhat_first = source * inv_first
    grad_gain_first = jnp.sum(grad_first * xhat_first, 0)
    scaled_first = grad_first * gain_first
    grad_source = inv_first * (scaled_first - xhat_first * jnp.mean(scaled_first * xhat_first, -1, keepdims=True))
    tokens_half = (grad_source + grad_resid).astype(BF16)
    output = joined(output_half, core_swap(output_half))
    grad_tokens = joined(tokens_half, core_swap(tokens_half))
    small = jnp.concatenate([grad_router.T, grad_gain_second[None], grad_gain_first[None]], 0)
    small = jnp.pad(small, ((0, -small.shape[0] % 8), (0, 0)))
    local = w3.shape[2]
    extra = low(small + core_swap(small)).reshape(-1, local)

    carried = ()
    arrived, sending = ring.reduce_start(grads)
    far = devices_dp // 2
    chunks = None
    step = 0

    def advance(step, arrived, deps):
        nonlocal chunks
        if step < far - 1:
            return ring.reduce_step(grads, arrived, far - 1 - step, deps)
        if step == far - 1:
            chunks = [ring.reduce_end(grads, arrived, extra, deps)]
            r = l = chunks[0]
        else:
            r, l = after(arrived, deps) if deps else arrived
            chunks.extend([r, l])
        if step < 2 * far - 2:
            sending = (r, l)
            r, l = ring.to_right(r), ring.to_left(l)
        else:
            cut = r.shape[0] // 32 * 16
            sending = (r[:cut], l[cut:])
            r, l = ring.to_right(sending[0]), ring.to_left(sending[1])
            chunks.append(jnp.concatenate([r, l], 0))
        return (r, l), sending

    steps = 2 * far - 1
    while step < far - 1:
        arrived, sending = advance(step, arrived, ())
        step += 1
    for level in range(buckets):
        carried = weight_gradients(level, row_bounds[level], sents, cots, w_up, w_down, tuple(carried), sending)
        if step < steps:
            arrived, sending = advance(step, arrived, (carried[0],))
            step += 1
        else:
            sending = ()
    while step < steps:
        arrived, sending = advance(step, arrived, ())
        step += 1
    grad_up, grad_down = carried
    order = jnp.stack(ring.indices()).astype(jnp.int32)
    size = model // devices_dp
    unpacked = unpack(order[:-1], chunks[:-1], size, devices_dp)
    grad_wqkv, grad_wout = unpack(order[-1:], chunks[-1:], size, devices_dp, unpacked)
    terms = jnp.stack([x[4 * size:] for x in chunks])
    by_place = jnp.zeros((devices_dp,), jnp.int32).at[order].set(jnp.arange(devices_dp, dtype=jnp.int32))
    small = jnp.sum(terms[by_place].astype(F32), 0).reshape(small.shape)

    return (
        output,
        grad_tokens,
        small[buckets + 1],
        jnp.transpose(grad_wqkv, (1, 0, 2)),
        grad_wout,
        small[buckets],
        small[:buckets].T,
        grad_up,
        grad_down,
    )


def solution(mesh):
    placed = (
        P("dp", None),
        P(),
        P(None, None, "mp"),
        P("mp", None),
        P(),
        P(),
        P(None, None, "mp"),
        P(None, "mp", None),
        P("dp"),
        P("dp", None),
    )
    return jax.shard_map(
        on_device,
        mesh=mesh,
        in_specs=placed,
        out_specs=(
            P("dp", None),
            P("dp", None),
            P(),
            P(None, None, "mp"),
            P("mp", None),
            P(),
            P(),
            P(None, None, "mp"),
            P(None, "mp", None),
        ),
        check_vma=False,
    )
```

```python
from functools import partial

import jax
import jax.numpy as jnp
from jax import lax
from jax.experimental import pallas as pl
from jax.experimental.pallas import tpu as pltpu
from jax.sharding import PartitionSpec as P

HEAD = 128
HIGHEST = lax.Precision.HIGHEST
EPSILON = 1e-05
F32 = jnp.float32
BF16 = jnp.bfloat16
VMEM_LIMIT = 56 * 1024 * 1024
COST = 4
NN = (((1,), (0,)), ((), ()))
NT = (((1,), (1,)), ((), ()))
TN = (((0,), (0,)), ((), ()))


def dot(a, b, dims=NN):
    return lax.dot_general(a, b, dims, preferred_element_type=F32)


def low(x):
    return lax.reduce_precision(x, 8, 7).astype(BF16)


def params():
    return pltpu.CompilerParams(vmem_limit_bytes=VMEM_LIMIT)


def cost(flops, nbytes, transcendentals=0):
    return pl.CostEstimate(flops=flops // COST, bytes_accessed=nbytes // COST, transcendentals=transcendentals // COST)


def rotary_table(length, head_size):
    position = jnp.arange(length, dtype=F32)
    inverse = 10000.0 ** (-jnp.arange(0, head_size, 2, dtype=F32) / head_size)
    angles = position[:, None] * inverse[None, :]
    angles = jnp.concatenate([angles, angles], -1)
    sign = jnp.where(jnp.arange(head_size) < head_size // 2, -1.0, 1.0)
    return jnp.cos(angles), jnp.sin(angles) * sign


def attend_kernel(x_ref, gain_ref, w_ref, cos_ref, sin_ref, wout_ref,
                  mine_ref, other_ref, normed_ref, qkv_ref, lse_ref, mixed_ref, *, heads, steps):
    g = pl.program_id(0)
    length = x_ref.shape[0]
    half = length // 2
    scale = HEAD ** -0.5

    @pl.when(g == 0)
    def _():
        values = x_ref[...].astype(F32)
        inv = lax.rsqrt(jnp.mean(values * values, -1, keepdims=True) + EPSILON)
        normed_ref[...] = (values * inv * gain_ref[...]).astype(BF16)

    normed = normed_ref[...]
    cos, sin = cos_ref[...], sin_ref[...]
    projected = [dot(normed, w_ref[c]) for c in range(3)]
    for h in range(heads):
        cols = slice(h * HEAD, (h + 1) * HEAD)
        q, k, v = (p[:, cols] for p in projected)
        q = (q * cos + pltpu.roll(q, HEAD // 2, 1) * sin).astype(BF16)
        k = (k * cos + pltpu.roll(k, HEAD // 2, 1) * sin).astype(BF16)
        v = v.astype(BF16)
        qkv_ref[0, :, cols] = q
        qkv_ref[1, :, cols] = k
        qkv_ref[2, :, cols] = v
        for b in range(2):
            rows = slice(b * half, (b + 1) * half)
            keys = (b + 1) * half
            scores = dot(q[rows], k[:keys], NT) * scale
            at = lax.broadcasted_iota(jnp.int32, scores.shape, 0) + b * half
            to = lax.broadcasted_iota(jnp.int32, scores.shape, 1)
            scores = jnp.where(at >= to, scores, -1000000000.0)
            top = jnp.max(scores, -1, keepdims=True)
            weights = jnp.exp(scores - top)
            total = jnp.sum(weights, -1, keepdims=True)
            lse_ref[h, rows, :] = jnp.broadcast_to(top + jnp.log(total), (half, HEAD))
            low = (weights * (1.0 / total)).astype(BF16)
            mixed_ref[rows, pl.ds(pl.multiple_of((g * heads + h) * HEAD, HEAD), HEAD)] = dot(low, v[:keys]).astype(BF16)

    @pl.when(g == steps - 1)
    def _():
        core = lax.rem(lax.axis_index("mp"), 2)
        for ref, c in ((other_ref, 1 - core), (mine_ref, core)):
            rows = pl.ds(pl.multiple_of(c * half, half), half)
            ref[...] = dot(mixed_ref[rows, :], wout_ref[...]).astype(BF16)


def attend(tokens, gain, w3, cos, sin, w_out):
    length, model = tokens.shape
    local = w3.shape[2]
    local_heads = local // HEAD
    heads = 2 if local_heads % 2 == 0 else 1
    steps = local_heads // heads
    wide = heads * HEAD
    full = lambda *shape: pl.BlockSpec(shape, lambda g: (0,) * len(shape))
    return pl.pallas_call(
        partial(attend_kernel, heads=heads, steps=steps),
        grid=(steps,),
        in_specs=[
            full(length, model), full(1, model),
            pl.BlockSpec((3, model, wide), lambda g: (0, 0, g)),
            full(length, HEAD), full(length, HEAD), full(local, model),
        ],
        out_specs=[
            full(length // 2, model), full(length // 2, model), full(length, model),
            pl.BlockSpec((3, length, wide), lambda g: (0, 0, g)),
            pl.BlockSpec((heads, length, HEAD), lambda g: (g, 0, 0)),
            full(length, local),
        ],
        out_shape=[
            jax.ShapeDtypeStruct((length // 2, model), BF16),
            jax.ShapeDtypeStruct((length // 2, model), BF16),
            jax.ShapeDtypeStruct((length, model), BF16),
            jax.ShapeDtypeStruct((3, length, local), BF16),
            jax.ShapeDtypeStruct((local_heads, length, HEAD), F32),
            jax.ShapeDtypeStruct((length, local), BF16),
        ],
        compiler_params=params(),
        cost_estimate=cost(2 * length * model * local * 4 + 4 * length * length * local,
                           2 * (2 * length * model + 4 * model * local), length * length * local_heads),
        name="attend",
    )(tokens, gain, w3, cos, sin, w_out)


def attend_back_kernel(ga_ref, normed_ref, qkv_ref, lse_ref, mixed_ref, wout_ref, w_ref, cos_ref, sin_ref,
                       *rest, heads, steps, deps):
    grad_ref, first_ref, acc_ref = rest[deps:]
    g = pl.program_id(0)
    length = ga_ref.shape[0]
    half = length // 2
    scale = HEAD ** -0.5
    cos, sin = cos_ref[...], sin_ref[...]
    ga = ga_ref[...]
    gmixed = dot(ga, wout_ref[...], NT).astype(BF16)
    gproj = [[], [], []]
    for h in range(heads):
        cols = slice(h * HEAD, (h + 1) * HEAD)
        q, k, v = (qkv_ref[c, :, cols] for c in range(3))
        gm = gmixed[:, cols]
        gq, gk, gv = [], [None, None], [None, None]
        for b in range(2):
            rows = slice(b * half, (b + 1) * half)
            keys = (b + 1) * half
            scores = dot(q[rows], k[:keys], NT) * scale
            at = lax.broadcasted_iota(jnp.int32, scores.shape, 0) + b * half
            to = lax.broadcasted_iota(jnp.int32, scores.shape, 1)
            probs = jnp.where(at >= to, jnp.exp(scores - lse_ref[h, rows, :1]), 0.0)
            gprobs = dot(gm[rows], v[:keys], NT)
            gscores = probs * (gprobs - jnp.sum(gprobs * probs, -1, keepdims=True))
            gs = gscores.astype(BF16)
            low_probs = probs.astype(BF16)
            gq.append(dot(gs, k[:keys]) * scale)
            for j in range(b + 1):
                part = slice(j * half, (j + 1) * half)
                a = dot(gs[:, part], q[rows], TN) * scale
                c = dot(low_probs[:, part], gm[rows], TN)
                gk[j] = a if gk[j] is None else gk[j] + a
                gv[j] = c if gv[j] is None else gv[j] + c
        gq = jnp.concatenate(gq, 0)
        gk = jnp.concatenate(gk, 0)
        gv = jnp.concatenate(gv, 0)
        gproj[0].append((gq * cos - pltpu.roll(gq, HEAD // 2, 1) * sin).astype(BF16))
        gproj[1].append((gk * cos - pltpu.roll(gk, HEAD // 2, 1) * sin).astype(BF16))
        gproj[2].append(gv.astype(BF16))
    gproj = [jnp.concatenate(p, 1) for p in gproj]

    @pl.when(g == 0)
    def _():
        acc_ref[...] = jnp.zeros_like(acc_ref)

    grad_ref[3] = dot(ga, mixed_ref[...], TN).astype(BF16)
    for c in range(3):
        grad_ref[c] = dot(normed_ref[...], gproj[c], TN).astype(BF16)
        acc_ref[...] += dot(gproj[c], w_ref[c], NT)

    @pl.when(g == steps - 1)
    def _():
        first_ref[...] = acc_ref[...].astype(BF16)


def attend_back(ga, normed, qkv, lse, mixed, w_out, w3, cos, sin, deps=()):
    length, model = ga.shape
    local = w3.shape[2]
    local_heads = local // HEAD
    heads = 2 if local_heads % 2 == 0 else 1
    steps = local_heads // heads
    wide = heads * HEAD
    full = lambda *shape: pl.BlockSpec(shape, lambda g: (0,) * len(shape))
    return pl.pallas_call(
        partial(attend_back_kernel, heads=heads, steps=steps, deps=len(deps)),
        grid=(steps,),
        in_specs=[
            full(length, model), full(length, model),
            pl.BlockSpec((3, length, wide), lambda g: (0, 0, g)),
            pl.BlockSpec((heads, length, HEAD), lambda g: (g, 0, 0)),
            pl.BlockSpec((length, wide), lambda g: (0, g)),
            pl.BlockSpec((wide, model), lambda g: (g, 0)),
            pl.BlockSpec((3, model, wide), lambda g: (0, 0, g)),
            full(length, HEAD), full(length, HEAD),
        ] + [pl.BlockSpec(memory_space=pl.ANY)] * len(deps),
        out_specs=[pl.BlockSpec((4, model, wide), lambda g: (0, 0, g)), full(length, model)],
        out_shape=[
            jax.ShapeDtypeStruct((4, model, local), BF16),
            jax.ShapeDtypeStruct((length, model), BF16),
        ],
        scratch_shapes=[pltpu.VMEM((length, model), F32)],
        compiler_params=params(),
        cost_estimate=cost(2 * length * model * local * 8 + 10 * length * length * local,
                           2 * (4 * length * model + 8 * model * local), length * length * local_heads),
        name="attend_back",
    )(ga, normed, qkv, lse, mixed, w_out, w3, cos, sin, *deps)


def own_grad_kernel(sent_ref, cot_ref, bucket_ref, gate_ref, unsort_ref, up_ref, down_ref, *rest, row_bounds, deps):
    mine_ref, other_ref, act_ref, acc_ref = rest[deps:]
    level = pl.program_id(0)
    for q, rows in enumerate(row_bounds):
        @pl.when(level == q)
        def _(q=q, rows=rows):
            keep = bucket_ref[:rows, :1] >= q
            pre = dot(sent_ref[:rows], up_ref[0])
            active = jnp.where(keep, jnp.maximum(pre, 0.0), 0.0)
            act_ref[0, :rows] = (active * active).astype(BF16)
            gact = dot(cot_ref[:rows], down_ref[0], NT)
            gpre = (gact * (2.0 * gate_ref[:rows, :1]) * active).astype(BF16)
            s = dot(gpre, up_ref[0], NT)
            if q == 0:
                acc_ref[...] = s
            else:
                acc_ref[:rows] += s
            if q == len(row_bounds) - 1:
                half = mine_ref.shape[0]
                total = acc_ref[...].astype(BF16)
                other_ref[...] = dot(unsort_ref[half:], total).astype(BF16)
                mine_ref[...] = dot(unsort_ref[:half], total).astype(BF16)


def own_grad(sent, cot, bucket, gate, unsort, w_up, w_down, row_bounds, deps=()):
    length, model = sent.shape
    levels, _, hidden = w_up.shape
    full = lambda *shape: pl.BlockSpec(shape, lambda q: (0,) * len(shape))
    return pl.pallas_call(
        partial(own_grad_kernel, row_bounds=tuple(row_bounds), deps=len(deps)),
        grid=(levels,),
        in_specs=[
            full(length, model), full(length, model), full(length, 128), full(length, 128), full(length, length),
            pl.BlockSpec((1, model, hidden), lambda q: (q, 0, 0)),
            pl.BlockSpec((1, hidden, model), lambda q: (q, 0, 0)),
        ] + [pl.BlockSpec(memory_space=pl.ANY)] * len(deps),
        out_specs=[full(length // 2, model)] * 2 + [pl.BlockSpec((1, length, hidden), lambda q: (q, 0, 0))],
        out_shape=[jax.ShapeDtypeStruct((length // 2, model), BF16)] * 2
        + [jax.ShapeDtypeStruct((levels, length, hidden), BF16)],
        scratch_shapes=[pltpu.VMEM((length, model), F32)],
        compiler_params=params(),
        cost_estimate=cost(6 * sum(row_bounds) * model * hidden, 4 * levels * model * hidden + 6 * length * model),
        name="own_grad",
    )(sent, cot, bucket, gate, unsort, w_up, w_down, *deps)


def own_forward_kernel(act_ref, cot_ref, unsort_ref, down_ref, *rest, row_bounds, deps):
    ffn_ref, ggate_ref, acc_ref = rest[deps:]
    level = pl.program_id(0)
    for q, rows in enumerate(row_bounds):
        @pl.when(level == q)
        def _(q=q, rows=rows):
            f = dot(act_ref[0, :rows], down_ref[0])
            if q == 0:
                acc_ref[...] = f
            else:
                acc_ref[:rows] += f
            if q == len(row_bounds) - 1:
                total = acc_ref[...]
                ggate = jnp.sum(total * cot_ref[...].astype(F32), -1, keepdims=True)
                ggate_ref[...] = jnp.broadcast_to(ggate, ggate_ref.shape)
                ffn_ref[...] = dot(unsort_ref[...], total.astype(BF16)).astype(BF16)


def own_forward(act, cot, unsort, w_down, row_bounds, deps=()):
    length, model = cot.shape
    levels, hidden, _ = w_down.shape
    full = lambda *shape: pl.BlockSpec(shape, lambda q: (0,) * len(shape))
    return pl.pallas_call(
        partial(own_forward_kernel, row_bounds=tuple(row_bounds), deps=len(deps)),
        grid=(levels,),
        in_specs=[
            pl.BlockSpec((1, length, hidden), lambda q: (q, 0, 0)),
            full(length, model), full(length, length),
            pl.BlockSpec((1, hidden, model), lambda q: (q, 0, 0)),
        ] + [pl.BlockSpec(memory_space=pl.ANY)] * len(deps),
        out_specs=[full(length, model), full(length, 128)],
        out_shape=[jax.ShapeDtypeStruct((length, model), BF16), jax.ShapeDtypeStruct((length, 128), F32)],
        scratch_shapes=[pltpu.VMEM((length, model), F32)],
        compiler_params=params(),
        cost_estimate=cost(2 * sum(row_bounds) * model * hidden, 2 * levels * model * hidden + 6 * length * model),
        name="own_forward",
    )(act, cot, unsort, w_down, *deps)


AUX = 16


def gates_and_buckets(aux):
    row = lax.broadcasted_iota(jnp.int32, (AUX, 128), 0)
    gates = dot(aux, (row < 3).astype(BF16), TN)
    buckets = dot(aux, (row == 3).astype(BF16), TN)
    return gates, buckets


def weight_kernel(s_ref, aux_ref, c_ref, up_ref, down_ref, *refs, level, start, rows, group, fresh, carried, deps):
    gup_ref, gdown_ref, up_buf, down_buf, s_buf, aux_buf, c_buf, gup, gdown, sems = refs[carried + deps:]
    b = pl.program_id(0)
    steps = pl.num_programs(0)
    slices, piece = s_ref.shape[1], s_ref.shape[3]
    length = c_ref.shape[2]
    aux_at = aux_ref.shape[2] - AUX
    span = pl.ds(0, rows)

    def tokens_of(step, slot):
        out = []
        for j in range(group):
            block = step * group + j
            to = pl.ds(j * rows, rows)
            for m in range(slices):
                out.append((s_ref.at[block, m, span], s_buf.at[slot, to, pl.ds(m * piece, piece)]))
            for m in range(length // piece):
                out.append((aux_ref.at[block, m, pl.ds(aux_at, AUX)], aux_buf.at[slot, j, pl.ds(0, AUX), pl.ds(m * piece, piece)]))
        return [pltpu.make_async_copy(x, y, sems.at[slot, i]) for i, (x, y) in enumerate(out)]

    def cots_of(step, slot):
        out = []
        for j in range(group):
            block = step * group + j
            to = pl.ds(j * rows, rows)
            for m in range(slices):
                out.append((c_ref.at[block, m, pl.ds(start, rows)], c_buf.at[slot, to, pl.ds(m * piece, piece)]))
        return [pltpu.make_async_copy(x, y, sems.at[2 + slot, i]) for i, (x, y) in enumerate(out)]

    up_copy = pltpu.make_async_copy(up_ref.at[level], up_buf, sems.at[4, 0])
    down_copy = pltpu.make_async_copy(down_ref.at[level], down_buf, sems.at[4, 1])
    ends = [pltpu.make_async_copy(gup, gup_ref.at[level], sems.at[4, 2]),
            pltpu.make_async_copy(gdown, gdown_ref.at[level], sems.at[4, 3])]
    begins = [] if fresh else [
        pltpu.make_async_copy(refs[0].at[level], gup, sems.at[5, 0]),
        pltpu.make_async_copy(refs[1].at[level], gdown, sems.at[5, 1])]
    slot = lax.rem(b, 2)

    @pl.when(b == 0)
    def _():
        for c in [up_copy] + tokens_of(0, 0) + [down_copy] + cots_of(0, 0) + begins:
            c.start()

    @pl.when(b + 1 < steps)
    def _():
        for c in tokens_of(b + 1, 1 - slot) + cots_of(b + 1, 1 - slot):
            c.start()

    @pl.when(b == 0)
    def _():
        up_copy.wait()

    for c in tokens_of(b, slot):
        c.wait()
    columns = [gates_and_buckets(aux_buf[slot, j]) for j in range(group)]
    gate = jnp.concatenate([g[start:start + rows, :1] for g, _ in columns], 0)
    keep = jnp.concatenate([k[start:start + rows, :1] for _, k in columns], 0) >= level
    pre = dot(s_buf[slot], up_buf[...])
    active = jnp.where(keep, jnp.maximum(pre, 0.0), 0.0)
    act = (active * active * gate).astype(BF16)

    @pl.when(b == 0)
    def _():
        down_copy.wait()

    for c in cots_of(b, slot):
        c.wait()
    gact = dot(c_buf[slot], down_buf[...], NT)
    gpre = (gact * (2.0 * gate) * active).astype(BF16)

    @pl.when(b == 0)
    def _():
        if fresh:
            gup[...] = dot(s_buf[slot], gpre, TN)
            gdown[...] = dot(act, c_buf[slot], TN)
        else:
            for c in begins:
                c.wait()
            gup[...] += dot(s_buf[slot], gpre, TN)
            gdown[...] += dot(act, c_buf[slot], TN)

    @pl.when(jnp.logical_and(b > 0, b < steps - 1))
    def _():
        gup[...] += dot(s_buf[slot], gpre, TN)
        gdown[...] += dot(act, c_buf[slot], TN)

    @pl.when(b == steps - 1)
    def _():
        gup[...] += dot(s_buf[slot], gpre, TN)
        ends[0].start()
        gdown[...] += dot(act, c_buf[slot], TN)
        ends[1].start()
        for c in ends:
            c.wait()


def weight_gradients(level, start, rows, sents, aux, cots, w_up, w_down, carried, fresh, deps=()):
    levels, model, hidden = w_up.shape
    blocks, slices, length, piece = cots.shape
    group = max(1, min(4, 1024 // rows))
    while blocks % group or blocks // group < 2:
        group -= 1
    copies = group * (slices + length // piece)
    anywhere = pl.BlockSpec(memory_space=pl.ANY)
    return pl.pallas_call(
        partial(weight_kernel, level=level, start=start, rows=rows, group=group, fresh=fresh, carried=len(carried),
                deps=len(deps)),
        grid=(blocks // group,),
        in_specs=[anywhere] * (5 + len(carried) + len(deps)),
        out_specs=[anywhere] * 2,
        out_shape=[jax.ShapeDtypeStruct((levels, model, hidden), F32), jax.ShapeDtypeStruct((levels, hidden, model), F32)],
        input_output_aliases={5: 0, 6: 1} if carried else {},
        scratch_shapes=[
            pltpu.VMEM((model, hidden), BF16), pltpu.VMEM((hidden, model), BF16),
            pltpu.VMEM((2, group * rows, model), BF16), pltpu.VMEM((2, group, AUX, length), BF16),
            pltpu.VMEM((2, group * rows, model), BF16),
            pltpu.VMEM((model, hidden), F32), pltpu.VMEM((hidden, model), F32),
            pltpu.SemaphoreType.DMA((6, max(4, copies))),
        ],
        compiler_params=params(),
        cost_estimate=cost(8 * blocks * rows * model * hidden, 4 * blocks * length * model + 16 * model * hidden),
        name=f"weight_gradients_{level}_from_{start}",
    )(sents, aux, cots, w_up, w_down, *carried, *deps)


def unpack_kernel(order_ref, *refs, count, carried):
    chunk_refs = refs[:count]
    qkv_ref, out_ref = refs[count + carried:]
    size = qkv_ref.shape[1]
    for k in range(count):
        @pl.when(pl.program_id(0) == k)
        def _(k=k):
            for c in range(3):
                qkv_ref[c] = chunk_refs[k][c * size:(c + 1) * size].astype(F32)
            out_ref[...] = chunk_refs[k][3 * size:4 * size].astype(F32).T


def unpack(order, chunks, size, total, carried=()):
    height, local = chunks[0].shape
    anywhere = pl.BlockSpec(memory_space=pl.ANY)
    count = len(chunks)
    return pl.pallas_call(
        partial(unpack_kernel, count=count, carried=len(carried)),
        grid_spec=pltpu.PrefetchScalarGridSpec(
            num_scalar_prefetch=1,
            grid=(count,),
            in_specs=[pl.BlockSpec((height, local), lambda b, o: (0, 0), pipeline_mode=pl.Buffered(1))] * count
            + [anywhere] * len(carried),
            out_specs=[
                pl.BlockSpec((3, size, local), lambda b, o: (0, o[b], 0)),
                pl.BlockSpec((local, size), lambda b, o: (0, o[b])),
            ],
        ),
        out_shape=[
            jax.ShapeDtypeStruct((3, total * size, local), F32),
            jax.ShapeDtypeStruct((local, total * size), F32),
        ],
        input_output_aliases={count + 1: 0, count + 2: 1} if carried else {},
        compiler_params=params(),
        cost_estimate=cost(0, 24 * count * size * local),
        name="unpack_some" if not carried else "unpack_rest",
    )(order, *chunks, *carried)


def add_kernel(*refs, count):
    total = refs[0][...].astype(F32)
    for ref in refs[1:count]:
        total = total + ref[...].astype(F32)
    refs[-1][...] = total.astype(BF16)


def add_rows(parts, deps=()):
    rows, columns = parts[0].shape
    block = pl.BlockSpec((rows // 4, columns), lambda i: (i, 0))
    return pl.pallas_call(
        partial(add_kernel, count=len(parts)),
        grid=(4,),
        in_specs=[block] * len(parts) + [pl.BlockSpec(memory_space=pl.ANY)] * len(deps),
        out_specs=block,
        out_shape=jax.ShapeDtypeStruct((rows, columns), BF16),
        compiler_params=params(),
        cost_estimate=cost(rows * columns, 6 * rows * columns),
        name="add_rows",
    )(*parts, *deps)


def pass_kernel(*refs):
    pass


def after(arrays, deps):
    anywhere = pl.BlockSpec(memory_space=pl.ANY)
    return pl.pallas_call(
        pass_kernel,
        in_specs=[anywhere] * (len(arrays) + len(deps)),
        out_specs=[anywhere] * len(arrays),
        out_shape=[jax.ShapeDtypeStruct(x.shape, x.dtype) for x in arrays],
        input_output_aliases={i: i for i in range(len(arrays))},
        compiler_params=params(),
        cost_estimate=cost(0, 0),
        name="after",
    )(*arrays, *deps)


def join_kernel(index_ref, right_local, left_local, right_ref, left_ref, *rest, cut, deps):
    right_out, left_out = rest[deps:]
    size = right_local.shape[1]
    if right_ref.shape[1] == size:
        right_out[0] = (right_local[0].astype(F32) + right_ref[0].astype(F32)).astype(BF16)
        left_out[0] = (left_local[0].astype(F32) + left_ref[0].astype(F32)).astype(BF16)
    else:
        right_out[0, :cut] = (right_local[0, :cut].astype(F32) + right_ref[0].astype(F32)).astype(BF16)
        right_out[0, cut:] = right_local[0, cut:]
        left_out[0, :cut] = left_local[0, :cut]
        left_out[0, cut:] = (left_local[0, cut:].astype(F32) + left_ref[0].astype(F32)).astype(BF16)


def join(grads, indices, right, left, size, deps=()):
    kinds, _, local = grads.shape
    arrived = right.shape[1]
    out = pl.BlockSpec((1, size, local), lambda i, o: (i, 0, 0))
    return pl.pallas_call(
        partial(join_kernel, cut=size // 2, deps=len(deps)),
        grid_spec=pltpu.PrefetchScalarGridSpec(
            num_scalar_prefetch=1,
            grid=(kinds,),
            in_specs=[
                pl.BlockSpec((1, size, local), lambda i, o: (i, o[0], 0)),
                pl.BlockSpec((1, size, local), lambda i, o: (i, o[1], 0)),
                pl.BlockSpec((1, arrived, local), lambda i, o: (i, 0, 0)),
                pl.BlockSpec((1, arrived, local), lambda i, o: (i, 0, 0)),
            ] + [pl.BlockSpec(memory_space=pl.ANY)] * len(deps),
            out_specs=[out, out],
        ),
        out_shape=[jax.ShapeDtypeStruct((kinds, size, local), BF16)] * 2,
        compiler_params=params(),
        cost_estimate=cost(2 * kinds * size * local, 12 * kinds * size * local),
        name="join",
    )(indices, grads, grads, right, left, *deps)


def join_own_kernel(index_ref, local_ref, right_ref, left_ref, extra_ref, *rest):
    kinds, size, _ = right_ref.shape
    for c in range(kinds):
        total = local_ref[c].astype(F32) + right_ref[c].astype(F32) + left_ref[c].astype(F32)
        rest[-1][c * size:(c + 1) * size] = total.astype(BF16)
    rest[-1][kinds * size:] = extra_ref[...]


def join_own(grads, indices, right, left, extra, deps=()):
    kinds, size, local = right.shape
    block = pl.BlockSpec((kinds, size, local), lambda i, o: (0, 0, 0))
    height = kinds * size + extra.shape[0]
    return pl.pallas_call(
        join_own_kernel,
        grid_spec=pltpu.PrefetchScalarGridSpec(
            num_scalar_prefetch=1,
            grid=(1,),
            in_specs=[pl.BlockSpec((kinds, size, local), lambda i, o: (0, o[0], 0)), block, block,
                      pl.BlockSpec(extra.shape, lambda i, o: (0, 0))]
            + [pl.BlockSpec(memory_space=pl.ANY)] * len(deps),
            out_specs=pl.BlockSpec((height, local), lambda i, o: (0, 0)),
        ),
        out_shape=jax.ShapeDtypeStruct((height, local), BF16),
        compiler_params=params(),
        cost_estimate=cost(2 * kinds * size * local, 8 * kinds * size * local),
        name="join_own",
    )(indices, grads, right, left, extra, *deps)


def ring_order(count):
    nz = 4 if count % 4 == 0 else 1
    ny = count // nz
    if nz == 1 or ny % 2:
        return list(range(count))
    order = [(z, 0) for z in range(nz)]
    for y in range(1, ny):
        line = list(range(1, nz))
        order += [(z, y) for z in (reversed(line) if y % 2 else line)]
    order += [(0, y) for y in range(ny - 1, 0, -1)]
    return [z * ny + y for z, y in order]


class Ring:
    def __init__(self):
        self.log = []
        self.count = lax.axis_size("dp")
        self.order = ring_order(self.count)
        n = self.count
        place = [0] * n
        for p, d in enumerate(self.order):
            place[d] = p
        self.position = jnp.array(place, jnp.int32)[lax.axis_index("dp")]
        self.right = [(self.order[p], self.order[(p + 1) % n]) for p in range(n)]
        self.left = [(self.order[(p + 1) % n], self.order[p]) for p in range(n)]

    def to_right(self, x):
        out = lax.ppermute(x, "dp", self.right)
        self.log.append(out)
        return out

    def to_left(self, x):
        out = lax.ppermute(x, "dp", self.left)
        self.log.append(out)
        return out

    def logged(self, f, *args):
        self.log = []
        out = f(*args)
        pairs = [tuple(self.log[i:i + 2]) for i in range(0, len(self.log), 2)]
        self.log = []
        return out, pairs

    def gather(self, x, axis):
        out = [x]
        r = l = x
        for _ in range(self.count // 2 - 1):
            r, l = self.to_right(r), self.to_left(l)
            out += [r, l]
        size = x.shape[axis]
        cut = size // 32 * 16
        first = self.to_right(lax.slice_in_dim(r, 0, cut, axis=axis))
        second = self.to_left(lax.slice_in_dim(l, cut, size, axis=axis))
        out.append(jnp.concatenate([first, second], axis))
        return out

    def offsets(self):
        out = [0]
        for k in range(1, self.count // 2):
            out += [-k, k]
        return out + [self.count // 2]

    def indices(self):
        return [(self.position + k) % self.count for k in self.offsets()]

    def reduce_start(self, x):
        size = x.shape[1] // self.count
        cut = size // 2
        far = self.count // 2
        at = ((self.position + far) % self.count) * size
        r = lax.dynamic_slice_in_dim(x, at, cut, axis=1)
        l = lax.dynamic_slice_in_dim(x, at + cut, cut, axis=1)
        return (self.to_right(r), self.to_left(l)), (r, l)

    def reduce_step(self, x, arrived, k, deps=()):
        indices = jnp.stack([(self.position + k) % self.count, (self.position - k) % self.count]).astype(jnp.int32)
        r, l = join(x, indices, *arrived, x.shape[1] // self.count, deps)
        return (self.to_right(r), self.to_left(l)), (r, l)

    def reduce_end(self, x, arrived, extra, deps=()):
        return join_own(x, self.position[None].astype(jnp.int32), *arrived, extra, deps)


def core_swap(x):
    n = lax.axis_size("mp")
    return lax.ppermute(x, "mp", [(i, i ^ 1) for i in range(n)])


def sum_over_x(x):
    n = lax.axis_size("mp") // 2
    index = lax.axis_index("mp")
    parts = [x] + [
        lax.ppermute(x, "mp", [(i, (i + 2 * k) % (2 * n)) for i in range(2 * n)]) for k in range(1, n)
    ]
    if n == 1:
        return x.astype(F32)
    if n == 2:
        return parts[0].astype(F32) + parts[1].astype(F32)
    stacked = jnp.stack(parts)
    total = None
    for j in range(n):
        term = lax.dynamic_index_in_dim(stacked, (index // 2 - j) % n, 0, keepdims=False).astype(F32)
        total = term if total is None else total + term
    return total


def on_device(tokens, gain_first, w_qkv, w_out, gain_second, router, w_up, w_down, slot, cotangent):
    length, model = tokens.shape
    buckets = w_up.shape[0]
    devices_dp = lax.axis_size("dp")
    groups = devices_dp // buckets
    capacity = length * 5 // (4 * devices_dp)
    row_bounds = [min(length, (buckets - level) * groups * capacity) for level in range(buckets)]
    ring = Ring()
    core = lax.axis_index("mp") % 2
    half = length // 2

    bucket_ids = slot // capacity // groups
    places = jnp.arange(length, dtype=jnp.int32)
    key = (buckets - 1 - bucket_ids) * length + places
    rank = jnp.sum((key[None, :] < key[:, None]).astype(jnp.int32), 1)
    rank_here = jnp.roll(rank, -core * half)
    sort_rows = places[:, None] == rank[None, :]
    sort_here = places[:, None] == rank_here[None, :]
    sort_low = sort_here.astype(BF16)
    unsort_low = (rank_here[:, None] == places[None, :]).astype(BF16)
    bucket_sorted = jnp.sum(jnp.where(sort_rows, bucket_ids[None, :], 0), 1)

    def part_of(x, c, axis=0):
        size = x.shape[axis] // 2
        return lax.dynamic_slice_in_dim(x, c * size, size, axis=axis)

    def own_rows(x):
        return part_of(x, core)

    def other_rows(x):
        return part_of(x, 1 - core)

    def joined(mine, other):
        return jnp.concatenate([jnp.where(core == 0, mine, other), jnp.where(core == 0, other, mine)], 0)

    cot_sorted = dot(sort_rows.astype(BF16), cotangent).astype(BF16)
    slices = lax.axis_size("mp")
    piece = model // slices
    me = lax.axis_index("mp")
    cot_piece = lax.dynamic_slice_in_dim(cot_sorted, me * piece, piece, axis=1)
    cots = lax.all_gather(cot_piece, ("dp", "mp"), axis=0).reshape(devices_dp, slices, length, piece)

    w3 = jnp.transpose(w_qkv, (1, 0, 2))
    cos, sin = rotary_table(length, HEAD)
    part_mine, part_other, normed_low, qkv, lse, mixed = attend(tokens, gain_first[None, :], w3, cos, sin, w_out)
    attn_rows = add_rows([part_mine, core_swap(part_other)], (cot_piece,))
    attn = sum_over_x(attn_rows)

    resid = own_rows(tokens).astype(F32) + attn
    inv = lax.rsqrt(jnp.mean(resid * resid, -1, keepdims=True) + EPSILON)
    xhat = resid * inv
    normed_second = xhat * gain_second
    logits = jnp.dot(normed_second, router, precision=HIGHEST)
    prob = jax.nn.softmax(logits, axis=-1)
    onehot = (own_rows(bucket_ids)[:, None] == jnp.arange(buckets)[None, :]).astype(F32)
    gate = buckets * jnp.sum(prob * onehot, -1)
    sent_half = normed_second.astype(BF16)
    sent_both = jnp.concatenate([sent_half, core_swap(sent_half)], 0)
    gate_both = jnp.concatenate([gate, core_swap(gate)], 0)
    gate_sorted = jnp.sum(jnp.where(sort_here, gate_both[None, :], 0.0), 1)

    sent_sorted = dot(sort_low, sent_both).astype(BF16)

    gate_1 = low(gate_sorted)
    gate_2 = low(gate_sorted - gate_1.astype(F32))
    gate_3 = low(gate_sorted - gate_1.astype(F32) - gate_2.astype(F32))
    aux = jnp.stack([gate_1, gate_2, gate_3, bucket_sorted.astype(BF16)] + [jnp.zeros_like(gate_1)] * (AUX - 4))
    sent_mine = lax.dynamic_slice_in_dim(sent_sorted, me * piece, piece, axis=1)
    sent_piece = jnp.concatenate([
        sent_mine[:half], lax.dynamic_slice_in_dim(aux, (me % (length // piece)) * piece, piece, axis=1)], 0)
    sents = lax.all_gather(sent_piece, ("dp", "mp"), axis=0).reshape(devices_dp, slices, half + AUX, piece)

    wide = lambda x: jnp.broadcast_to(x[:, None], (length, 128))
    gsent_mine, gsent_other, act = own_grad(
        sent_sorted, cot_sorted, wide(bucket_sorted), wide(gate_sorted), unsort_low, w_up, w_down, row_bounds,
        (sent_piece,))
    gsent_rows = add_rows([gsent_mine, core_swap(gsent_other)])
    sent_more, = after([sent_mine[half:]], (gsent_rows,))
    sents_more = lax.all_gather(sent_more, ("dp", "mp"), axis=0).reshape(devices_dp, slices, half, piece)
    grad_sent = sum_over_x(gsent_rows).astype(BF16).astype(F32)
    ffn_part, ggate_part = own_forward(
        act, cot_sorted, sort_rows.astype(BF16).T, w_down, row_bounds, (gsent_rows, sent_more))
    ggate_part = jnp.sum(jnp.where(sort_rows, ggate_part[:, :1], 0.0), 0)
    grad_gate = ggate_part + core_swap(ggate_part)
    grad_gate = sum_over_x(own_rows(grad_gate))

    grad_output = own_rows(cotangent).astype(F32)
    grad_prob = buckets * grad_gate[:, None] * onehot
    grad_logits = prob * (grad_prob - jnp.sum(grad_prob * prob, -1, keepdims=True))
    grad_router = jnp.dot(normed_second.T, grad_logits, precision=HIGHEST)
    grad_second = grad_sent + jnp.dot(grad_logits, router.T, precision=HIGHEST)
    grad_gain_second = jnp.sum(grad_second * xhat, 0)
    scaled = grad_second * gain_second
    grad_resid = grad_output + inv * (scaled - xhat * jnp.mean(scaled * xhat, -1, keepdims=True))
    ga_half = low(grad_resid)
    grad_attn = joined(ga_half, core_swap(ga_half))

    grads, first_part = attend_back(
        grad_attn, normed_low, qkv, lse, mixed, w_out, w3, cos, sin)

    carried = ()
    arrived, sending = ring.reduce_start(grads)
    far = devices_dp // 2
    chunks = None
    step = 0

    def advance(step, arrived, deps):
        nonlocal chunks
        if step < far - 1:
            return ring.reduce_step(grads, arrived, far - 1 - step, deps)
        if step == far - 1:
            chunks = [ring.reduce_end(grads, arrived, extra, deps)]
            r = l = chunks[0]
        else:
            r, l = after(arrived, deps) if deps else arrived
            chunks.extend([r, l])
        if step < 2 * far - 2:
            sending = (r, l)
            r, l = ring.to_right(r), ring.to_left(l)
        else:
            cut = r.shape[0] // 32 * 16
            sending = (r[:cut], l[cut:])
            r, l = ring.to_right(sending[0]), ring.to_left(sending[1])
            chunks.append(jnp.concatenate([r, l], 0))
        return (r, l), sending

    steps = 2 * far - 1
    while step < min(far - 1, 1):
        arrived, sending = advance(step, arrived, ())
        step += 1
    ring_busy = tuple(sending)

    ffn_rows = sum_over_x(add_rows([own_rows(ffn_part), core_swap(other_rows(ffn_part))], ring_busy)).astype(BF16).astype(F32)
    output_half = (resid + gate[:, None] * ffn_rows).astype(BF16)

    grad_first = sum_over_x(add_rows([own_rows(first_part), core_swap(other_rows(first_part))], ring_busy)).astype(BF16).astype(F32)
    source = own_rows(tokens).astype(F32)
    inv_first = lax.rsqrt(jnp.mean(source * source, -1, keepdims=True) + EPSILON)
    xhat_first = source * inv_first
    grad_gain_first = jnp.sum(grad_first * xhat_first, 0)
    scaled_first = grad_first * gain_first
    grad_source = inv_first * (scaled_first - xhat_first * jnp.mean(scaled_first * xhat_first, -1, keepdims=True))
    tokens_half = (grad_source + grad_resid).astype(BF16)
    output = joined(output_half, core_swap(output_half))
    grad_tokens = joined(tokens_half, core_swap(tokens_half))
    small = jnp.concatenate([grad_router.T, grad_gain_second[None], grad_gain_first[None]], 0)
    small = jnp.pad(small, ((0, -small.shape[0] % 8), (0, 0)))
    local = w3.shape[2]
    extra = low(small + core_swap(small)).reshape(-1, local)

    calls = [(level, 0, min(rows, half), sents, True) for level, rows in enumerate(row_bounds)]
    calls += [(level, half, rows - half, sents_more, False) for level, rows in enumerate(row_bounds) if rows > half]
    for level, start, rows, tokens_all, fresh in calls:
        carried = weight_gradients(
            level, start, rows, tokens_all, sents, cots, w_up, w_down, tuple(carried), fresh, sending)
        if step < steps:
            arrived, sending = advance(step, arrived, (carried[0],))
            step += 1
        else:
            sending = ()
    while step < steps:
        arrived, sending = advance(step, arrived, ())
        step += 1
    grad_up, grad_down = carried
    order = jnp.stack(ring.indices()).astype(jnp.int32)
    size = model // devices_dp
    unpacked = unpack(order[:-1], chunks[:-1], size, devices_dp)
    grad_wqkv, grad_wout = unpack(order[-1:], chunks[-1:], size, devices_dp, unpacked)
    terms = jnp.stack([x[4 * size:] for x in chunks])
    by_place = jnp.zeros((devices_dp,), jnp.int32).at[order].set(jnp.arange(devices_dp, dtype=jnp.int32))
    small = jnp.sum(terms[by_place].astype(F32), 0).reshape(small.shape)

    return (
        output,
        grad_tokens,
        small[buckets + 1],
        jnp.transpose(grad_wqkv, (1, 0, 2)),
        grad_wout,
        small[buckets],
        small[:buckets].T,
        grad_up,
        grad_down,
    )


def solution(mesh):
    placed = (
        P("dp", None),
        P(),
        P(None, None, "mp"),
        P("mp", None),
        P(),
        P(),
        P(None, None, "mp"),
        P(None, "mp", None),
        P("dp"),
        P("dp", None),
    )
    return jax.shard_map(
        on_device,
        mesh=mesh,
        in_specs=placed,
        out_specs=(
            P("dp", None),
            P("dp", None),
            P(),
            P(None, None, "mp"),
            P("mp", None),
            P(),
            P(),
            P(None, None, "mp"),
            P(None, "mp", None),
        ),
        check_vma=False,
    )
```

```python
from functools import partial

import jax
import jax.numpy as jnp
from jax import lax
from jax.experimental import pallas as pl
from jax.experimental.pallas import tpu as pltpu
from jax.sharding import PartitionSpec as P

HEAD = 128
HIGHEST = lax.Precision.HIGHEST
EPSILON = 1e-05
F32 = jnp.float32
BF16 = jnp.bfloat16
VMEM_LIMIT = 56 * 1024 * 1024
COST = 4
NN = (((1,), (0,)), ((), ()))
NT = (((1,), (1,)), ((), ()))
TN = (((0,), (0,)), ((), ()))


def dot(a, b, dims=NN):
    return lax.dot_general(a, b, dims, preferred_element_type=F32)


def low(x):
    return lax.reduce_precision(x, 8, 7).astype(BF16)


def params():
    return pltpu.CompilerParams(vmem_limit_bytes=VMEM_LIMIT)


def cost(flops, nbytes, transcendentals=0):
    return pl.CostEstimate(flops=flops // COST, bytes_accessed=nbytes // COST, transcendentals=transcendentals // COST)


def rotary_table(length, head_size):
    position = jnp.arange(length, dtype=F32)
    inverse = 10000.0 ** (-jnp.arange(0, head_size, 2, dtype=F32) / head_size)
    angles = position[:, None] * inverse[None, :]
    angles = jnp.concatenate([angles, angles], -1)
    sign = jnp.where(jnp.arange(head_size) < head_size // 2, -1.0, 1.0)
    return jnp.cos(angles), jnp.sin(angles) * sign


def attend_kernel(x_ref, gain_ref, w_ref, cos_ref, sin_ref, wout_ref,
                  mine_ref, other_ref, normed_ref, qkv_ref, lse_ref, mixed_ref, *, heads, steps):
    g = pl.program_id(0)
    length = x_ref.shape[0]
    half = length // 2
    scale = HEAD ** -0.5

    @pl.when(g == 0)
    def _():
        values = x_ref[...].astype(F32)
        inv = lax.rsqrt(jnp.mean(values * values, -1, keepdims=True) + EPSILON)
        normed_ref[...] = (values * inv * gain_ref[...]).astype(BF16)

    normed = normed_ref[...]
    cos, sin = cos_ref[...], sin_ref[...]
    projected = [dot(normed, w_ref[c]) for c in range(3)]
    for h in range(heads):
        cols = slice(h * HEAD, (h + 1) * HEAD)
        q, k, v = (p[:, cols] for p in projected)
        q = (q * cos + pltpu.roll(q, HEAD // 2, 1) * sin).astype(BF16)
        k = (k * cos + pltpu.roll(k, HEAD // 2, 1) * sin).astype(BF16)
        v = v.astype(BF16)
        qkv_ref[0, :, cols] = q
        qkv_ref[1, :, cols] = k
        qkv_ref[2, :, cols] = v
        for b in range(2):
            rows = slice(b * half, (b + 1) * half)
            keys = (b + 1) * half
            scores = dot(q[rows], k[:keys], NT) * scale
            at = lax.broadcasted_iota(jnp.int32, scores.shape, 0) + b * half
            to = lax.broadcasted_iota(jnp.int32, scores.shape, 1)
            scores = jnp.where(at >= to, scores, -1000000000.0)
            top = jnp.max(scores, -1, keepdims=True)
            weights = jnp.exp(scores - top)
            total = jnp.sum(weights, -1, keepdims=True)
            lse_ref[h, rows, :] = jnp.broadcast_to(top + jnp.log(total), (half, HEAD))
            low = (weights * (1.0 / total)).astype(BF16)
            mixed_ref[rows, pl.ds(pl.multiple_of((g * heads + h) * HEAD, HEAD), HEAD)] = dot(low, v[:keys]).astype(BF16)

    @pl.when(g == steps - 1)
    def _():
        core = lax.rem(lax.axis_index("mp"), 2)
        for ref, c in ((other_ref, 1 - core), (mine_ref, core)):
            rows = pl.ds(pl.multiple_of(c * half, half), half)
            ref[...] = dot(mixed_ref[rows, :], wout_ref[...]).astype(BF16)


def attend(tokens, gain, w3, cos, sin, w_out):
    length, model = tokens.shape
    local = w3.shape[2]
    local_heads = local // HEAD
    heads = 2 if local_heads % 2 == 0 else 1
    steps = local_heads // heads
    wide = heads * HEAD
    full = lambda *shape: pl.BlockSpec(shape, lambda g: (0,) * len(shape))
    return pl.pallas_call(
        partial(attend_kernel, heads=heads, steps=steps),
        grid=(steps,),
        in_specs=[
            full(length, model), full(1, model),
            pl.BlockSpec((3, model, wide), lambda g: (0, 0, g)),
            full(length, HEAD), full(length, HEAD), full(local, model),
        ],
        out_specs=[
            full(length // 2, model), full(length // 2, model), full(length, model),
            pl.BlockSpec((3, length, wide), lambda g: (0, 0, g)),
            pl.BlockSpec((heads, length, HEAD), lambda g: (g, 0, 0)),
            full(length, local),
        ],
        out_shape=[
            jax.ShapeDtypeStruct((length // 2, model), BF16),
            jax.ShapeDtypeStruct((length // 2, model), BF16),
            jax.ShapeDtypeStruct((length, model), BF16),
            jax.ShapeDtypeStruct((3, length, local), BF16),
            jax.ShapeDtypeStruct((local_heads, length, HEAD), F32),
            jax.ShapeDtypeStruct((length, local), BF16),
        ],
        compiler_params=params(),
        cost_estimate=cost(2 * length * model * local * 4 + 4 * length * length * local,
                           2 * (2 * length * model + 4 * model * local), length * length * local_heads),
        name="attend",
    )(tokens, gain, w3, cos, sin, w_out)


def attend_back_kernel(ga_ref, normed_ref, qkv_ref, lse_ref, mixed_ref, wout_ref, w_ref, cos_ref, sin_ref,
                       *rest, heads, steps, deps):
    grad_ref, first_ref, acc_ref = rest[deps:]
    g = pl.program_id(0)
    length = ga_ref.shape[0]
    half = length // 2
    scale = HEAD ** -0.5
    cos, sin = cos_ref[...], sin_ref[...]
    ga = ga_ref[...]
    gmixed = dot(ga, wout_ref[...], NT).astype(BF16)
    gproj = [[], [], []]
    for h in range(heads):
        cols = slice(h * HEAD, (h + 1) * HEAD)
        q, k, v = (qkv_ref[c, :, cols] for c in range(3))
        gm = gmixed[:, cols]
        gq, gk, gv = [], [None, None], [None, None]
        for b in range(2):
            rows = slice(b * half, (b + 1) * half)
            keys = (b + 1) * half
            scores = dot(q[rows], k[:keys], NT) * scale
            at = lax.broadcasted_iota(jnp.int32, scores.shape, 0) + b * half
            to = lax.broadcasted_iota(jnp.int32, scores.shape, 1)
            probs = jnp.where(at >= to, jnp.exp(scores - lse_ref[h, rows, :1]), 0.0)
            gprobs = dot(gm[rows], v[:keys], NT)
            gscores = probs * (gprobs - jnp.sum(gprobs * probs, -1, keepdims=True))
            gs = gscores.astype(BF16)
            low_probs = probs.astype(BF16)
            gq.append(dot(gs, k[:keys]) * scale)
            for j in range(b + 1):
                part = slice(j * half, (j + 1) * half)
                a = dot(gs[:, part], q[rows], TN) * scale
                c = dot(low_probs[:, part], gm[rows], TN)
                gk[j] = a if gk[j] is None else gk[j] + a
                gv[j] = c if gv[j] is None else gv[j] + c
        gq = jnp.concatenate(gq, 0)
        gk = jnp.concatenate(gk, 0)
        gv = jnp.concatenate(gv, 0)
        gproj[0].append((gq * cos - pltpu.roll(gq, HEAD // 2, 1) * sin).astype(BF16))
        gproj[1].append((gk * cos - pltpu.roll(gk, HEAD // 2, 1) * sin).astype(BF16))
        gproj[2].append(gv.astype(BF16))
    gproj = [jnp.concatenate(p, 1) for p in gproj]

    @pl.when(g == 0)
    def _():
        acc_ref[...] = jnp.zeros_like(acc_ref)

    grad_ref[3] = dot(ga, mixed_ref[...], TN).astype(BF16)
    for c in range(3):
        grad_ref[c] = dot(normed_ref[...], gproj[c], TN).astype(BF16)
        acc_ref[...] += dot(gproj[c], w_ref[c], NT)

    @pl.when(g == steps - 1)
    def _():
        first_ref[...] = acc_ref[...].astype(BF16)


def attend_back(ga, normed, qkv, lse, mixed, w_out, w3, cos, sin, deps=()):
    length, model = ga.shape
    local = w3.shape[2]
    local_heads = local // HEAD
    heads = 2 if local_heads % 2 == 0 else 1
    steps = local_heads // heads
    wide = heads * HEAD
    full = lambda *shape: pl.BlockSpec(shape, lambda g: (0,) * len(shape))
    return pl.pallas_call(
        partial(attend_back_kernel, heads=heads, steps=steps, deps=len(deps)),
        grid=(steps,),
        in_specs=[
            full(length, model), full(length, model),
            pl.BlockSpec((3, length, wide), lambda g: (0, 0, g)),
            pl.BlockSpec((heads, length, HEAD), lambda g: (g, 0, 0)),
            pl.BlockSpec((length, wide), lambda g: (0, g)),
            pl.BlockSpec((wide, model), lambda g: (g, 0)),
            pl.BlockSpec((3, model, wide), lambda g: (0, 0, g)),
            full(length, HEAD), full(length, HEAD),
        ] + [pl.BlockSpec(memory_space=pl.ANY)] * len(deps),
        out_specs=[pl.BlockSpec((4, model, wide), lambda g: (0, 0, g)), full(length, model)],
        out_shape=[
            jax.ShapeDtypeStruct((4, model, local), BF16),
            jax.ShapeDtypeStruct((length, model), BF16),
        ],
        scratch_shapes=[pltpu.VMEM((length, model), F32)],
        compiler_params=params(),
        cost_estimate=cost(2 * length * model * local * 8 + 10 * length * length * local,
                           2 * (4 * length * model + 8 * model * local), length * length * local_heads),
        name="attend_back",
    )(ga, normed, qkv, lse, mixed, w_out, w3, cos, sin, *deps)


def own_grad_kernel(sent_ref, cot_ref, bucket_ref, gate_ref, unsort_ref, up_ref, down_ref, *rest, row_bounds, deps):
    mine_ref, other_ref, act_ref, acc_ref = rest[deps:]
    level = pl.program_id(0)
    for q, rows in enumerate(row_bounds):
        @pl.when(level == q)
        def _(q=q, rows=rows):
            keep = bucket_ref[:rows, :1] >= q
            pre = dot(sent_ref[:rows], up_ref[0])
            active = jnp.where(keep, jnp.maximum(pre, 0.0), 0.0)
            act_ref[0, :rows] = (active * active).astype(BF16)
            gact = dot(cot_ref[:rows], down_ref[0], NT)
            gpre = (gact * (2.0 * gate_ref[:rows, :1]) * active).astype(BF16)
            s = dot(gpre, up_ref[0], NT)
            if q == 0:
                acc_ref[...] = s
            else:
                acc_ref[:rows] += s
            if q == len(row_bounds) - 1:
                half = mine_ref.shape[0]
                total = acc_ref[...].astype(BF16)
                other_ref[...] = dot(unsort_ref[half:], total).astype(BF16)
                mine_ref[...] = dot(unsort_ref[:half], total).astype(BF16)


def own_grad(sent, cot, bucket, gate, unsort, w_up, w_down, row_bounds, deps=()):
    length, model = sent.shape
    levels, _, hidden = w_up.shape
    full = lambda *shape: pl.BlockSpec(shape, lambda q: (0,) * len(shape))
    return pl.pallas_call(
        partial(own_grad_kernel, row_bounds=tuple(row_bounds), deps=len(deps)),
        grid=(levels,),
        in_specs=[
            full(length, model), full(length, model), full(length, 128), full(length, 128), full(length, length),
            pl.BlockSpec((1, model, hidden), lambda q: (q, 0, 0)),
            pl.BlockSpec((1, hidden, model), lambda q: (q, 0, 0)),
        ] + [pl.BlockSpec(memory_space=pl.ANY)] * len(deps),
        out_specs=[full(length // 2, model)] * 2 + [pl.BlockSpec((1, length, hidden), lambda q: (q, 0, 0))],
        out_shape=[jax.ShapeDtypeStruct((length // 2, model), BF16)] * 2
        + [jax.ShapeDtypeStruct((levels, length, hidden), BF16)],
        scratch_shapes=[pltpu.VMEM((length, model), F32)],
        compiler_params=params(),
        cost_estimate=cost(6 * sum(row_bounds) * model * hidden, 4 * levels * model * hidden + 6 * length * model),
        name="own_grad",
    )(sent, cot, bucket, gate, unsort, w_up, w_down, *deps)


def own_forward_kernel(act_ref, cot_ref, unsort_ref, down_ref, *rest, row_bounds, deps):
    ffn_ref, ggate_ref, acc_ref = rest[deps:]
    level = pl.program_id(0)
    for q, rows in enumerate(row_bounds):
        @pl.when(level == q)
        def _(q=q, rows=rows):
            f = dot(act_ref[0, :rows], down_ref[0])
            if q == 0:
                acc_ref[...] = f
            else:
                acc_ref[:rows] += f
            if q == len(row_bounds) - 1:
                total = acc_ref[...]
                ggate = jnp.sum(total * cot_ref[...].astype(F32), -1, keepdims=True)
                ggate_ref[...] = jnp.broadcast_to(ggate, ggate_ref.shape)
                ffn_ref[...] = dot(unsort_ref[...], total.astype(BF16)).astype(BF16)


def own_forward(act, cot, unsort, w_down, row_bounds, deps=()):
    length, model = cot.shape
    levels, hidden, _ = w_down.shape
    full = lambda *shape: pl.BlockSpec(shape, lambda q: (0,) * len(shape))
    return pl.pallas_call(
        partial(own_forward_kernel, row_bounds=tuple(row_bounds), deps=len(deps)),
        grid=(levels,),
        in_specs=[
            pl.BlockSpec((1, length, hidden), lambda q: (q, 0, 0)),
            full(length, model), full(length, length),
            pl.BlockSpec((1, hidden, model), lambda q: (q, 0, 0)),
        ] + [pl.BlockSpec(memory_space=pl.ANY)] * len(deps),
        out_specs=[full(length, model), full(length, 128)],
        out_shape=[jax.ShapeDtypeStruct((length, model), BF16), jax.ShapeDtypeStruct((length, 128), F32)],
        scratch_shapes=[pltpu.VMEM((length, model), F32)],
        compiler_params=params(),
        cost_estimate=cost(2 * sum(row_bounds) * model * hidden, 2 * levels * model * hidden + 6 * length * model),
        name="own_forward",
    )(act, cot, unsort, w_down, *deps)


AUX = 16


def gates_and_buckets(aux):
    row = lax.broadcasted_iota(jnp.int32, (AUX, 128), 0)
    gates = dot(aux, (row < 3).astype(BF16), TN)
    buckets = dot(aux, (row == 3).astype(BF16), TN)
    return gates, buckets


def weight_kernel(*refs, level, rows, group, offsets, fresh, carried, deps):
    count = len(offsets)
    pieces, refs = refs[:4 * count], refs[4 * count:]
    up_ref, down_ref = refs[:2]
    sums = refs[2:2 + carried]
    gup_ref, gdown_ref, up_buf, down_buf, s_buf, aux_buf, c_buf, gup, gdown, sems = refs[2 + carried + deps:]
    b = pl.program_id(0)
    steps = count // group
    core = lax.rem(lax.axis_index("mp"), 2)
    length, part = aux_buf.shape[3], s_buf.shape[2] // 2
    columns = lambda c: pl.ds(pl.multiple_of(c * part, part), part)
    slot = lax.rem(b, 2)

    def tokens_of(step):
        out = []
        for j in range(group):
            k = step * group + j
            to = pl.ds(j * rows, rows)
            mine, other = pieces[4 * k + 2], pieces[4 * k + 3]
            at = offsets[k]
            out += [
                (mine.at[pl.ds(at[2], rows)], s_buf.at[step % 2, to, columns(core)]),
                (other.at[pl.ds(at[3], rows)], s_buf.at[step % 2, to, columns(1 - core)]),
                (mine.at[pl.ds(at[2] + length, AUX), pl.ds(0, length)], aux_buf.at[step % 2, j]),
            ]
        return [pltpu.make_async_copy(x, y, sems.at[step % 2, i]) for i, (x, y) in enumerate(out)]

    def cots_of(step):
        out = []
        for j in range(group):
            k = step * group + j
            to = pl.ds(j * rows, rows)
            at = offsets[k]
            out += [
                (pieces[4 * k].at[pl.ds(at[0], rows)], c_buf.at[step % 2, to, columns(core)]),
                (pieces[4 * k + 1].at[pl.ds(at[1], rows)], c_buf.at[step % 2, to, columns(1 - core)]),
            ]
        return [pltpu.make_async_copy(x, y, sems.at[2 + step % 2, i]) for i, (x, y) in enumerate(out)]

    up_copy = pltpu.make_async_copy(up_ref.at[level], up_buf, sems.at[4, 0])
    down_copy = pltpu.make_async_copy(down_ref.at[level], down_buf, sems.at[4, 1])
    ends = [pltpu.make_async_copy(gup, gup_ref.at[level], sems.at[4, 2]),
            pltpu.make_async_copy(gdown, gdown_ref.at[level], sems.at[4, 3])]
    begins = [] if fresh else [
        pltpu.make_async_copy(sums[0].at[level], gup, sems.at[5, 0]),
        pltpu.make_async_copy(sums[1].at[level], gdown, sems.at[5, 1])]

    @pl.when(b == 0)
    def _():
        for c in [up_copy] + tokens_of(0) + [down_copy] + cots_of(0) + begins:
            c.start()

    for step in range(1, steps):
        @pl.when(b == step - 1)
        def _(step=step):
            for c in tokens_of(step) + cots_of(step):
                c.start()

    @pl.when(b == 0)
    def _():
        up_copy.wait()

    for step in range(steps):
        @pl.when(b == step)
        def _(step=step):
            for c in tokens_of(step):
                c.wait()

    columns_of = [gates_and_buckets(aux_buf[slot, j]) for j in range(group)]
    gate = jnp.concatenate([g[:rows, :1] for g, _ in columns_of], 0)
    keep = jnp.concatenate([k[:rows, :1] for _, k in columns_of], 0) >= level
    pre = dot(s_buf[slot], up_buf[...])
    active = jnp.where(keep, jnp.maximum(pre, 0.0), 0.0)
    act = (active * active * gate).astype(BF16)

    @pl.when(b == 0)
    def _():
        down_copy.wait()

    for step in range(steps):
        @pl.when(b == step)
        def _(step=step):
            for c in cots_of(step):
                c.wait()

    gact = dot(c_buf[slot], down_buf[...], NT)
    gpre = (gact * (2.0 * gate) * active).astype(BF16)

    @pl.when(b == 0)
    def _():
        if fresh:
            gup[...] = dot(s_buf[slot], gpre, TN)
            gdown[...] = dot(act, c_buf[slot], TN)
        else:
            for c in begins:
                c.wait()
            gup[...] += dot(s_buf[slot], gpre, TN)
            gdown[...] += dot(act, c_buf[slot], TN)

    if steps > 2:
        @pl.when(jnp.logical_and(b > 0, b < steps - 1))
        def _():
            gup[...] += dot(s_buf[slot], gpre, TN)
            gdown[...] += dot(act, c_buf[slot], TN)

    @pl.when(b == steps - 1)
    def _():
        gup[...] += dot(s_buf[slot], gpre, TN)
        ends[0].start()
        gdown[...] += dot(act, c_buf[slot], TN)
        ends[1].start()
        for c in ends:
            c.wait()


def weight_gradients(level, rows, length, blocks, w_up, w_down, carried, fresh, deps=()):
    levels, model, hidden = w_up.shape
    count = len(blocks)
    group = 2
    anywhere = pl.BlockSpec(memory_space=pl.ANY)
    arrays = [x for block in blocks for x, _ in block]
    offsets = tuple(tuple(at for _, at in block) for block in blocks)
    first = len(arrays) + 2
    return pl.pallas_call(
        partial(weight_kernel, level=level, rows=rows, group=group, offsets=offsets, fresh=fresh, carried=len(carried),
                deps=len(deps)),
        grid=(count // group,),
        in_specs=[anywhere] * (first + len(carried) + len(deps)),
        out_specs=[anywhere] * 2,
        out_shape=[jax.ShapeDtypeStruct((levels, model, hidden), F32), jax.ShapeDtypeStruct((levels, hidden, model), F32)],
        input_output_aliases={first: 0, first + 1: 1} if carried else {},
        scratch_shapes=[
            pltpu.VMEM((model, hidden), BF16), pltpu.VMEM((hidden, model), BF16),
            pltpu.VMEM((2, group * rows, model), BF16), pltpu.VMEM((2, group, AUX, length), BF16),
            pltpu.VMEM((2, group * rows, model), BF16),
            pltpu.VMEM((model, hidden), F32), pltpu.VMEM((hidden, model), F32),
            pltpu.SemaphoreType.DMA((6, 3 * group)),
        ],
        compiler_params=params(),
        cost_estimate=cost(8 * count * rows * model * hidden, 4 * count * rows * model + 16 * model * hidden),
        name=f"weight_gradients_{level}" + ("" if fresh else "_more"),
    )(*arrays, w_up, w_down, *carried, *deps)


def unpack_kernel(order_ref, *refs, count, carried):
    chunk_refs = refs[:count]
    qkv_ref, out_ref = refs[count + carried:]
    size = qkv_ref.shape[1]
    for k in range(count):
        @pl.when(pl.program_id(0) == k)
        def _(k=k):
            for c in range(3):
                qkv_ref[c] = chunk_refs[k][c * size:(c + 1) * size].astype(F32)
            out_ref[...] = chunk_refs[k][3 * size:4 * size].astype(F32).T


def unpack(order, chunks, size, total, carried=()):
    height, local = chunks[0].shape
    anywhere = pl.BlockSpec(memory_space=pl.ANY)
    count = len(chunks)
    return pl.pallas_call(
        partial(unpack_kernel, count=count, carried=len(carried)),
        grid_spec=pltpu.PrefetchScalarGridSpec(
            num_scalar_prefetch=1,
            grid=(count,),
            in_specs=[pl.BlockSpec((height, local), lambda b, o: (0, 0), pipeline_mode=pl.Buffered(1))] * count
            + [anywhere] * len(carried),
            out_specs=[
                pl.BlockSpec((3, size, local), lambda b, o: (0, o[b], 0)),
                pl.BlockSpec((local, size), lambda b, o: (0, o[b])),
            ],
        ),
        out_shape=[
            jax.ShapeDtypeStruct((3, total * size, local), F32),
            jax.ShapeDtypeStruct((local, total * size), F32),
        ],
        input_output_aliases={count + 1: 0, count + 2: 1} if carried else {},
        compiler_params=params(),
        cost_estimate=cost(0, 24 * count * size * local),
        name="unpack_some" if not carried else "unpack_rest",
    )(order, *chunks, *carried)


def add_kernel(*refs, count):
    total = refs[0][...].astype(F32)
    for ref in refs[1:count]:
        total = total + ref[...].astype(F32)
    refs[-1][...] = total.astype(BF16)


def add_rows(parts, deps=()):
    rows, columns = parts[0].shape
    block = pl.BlockSpec((rows // 4, columns), lambda i: (i, 0))
    return pl.pallas_call(
        partial(add_kernel, count=len(parts)),
        grid=(4,),
        in_specs=[block] * len(parts) + [pl.BlockSpec(memory_space=pl.ANY)] * len(deps),
        out_specs=block,
        out_shape=jax.ShapeDtypeStruct((rows, columns), BF16),
        compiler_params=params(),
        cost_estimate=cost(rows * columns, 6 * rows * columns),
        name="add_rows",
    )(*parts, *deps)


def pass_kernel(*refs):
    pass


def after(arrays, deps):
    anywhere = pl.BlockSpec(memory_space=pl.ANY)
    return pl.pallas_call(
        pass_kernel,
        in_specs=[anywhere] * (len(arrays) + len(deps)),
        out_specs=[anywhere] * len(arrays),
        out_shape=[jax.ShapeDtypeStruct(x.shape, x.dtype) for x in arrays],
        input_output_aliases={i: i for i in range(len(arrays))},
        compiler_params=params(),
        cost_estimate=cost(0, 0),
        name="after",
    )(*arrays, *deps)


def join_kernel(index_ref, right_local, left_local, right_ref, left_ref, *rest, cut, deps):
    right_out, left_out = rest[deps:]
    size = right_local.shape[1]
    if right_ref.shape[1] == size:
        right_out[0] = (right_local[0].astype(F32) + right_ref[0].astype(F32)).astype(BF16)
        left_out[0] = (left_local[0].astype(F32) + left_ref[0].astype(F32)).astype(BF16)
    else:
        right_out[0, :cut] = (right_local[0, :cut].astype(F32) + right_ref[0].astype(F32)).astype(BF16)
        right_out[0, cut:] = right_local[0, cut:]
        left_out[0, :cut] = left_local[0, :cut]
        left_out[0, cut:] = (left_local[0, cut:].astype(F32) + left_ref[0].astype(F32)).astype(BF16)


def join(grads, indices, right, left, size, deps=()):
    kinds, _, local = grads.shape
    arrived = right.shape[1]
    out = pl.BlockSpec((1, size, local), lambda i, o: (i, 0, 0))
    return pl.pallas_call(
        partial(join_kernel, cut=size // 2, deps=len(deps)),
        grid_spec=pltpu.PrefetchScalarGridSpec(
            num_scalar_prefetch=1,
            grid=(kinds,),
            in_specs=[
                pl.BlockSpec((1, size, local), lambda i, o: (i, o[0], 0)),
                pl.BlockSpec((1, size, local), lambda i, o: (i, o[1], 0)),
                pl.BlockSpec((1, arrived, local), lambda i, o: (i, 0, 0)),
                pl.BlockSpec((1, arrived, local), lambda i, o: (i, 0, 0)),
            ] + [pl.BlockSpec(memory_space=pl.ANY)] * len(deps),
            out_specs=[out, out],
        ),
        out_shape=[jax.ShapeDtypeStruct((kinds, size, local), BF16)] * 2,
        compiler_params=params(),
        cost_estimate=cost(2 * kinds * size * local, 12 * kinds * size * local),
        name="join",
    )(indices, grads, grads, right, left, *deps)


def join_own_kernel(index_ref, local_ref, right_ref, left_ref, extra_ref, *rest):
    kinds, size, _ = right_ref.shape
    for c in range(kinds):
        total = local_ref[c].astype(F32) + right_ref[c].astype(F32) + left_ref[c].astype(F32)
        rest[-1][c * size:(c + 1) * size] = total.astype(BF16)
    rest[-1][kinds * size:] = extra_ref[...]


def join_own(grads, indices, right, left, extra, deps=()):
    kinds, size, local = right.shape
    block = pl.BlockSpec((kinds, size, local), lambda i, o: (0, 0, 0))
    height = kinds * size + extra.shape[0]
    return pl.pallas_call(
        join_own_kernel,
        grid_spec=pltpu.PrefetchScalarGridSpec(
            num_scalar_prefetch=1,
            grid=(1,),
            in_specs=[pl.BlockSpec((kinds, size, local), lambda i, o: (0, o[0], 0)), block, block,
                      pl.BlockSpec(extra.shape, lambda i, o: (0, 0))]
            + [pl.BlockSpec(memory_space=pl.ANY)] * len(deps),
            out_specs=pl.BlockSpec((height, local), lambda i, o: (0, 0)),
        ),
        out_shape=jax.ShapeDtypeStruct((height, local), BF16),
        compiler_params=params(),
        cost_estimate=cost(2 * kinds * size * local, 8 * kinds * size * local),
        name="join_own",
    )(indices, grads, right, left, extra, *deps)


def ring_order(count):
    nz = 4 if count % 4 == 0 else 1
    ny = count // nz
    if nz == 1 or ny % 2:
        return list(range(count))
    order = [(z, 0) for z in range(nz)]
    for y in range(1, ny):
        line = list(range(1, nz))
        order += [(z, y) for z in (reversed(line) if y % 2 else line)]
    order += [(0, y) for y in range(ny - 1, 0, -1)]
    return [z * ny + y for z, y in order]


class Ring:
    def __init__(self):
        self.log = []
        self.count = lax.axis_size("dp")
        self.order = ring_order(self.count)
        n = self.count
        place = [0] * n
        for p, d in enumerate(self.order):
            place[d] = p
        self.position = jnp.array(place, jnp.int32)[lax.axis_index("dp")]
        self.right = [(self.order[p], self.order[(p + 1) % n]) for p in range(n)]
        self.left = [(self.order[(p + 1) % n], self.order[p]) for p in range(n)]

    def to_right(self, x):
        out = lax.ppermute(x, "dp", self.right)
        self.log.append(out)
        return out

    def to_left(self, x):
        out = lax.ppermute(x, "dp", self.left)
        self.log.append(out)
        return out

    def logged(self, f, *args):
        self.log = []
        out = f(*args)
        pairs = [tuple(self.log[i:i + 2]) for i in range(0, len(self.log), 2)]
        self.log = []
        return out, pairs

    def gather(self, x, axis):
        out = [x]
        r = l = x
        for _ in range(self.count // 2 - 1):
            r, l = self.to_right(r), self.to_left(l)
            out += [r, l]
        size = x.shape[axis]
        cut = size // 32 * 16
        first = self.to_right(lax.slice_in_dim(r, 0, cut, axis=axis))
        second = self.to_left(lax.slice_in_dim(l, cut, size, axis=axis))
        out.append(jnp.concatenate([first, second], axis))
        return out

    def offsets(self):
        out = [0]
        for k in range(1, self.count // 2):
            out += [-k, k]
        return out + [self.count // 2]

    def indices(self):
        return [(self.position + k) % self.count for k in self.offsets()]

    def reduce_start(self, x):
        size = x.shape[1] // self.count
        cut = size // 2
        far = self.count // 2
        at = ((self.position + far) % self.count) * size
        r = lax.dynamic_slice_in_dim(x, at, cut, axis=1)
        l = lax.dynamic_slice_in_dim(x, at + cut, cut, axis=1)
        return (self.to_right(r), self.to_left(l)), (r, l)

    def reduce_step(self, x, arrived, k, deps=()):
        indices = jnp.stack([(self.position + k) % self.count, (self.position - k) % self.count]).astype(jnp.int32)
        r, l = join(x, indices, *arrived, x.shape[1] // self.count, deps)
        return (self.to_right(r), self.to_left(l)), (r, l)

    def reduce_end(self, x, arrived, extra, deps=()):
        return join_own(x, self.position[None].astype(jnp.int32), *arrived, extra, deps)


def core_swap(x):
    n = lax.axis_size("mp")
    return lax.ppermute(x, "mp", [(i, i ^ 1) for i in range(n)])


def sum_over_x(x, deps=()):
    n = lax.axis_size("mp") // 2
    index = lax.axis_index("mp")
    parts = [x] + [
        lax.ppermute(x, "mp", [(i, (i + 2 * k) % (2 * n)) for i in range(2 * n)]) for k in range(1, n)
    ]
    if n == 1:
        return x.astype(F32)
    if deps:
        parts[1:] = after(parts[1:], deps)
    if n == 2:
        return parts[0].astype(F32) + parts[1].astype(F32)
    stacked = jnp.stack(parts)
    total = None
    for j in range(n):
        term = lax.dynamic_index_in_dim(stacked, (index // 2 - j) % n, 0, keepdims=False).astype(F32)
        total = term if total is None else total + term
    return total


def on_device(tokens, gain_first, w_qkv, w_out, gain_second, router, w_up, w_down, slot, cotangent):
    length, model = tokens.shape
    buckets = w_up.shape[0]
    devices_dp = lax.axis_size("dp")
    groups = devices_dp // buckets
    capacity = length * 5 // (4 * devices_dp)
    row_bounds = [min(length, (buckets - level) * groups * capacity) for level in range(buckets)]
    ring = Ring()
    core = lax.axis_index("mp") % 2
    half = length // 2

    bucket_ids = slot // capacity // groups
    places = jnp.arange(length, dtype=jnp.int32)
    key = (buckets - 1 - bucket_ids) * length + places
    rank = jnp.sum((key[None, :] < key[:, None]).astype(jnp.int32), 1)
    rank_here = jnp.roll(rank, -core * half)
    sort_rows = places[:, None] == rank[None, :]
    sort_here = places[:, None] == rank_here[None, :]
    sort_low = sort_here.astype(BF16)
    unsort_low = (rank_here[:, None] == places[None, :]).astype(BF16)
    bucket_sorted = jnp.sum(jnp.where(sort_rows, bucket_ids[None, :], 0), 1)

    def part_of(x, c, axis=0):
        size = x.shape[axis] // 2
        return lax.dynamic_slice_in_dim(x, c * size, size, axis=axis)

    def own_rows(x):
        return part_of(x, core)

    def other_rows(x):
        return part_of(x, 1 - core)

    def joined(mine, other):
        return jnp.concatenate([jnp.where(core == 0, mine, other), jnp.where(core == 0, other, mine)], 0)

    cot_sorted = dot(sort_rows.astype(BF16), cotangent).astype(BF16)

    w3 = jnp.transpose(w_qkv, (1, 0, 2))
    cos, sin = rotary_table(length, HEAD)
    part_mine, part_other, normed_low, qkv, lse, mixed = attend(tokens, gain_first[None, :], w3, cos, sin, w_out)
    attn_rows = add_rows([part_mine, core_swap(part_other)])
    attn = sum_over_x(attn_rows)

    resid = own_rows(tokens).astype(F32) + attn
    inv = lax.rsqrt(jnp.mean(resid * resid, -1, keepdims=True) + EPSILON)
    xhat = resid * inv
    normed_second = xhat * gain_second
    logits = jnp.dot(normed_second, router, precision=HIGHEST)
    prob = jax.nn.softmax(logits, axis=-1)
    onehot = (own_rows(bucket_ids)[:, None] == jnp.arange(buckets)[None, :]).astype(F32)
    gate = buckets * jnp.sum(prob * onehot, -1)
    sent_half = normed_second.astype(BF16)
    sent_both = jnp.concatenate([sent_half, core_swap(sent_half)], 0)
    gate_both = jnp.concatenate([gate, core_swap(gate)], 0)
    gate_sorted = jnp.sum(jnp.where(sort_here, gate_both[None, :], 0.0), 1)

    sent_sorted = dot(sort_low, sent_both).astype(BF16)

    gate_1 = low(gate_sorted)
    gate_2 = low(gate_sorted - gate_1.astype(F32))
    gate_3 = low(gate_sorted - gate_1.astype(F32) - gate_2.astype(F32))
    aux = jnp.stack([gate_1, gate_2, gate_3, bucket_sorted.astype(BF16)] + [jnp.zeros_like(gate_1)] * (AUX - 4))
    aux = jnp.pad(aux, ((0, 0), (0, model // 2 - length)))
    both = jnp.concatenate([part_of(cot_sorted, core, 1), part_of(sent_sorted, core, 1), aux], 0)
    height = length
    blocks = [((both, 0), (part_of(cot_sorted, 1 - core, 1), 0), (both, height), (part_of(sent_sorted, 1 - core, 1), 0))]

    def block(mine, other):
        return (mine, 0), (other, 0), (mine, height), (other, height)

    r, l = ring.to_right(both), ring.to_left(both)

    wide = lambda x: jnp.broadcast_to(x[:, None], (length, 128))
    gsent_mine, gsent_other, act = own_grad(
        sent_sorted, cot_sorted, wide(bucket_sorted), wide(gate_sorted), unsort_low, w_up, w_down, row_bounds,
        (both,))
    gsent_rows = add_rows([gsent_mine, core_swap(gsent_other)])
    grad_sent = sum_over_x(gsent_rows).astype(BF16).astype(F32)
    ffn_part, ggate_part = own_forward(
        act, cot_sorted, sort_rows.astype(BF16).T, w_down, row_bounds, (gsent_rows,))
    far = devices_dp // 2
    met = []

    def forward(arrived, deps):
        r, l = after(arrived, deps)
        if len(met) < far:
            met.extend([(r, core_swap(r)), (l, core_swap(l))])
        else:
            met.extend([(r, None), (l, None)])
        if len(met) < 2 * far - 2:
            return ring.to_right(r), ring.to_left(l)
        return ring.to_right(r[:height]), ring.to_left(l[height:])

    r, l = forward((r, l), (ffn_part,))
    ggate_part = jnp.sum(jnp.where(sort_rows, ggate_part[:, :1], 0.0), 0)
    grad_gate = ggate_part + core_swap(ggate_part)
    grad_gate = sum_over_x(own_rows(grad_gate))

    grad_output = own_rows(cotangent).astype(F32)
    grad_prob = buckets * grad_gate[:, None] * onehot
    grad_logits = prob * (grad_prob - jnp.sum(grad_prob * prob, -1, keepdims=True))
    grad_router = jnp.dot(normed_second.T, grad_logits, precision=HIGHEST)
    grad_second = grad_sent + jnp.dot(grad_logits, router.T, precision=HIGHEST)
    grad_gain_second = jnp.sum(grad_second * xhat, 0)
    scaled = grad_second * gain_second
    grad_resid = grad_output + inv * (scaled - xhat * jnp.mean(scaled * xhat, -1, keepdims=True))
    ga_half = low(grad_resid)
    grad_attn = joined(ga_half, core_swap(ga_half))

    grads, first_part = attend_back(
        grad_attn, normed_low, qkv, lse, mixed, w_out, w3, cos, sin, met[0] + met[1])

    carried = ()
    arrived, sending = ring.reduce_start(grads)
    chunks = None
    step = 0

    def advance(step, arrived, deps):
        nonlocal chunks
        if step < far - 1:
            return ring.reduce_step(grads, arrived, far - 1 - step, deps)
        if step == far - 1:
            chunks = [ring.reduce_end(grads, arrived, extra, deps)]
            r = l = chunks[0]
        else:
            r, l = after(arrived, deps) if deps else arrived
            chunks.extend([r, l])
        if step < 2 * far - 2:
            sending = (r, l)
            r, l = ring.to_right(r), ring.to_left(l)
        else:
            cut = r.shape[0] // 32 * 16
            sending = (r[:cut], l[cut:])
            r, l = ring.to_right(sending[0]), ring.to_left(sending[1])
            chunks.append(jnp.concatenate([r, l], 0))
        return (r, l), sending

    steps = 2 * far - 1
    while len(met) < far:
        r, l = forward((r, l), (grads,))
    near = len(met)
    sending = sending + met[-2] + met[-1][:1]
    blocks += [block(*x) for x in met[:far - 1]]
    carried = ()
    calls = [(level, rows, True) for level, rows in enumerate(row_bounds)]
    later = [block(*x) for x in met[far - 1:]]
    grad_first = ffn_rows = extra = None
    slots = [0] + list(range(2, buckets)) + [1]
    for slot_at, level in enumerate(slots):
        rows = row_bounds[level]
        carried = weight_gradients(level, rows, length, blocks, w_up, w_down, tuple(carried), True, sending)
        if slot_at == 0:
            first_other, = after([other_rows(first_part)], (carried[0],))
            first_other = core_swap(first_other)
        if slot_at == 1:
            first_rows = add_rows([own_rows(first_part), first_other], (carried[0],))
        if slot_at == 2:
            grad_first = sum_over_x(first_rows, (carried[0],)).astype(BF16).astype(F32)
            source = own_rows(tokens).astype(F32)
            inv_first = lax.rsqrt(jnp.mean(source * source, -1, keepdims=True) + EPSILON)
            xhat_first = source * inv_first
            grad_gain_first = jnp.sum(grad_first * xhat_first, 0)
            scaled_first = grad_first * gain_first
            grad_source = inv_first * (
                scaled_first - xhat_first * jnp.mean(scaled_first * xhat_first, -1, keepdims=True))
            tokens_half = (grad_source + grad_resid).astype(BF16)
            small = jnp.concatenate([grad_router.T, grad_gain_second[None], grad_gain_first[None]], 0)
            small = jnp.pad(small, ((0, -small.shape[0] % 8), (0, 0)))
            small_other = core_swap(small)
        if slot_at == 3:
            small_other, = after([small_other], (carried[0],))
            extra = low(small + small_other).reshape(-1, w3.shape[2])
            tokens_half, = after([tokens_half], (carried[0],))
            tokens_other = core_swap(tokens_half)
            r, l, *held = after([r, l] + [x for x, _ in met[far:]], (carried[0],))
        arrived, sending = advance(step, arrived, (carried[0],))
        step += 1
        if slot_at == 0:
            sending = sending + tuple(x for _, x in met[far - 1:])
        if slot_at == 2:
            while len(met) < 2 * far - 2:
                r, l = forward((r, l), (carried[0],))
            sending = sending + tuple(pair[0] for pair in met[far:])
    later += [block(x, core_swap(x)) for x in held]
    later.append(((r, 0), (core_swap(r), 0), (l, 0), (core_swap(l), 0)))
    steps = 2 * far - 1
    for level, rows in enumerate(row_bounds):
        if level == buckets - 1 and step == steps:
            order = jnp.stack(ring.indices()).astype(jnp.int32)
            size = model // devices_dp
            unpacked = unpack(order[:-1], chunks[:-1], size, devices_dp)
            sending = sending + (unpacked[0],)
        carried = weight_gradients(level, rows, length, later, w_up, w_down, tuple(carried), False, sending)
        if level == 0:
            ffn_other, tokens_other = after([other_rows(ffn_part), tokens_other], (carried[0],))
            ffn_other = core_swap(ffn_other)
        if level == 1:
            ffn_sum = add_rows([own_rows(ffn_part), ffn_other], (carried[0],))
        if level == 2:
            ffn_rows = sum_over_x(ffn_sum, (carried[0],)).astype(BF16).astype(F32)
            output_half = (resid + gate[:, None] * ffn_rows).astype(BF16)
            output_other = core_swap(output_half)
        if level == 3:
            output_other, = after([output_other], (carried[0],))
        sending = ()
        if step < steps:
            arrived, sending = advance(step, arrived, (carried[0],))
            step += 1
    while step < steps:
        arrived, sending = advance(step, arrived, ())
        step += 1
    grad_up, grad_down = carried
    output = joined(output_half, output_other)
    grad_tokens = joined(tokens_half, tokens_other)
    order = jnp.stack(ring.indices()).astype(jnp.int32)
    size = model // devices_dp
    if devices_dp != 8:
        unpacked = unpack(order[:-1], chunks[:-1], size, devices_dp)
    grad_wqkv, grad_wout = unpack(order[-1:], chunks[-1:], size, devices_dp, unpacked)
    terms = jnp.stack([x[4 * size:] for x in chunks])
    by_place = jnp.zeros((devices_dp,), jnp.int32).at[order].set(jnp.arange(devices_dp, dtype=jnp.int32))
    small = jnp.sum(terms[by_place].astype(F32), 0).reshape(small.shape)

    return (
        output,
        grad_tokens,
        small[buckets + 1],
        jnp.transpose(grad_wqkv, (1, 0, 2)),
        grad_wout,
        small[buckets],
        small[:buckets].T,
        grad_up,
        grad_down,
    )


def solution(mesh):
    placed = (
        P("dp", None),
        P(),
        P(None, None, "mp"),
        P("mp", None),
        P(),
        P(),
        P(None, None, "mp"),
        P(None, "mp", None),
        P("dp"),
        P("dp", None),
    )
    return jax.shard_map(
        on_device,
        mesh=mesh,
        in_specs=placed,
        out_specs=(
            P("dp", None),
            P("dp", None),
            P(),
            P(None, None, "mp"),
            P("mp", None),
            P(),
            P(),
            P(None, None, "mp"),
            P(None, "mp", None),
        ),
        check_vma=False,
    )
```

```python
from functools import partial

import jax
import jax.numpy as jnp
from jax import lax
from jax.experimental import pallas as pl
from jax.experimental.pallas import tpu as pltpu
from jax.sharding import PartitionSpec as P

HEAD = 128
HIGHEST = lax.Precision.HIGHEST
EPSILON = 1e-05
F32 = jnp.float32
BF16 = jnp.bfloat16
VMEM_LIMIT = 56 * 1024 * 1024
COST = 4
NN = (((1,), (0,)), ((), ()))
NT = (((1,), (1,)), ((), ()))
TN = (((0,), (0,)), ((), ()))


def dot(a, b, dims=NN):
    return lax.dot_general(a, b, dims, preferred_element_type=F32)


def low(x):
    return lax.reduce_precision(x, 8, 7).astype(BF16)


def params():
    return pltpu.CompilerParams(vmem_limit_bytes=VMEM_LIMIT)


def cost(flops, nbytes, transcendentals=0):
    return pl.CostEstimate(flops=flops // COST, bytes_accessed=nbytes // COST, transcendentals=transcendentals // COST)


def rotary_table(length, head_size):
    position = jnp.arange(length, dtype=F32)
    inverse = 10000.0 ** (-jnp.arange(0, head_size, 2, dtype=F32) / head_size)
    angles = position[:, None] * inverse[None, :]
    angles = jnp.concatenate([angles, angles], -1)
    sign = jnp.where(jnp.arange(head_size) < head_size // 2, -1.0, 1.0)
    return jnp.cos(angles), jnp.sin(angles) * sign


def attend_kernel(x_ref, gain_ref, w_ref, cos_ref, sin_ref, wout_ref,
                  mine_ref, other_ref, normed_ref, qkv_ref, lse_ref, mixed_ref, *, heads, steps):
    g = pl.program_id(0)
    length = x_ref.shape[0]
    half = length // 2
    scale = HEAD ** -0.5

    @pl.when(g == 0)
    def _():
        values = x_ref[...].astype(F32)
        inv = lax.rsqrt(jnp.mean(values * values, -1, keepdims=True) + EPSILON)
        normed_ref[...] = (values * inv * gain_ref[...]).astype(BF16)

    normed = normed_ref[...]
    cos, sin = cos_ref[...], sin_ref[...]
    projected = [dot(normed, w_ref[c]) for c in range(3)]
    for h in range(heads):
        cols = slice(h * HEAD, (h + 1) * HEAD)
        q, k, v = (p[:, cols] for p in projected)
        q = (q * cos + pltpu.roll(q, HEAD // 2, 1) * sin).astype(BF16)
        k = (k * cos + pltpu.roll(k, HEAD // 2, 1) * sin).astype(BF16)
        v = v.astype(BF16)
        qkv_ref[0, :, cols] = q
        qkv_ref[1, :, cols] = k
        qkv_ref[2, :, cols] = v
        for b in range(2):
            rows = slice(b * half, (b + 1) * half)
            keys = (b + 1) * half
            scores = dot(q[rows], k[:keys], NT) * scale
            at = lax.broadcasted_iota(jnp.int32, scores.shape, 0) + b * half
            to = lax.broadcasted_iota(jnp.int32, scores.shape, 1)
            scores = jnp.where(at >= to, scores, -1000000000.0)
            top = jnp.max(scores, -1, keepdims=True)
            weights = jnp.exp(scores - top)
            total = jnp.sum(weights, -1, keepdims=True)
            lse_ref[h, rows, :] = jnp.broadcast_to(top + jnp.log(total), (half, HEAD))
            low = (weights * (1.0 / total)).astype(BF16)
            mixed_ref[rows, pl.ds(pl.multiple_of((g * heads + h) * HEAD, HEAD), HEAD)] = dot(low, v[:keys]).astype(BF16)

    @pl.when(g == steps - 1)
    def _():
        core = lax.rem(lax.axis_index("mp"), 2)
        for ref, c in ((other_ref, 1 - core), (mine_ref, core)):
            rows = pl.ds(pl.multiple_of(c * half, half), half)
            ref[...] = dot(mixed_ref[rows, :], wout_ref[...]).astype(BF16)


def attend(tokens, gain, w3, cos, sin, w_out):
    length, model = tokens.shape
    local = w3.shape[2]
    local_heads = local // HEAD
    heads = 2 if local_heads % 2 == 0 else 1
    steps = local_heads // heads
    wide = heads * HEAD
    full = lambda *shape: pl.BlockSpec(shape, lambda g: (0,) * len(shape))
    return pl.pallas_call(
        partial(attend_kernel, heads=heads, steps=steps),
        grid=(steps,),
        in_specs=[
            full(length, model), full(1, model),
            pl.BlockSpec((3, model, wide), lambda g: (0, 0, g)),
            full(length, HEAD), full(length, HEAD), full(local, model),
        ],
        out_specs=[
            full(length // 2, model), full(length // 2, model), full(length, model),
            pl.BlockSpec((3, length, wide), lambda g: (0, 0, g)),
            pl.BlockSpec((heads, length, HEAD), lambda g: (g, 0, 0)),
            full(length, local),
        ],
        out_shape=[
            jax.ShapeDtypeStruct((length // 2, model), BF16),
            jax.ShapeDtypeStruct((length // 2, model), BF16),
            jax.ShapeDtypeStruct((length, model), BF16),
            jax.ShapeDtypeStruct((3, length, local), BF16),
            jax.ShapeDtypeStruct((local_heads, length, HEAD), F32),
            jax.ShapeDtypeStruct((length, local), BF16),
        ],
        compiler_params=params(),
        cost_estimate=cost(2 * length * model * local * 4 + 4 * length * length * local,
                           2 * (2 * length * model + 4 * model * local), length * length * local_heads),
        name="attend",
    )(tokens, gain, w3, cos, sin, w_out)


def attend_back_kernel(ga_ref, normed_ref, qkv_ref, lse_ref, mixed_ref, wout_ref, w_ref, cos_ref, sin_ref,
                       *rest, heads, steps, deps):
    grad_ref, first_ref, acc_ref = rest[deps:]
    g = pl.program_id(0)
    length = ga_ref.shape[0]
    half = length // 2
    scale = HEAD ** -0.5
    cos, sin = cos_ref[...], sin_ref[...]
    ga = ga_ref[...]
    gmixed = dot(ga, wout_ref[...], NT).astype(BF16)
    gproj = [[], [], []]
    for h in range(heads):
        cols = slice(h * HEAD, (h + 1) * HEAD)
        q, k, v = (qkv_ref[c, :, cols] for c in range(3))
        gm = gmixed[:, cols]
        gq, gk, gv = [], [None, None], [None, None]
        for b in range(2):
            rows = slice(b * half, (b + 1) * half)
            keys = (b + 1) * half
            scores = dot(q[rows], k[:keys], NT) * scale
            at = lax.broadcasted_iota(jnp.int32, scores.shape, 0) + b * half
            to = lax.broadcasted_iota(jnp.int32, scores.shape, 1)
            probs = jnp.where(at >= to, jnp.exp(scores - lse_ref[h, rows, :1]), 0.0)
            gprobs = dot(gm[rows], v[:keys], NT)
            gscores = probs * (gprobs - jnp.sum(gprobs * probs, -1, keepdims=True))
            gs = gscores.astype(BF16)
            low_probs = probs.astype(BF16)
            gq.append(dot(gs, k[:keys]) * scale)
            for j in range(b + 1):
                part = slice(j * half, (j + 1) * half)
                a = dot(gs[:, part], q[rows], TN) * scale
                c = dot(low_probs[:, part], gm[rows], TN)
                gk[j] = a if gk[j] is None else gk[j] + a
                gv[j] = c if gv[j] is None else gv[j] + c
        gq = jnp.concatenate(gq, 0)
        gk = jnp.concatenate(gk, 0)
        gv = jnp.concatenate(gv, 0)
        gproj[0].append((gq * cos - pltpu.roll(gq, HEAD // 2, 1) * sin).astype(BF16))
        gproj[1].append((gk * cos - pltpu.roll(gk, HEAD // 2, 1) * sin).astype(BF16))
        gproj[2].append(gv.astype(BF16))
    gproj = [jnp.concatenate(p, 1) for p in gproj]

    @pl.when(g == 0)
    def _():
        acc_ref[...] = jnp.zeros_like(acc_ref)

    grad_ref[3] = dot(ga, mixed_ref[...], TN).astype(BF16)
    for c in range(3):
        grad_ref[c] = dot(normed_ref[...], gproj[c], TN).astype(BF16)
        acc_ref[...] += dot(gproj[c], w_ref[c], NT)

    @pl.when(g == steps - 1)
    def _():
        first_ref[...] = acc_ref[...].astype(BF16)


def attend_back(ga, normed, qkv, lse, mixed, w_out, w3, cos, sin, deps=()):
    length, model = ga.shape
    local = w3.shape[2]
    local_heads = local // HEAD
    heads = 2 if local_heads % 2 == 0 else 1
    steps = local_heads // heads
    wide = heads * HEAD
    full = lambda *shape: pl.BlockSpec(shape, lambda g: (0,) * len(shape))
    return pl.pallas_call(
        partial(attend_back_kernel, heads=heads, steps=steps, deps=len(deps)),
        grid=(steps,),
        in_specs=[
            full(length, model), full(length, model),
            pl.BlockSpec((3, length, wide), lambda g: (0, 0, g)),
            pl.BlockSpec((heads, length, HEAD), lambda g: (g, 0, 0)),
            pl.BlockSpec((length, wide), lambda g: (0, g)),
            pl.BlockSpec((wide, model), lambda g: (g, 0)),
            pl.BlockSpec((3, model, wide), lambda g: (0, 0, g)),
            full(length, HEAD), full(length, HEAD),
        ] + [pl.BlockSpec(memory_space=pl.ANY)] * len(deps),
        out_specs=[pl.BlockSpec((4, model, wide), lambda g: (0, 0, g)), full(length, model)],
        out_shape=[
            jax.ShapeDtypeStruct((4, model, local), BF16),
            jax.ShapeDtypeStruct((length, model), BF16),
        ],
        scratch_shapes=[pltpu.VMEM((length, model), F32)],
        compiler_params=params(),
        cost_estimate=cost(2 * length * model * local * 8 + 10 * length * length * local,
                           2 * (4 * length * model + 8 * model * local), length * length * local_heads),
        name="attend_back",
    )(ga, normed, qkv, lse, mixed, w_out, w3, cos, sin, *deps)


def own_grad_kernel(sent_ref, cot_ref, bucket_ref, gate_ref, unsort_ref, up_ref, down_ref, *rest, row_bounds, deps):
    mine_ref, other_ref, act_ref, acc_ref = rest[deps:]
    level = pl.program_id(0)
    for q, rows in enumerate(row_bounds):
        @pl.when(level == q)
        def _(q=q, rows=rows):
            keep = bucket_ref[:rows, :1] >= q
            pre = dot(sent_ref[:rows], up_ref[0])
            active = jnp.where(keep, jnp.maximum(pre, 0.0), 0.0)
            act_ref[0, :rows] = (active * active).astype(BF16)
            gact = dot(cot_ref[:rows], down_ref[0], NT)
            gpre = (gact * (2.0 * gate_ref[:rows, :1]) * active).astype(BF16)
            s = dot(gpre, up_ref[0], NT)
            if q == 0:
                acc_ref[...] = s
            else:
                acc_ref[:rows] += s
            if q == len(row_bounds) - 1:
                half = mine_ref.shape[0]
                total = acc_ref[...].astype(BF16)
                other_ref[...] = dot(unsort_ref[half:], total).astype(BF16)
                mine_ref[...] = dot(unsort_ref[:half], total).astype(BF16)


def own_grad(sent, cot, bucket, gate, unsort, w_up, w_down, row_bounds, deps=()):
    length, model = sent.shape
    levels, _, hidden = w_up.shape
    full = lambda *shape: pl.BlockSpec(shape, lambda q: (0,) * len(shape))
    return pl.pallas_call(
        partial(own_grad_kernel, row_bounds=tuple(row_bounds), deps=len(deps)),
        grid=(levels,),
        in_specs=[
            full(length, model), full(length, model), full(length, 128), full(length, 128), full(length, length),
            pl.BlockSpec((1, model, hidden), lambda q: (q, 0, 0)),
            pl.BlockSpec((1, hidden, model), lambda q: (q, 0, 0)),
        ] + [pl.BlockSpec(memory_space=pl.ANY)] * len(deps),
        out_specs=[full(length // 2, model)] * 2 + [pl.BlockSpec((1, length, hidden), lambda q: (q, 0, 0))],
        out_shape=[jax.ShapeDtypeStruct((length // 2, model), BF16)] * 2
        + [jax.ShapeDtypeStruct((levels, length, hidden), BF16)],
        scratch_shapes=[pltpu.VMEM((length, model), F32)],
        compiler_params=params(),
        cost_estimate=cost(6 * sum(row_bounds) * model * hidden, 4 * levels * model * hidden + 6 * length * model),
        name="own_grad",
    )(sent, cot, bucket, gate, unsort, w_up, w_down, *deps)


def own_forward_kernel(act_ref, cot_ref, unsort_ref, down_ref, *rest, row_bounds, deps):
    ffn_ref, ggate_ref, acc_ref = rest[deps:]
    level = pl.program_id(0)
    for q, rows in enumerate(row_bounds):
        @pl.when(level == q)
        def _(q=q, rows=rows):
            f = dot(act_ref[0, :rows], down_ref[0])
            if q == 0:
                acc_ref[...] = f
            else:
                acc_ref[:rows] += f
            if q == len(row_bounds) - 1:
                total = acc_ref[...]
                ggate = jnp.sum(total * cot_ref[...].astype(F32), -1, keepdims=True)
                ggate_ref[...] = jnp.broadcast_to(ggate, ggate_ref.shape)
                ffn_ref[...] = dot(unsort_ref[...], total.astype(BF16)).astype(BF16)


def own_forward(act, cot, unsort, w_down, row_bounds, deps=()):
    length, model = cot.shape
    levels, hidden, _ = w_down.shape
    full = lambda *shape: pl.BlockSpec(shape, lambda q: (0,) * len(shape))
    return pl.pallas_call(
        partial(own_forward_kernel, row_bounds=tuple(row_bounds), deps=len(deps)),
        grid=(levels,),
        in_specs=[
            pl.BlockSpec((1, length, hidden), lambda q: (q, 0, 0)),
            full(length, model), full(length, length),
            pl.BlockSpec((1, hidden, model), lambda q: (q, 0, 0)),
        ] + [pl.BlockSpec(memory_space=pl.ANY)] * len(deps),
        out_specs=[full(length, model), full(length, 128)],
        out_shape=[jax.ShapeDtypeStruct((length, model), BF16), jax.ShapeDtypeStruct((length, 128), F32)],
        scratch_shapes=[pltpu.VMEM((length, model), F32)],
        compiler_params=params(),
        cost_estimate=cost(2 * sum(row_bounds) * model * hidden, 2 * levels * model * hidden + 6 * length * model),
        name="own_forward",
    )(act, cot, unsort, w_down, *deps)


AUX = 16


def gates_and_buckets(aux):
    row = lax.broadcasted_iota(jnp.int32, (AUX, 128), 0)
    gates = dot(aux, (row < 3).astype(BF16), TN)
    buckets = dot(aux, (row == 3).astype(BF16), TN)
    return gates, buckets


def weight_kernel(*refs, level, rows, group, offsets, fresh, carried, deps):
    count = len(offsets)
    pieces, refs = refs[:4 * count], refs[4 * count:]
    up_ref, down_ref = refs[:2]
    sums = refs[2:2 + carried]
    gup_ref, gdown_ref, up_buf, down_buf, s_buf, aux_buf, c_buf, gup, gdown, sems = refs[2 + carried + deps:]
    b = pl.program_id(0)
    steps = count // group
    core = lax.rem(lax.axis_index("mp"), 2)
    length, part = aux_buf.shape[3], s_buf.shape[2] // 2
    columns = lambda c: pl.ds(pl.multiple_of(c * part, part), part)
    slot = lax.rem(b, 2)

    def tokens_of(step):
        out = []
        for j in range(group):
            k = step * group + j
            to = pl.ds(j * rows, rows)
            mine, other = pieces[4 * k + 2], pieces[4 * k + 3]
            at = offsets[k]
            out += [
                (mine.at[pl.ds(at[2], rows)], s_buf.at[step % 2, to, columns(core)]),
                (other.at[pl.ds(at[3], rows)], s_buf.at[step % 2, to, columns(1 - core)]),
                (mine.at[pl.ds(at[2] + length, AUX), pl.ds(0, length)], aux_buf.at[step % 2, j]),
            ]
        return [pltpu.make_async_copy(x, y, sems.at[step % 2, i]) for i, (x, y) in enumerate(out)]

    def cots_of(step):
        out = []
        for j in range(group):
            k = step * group + j
            to = pl.ds(j * rows, rows)
            at = offsets[k]
            out += [
                (pieces[4 * k].at[pl.ds(at[0], rows)], c_buf.at[step % 2, to, columns(core)]),
                (pieces[4 * k + 1].at[pl.ds(at[1], rows)], c_buf.at[step % 2, to, columns(1 - core)]),
            ]
        return [pltpu.make_async_copy(x, y, sems.at[2 + step % 2, i]) for i, (x, y) in enumerate(out)]

    up_copy = pltpu.make_async_copy(up_ref.at[level], up_buf, sems.at[4, 0])
    down_copy = pltpu.make_async_copy(down_ref.at[level], down_buf, sems.at[4, 1])
    ends = [pltpu.make_async_copy(gup, gup_ref.at[level], sems.at[4, 2]),
            pltpu.make_async_copy(gdown, gdown_ref.at[level], sems.at[4, 3])]
    begins = [] if fresh else [
        pltpu.make_async_copy(sums[0].at[level], gup, sems.at[5, 0]),
        pltpu.make_async_copy(sums[1].at[level], gdown, sems.at[5, 1])]

    @pl.when(b == 0)
    def _():
        for c in [up_copy] + tokens_of(0) + [down_copy] + cots_of(0) + begins:
            c.start()

    for step in range(1, steps):
        @pl.when(b == step - 1)
        def _(step=step):
            for c in tokens_of(step) + cots_of(step):
                c.start()

    @pl.when(b == 0)
    def _():
        up_copy.wait()

    for step in range(steps):
        @pl.when(b == step)
        def _(step=step):
            for c in tokens_of(step):
                c.wait()

    columns_of = [gates_and_buckets(aux_buf[slot, j]) for j in range(group)]
    gate = jnp.concatenate([g[:rows, :1] for g, _ in columns_of], 0)
    keep = jnp.concatenate([k[:rows, :1] for _, k in columns_of], 0) >= level
    pre = dot(s_buf[slot], up_buf[...])
    active = jnp.where(keep, jnp.maximum(pre, 0.0), 0.0)
    act = (active * active * gate).astype(BF16)

    @pl.when(b == 0)
    def _():
        down_copy.wait()

    for step in range(steps):
        @pl.when(b == step)
        def _(step=step):
            for c in cots_of(step):
                c.wait()

    gact = dot(c_buf[slot], down_buf[...], NT)
    gpre = (gact * (2.0 * gate) * active).astype(BF16)

    @pl.when(b == 0)
    def _():
        if fresh:
            gup[...] = dot(s_buf[slot], gpre, TN)
            gdown[...] = dot(act, c_buf[slot], TN)
        else:
            for c in begins:
                c.wait()
            gup[...] += dot(s_buf[slot], gpre, TN)
            gdown[...] += dot(act, c_buf[slot], TN)

    if steps > 2:
        @pl.when(jnp.logical_and(b > 0, b < steps - 1))
        def _():
            gup[...] += dot(s_buf[slot], gpre, TN)
            gdown[...] += dot(act, c_buf[slot], TN)

    @pl.when(b == steps - 1)
    def _():
        gup[...] += dot(s_buf[slot], gpre, TN)
        ends[0].start()
        gdown[...] += dot(act, c_buf[slot], TN)
        ends[1].start()
        for c in ends:
            c.wait()


def weight_gradients(level, rows, length, blocks, w_up, w_down, carried, fresh, deps=()):
    levels, model, hidden = w_up.shape
    count = len(blocks)
    group = 2
    anywhere = pl.BlockSpec(memory_space=pl.ANY)
    arrays = [x for block in blocks for x, _ in block]
    offsets = tuple(tuple(at for _, at in block) for block in blocks)
    first = len(arrays) + 2
    return pl.pallas_call(
        partial(weight_kernel, level=level, rows=rows, group=group, offsets=offsets, fresh=fresh, carried=len(carried),
                deps=len(deps)),
        grid=(count // group,),
        in_specs=[anywhere] * (first + len(carried) + len(deps)),
        out_specs=[anywhere] * 2,
        out_shape=[jax.ShapeDtypeStruct((levels, model, hidden), F32), jax.ShapeDtypeStruct((levels, hidden, model), F32)],
        input_output_aliases={first: 0, first + 1: 1} if carried else {},
        scratch_shapes=[
            pltpu.VMEM((model, hidden), BF16), pltpu.VMEM((hidden, model), BF16),
            pltpu.VMEM((2, group * rows, model), BF16), pltpu.VMEM((2, group, AUX, length), BF16),
            pltpu.VMEM((2, group * rows, model), BF16),
            pltpu.VMEM((model, hidden), F32), pltpu.VMEM((hidden, model), F32),
            pltpu.SemaphoreType.DMA((6, 3 * group)),
        ],
        compiler_params=params(),
        cost_estimate=cost(8 * count * rows * model * hidden, 4 * count * rows * model + 16 * model * hidden),
        name=f"weight_gradients_{level}" + ("" if fresh else "_more"),
    )(*arrays, w_up, w_down, *carried, *deps)


def unpack_kernel(order_ref, *refs, count, carried):
    chunk_refs = refs[:count]
    qkv_ref, out_ref = refs[count + carried:]
    size = qkv_ref.shape[1]
    for k in range(count):
        @pl.when(pl.program_id(0) == k)
        def _(k=k):
            for c in range(3):
                qkv_ref[c] = chunk_refs[k][c * size:(c + 1) * size].astype(F32)
            out_ref[...] = chunk_refs[k][3 * size:4 * size].astype(F32).T


def unpack(order, chunks, size, total, carried=()):
    height, local = chunks[0].shape
    anywhere = pl.BlockSpec(memory_space=pl.ANY)
    count = len(chunks)
    return pl.pallas_call(
        partial(unpack_kernel, count=count, carried=len(carried)),
        grid_spec=pltpu.PrefetchScalarGridSpec(
            num_scalar_prefetch=1,
            grid=(count,),
            in_specs=[pl.BlockSpec((height, local), lambda b, o: (0, 0), pipeline_mode=pl.Buffered(1))] * count
            + [anywhere] * len(carried),
            out_specs=[
                pl.BlockSpec((3, size, local), lambda b, o: (0, o[b], 0)),
                pl.BlockSpec((local, size), lambda b, o: (0, o[b])),
            ],
        ),
        out_shape=[
            jax.ShapeDtypeStruct((3, total * size, local), F32),
            jax.ShapeDtypeStruct((local, total * size), F32),
        ],
        input_output_aliases={count + 1: 0, count + 2: 1} if carried else {},
        compiler_params=params(),
        cost_estimate=cost(0, 24 * count * size * local),
        name="unpack_some" if not carried else "unpack_rest",
    )(order, *chunks, *carried)


def add_kernel(*refs, count):
    total = refs[0][...].astype(F32)
    for ref in refs[1:count]:
        total = total + ref[...].astype(F32)
    refs[-1][...] = total.astype(BF16)


def add_rows(parts, deps=()):
    rows, columns = parts[0].shape
    block = pl.BlockSpec((rows // 4, columns), lambda i: (i, 0))
    return pl.pallas_call(
        partial(add_kernel, count=len(parts)),
        grid=(4,),
        in_specs=[block] * len(parts) + [pl.BlockSpec(memory_space=pl.ANY)] * len(deps),
        out_specs=block,
        out_shape=jax.ShapeDtypeStruct((rows, columns), BF16),
        compiler_params=params(),
        cost_estimate=cost(rows * columns, 6 * rows * columns),
        name="add_rows",
    )(*parts, *deps)


def pass_kernel(*refs):
    pass


def after(arrays, deps):
    anywhere = pl.BlockSpec(memory_space=pl.ANY)
    return pl.pallas_call(
        pass_kernel,
        in_specs=[anywhere] * (len(arrays) + len(deps)),
        out_specs=[anywhere] * len(arrays),
        out_shape=[jax.ShapeDtypeStruct(x.shape, x.dtype) for x in arrays],
        input_output_aliases={i: i for i in range(len(arrays))},
        compiler_params=params(),
        cost_estimate=cost(0, 0),
        name="after",
    )(*arrays, *deps)


def join_kernel(index_ref, right_local, left_local, right_ref, left_ref, *rest, cut, deps):
    right_out, left_out = rest[deps:]
    size = right_local.shape[1]
    if right_ref.shape[1] == size:
        right_out[0] = (right_local[0].astype(F32) + right_ref[0].astype(F32)).astype(BF16)
        left_out[0] = (left_local[0].astype(F32) + left_ref[0].astype(F32)).astype(BF16)
    else:
        right_out[0, :cut] = (right_local[0, :cut].astype(F32) + right_ref[0].astype(F32)).astype(BF16)
        right_out[0, cut:] = right_local[0, cut:]
        left_out[0, :cut] = left_local[0, :cut]
        left_out[0, cut:] = (left_local[0, cut:].astype(F32) + left_ref[0].astype(F32)).astype(BF16)


def join(grads, indices, right, left, size, deps=()):
    kinds, _, local = grads.shape
    arrived = right.shape[1]
    out = pl.BlockSpec((1, size, local), lambda i, o: (i, 0, 0))
    return pl.pallas_call(
        partial(join_kernel, cut=size // 2, deps=len(deps)),
        grid_spec=pltpu.PrefetchScalarGridSpec(
            num_scalar_prefetch=1,
            grid=(kinds,),
            in_specs=[
                pl.BlockSpec((1, size, local), lambda i, o: (i, o[0], 0)),
                pl.BlockSpec((1, size, local), lambda i, o: (i, o[1], 0)),
                pl.BlockSpec((1, arrived, local), lambda i, o: (i, 0, 0)),
                pl.BlockSpec((1, arrived, local), lambda i, o: (i, 0, 0)),
            ] + [pl.BlockSpec(memory_space=pl.ANY)] * len(deps),
            out_specs=[out, out],
        ),
        out_shape=[jax.ShapeDtypeStruct((kinds, size, local), BF16)] * 2,
        compiler_params=params(),
        cost_estimate=cost(2 * kinds * size * local, 12 * kinds * size * local),
        name="join",
    )(indices, grads, grads, right, left, *deps)


def join_own_kernel(index_ref, local_ref, right_ref, left_ref, extra_ref, *rest):
    kinds, size, _ = right_ref.shape
    for c in range(kinds):
        total = local_ref[c].astype(F32) + right_ref[c].astype(F32) + left_ref[c].astype(F32)
        rest[-1][c * size:(c + 1) * size] = total.astype(BF16)
    rest[-1][kinds * size:] = extra_ref[...]


def join_own(grads, indices, right, left, extra, deps=()):
    kinds, size, local = right.shape
    block = pl.BlockSpec((kinds, size, local), lambda i, o: (0, 0, 0))
    height = kinds * size + extra.shape[0]
    return pl.pallas_call(
        join_own_kernel,
        grid_spec=pltpu.PrefetchScalarGridSpec(
            num_scalar_prefetch=1,
            grid=(1,),
            in_specs=[pl.BlockSpec((kinds, size, local), lambda i, o: (0, o[0], 0)), block, block,
                      pl.BlockSpec(extra.shape, lambda i, o: (0, 0))]
            + [pl.BlockSpec(memory_space=pl.ANY)] * len(deps),
            out_specs=pl.BlockSpec((height, local), lambda i, o: (0, 0)),
        ),
        out_shape=jax.ShapeDtypeStruct((height, local), BF16),
        compiler_params=params(),
        cost_estimate=cost(2 * kinds * size * local, 8 * kinds * size * local),
        name="join_own",
    )(indices, grads, right, left, extra, *deps)


def ring_order(count):
    nz = 4 if count % 4 == 0 else 1
    ny = count // nz
    if nz == 1 or ny % 2:
        return list(range(count))
    order = [(z, 0) for z in range(nz)]
    for y in range(1, ny):
        line = list(range(1, nz))
        order += [(z, y) for z in (reversed(line) if y % 2 else line)]
    order += [(0, y) for y in range(ny - 1, 0, -1)]
    return [z * ny + y for z, y in order]


class Ring:
    def __init__(self):
        self.log = []
        self.count = lax.axis_size("dp")
        self.order = ring_order(self.count)
        n = self.count
        place = [0] * n
        for p, d in enumerate(self.order):
            place[d] = p
        self.position = jnp.array(place, jnp.int32)[lax.axis_index("dp")]
        self.right = [(self.order[p], self.order[(p + 1) % n]) for p in range(n)]
        self.left = [(self.order[(p + 1) % n], self.order[p]) for p in range(n)]

    def to_right(self, x):
        out = lax.ppermute(x, "dp", self.right)
        self.log.append(out)
        return out

    def to_left(self, x):
        out = lax.ppermute(x, "dp", self.left)
        self.log.append(out)
        return out

    def logged(self, f, *args):
        self.log = []
        out = f(*args)
        pairs = [tuple(self.log[i:i + 2]) for i in range(0, len(self.log), 2)]
        self.log = []
        return out, pairs

    def gather(self, x, axis):
        out = [x]
        r = l = x
        for _ in range(self.count // 2 - 1):
            r, l = self.to_right(r), self.to_left(l)
            out += [r, l]
        size = x.shape[axis]
        cut = size // 32 * 16
        first = self.to_right(lax.slice_in_dim(r, 0, cut, axis=axis))
        second = self.to_left(lax.slice_in_dim(l, cut, size, axis=axis))
        out.append(jnp.concatenate([first, second], axis))
        return out

    def offsets(self):
        out = [0]
        for k in range(1, self.count // 2):
            out += [-k, k]
        return out + [self.count // 2]

    def indices(self):
        return [(self.position + k) % self.count for k in self.offsets()]

    def reduce_start(self, x):
        size = x.shape[1] // self.count
        cut = size // 2
        far = self.count // 2
        at = ((self.position + far) % self.count) * size
        r = lax.dynamic_slice_in_dim(x, at, cut, axis=1)
        l = lax.dynamic_slice_in_dim(x, at + cut, cut, axis=1)
        return (self.to_right(r), self.to_left(l)), (r, l)

    def reduce_step(self, x, arrived, k, deps=()):
        indices = jnp.stack([(self.position + k) % self.count, (self.position - k) % self.count]).astype(jnp.int32)
        r, l = join(x, indices, *arrived, x.shape[1] // self.count, deps)
        return (self.to_right(r), self.to_left(l)), (r, l)

    def reduce_end(self, x, arrived, extra, deps=()):
        return join_own(x, self.position[None].astype(jnp.int32), *arrived, extra, deps)


def core_swap(x):
    n = lax.axis_size("mp")
    return lax.ppermute(x, "mp", [(i, i ^ 1) for i in range(n)])


def sum_over_x(x, deps=()):
    n = lax.axis_size("mp") // 2
    index = lax.axis_index("mp")
    parts = [x] + [
        lax.ppermute(x, "mp", [(i, (i + 2 * k) % (2 * n)) for i in range(2 * n)]) for k in range(1, n)
    ]
    if n == 1:
        return x.astype(F32)
    if deps:
        parts[1:] = after(parts[1:], deps)
    if n == 2:
        return parts[0].astype(F32) + parts[1].astype(F32)
    stacked = jnp.stack(parts)
    total = None
    for j in range(n):
        term = lax.dynamic_index_in_dim(stacked, (index // 2 - j) % n, 0, keepdims=False).astype(F32)
        total = term if total is None else total + term
    return total


def on_device(tokens, gain_first, w_qkv, w_out, gain_second, router, w_up, w_down, slot, cotangent):
    length, model = tokens.shape
    buckets = w_up.shape[0]
    devices_dp = lax.axis_size("dp")
    groups = devices_dp // buckets
    capacity = length * 5 // (4 * devices_dp)
    row_bounds = [min(length, (buckets - level) * groups * capacity) for level in range(buckets)]
    ring = Ring()
    core = lax.axis_index("mp") % 2
    half = length // 2

    bucket_ids = slot // capacity // groups
    places = jnp.arange(length, dtype=jnp.int32)
    key = (buckets - 1 - bucket_ids) * length + places
    rank = jnp.sum((key[None, :] < key[:, None]).astype(jnp.int32), 1)
    rank_here = jnp.roll(rank, -core * half)
    sort_rows = places[:, None] == rank[None, :]
    sort_here = places[:, None] == rank_here[None, :]
    sort_low = sort_here.astype(BF16)
    unsort_low = (rank_here[:, None] == places[None, :]).astype(BF16)
    bucket_sorted = jnp.sum(jnp.where(sort_rows, bucket_ids[None, :], 0), 1)

    def part_of(x, c, axis=0):
        size = x.shape[axis] // 2
        return lax.dynamic_slice_in_dim(x, c * size, size, axis=axis)

    def own_rows(x):
        return part_of(x, core)

    def other_rows(x):
        return part_of(x, 1 - core)

    def joined(mine, other):
        return jnp.concatenate([jnp.where(core == 0, mine, other), jnp.where(core == 0, other, mine)], 0)

    cot_sorted = dot(sort_rows.astype(BF16), cotangent).astype(BF16)

    cot_own = part_of(cot_sorted, core, 1)
    cot_first = ring.to_right(cot_own), ring.to_left(cot_own)

    w3 = jnp.transpose(w_qkv, (1, 0, 2))
    cos, sin = rotary_table(length, HEAD)
    part_mine, part_other, normed_low, qkv, lse, mixed = attend(tokens, gain_first[None, :], w3, cos, sin, w_out)
    attn_rows = add_rows([part_mine, core_swap(part_other)])
    attn = sum_over_x(attn_rows)

    resid = own_rows(tokens).astype(F32) + attn
    inv = lax.rsqrt(jnp.mean(resid * resid, -1, keepdims=True) + EPSILON)
    xhat = resid * inv
    normed_second = xhat * gain_second
    logits = jnp.dot(normed_second, router, precision=HIGHEST)
    prob = jax.nn.softmax(logits, axis=-1)
    onehot = (own_rows(bucket_ids)[:, None] == jnp.arange(buckets)[None, :]).astype(F32)
    gate = buckets * jnp.sum(prob * onehot, -1)
    sent_half = normed_second.astype(BF16)
    sent_both = jnp.concatenate([sent_half, core_swap(sent_half)], 0)
    gate_both = jnp.concatenate([gate, core_swap(gate)], 0)
    gate_sorted = jnp.sum(jnp.where(sort_here, gate_both[None, :], 0.0), 1)

    sent_sorted = dot(sort_low, sent_both).astype(BF16)

    gate_1 = low(gate_sorted)
    gate_2 = low(gate_sorted - gate_1.astype(F32))
    gate_3 = low(gate_sorted - gate_1.astype(F32) - gate_2.astype(F32))
    aux = jnp.stack([gate_1, gate_2, gate_3, bucket_sorted.astype(BF16)] + [jnp.zeros_like(gate_1)] * (AUX - 4))
    aux = jnp.pad(aux, ((0, 0), (0, model // 2 - length)))
    sent_own = jnp.concatenate([part_of(sent_sorted, core, 1), aux], 0)
    height = length
    blocks = [((cot_own, 0), (part_of(cot_sorted, 1 - core, 1), 0), (sent_own, 0), (part_of(sent_sorted, 1 - core, 1), 0))]

    def block(mine, other):
        return (mine, 0), (other, 0), (mine, height), (other, height)

    sent_first = ring.to_right(sent_own), ring.to_left(sent_own)

    wide = lambda x: jnp.broadcast_to(x[:, None], (length, 128))
    gsent_mine, gsent_other, act = own_grad(
        sent_sorted, cot_sorted, wide(bucket_sorted), wide(gate_sorted), unsort_low, w_up, w_down, row_bounds,
        cot_first + (sent_own,))
    gsent_rows = add_rows([gsent_mine, core_swap(gsent_other)])
    grad_sent = sum_over_x(gsent_rows).astype(BF16).astype(F32)
    ffn_part, ggate_part = own_forward(
        act, cot_sorted, sort_rows.astype(BF16).T, w_down, row_bounds, (gsent_rows,))
    far = devices_dp // 2
    met = []

    def forward(arrived, deps):
        if len(arrived) == 4:
            cot_r, cot_l, sent_r, sent_l = after(arrived, deps)
            r, l = jnp.concatenate([cot_r, sent_r], 0), jnp.concatenate([cot_l, sent_l], 0)
        else:
            r, l = after(arrived, deps)
        if len(met) < far:
            met.extend([(r, core_swap(r)), (l, core_swap(l))])
        else:
            met.extend([(r, None), (l, None)])
        if len(met) < 2 * far - 2:
            return ring.to_right(r), ring.to_left(l)
        return ring.to_right(r[:height]), ring.to_left(l[height:])

    r, l = forward(cot_first + sent_first, (ffn_part,))
    ggate_part = jnp.sum(jnp.where(sort_rows, ggate_part[:, :1], 0.0), 0)
    grad_gate = ggate_part + core_swap(ggate_part)
    grad_gate = sum_over_x(own_rows(grad_gate))

    grad_output = own_rows(cotangent).astype(F32)
    grad_prob = buckets * grad_gate[:, None] * onehot
    grad_logits = prob * (grad_prob - jnp.sum(grad_prob * prob, -1, keepdims=True))
    grad_router = jnp.dot(normed_second.T, grad_logits, precision=HIGHEST)
    grad_second = grad_sent + jnp.dot(grad_logits, router.T, precision=HIGHEST)
    grad_gain_second = jnp.sum(grad_second * xhat, 0)
    scaled = grad_second * gain_second
    grad_resid = grad_output + inv * (scaled - xhat * jnp.mean(scaled * xhat, -1, keepdims=True))
    ga_half = low(grad_resid)
    grad_attn = joined(ga_half, core_swap(ga_half))

    grads, first_part = attend_back(
        grad_attn, normed_low, qkv, lse, mixed, w_out, w3, cos, sin, met[0] + met[1])

    carried = ()
    arrived, sending = ring.reduce_start(grads)
    chunks = None
    step = 0

    def advance(step, arrived, deps):
        nonlocal chunks
        if step < far - 1:
            return ring.reduce_step(grads, arrived, far - 1 - step, deps)
        if step == far - 1:
            chunks = [ring.reduce_end(grads, arrived, extra, deps)]
            r = l = chunks[0]
        else:
            r, l = after(arrived, deps) if deps else arrived
            chunks.extend([r, l])
        if step < 2 * far - 2:
            sending = (r, l)
            r, l = ring.to_right(r), ring.to_left(l)
        else:
            cut = r.shape[0] // 32 * 16
            sending = (r[:cut], l[cut:])
            r, l = ring.to_right(sending[0]), ring.to_left(sending[1])
            chunks.append(jnp.concatenate([r, l], 0))
        return (r, l), sending

    steps = 2 * far - 1
    while len(met) < far:
        r, l = forward((r, l), (grads,))
    near = len(met)
    sending = sending + met[-2] + met[-1][:1]
    blocks += [block(*x) for x in met[:far - 1]]
    carried = ()
    calls = [(level, rows, True) for level, rows in enumerate(row_bounds)]
    later = [block(*x) for x in met[far - 1:]]
    extra = None
    slots = [0] + list(range(2, buckets)) + [1]
    for slot_at, level in enumerate(slots):
        rows = row_bounds[level]
        carried = weight_gradients(level, rows, length, blocks, w_up, w_down, tuple(carried), True, sending)
        if slot_at == 0:
            first_other, = after([other_rows(first_part)], (carried[0],))
            first_other = core_swap(first_other)
        if slot_at == 1:
            first_rows = add_rows([own_rows(first_part), first_other], (carried[0],))
        if slot_at == 2:
            grad_first = sum_over_x(first_rows, (carried[0],)).astype(BF16).astype(F32)
            source = own_rows(tokens).astype(F32)
            inv_first = lax.rsqrt(jnp.mean(source * source, -1, keepdims=True) + EPSILON)
            xhat_first = source * inv_first
            grad_gain_first = jnp.sum(grad_first * xhat_first, 0)
            scaled_first = grad_first * gain_first
            grad_source = inv_first * (
                scaled_first - xhat_first * jnp.mean(scaled_first * xhat_first, -1, keepdims=True))
            tokens_half = (grad_source + grad_resid).astype(BF16)
            small = jnp.concatenate([grad_router.T, grad_gain_second[None], grad_gain_first[None]], 0)
            small = jnp.pad(small, ((0, -small.shape[0] % 8), (0, 0)))
            small_other = core_swap(small)
        if slot_at == 3:
            small_other, = after([small_other], (carried[0],))
            extra = low(small + small_other).reshape(-1, w3.shape[2])
        arrived, sending = advance(step, arrived, (carried[0],))
        step += 1
        if slot_at == 3:
            r, l, *held = after([r, l] + [x for x, _ in met[far:]], (carried[0], sending[0]))
        if slot_at == 0:
            sending = sending + tuple(x for _, x in met[far - 1:])
        if slot_at == 2:
            while len(met) < 2 * far - 2:
                r, l = forward((r, l), (carried[0],))
            sending = sending + tuple(pair[0] for pair in met[far:])
    later += [block(x, core_swap(x)) for x in held]
    later.append(((r, 0), (core_swap(r), 0), (l, 0), (core_swap(l), 0)))
    steps = 2 * far - 1
    for level, rows in enumerate(row_bounds):
        if level == buckets - 1 and step == steps:
            order = jnp.stack(ring.indices()).astype(jnp.int32)
            size = model // devices_dp
            unpacked = unpack(order[:-1], chunks[:-1], size, devices_dp)
            sending = sending + (unpacked[0],)
        carried = weight_gradients(level, rows, length, later, w_up, w_down, tuple(carried), False, sending)
        ready = ()
        if level == 0:
            others = [core_swap(x) for x in after([tokens_half, other_rows(ffn_part)], (carried[0],))]
        if level == 1:
            others = after(others, (carried[0],))
            grad_tokens = joined(tokens_half, others[0])
            ffn_sum = add_rows([own_rows(ffn_part), others[1]])
            ready = (grad_tokens, ffn_sum)
        if level == 2:
            ffn_rows = sum_over_x(ffn_sum, (carried[0],)).astype(BF16).astype(F32)
            output_half = (resid + gate[:, None] * ffn_rows).astype(BF16)
            output_other = core_swap(output_half)
            ready = (output_half,)
        if level == 3:
            output_other, = after([output_other], (carried[0],))
            output = joined(output_half, output_other)
        sending = ()
        if step < steps:
            arrived, sending = advance(step, arrived, (carried[0],))
            step += 1
        sending = sending + ready
    while step < steps:
        arrived, sending = advance(step, arrived, ())
        step += 1
    grad_up, grad_down = carried
    order = jnp.stack(ring.indices()).astype(jnp.int32)
    size = model // devices_dp
    if devices_dp != 8:
        unpacked = unpack(order[:-1], chunks[:-1], size, devices_dp)
    grad_wqkv, grad_wout = unpack(order[-1:], chunks[-1:], size, devices_dp, unpacked)
    terms = jnp.stack([x[4 * size:] for x in chunks])
    by_place = jnp.zeros((devices_dp,), jnp.int32).at[order].set(jnp.arange(devices_dp, dtype=jnp.int32))
    small = jnp.sum(terms[by_place].astype(F32), 0).reshape(small.shape)

    return (
        output,
        grad_tokens,
        small[buckets + 1],
        jnp.transpose(grad_wqkv, (1, 0, 2)),
        grad_wout,
        small[buckets],
        small[:buckets].T,
        grad_up,
        grad_down,
    )


def solution(mesh):
    placed = (
        P("dp", None),
        P(),
        P(None, None, "mp"),
        P("mp", None),
        P(),
        P(),
        P(None, None, "mp"),
        P(None, "mp", None),
        P("dp"),
        P("dp", None),
    )
    return jax.shard_map(
        on_device,
        mesh=mesh,
        in_specs=placed,
        out_specs=(
            P("dp", None),
            P("dp", None),
            P(),
            P(None, None, "mp"),
            P("mp", None),
            P(),
            P(),
            P(None, None, "mp"),
            P(None, "mp", None),
        ),
        check_vma=False,
    )
```

```python
from functools import partial

import jax
import jax.numpy as jnp
from jax import lax
from jax.experimental import pallas as pl
from jax.experimental.pallas import tpu as pltpu
from jax.sharding import PartitionSpec as P

HEAD = 128
HIGHEST = lax.Precision.HIGHEST
EPSILON = 1e-05
F32 = jnp.float32
BF16 = jnp.bfloat16
VMEM_LIMIT = 56 * 1024 * 1024
COST = 4
NN = (((1,), (0,)), ((), ()))
NT = (((1,), (1,)), ((), ()))
TN = (((0,), (0,)), ((), ()))


def dot(a, b, dims=NN):
    return lax.dot_general(a, b, dims, preferred_element_type=F32)


def low(x):
    return lax.reduce_precision(x, 8, 7).astype(BF16)


def params():
    return pltpu.CompilerParams(vmem_limit_bytes=VMEM_LIMIT)


def cost(flops, nbytes, transcendentals=0):
    return pl.CostEstimate(flops=flops // COST, bytes_accessed=nbytes // COST, transcendentals=transcendentals // COST)


def rotary_table(length, head_size):
    position = jnp.arange(length, dtype=F32)
    inverse = 10000.0 ** (-jnp.arange(0, head_size, 2, dtype=F32) / head_size)
    angles = position[:, None] * inverse[None, :]
    angles = jnp.concatenate([angles, angles], -1)
    sign = jnp.where(jnp.arange(head_size) < head_size // 2, -1.0, 1.0)
    return jnp.cos(angles), jnp.sin(angles) * sign


def attend_kernel(x_ref, gain_ref, w_ref, cos_ref, sin_ref, wout_ref,
                  mine_ref, other_ref, normed_ref, qkv_ref, lse_ref, mixed_ref, *, heads, steps):
    g = pl.program_id(0)
    length = x_ref.shape[0]
    half = length // 2
    scale = HEAD ** -0.5

    @pl.when(g == 0)
    def _():
        values = x_ref[...].astype(F32)
        inv = lax.rsqrt(jnp.mean(values * values, -1, keepdims=True) + EPSILON)
        normed_ref[...] = (values * inv * gain_ref[...]).astype(BF16)

    normed = normed_ref[...]
    cos, sin = cos_ref[...], sin_ref[...]
    projected = [dot(normed, w_ref[c]) for c in range(3)]
    for h in range(heads):
        cols = slice(h * HEAD, (h + 1) * HEAD)
        q, k, v = (p[:, cols] for p in projected)
        q = (q * cos + pltpu.roll(q, HEAD // 2, 1) * sin).astype(BF16)
        k = (k * cos + pltpu.roll(k, HEAD // 2, 1) * sin).astype(BF16)
        v = v.astype(BF16)
        qkv_ref[0, :, cols] = q
        qkv_ref[1, :, cols] = k
        qkv_ref[2, :, cols] = v
        for b in range(2):
            rows = slice(b * half, (b + 1) * half)
            keys = (b + 1) * half
            scores = dot(q[rows], k[:keys], NT) * scale
            at = lax.broadcasted_iota(jnp.int32, scores.shape, 0) + b * half
            to = lax.broadcasted_iota(jnp.int32, scores.shape, 1)
            scores = jnp.where(at >= to, scores, -1000000000.0)
            top = jnp.max(scores, -1, keepdims=True)
            weights = jnp.exp(scores - top)
            total = jnp.sum(weights, -1, keepdims=True)
            lse_ref[h, rows, :] = jnp.broadcast_to(top + jnp.log(total), (half, HEAD))
            low = (weights * (1.0 / total)).astype(BF16)
            mixed_ref[rows, pl.ds(pl.multiple_of((g * heads + h) * HEAD, HEAD), HEAD)] = dot(low, v[:keys]).astype(BF16)

    @pl.when(g == steps - 1)
    def _():
        core = lax.rem(lax.axis_index("mp"), 2)
        for ref, c in ((other_ref, 1 - core), (mine_ref, core)):
            rows = pl.ds(pl.multiple_of(c * half, half), half)
            ref[...] = dot(mixed_ref[rows, :], wout_ref[...]).astype(BF16)


def attend(tokens, gain, w3, cos, sin, w_out):
    length, model = tokens.shape
    local = w3.shape[2]
    local_heads = local // HEAD
    heads = 2 if local_heads % 2 == 0 else 1
    steps = local_heads // heads
    wide = heads * HEAD
    full = lambda *shape: pl.BlockSpec(shape, lambda g: (0,) * len(shape))
    return pl.pallas_call(
        partial(attend_kernel, heads=heads, steps=steps),
        grid=(steps,),
        in_specs=[
            full(length, model), full(1, model),
            pl.BlockSpec((3, model, wide), lambda g: (0, 0, g)),
            full(length, HEAD), full(length, HEAD), full(local, model),
        ],
        out_specs=[
            full(length // 2, model), full(length // 2, model), full(length, model),
            pl.BlockSpec((3, length, wide), lambda g: (0, 0, g)),
            pl.BlockSpec((heads, length, HEAD), lambda g: (g, 0, 0)),
            full(length, local),
        ],
        out_shape=[
            jax.ShapeDtypeStruct((length // 2, model), BF16),
            jax.ShapeDtypeStruct((length // 2, model), BF16),
            jax.ShapeDtypeStruct((length, model), BF16),
            jax.ShapeDtypeStruct((3, length, local), BF16),
            jax.ShapeDtypeStruct((local_heads, length, HEAD), F32),
            jax.ShapeDtypeStruct((length, local), BF16),
        ],
        compiler_params=params(),
        cost_estimate=cost(2 * length * model * local * 4 + 4 * length * length * local,
                           2 * (2 * length * model + 4 * model * local), length * length * local_heads),
        name="attend",
    )(tokens, gain, w3, cos, sin, w_out)


def attend_back_kernel(ga_ref, normed_ref, qkv_ref, lse_ref, mixed_ref, wout_ref, w_ref, cos_ref, sin_ref,
                       *rest, heads, steps, deps):
    grad_ref, first_ref, acc_ref = rest[deps:]
    g = pl.program_id(0)
    length = ga_ref.shape[0]
    half = length // 2
    scale = HEAD ** -0.5
    cos, sin = cos_ref[...], sin_ref[...]
    ga = ga_ref[...]
    gmixed = dot(ga, wout_ref[...], NT).astype(BF16)
    gproj = [[], [], []]
    for h in range(heads):
        cols = slice(h * HEAD, (h + 1) * HEAD)
        q, k, v = (qkv_ref[c, :, cols] for c in range(3))
        gm = gmixed[:, cols]
        gq, gk, gv = [], [None, None], [None, None]
        for b in range(2):
            rows = slice(b * half, (b + 1) * half)
            keys = (b + 1) * half
            scores = dot(q[rows], k[:keys], NT) * scale
            at = lax.broadcasted_iota(jnp.int32, scores.shape, 0) + b * half
            to = lax.broadcasted_iota(jnp.int32, scores.shape, 1)
            probs = jnp.where(at >= to, jnp.exp(scores - lse_ref[h, rows, :1]), 0.0)
            gprobs = dot(gm[rows], v[:keys], NT)
            gscores = probs * (gprobs - jnp.sum(gprobs * probs, -1, keepdims=True))
            gs = gscores.astype(BF16)
            low_probs = probs.astype(BF16)
            gq.append(dot(gs, k[:keys]) * scale)
            for j in range(b + 1):
                part = slice(j * half, (j + 1) * half)
                a = dot(gs[:, part], q[rows], TN) * scale
                c = dot(low_probs[:, part], gm[rows], TN)
                gk[j] = a if gk[j] is None else gk[j] + a
                gv[j] = c if gv[j] is None else gv[j] + c
        gq = jnp.concatenate(gq, 0)
        gk = jnp.concatenate(gk, 0)
        gv = jnp.concatenate(gv, 0)
        gproj[0].append((gq * cos - pltpu.roll(gq, HEAD // 2, 1) * sin).astype(BF16))
        gproj[1].append((gk * cos - pltpu.roll(gk, HEAD // 2, 1) * sin).astype(BF16))
        gproj[2].append(gv.astype(BF16))
    gproj = [jnp.concatenate(p, 1) for p in gproj]

    @pl.when(g == 0)
    def _():
        acc_ref[...] = jnp.zeros_like(acc_ref)

    grad_ref[3] = dot(ga, mixed_ref[...], TN).astype(BF16)
    for c in range(3):
        grad_ref[c] = dot(normed_ref[...], gproj[c], TN).astype(BF16)
        acc_ref[...] += dot(gproj[c], w_ref[c], NT)

    @pl.when(g == steps - 1)
    def _():
        first_ref[...] = acc_ref[...].astype(BF16)


def attend_back(ga, normed, qkv, lse, mixed, w_out, w3, cos, sin, deps=()):
    length, model = ga.shape
    local = w3.shape[2]
    local_heads = local // HEAD
    heads = 2 if local_heads % 2 == 0 else 1
    steps = local_heads // heads
    wide = heads * HEAD
    full = lambda *shape: pl.BlockSpec(shape, lambda g: (0,) * len(shape))
    return pl.pallas_call(
        partial(attend_back_kernel, heads=heads, steps=steps, deps=len(deps)),
        grid=(steps,),
        in_specs=[
            full(length, model), full(length, model),
            pl.BlockSpec((3, length, wide), lambda g: (0, 0, g)),
            pl.BlockSpec((heads, length, HEAD), lambda g: (g, 0, 0)),
            pl.BlockSpec((length, wide), lambda g: (0, g)),
            pl.BlockSpec((wide, model), lambda g: (g, 0)),
            pl.BlockSpec((3, model, wide), lambda g: (0, 0, g)),
            full(length, HEAD), full(length, HEAD),
        ] + [pl.BlockSpec(memory_space=pl.ANY)] * len(deps),
        out_specs=[pl.BlockSpec((4, model, wide), lambda g: (0, 0, g)), full(length, model)],
        out_shape=[
            jax.ShapeDtypeStruct((4, model, local), BF16),
            jax.ShapeDtypeStruct((length, model), BF16),
        ],
        scratch_shapes=[pltpu.VMEM((length, model), F32)],
        compiler_params=params(),
        cost_estimate=cost(2 * length * model * local * 8 + 10 * length * length * local,
                           2 * (4 * length * model + 8 * model * local), length * length * local_heads),
        name="attend_back",
    )(ga, normed, qkv, lse, mixed, w_out, w3, cos, sin, *deps)


def own_grad_kernel(sent_ref, cot_ref, bucket_ref, gate_ref, unsort_ref, up_ref, down_ref, *rest, row_bounds, deps):
    mine_ref, other_ref, act_ref, acc_ref = rest[deps:]
    level = pl.program_id(0)
    for q, rows in enumerate(row_bounds):
        @pl.when(level == q)
        def _(q=q, rows=rows):
            keep = bucket_ref[:rows, :1] >= q
            pre = dot(sent_ref[:rows], up_ref[0])
            active = jnp.where(keep, jnp.maximum(pre, 0.0), 0.0)
            act_ref[0, :rows] = (active * active).astype(BF16)
            gact = dot(cot_ref[:rows], down_ref[0], NT)
            gpre = (gact * (2.0 * gate_ref[:rows, :1]) * active).astype(BF16)
            s = dot(gpre, up_ref[0], NT)
            if q == 0:
                acc_ref[...] = s
            else:
                acc_ref[:rows] += s
            if q == len(row_bounds) - 1:
                half = mine_ref.shape[0]
                total = acc_ref[...].astype(BF16)
                other_ref[...] = dot(unsort_ref[half:], total).astype(BF16)
                mine_ref[...] = dot(unsort_ref[:half], total).astype(BF16)


def own_grad(sent, cot, bucket, gate, unsort, w_up, w_down, row_bounds, deps=()):
    length, model = sent.shape
    levels, _, hidden = w_up.shape
    full = lambda *shape: pl.BlockSpec(shape, lambda q: (0,) * len(shape))
    return pl.pallas_call(
        partial(own_grad_kernel, row_bounds=tuple(row_bounds), deps=len(deps)),
        grid=(levels,),
        in_specs=[
            full(length, model), full(length, model), full(length, 128), full(length, 128), full(length, length),
            pl.BlockSpec((1, model, hidden), lambda q: (q, 0, 0)),
            pl.BlockSpec((1, hidden, model), lambda q: (q, 0, 0)),
        ] + [pl.BlockSpec(memory_space=pl.ANY)] * len(deps),
        out_specs=[full(length // 2, model)] * 2 + [pl.BlockSpec((1, length, hidden), lambda q: (q, 0, 0))],
        out_shape=[jax.ShapeDtypeStruct((length // 2, model), BF16)] * 2
        + [jax.ShapeDtypeStruct((levels, length, hidden), BF16)],
        scratch_shapes=[pltpu.VMEM((length, model), F32)],
        compiler_params=params(),
        cost_estimate=cost(6 * sum(row_bounds) * model * hidden, 4 * levels * model * hidden + 6 * length * model),
        name="own_grad",
    )(sent, cot, bucket, gate, unsort, w_up, w_down, *deps)


def own_forward_kernel(act_ref, cot_ref, unsort_ref, down_ref, *rest, row_bounds, deps):
    ffn_ref, ggate_ref, acc_ref = rest[deps:]
    level = pl.program_id(0)
    for q, rows in enumerate(row_bounds):
        @pl.when(level == q)
        def _(q=q, rows=rows):
            f = dot(act_ref[0, :rows], down_ref[0])
            if q == 0:
                acc_ref[...] = f
            else:
                acc_ref[:rows] += f
            if q == len(row_bounds) - 1:
                total = acc_ref[...]
                ggate = jnp.sum(total * cot_ref[...].astype(F32), -1, keepdims=True)
                ggate_ref[...] = jnp.broadcast_to(ggate, ggate_ref.shape)
                ffn_ref[...] = dot(unsort_ref[...], total.astype(BF16)).astype(BF16)


def own_forward(act, cot, unsort, w_down, row_bounds, deps=()):
    length, model = cot.shape
    levels, hidden, _ = w_down.shape
    full = lambda *shape: pl.BlockSpec(shape, lambda q: (0,) * len(shape))
    return pl.pallas_call(
        partial(own_forward_kernel, row_bounds=tuple(row_bounds), deps=len(deps)),
        grid=(levels,),
        in_specs=[
            pl.BlockSpec((1, length, hidden), lambda q: (q, 0, 0)),
            full(length, model), full(length, length),
            pl.BlockSpec((1, hidden, model), lambda q: (q, 0, 0)),
        ] + [pl.BlockSpec(memory_space=pl.ANY)] * len(deps),
        out_specs=[full(length, model), full(length, 128)],
        out_shape=[jax.ShapeDtypeStruct((length, model), BF16), jax.ShapeDtypeStruct((length, 128), F32)],
        scratch_shapes=[pltpu.VMEM((length, model), F32)],
        compiler_params=params(),
        cost_estimate=cost(2 * sum(row_bounds) * model * hidden, 2 * levels * model * hidden + 6 * length * model),
        name="own_forward",
    )(act, cot, unsort, w_down, *deps)


AUX = 16


def gates_and_buckets(aux):
    row = lax.broadcasted_iota(jnp.int32, (AUX, 128), 0)
    gates = dot(aux, (row < 3).astype(BF16), TN)
    buckets = dot(aux, (row == 3).astype(BF16), TN)
    return gates, buckets


def weight_kernel(*refs, level, rows, group, offsets, fresh, carried, deps):
    count = len(offsets)
    pieces, refs = refs[:4 * count], refs[4 * count:]
    up_ref, down_ref = refs[:2]
    sums = refs[2:2 + carried]
    gup_ref, gdown_ref, up_buf, down_buf, s_buf, aux_buf, c_buf, gup, gdown, sems = refs[2 + carried + deps:]
    b = pl.program_id(0)
    steps = count // group
    core = lax.rem(lax.axis_index("mp"), 2)
    length, part = aux_buf.shape[3], s_buf.shape[2] // 2
    columns = lambda c: pl.ds(pl.multiple_of(c * part, part), part)
    slot = lax.rem(b, 2)

    def tokens_of(step):
        out = []
        for j in range(group):
            k = step * group + j
            to = pl.ds(j * rows, rows)
            mine, other = pieces[4 * k + 2], pieces[4 * k + 3]
            at = offsets[k]
            out += [
                (mine.at[pl.ds(at[2], rows)], s_buf.at[step % 2, to, columns(core)]),
                (other.at[pl.ds(at[3], rows)], s_buf.at[step % 2, to, columns(1 - core)]),
                (mine.at[pl.ds(at[2] + length, AUX), pl.ds(0, length)], aux_buf.at[step % 2, j]),
            ]
        return [pltpu.make_async_copy(x, y, sems.at[step % 2, i]) for i, (x, y) in enumerate(out)]

    def cots_of(step):
        out = []
        for j in range(group):
            k = step * group + j
            to = pl.ds(j * rows, rows)
            at = offsets[k]
            out += [
                (pieces[4 * k].at[pl.ds(at[0], rows)], c_buf.at[step % 2, to, columns(core)]),
                (pieces[4 * k + 1].at[pl.ds(at[1], rows)], c_buf.at[step % 2, to, columns(1 - core)]),
            ]
        return [pltpu.make_async_copy(x, y, sems.at[2 + step % 2, i]) for i, (x, y) in enumerate(out)]

    up_copy = pltpu.make_async_copy(up_ref.at[level], up_buf, sems.at[4, 0])
    down_copy = pltpu.make_async_copy(down_ref.at[level], down_buf, sems.at[4, 1])
    ends = [pltpu.make_async_copy(gup, gup_ref.at[level], sems.at[4, 2]),
            pltpu.make_async_copy(gdown, gdown_ref.at[level], sems.at[4, 3])]
    begins = [] if fresh else [
        pltpu.make_async_copy(sums[0].at[level], gup, sems.at[5, 0]),
        pltpu.make_async_copy(sums[1].at[level], gdown, sems.at[5, 1])]

    @pl.when(b == 0)
    def _():
        for c in [up_copy] + tokens_of(0) + [down_copy] + cots_of(0) + begins:
            c.start()

    for step in range(1, steps):
        @pl.when(b == step - 1)
        def _(step=step):
            for c in tokens_of(step) + cots_of(step):
                c.start()

    @pl.when(b == 0)
    def _():
        up_copy.wait()

    for step in range(steps):
        @pl.when(b == step)
        def _(step=step):
            for c in tokens_of(step):
                c.wait()

    columns_of = [gates_and_buckets(aux_buf[slot, j]) for j in range(group)]
    gate = jnp.concatenate([g[:rows, :1] for g, _ in columns_of], 0)
    keep = jnp.concatenate([k[:rows, :1] for _, k in columns_of], 0) >= level
    pre = dot(s_buf[slot], up_buf[...])
    active = jnp.where(keep, jnp.maximum(pre, 0.0), 0.0)
    act = (active * active * gate).astype(BF16)

    @pl.when(b == 0)
    def _():
        down_copy.wait()

    for step in range(steps):
        @pl.when(b == step)
        def _(step=step):
            for c in cots_of(step):
                c.wait()

    gact = dot(c_buf[slot], down_buf[...], NT)
    gpre = (gact * (2.0 * gate) * active).astype(BF16)

    @pl.when(b == 0)
    def _():
        if fresh:
            gup[...] = dot(s_buf[slot], gpre, TN)
            gdown[...] = dot(act, c_buf[slot], TN)
        else:
            for c in begins:
                c.wait()
            gup[...] += dot(s_buf[slot], gpre, TN)
            gdown[...] += dot(act, c_buf[slot], TN)

    if steps > 2:
        @pl.when(jnp.logical_and(b > 0, b < steps - 1))
        def _():
            gup[...] += dot(s_buf[slot], gpre, TN)
            gdown[...] += dot(act, c_buf[slot], TN)

    @pl.when(b == steps - 1)
    def _():
        gup[...] += dot(s_buf[slot], gpre, TN)
        ends[0].start()
        gdown[...] += dot(act, c_buf[slot], TN)
        ends[1].start()
        for c in ends:
            c.wait()


def weight_gradients(level, rows, length, blocks, w_up, w_down, carried, fresh, deps=()):
    levels, model, hidden = w_up.shape
    count = len(blocks)
    group = 2
    anywhere = pl.BlockSpec(memory_space=pl.ANY)
    arrays = [x for block in blocks for x, _ in block]
    offsets = tuple(tuple(at for _, at in block) for block in blocks)
    first = len(arrays) + 2
    return pl.pallas_call(
        partial(weight_kernel, level=level, rows=rows, group=group, offsets=offsets, fresh=fresh, carried=len(carried),
                deps=len(deps)),
        grid=(count // group,),
        in_specs=[anywhere] * (first + len(carried) + len(deps)),
        out_specs=[anywhere] * 2,
        out_shape=[jax.ShapeDtypeStruct((levels, model, hidden), F32), jax.ShapeDtypeStruct((levels, hidden, model), F32)],
        input_output_aliases={first: 0, first + 1: 1} if carried else {},
        scratch_shapes=[
            pltpu.VMEM((model, hidden), BF16), pltpu.VMEM((hidden, model), BF16),
            pltpu.VMEM((2, group * rows, model), BF16), pltpu.VMEM((2, group, AUX, length), BF16),
            pltpu.VMEM((2, group * rows, model), BF16),
            pltpu.VMEM((model, hidden), F32), pltpu.VMEM((hidden, model), F32),
            pltpu.SemaphoreType.DMA((6, 3 * group)),
        ],
        compiler_params=params(),
        cost_estimate=cost(8 * count * rows * model * hidden, 4 * count * rows * model + 16 * model * hidden),
        name=f"weight_gradients_{level}" + ("" if fresh else "_more"),
    )(*arrays, w_up, w_down, *carried, *deps)


def unpack_kernel(order_ref, *refs, count, carried):
    chunk_refs = refs[:count]
    qkv_ref, out_ref = refs[count + carried:]
    size = qkv_ref.shape[1]
    for k in range(count):
        @pl.when(pl.program_id(0) == k)
        def _(k=k):
            for c in range(3):
                qkv_ref[c] = chunk_refs[k][c * size:(c + 1) * size].astype(F32)
            out_ref[...] = chunk_refs[k][3 * size:4 * size].astype(F32).T


def unpack(order, chunks, size, total, carried=()):
    height, local = chunks[0].shape
    anywhere = pl.BlockSpec(memory_space=pl.ANY)
    count = len(chunks)
    return pl.pallas_call(
        partial(unpack_kernel, count=count, carried=len(carried)),
        grid_spec=pltpu.PrefetchScalarGridSpec(
            num_scalar_prefetch=1,
            grid=(count,),
            in_specs=[pl.BlockSpec((height, local), lambda b, o: (0, 0), pipeline_mode=pl.Buffered(1))] * count
            + [anywhere] * len(carried),
            out_specs=[
                pl.BlockSpec((3, size, local), lambda b, o: (0, o[b], 0)),
                pl.BlockSpec((local, size), lambda b, o: (0, o[b])),
            ],
        ),
        out_shape=[
            jax.ShapeDtypeStruct((3, total * size, local), F32),
            jax.ShapeDtypeStruct((local, total * size), F32),
        ],
        input_output_aliases={count + 1: 0, count + 2: 1} if carried else {},
        compiler_params=params(),
        cost_estimate=cost(0, 24 * count * size * local),
        name="unpack_some" if not carried else "unpack_rest",
    )(order, *chunks, *carried)


def add_kernel(*refs, count):
    total = refs[0][...].astype(F32)
    for ref in refs[1:count]:
        total = total + ref[...].astype(F32)
    refs[-1][...] = total.astype(BF16)


def add_rows(parts, deps=()):
    rows, columns = parts[0].shape
    block = pl.BlockSpec((rows // 4, columns), lambda i: (i, 0))
    return pl.pallas_call(
        partial(add_kernel, count=len(parts)),
        grid=(4,),
        in_specs=[block] * len(parts) + [pl.BlockSpec(memory_space=pl.ANY)] * len(deps),
        out_specs=block,
        out_shape=jax.ShapeDtypeStruct((rows, columns), BF16),
        compiler_params=params(),
        cost_estimate=cost(rows * columns, 6 * rows * columns),
        name="add_rows",
    )(*parts, *deps)


def pass_kernel(*refs):
    pass


def after(arrays, deps):
    anywhere = pl.BlockSpec(memory_space=pl.ANY)
    return pl.pallas_call(
        pass_kernel,
        in_specs=[anywhere] * (len(arrays) + len(deps)),
        out_specs=[anywhere] * len(arrays),
        out_shape=[jax.ShapeDtypeStruct(x.shape, x.dtype) for x in arrays],
        input_output_aliases={i: i for i in range(len(arrays))},
        compiler_params=params(),
        cost_estimate=cost(0, 0),
        name="after",
    )(*arrays, *deps)


def join_kernel(index_ref, right_local, left_local, right_ref, left_ref, *rest, cut, deps):
    right_out, left_out = rest[deps:]
    size = right_local.shape[1]
    if right_ref.shape[1] == size:
        right_out[0] = (right_local[0].astype(F32) + right_ref[0].astype(F32)).astype(BF16)
        left_out[0] = (left_local[0].astype(F32) + left_ref[0].astype(F32)).astype(BF16)
    else:
        right_out[0, :cut] = (right_local[0, :cut].astype(F32) + right_ref[0].astype(F32)).astype(BF16)
        right_out[0, cut:] = right_local[0, cut:]
        left_out[0, :cut] = left_local[0, :cut]
        left_out[0, cut:] = (left_local[0, cut:].astype(F32) + left_ref[0].astype(F32)).astype(BF16)


def join(grads, indices, right, left, size, deps=()):
    kinds, _, local = grads.shape
    arrived = right.shape[1]
    out = pl.BlockSpec((1, size, local), lambda i, o: (i, 0, 0))
    return pl.pallas_call(
        partial(join_kernel, cut=size // 2, deps=len(deps)),
        grid_spec=pltpu.PrefetchScalarGridSpec(
            num_scalar_prefetch=1,
            grid=(kinds,),
            in_specs=[
                pl.BlockSpec((1, size, local), lambda i, o: (i, o[0], 0)),
                pl.BlockSpec((1, size, local), lambda i, o: (i, o[1], 0)),
                pl.BlockSpec((1, arrived, local), lambda i, o: (i, 0, 0)),
                pl.BlockSpec((1, arrived, local), lambda i, o: (i, 0, 0)),
            ] + [pl.BlockSpec(memory_space=pl.ANY)] * len(deps),
            out_specs=[out, out],
        ),
        out_shape=[jax.ShapeDtypeStruct((kinds, size, local), BF16)] * 2,
        compiler_params=params(),
        cost_estimate=cost(2 * kinds * size * local, 12 * kinds * size * local),
        name="join",
    )(indices, grads, grads, right, left, *deps)


def join_own_kernel(index_ref, local_ref, right_ref, left_ref, extra_ref, *rest):
    kinds, size, _ = right_ref.shape
    for c in range(kinds):
        total = local_ref[c].astype(F32) + right_ref[c].astype(F32) + left_ref[c].astype(F32)
        rest[-1][c * size:(c + 1) * size] = total.astype(BF16)
    rest[-1][kinds * size:] = extra_ref[...]


def join_own(grads, indices, right, left, extra, deps=()):
    kinds, size, local = right.shape
    block = pl.BlockSpec((kinds, size, local), lambda i, o: (0, 0, 0))
    height = kinds * size + extra.shape[0]
    return pl.pallas_call(
        join_own_kernel,
        grid_spec=pltpu.PrefetchScalarGridSpec(
            num_scalar_prefetch=1,
            grid=(1,),
            in_specs=[pl.BlockSpec((kinds, size, local), lambda i, o: (0, o[0], 0)), block, block,
                      pl.BlockSpec(extra.shape, lambda i, o: (0, 0))]
            + [pl.BlockSpec(memory_space=pl.ANY)] * len(deps),
            out_specs=pl.BlockSpec((height, local), lambda i, o: (0, 0)),
        ),
        out_shape=jax.ShapeDtypeStruct((height, local), BF16),
        compiler_params=params(),
        cost_estimate=cost(2 * kinds * size * local, 8 * kinds * size * local),
        name="join_own",
    )(indices, grads, right, left, extra, *deps)


def ring_order(count):
    nz = 4 if count % 4 == 0 else 1
    ny = count // nz
    if nz == 1 or ny % 2:
        return list(range(count))
    order = [(z, 0) for z in range(nz)]
    for y in range(1, ny):
        line = list(range(1, nz))
        order += [(z, y) for z in (reversed(line) if y % 2 else line)]
    order += [(0, y) for y in range(ny - 1, 0, -1)]
    return [z * ny + y for z, y in order]


class Ring:
    def __init__(self):
        self.log = []
        self.count = lax.axis_size("dp")
        self.order = ring_order(self.count)
        n = self.count
        place = [0] * n
        for p, d in enumerate(self.order):
            place[d] = p
        self.position = jnp.array(place, jnp.int32)[lax.axis_index("dp")]
        self.right = [(self.order[p], self.order[(p + 1) % n]) for p in range(n)]
        self.left = [(self.order[(p + 1) % n], self.order[p]) for p in range(n)]

    def to_right(self, x):
        out = lax.ppermute(x, "dp", self.right)
        self.log.append(out)
        return out

    def to_left(self, x):
        out = lax.ppermute(x, "dp", self.left)
        self.log.append(out)
        return out

    def logged(self, f, *args):
        self.log = []
        out = f(*args)
        pairs = [tuple(self.log[i:i + 2]) for i in range(0, len(self.log), 2)]
        self.log = []
        return out, pairs

    def gather(self, x, axis):
        out = [x]
        r = l = x
        for _ in range(self.count // 2 - 1):
            r, l = self.to_right(r), self.to_left(l)
            out += [r, l]
        size = x.shape[axis]
        cut = size // 32 * 16
        first = self.to_right(lax.slice_in_dim(r, 0, cut, axis=axis))
        second = self.to_left(lax.slice_in_dim(l, cut, size, axis=axis))
        out.append(jnp.concatenate([first, second], axis))
        return out

    def offsets(self):
        out = [0]
        for k in range(1, self.count // 2):
            out += [-k, k]
        return out + [self.count // 2]

    def indices(self):
        return [(self.position + k) % self.count for k in self.offsets()]

    def reduce_start(self, x):
        size = x.shape[1] // self.count
        cut = size // 2
        far = self.count // 2
        at = ((self.position + far) % self.count) * size
        r = lax.dynamic_slice_in_dim(x, at, cut, axis=1)
        l = lax.dynamic_slice_in_dim(x, at + cut, cut, axis=1)
        return (self.to_right(r), self.to_left(l)), (r, l)

    def reduce_step(self, x, arrived, k, deps=()):
        indices = jnp.stack([(self.position + k) % self.count, (self.position - k) % self.count]).astype(jnp.int32)
        r, l = join(x, indices, *arrived, x.shape[1] // self.count, deps)
        return (self.to_right(r), self.to_left(l)), (r, l)

    def reduce_end(self, x, arrived, extra, deps=()):
        return join_own(x, self.position[None].astype(jnp.int32), *arrived, extra, deps)


def core_swap(x):
    n = lax.axis_size("mp")
    return lax.ppermute(x, "mp", [(i, i ^ 1) for i in range(n)])


def sum_over_x(x, deps=()):
    n = lax.axis_size("mp") // 2
    index = lax.axis_index("mp")
    parts = [x] + [
        lax.ppermute(x, "mp", [(i, (i + 2 * k) % (2 * n)) for i in range(2 * n)]) for k in range(1, n)
    ]
    if n == 1:
        return x.astype(F32)
    if deps:
        parts[1:] = after(parts[1:], deps)
    if n == 2:
        return parts[0].astype(F32) + parts[1].astype(F32)
    stacked = jnp.stack(parts)
    total = None
    for j in range(n):
        term = lax.dynamic_index_in_dim(stacked, (index // 2 - j) % n, 0, keepdims=False).astype(F32)
        total = term if total is None else total + term
    return total


def on_device(tokens, gain_first, w_qkv, w_out, gain_second, router, w_up, w_down, slot, cotangent):
    length, model = tokens.shape
    buckets = w_up.shape[0]
    devices_dp = lax.axis_size("dp")
    groups = devices_dp // buckets
    capacity = length * 5 // (4 * devices_dp)
    row_bounds = [min(length, (buckets - level) * groups * capacity) for level in range(buckets)]
    ring = Ring()
    core = lax.axis_index("mp") % 2
    half = length // 2

    bucket_ids = slot // capacity // groups
    places = jnp.arange(length, dtype=jnp.int32)
    key = (buckets - 1 - bucket_ids) * length + places
    rank = jnp.sum((key[None, :] < key[:, None]).astype(jnp.int32), 1)
    rank_here = jnp.roll(rank, -core * half)
    sort_rows = places[:, None] == rank[None, :]
    sort_here = places[:, None] == rank_here[None, :]
    sort_low = sort_here.astype(BF16)
    unsort_low = (rank_here[:, None] == places[None, :]).astype(BF16)
    bucket_sorted = jnp.sum(jnp.where(sort_rows, bucket_ids[None, :], 0), 1)

    def part_of(x, c, axis=0):
        size = x.shape[axis] // 2
        return lax.dynamic_slice_in_dim(x, c * size, size, axis=axis)

    def own_rows(x):
        return part_of(x, core)

    def other_rows(x):
        return part_of(x, 1 - core)

    def joined(mine, other):
        return jnp.concatenate([jnp.where(core == 0, mine, other), jnp.where(core == 0, other, mine)], 0)

    cot_sorted = dot(sort_rows.astype(BF16), cotangent).astype(BF16)

    cot_own = part_of(cot_sorted, core, 1)
    cot_first = ring.to_right(cot_own), ring.to_left(cot_own)

    w3 = jnp.transpose(w_qkv, (1, 0, 2))
    cos, sin = rotary_table(length, HEAD)
    part_mine, part_other, normed_low, qkv, lse, mixed = attend(tokens, gain_first[None, :], w3, cos, sin, w_out)
    attn_rows = add_rows([part_mine, core_swap(part_other)])
    attn = sum_over_x(attn_rows)

    resid = own_rows(tokens).astype(F32) + attn
    inv = lax.rsqrt(jnp.mean(resid * resid, -1, keepdims=True) + EPSILON)
    xhat = resid * inv
    normed_second = xhat * gain_second
    logits = jnp.dot(normed_second, router, precision=HIGHEST)
    prob = jax.nn.softmax(logits, axis=-1)
    onehot = (own_rows(bucket_ids)[:, None] == jnp.arange(buckets)[None, :]).astype(F32)
    gate = buckets * jnp.sum(prob * onehot, -1)
    sent_half = normed_second.astype(BF16)
    sent_both = jnp.concatenate([sent_half, core_swap(sent_half)], 0)
    gate_both = jnp.concatenate([gate, core_swap(gate)], 0)
    gate_sorted = jnp.sum(jnp.where(sort_here, gate_both[None, :], 0.0), 1)

    sent_sorted = dot(sort_low, sent_both).astype(BF16)

    gate_1 = low(gate_sorted)
    gate_2 = low(gate_sorted - gate_1.astype(F32))
    gate_3 = low(gate_sorted - gate_1.astype(F32) - gate_2.astype(F32))
    aux = jnp.stack([gate_1, gate_2, gate_3, bucket_sorted.astype(BF16)] + [jnp.zeros_like(gate_1)] * (AUX - 4))
    aux = jnp.pad(aux, ((0, 0), (0, model // 2 - length)))
    sent_own = jnp.concatenate([part_of(sent_sorted, core, 1), aux], 0)
    height = length
    blocks = [((cot_own, 0), (part_of(cot_sorted, 1 - core, 1), 0), (sent_own, 0), (part_of(sent_sorted, 1 - core, 1), 0))]

    def block(mine, other):
        return (mine, 0), (other, 0), (mine, height), (other, height)

    sent_first = ring.to_right(sent_own), ring.to_left(sent_own)

    wide = lambda x: jnp.broadcast_to(x[:, None], (length, 128))
    gsent_mine, gsent_other, act = own_grad(
        sent_sorted, cot_sorted, wide(bucket_sorted), wide(gate_sorted), unsort_low, w_up, w_down, row_bounds,
        cot_first + (sent_own,))
    gsent_rows = add_rows([gsent_mine, core_swap(gsent_other)])
    grad_sent = sum_over_x(gsent_rows).astype(BF16).astype(F32)
    ffn_part, ggate_part = own_forward(
        act, cot_sorted, sort_rows.astype(BF16).T, w_down, row_bounds, (gsent_rows,))
    far = devices_dp // 2
    met = []

    def forward(arrived, deps):
        if len(arrived) == 4:
            cot_r, cot_l, sent_r, sent_l = after(arrived, deps)
            r, l = jnp.concatenate([cot_r, sent_r], 0), jnp.concatenate([cot_l, sent_l], 0)
        else:
            r, l = after(arrived, deps)
        if len(met) < far:
            met.extend([(r, core_swap(r)), (l, core_swap(l))])
        else:
            met.extend([(r, None), (l, None)])
        if len(met) < 2 * far - 2:
            return ring.to_right(r), ring.to_left(l)
        return ring.to_right(r[:height]), ring.to_left(l[height:])

    r, l = forward(cot_first + sent_first, (ffn_part,))
    ggate_part = jnp.sum(jnp.where(sort_rows, ggate_part[:, :1], 0.0), 0)
    grad_gate = ggate_part + core_swap(ggate_part)
    grad_gate = sum_over_x(own_rows(grad_gate))

    grad_output = own_rows(cotangent).astype(F32)
    grad_prob = buckets * grad_gate[:, None] * onehot
    grad_logits = prob * (grad_prob - jnp.sum(grad_prob * prob, -1, keepdims=True))
    grad_router = jnp.dot(normed_second.T, grad_logits, precision=HIGHEST)
    grad_second = grad_sent + jnp.dot(grad_logits, router.T, precision=HIGHEST)
    grad_gain_second = jnp.sum(grad_second * xhat, 0)
    scaled = grad_second * gain_second
    grad_resid = grad_output + inv * (scaled - xhat * jnp.mean(scaled * xhat, -1, keepdims=True))
    ga_half = low(grad_resid)
    grad_attn = joined(ga_half, core_swap(ga_half))

    grads, first_part = attend_back(
        grad_attn, normed_low, qkv, lse, mixed, w_out, w3, cos, sin, (met[0][0], met[1][0]))

    ffn_other, = after([other_rows(ffn_part)], (grads,))
    ffn_sum = add_rows([own_rows(ffn_part), core_swap(ffn_other)])

    carried = ()
    arrived, sending = ring.reduce_start(grads)
    chunks = None
    step = 0

    def advance(step, arrived, deps):
        nonlocal chunks
        if step < far - 1:
            return ring.reduce_step(grads, arrived, far - 1 - step, deps)
        if step == far - 1:
            chunks = [ring.reduce_end(grads, arrived, extra, deps)]
            r = l = chunks[0]
        else:
            r, l = after(arrived, deps) if deps else arrived
            chunks.extend([r, l])
        if step < 2 * far - 2:
            sending = (r, l)
            r, l = ring.to_right(r), ring.to_left(l)
        else:
            cut = r.shape[0] // 32 * 16
            sending = (r[:cut], l[cut:])
            r, l = ring.to_right(sending[0]), ring.to_left(sending[1])
            chunks.append(jnp.concatenate([r, l], 0))
        return (r, l), sending

    steps = 2 * far - 1
    while len(met) < far:
        r, l = forward((r, l), (grads, ffn_sum, met[0][1], met[1][1]))
    near = len(met)
    sending = sending + met[-2] + met[-1]
    blocks += [block(*x) for x in met[:far - 1]]
    carried = ()
    calls = [(level, rows, True) for level, rows in enumerate(row_bounds)]
    later = [block(*x) for x in met[far - 1:]]
    extra = None
    slots = list(range(buckets))
    for slot_at, level in enumerate(slots):
        rows = row_bounds[level]
        carried = weight_gradients(level, rows, length, blocks, w_up, w_down, tuple(carried), True, sending)
        if slot_at == 0:
            ffn_rows = sum_over_x(ffn_sum, (carried[0],)).astype(BF16).astype(F32)
            output_half = (resid + gate[:, None] * ffn_rows).astype(BF16)
            first_other, = after([other_rows(first_part)], (carried[0], output_half))
            first_other = core_swap(first_other)
        if slot_at == 1:
            first_rows = add_rows([own_rows(first_part), first_other], (carried[0],))
        if slot_at == 2:
            grad_first = sum_over_x(first_rows, (carried[0],)).astype(BF16).astype(F32)
            source = own_rows(tokens).astype(F32)
            inv_first = lax.rsqrt(jnp.mean(source * source, -1, keepdims=True) + EPSILON)
            xhat_first = source * inv_first
            grad_gain_first = jnp.sum(grad_first * xhat_first, 0)
            scaled_first = grad_first * gain_first
            grad_source = inv_first * (
                scaled_first - xhat_first * jnp.mean(scaled_first * xhat_first, -1, keepdims=True))
            tokens_half = (grad_source + grad_resid).astype(BF16)
            small = jnp.concatenate([grad_router.T, grad_gain_second[None], grad_gain_first[None]], 0)
            small = jnp.pad(small, ((0, -small.shape[0] % 8), (0, 0)))
            small_other = core_swap(small)
        if slot_at == 3:
            small_other, = after([small_other], (carried[0],))
            extra = low(small + small_other).reshape(-1, w3.shape[2])
        arrived, sending = advance(step, arrived, (carried[0],))
        step += 1
        if slot_at == 3:
            r, l, *held = after([r, l] + [x for x, _ in met[far:]], (carried[0], sending[0]))
        if slot_at == 1:
            sending = sending + (output_half,)
        if slot_at == 2:
            sending = sending + (tokens_half, small)
            while len(met) < 2 * far - 2:
                r, l = forward((r, l), (carried[0],))
            sending = sending + tuple(pair[0] for pair in met[far:])
    later += [block(x, core_swap(x)) for x in held]
    later.append(((r, 0), (core_swap(r), 0), (l, 0), (core_swap(l), 0)))
    steps = 2 * far - 1
    for level, rows in enumerate(row_bounds):
        if level == buckets - 1 and step == steps:
            order = jnp.stack(ring.indices()).astype(jnp.int32)
            size = model // devices_dp
            unpacked = unpack(order[:-1], chunks[:-1], size, devices_dp)
            sending = sending + (unpacked[0],)
        carried = weight_gradients(level, rows, length, later, w_up, w_down, tuple(carried), False, sending)
        ready = ()
        if level == 0:
            others = [core_swap(x) for x in after([tokens_half, output_half], (carried[0],))]
        if level == 1:
            others = after(others, (carried[0],))
            grad_tokens = joined(tokens_half, others[0])
            output = joined(output_half, others[1])
            ready = (grad_tokens, output)
        sending = ()
        if step < steps:
            arrived, sending = advance(step, arrived, (carried[0],))
            step += 1
        sending = sending + ready
    while step < steps:
        arrived, sending = advance(step, arrived, ())
        step += 1
    grad_up, grad_down = carried
    order = jnp.stack(ring.indices()).astype(jnp.int32)
    size = model // devices_dp
    if devices_dp != 8:
        unpacked = unpack(order[:-1], chunks[:-1], size, devices_dp)
    grad_wqkv, grad_wout = unpack(order[-1:], chunks[-1:], size, devices_dp, unpacked)
    terms = jnp.stack([x[4 * size:] for x in chunks])
    by_place = jnp.zeros((devices_dp,), jnp.int32).at[order].set(jnp.arange(devices_dp, dtype=jnp.int32))
    small = jnp.sum(terms[by_place].astype(F32), 0).reshape(small.shape)

    return (
        output,
        grad_tokens,
        small[buckets + 1],
        jnp.transpose(grad_wqkv, (1, 0, 2)),
        grad_wout,
        small[buckets],
        small[:buckets].T,
        grad_up,
        grad_down,
    )


def solution(mesh):
    placed = (
        P("dp", None),
        P(),
        P(None, None, "mp"),
        P("mp", None),
        P(),
        P(),
        P(None, None, "mp"),
        P(None, "mp", None),
        P("dp"),
        P("dp", None),
    )
    return jax.shard_map(
        on_device,
        mesh=mesh,
        in_specs=placed,
        out_specs=(
            P("dp", None),
            P("dp", None),
            P(),
            P(None, None, "mp"),
            P("mp", None),
            P(),
            P(),
            P(None, None, "mp"),
            P(None, "mp", None),
        ),
        check_vma=False,
    )
```

```python
from functools import partial

import jax
import jax.numpy as jnp
from jax import lax
from jax.experimental import pallas as pl
from jax.experimental.pallas import tpu as pltpu
from jax.sharding import PartitionSpec as P

HEAD = 128
HIGHEST = lax.Precision.HIGHEST
EPSILON = 1e-05
F32 = jnp.float32
BF16 = jnp.bfloat16
VMEM_LIMIT = 56 * 1024 * 1024
COST = 4
NN = (((1,), (0,)), ((), ()))
NT = (((1,), (1,)), ((), ()))
TN = (((0,), (0,)), ((), ()))


def dot(a, b, dims=NN):
    return lax.dot_general(a, b, dims, preferred_element_type=F32)


def low(x):
    return lax.reduce_precision(x, 8, 7).astype(BF16)


def params():
    return pltpu.CompilerParams(vmem_limit_bytes=VMEM_LIMIT)


def cost(flops, nbytes, transcendentals=0):
    return pl.CostEstimate(flops=flops // COST, bytes_accessed=nbytes // COST, transcendentals=transcendentals // COST)


def rotary_table(length, head_size):
    position = jnp.arange(length, dtype=F32)
    inverse = 10000.0 ** (-jnp.arange(0, head_size, 2, dtype=F32) / head_size)
    angles = position[:, None] * inverse[None, :]
    angles = jnp.concatenate([angles, angles], -1)
    sign = jnp.where(jnp.arange(head_size) < head_size // 2, -1.0, 1.0)
    return jnp.cos(angles), jnp.sin(angles) * sign


def attend_kernel(x_ref, gain_ref, w_ref, cos_ref, sin_ref, wout_ref,
                  mine_ref, other_ref, normed_ref, qkv_ref, lse_ref, mixed_ref, *, heads, steps):
    g = pl.program_id(0)
    length = x_ref.shape[0]
    half = length // 2
    scale = HEAD ** -0.5

    @pl.when(g == 0)
    def _():
        values = x_ref[...].astype(F32)
        inv = lax.rsqrt(jnp.mean(values * values, -1, keepdims=True) + EPSILON)
        normed_ref[...] = (values * inv * gain_ref[...]).astype(BF16)

    normed = normed_ref[...]
    cos, sin = cos_ref[...], sin_ref[...]
    projected = [dot(normed, w_ref[c]) for c in range(3)]
    for h in range(heads):
        cols = slice(h * HEAD, (h + 1) * HEAD)
        q, k, v = (p[:, cols] for p in projected)
        q = (q * cos + pltpu.roll(q, HEAD // 2, 1) * sin).astype(BF16)
        k = (k * cos + pltpu.roll(k, HEAD // 2, 1) * sin).astype(BF16)
        v = v.astype(BF16)
        qkv_ref[0, :, cols] = q
        qkv_ref[1, :, cols] = k
        qkv_ref[2, :, cols] = v
        for b in range(2):
            rows = slice(b * half, (b + 1) * half)
            keys = (b + 1) * half
            scores = dot(q[rows], k[:keys], NT) * scale
            at = lax.broadcasted_iota(jnp.int32, scores.shape, 0) + b * half
            to = lax.broadcasted_iota(jnp.int32, scores.shape, 1)
            scores = jnp.where(at >= to, scores, -1000000000.0)
            top = jnp.max(scores, -1, keepdims=True)
            weights = jnp.exp(scores - top)
            total = jnp.sum(weights, -1, keepdims=True)
            lse_ref[h, rows, :] = jnp.broadcast_to(top + jnp.log(total), (half, HEAD))
            low = (weights * (1.0 / total)).astype(BF16)
            mixed_ref[rows, pl.ds(pl.multiple_of((g * heads + h) * HEAD, HEAD), HEAD)] = dot(low, v[:keys]).astype(BF16)

    @pl.when(g == steps - 1)
    def _():
        core = lax.rem(lax.axis_index("mp"), 2)
        for ref, c in ((other_ref, 1 - core), (mine_ref, core)):
            rows = pl.ds(pl.multiple_of(c * half, half), half)
            ref[...] = dot(mixed_ref[rows, :], wout_ref[...]).astype(BF16)


def attend(tokens, gain, w3, cos, sin, w_out):
    length, model = tokens.shape
    local = w3.shape[2]
    local_heads = local // HEAD
    heads = 2 if local_heads % 2 == 0 else 1
    steps = local_heads // heads
    wide = heads * HEAD
    full = lambda *shape: pl.BlockSpec(shape, lambda g: (0,) * len(shape))
    return pl.pallas_call(
        partial(attend_kernel, heads=heads, steps=steps),
        grid=(steps,),
        in_specs=[
            full(length, model), full(1, model),
            pl.BlockSpec((3, model, wide), lambda g: (0, 0, g)),
            full(length, HEAD), full(length, HEAD), full(local, model),
        ],
        out_specs=[
            full(length // 2, model), full(length // 2, model), full(length, model),
            pl.BlockSpec((3, length, wide), lambda g: (0, 0, g)),
            pl.BlockSpec((heads, length, HEAD), lambda g: (g, 0, 0)),
            full(length, local),
        ],
        out_shape=[
            jax.ShapeDtypeStruct((length // 2, model), BF16),
            jax.ShapeDtypeStruct((length // 2, model), BF16),
            jax.ShapeDtypeStruct((length, model), BF16),
            jax.ShapeDtypeStruct((3, length, local), BF16),
            jax.ShapeDtypeStruct((local_heads, length, HEAD), F32),
            jax.ShapeDtypeStruct((length, local), BF16),
        ],
        compiler_params=params(),
        cost_estimate=cost(2 * length * model * local * 4 + 4 * length * length * local,
                           2 * (2 * length * model + 4 * model * local), length * length * local_heads),
        name="attend",
    )(tokens, gain, w3, cos, sin, w_out)


def attend_back_kernel(ga_ref, normed_ref, qkv_ref, lse_ref, mixed_ref, wout_ref, w_ref, cos_ref, sin_ref,
                       *rest, heads, steps, deps):
    grad_ref, first_ref, acc_ref = rest[deps:]
    g = pl.program_id(0)
    length = ga_ref.shape[0]
    half = length // 2
    scale = HEAD ** -0.5
    cos, sin = cos_ref[...], sin_ref[...]
    ga = ga_ref[...]
    gmixed = dot(ga, wout_ref[...], NT).astype(BF16)
    gproj = [[], [], []]
    for h in range(heads):
        cols = slice(h * HEAD, (h + 1) * HEAD)
        q, k, v = (qkv_ref[c, :, cols] for c in range(3))
        gm = gmixed[:, cols]
        gq, gk, gv = [], [None, None], [None, None]
        for b in range(2):
            rows = slice(b * half, (b + 1) * half)
            keys = (b + 1) * half
            scores = dot(q[rows], k[:keys], NT) * scale
            at = lax.broadcasted_iota(jnp.int32, scores.shape, 0) + b * half
            to = lax.broadcasted_iota(jnp.int32, scores.shape, 1)
            probs = jnp.where(at >= to, jnp.exp(scores - lse_ref[h, rows, :1]), 0.0)
            gprobs = dot(gm[rows], v[:keys], NT)
            gscores = probs * (gprobs - jnp.sum(gprobs * probs, -1, keepdims=True))
            gs = gscores.astype(BF16)
            low_probs = probs.astype(BF16)
            gq.append(dot(gs, k[:keys]) * scale)
            for j in range(b + 1):
                part = slice(j * half, (j + 1) * half)
                a = dot(gs[:, part], q[rows], TN) * scale
                c = dot(low_probs[:, part], gm[rows], TN)
                gk[j] = a if gk[j] is None else gk[j] + a
                gv[j] = c if gv[j] is None else gv[j] + c
        gq = jnp.concatenate(gq, 0)
        gk = jnp.concatenate(gk, 0)
        gv = jnp.concatenate(gv, 0)
        gproj[0].append((gq * cos - pltpu.roll(gq, HEAD // 2, 1) * sin).astype(BF16))
        gproj[1].append((gk * cos - pltpu.roll(gk, HEAD // 2, 1) * sin).astype(BF16))
        gproj[2].append(gv.astype(BF16))
    gproj = [jnp.concatenate(p, 1) for p in gproj]

    @pl.when(g == 0)
    def _():
        acc_ref[...] = jnp.zeros_like(acc_ref)

    grad_ref[3] = dot(ga, mixed_ref[...], TN).astype(BF16)
    for c in range(3):
        grad_ref[c] = dot(normed_ref[...], gproj[c], TN).astype(BF16)
        acc_ref[...] += dot(gproj[c], w_ref[c], NT)

    @pl.when(g == steps - 1)
    def _():
        first_ref[...] = acc_ref[...].astype(BF16)


def attend_back(ga, normed, qkv, lse, mixed, w_out, w3, cos, sin, deps=()):
    length, model = ga.shape
    local = w3.shape[2]
    local_heads = local // HEAD
    heads = 2 if local_heads % 2 == 0 else 1
    steps = local_heads // heads
    wide = heads * HEAD
    full = lambda *shape: pl.BlockSpec(shape, lambda g: (0,) * len(shape))
    return pl.pallas_call(
        partial(attend_back_kernel, heads=heads, steps=steps, deps=len(deps)),
        grid=(steps,),
        in_specs=[
            full(length, model), full(length, model),
            pl.BlockSpec((3, length, wide), lambda g: (0, 0, g)),
            pl.BlockSpec((heads, length, HEAD), lambda g: (g, 0, 0)),
            pl.BlockSpec((length, wide), lambda g: (0, g)),
            pl.BlockSpec((wide, model), lambda g: (g, 0)),
            pl.BlockSpec((3, model, wide), lambda g: (0, 0, g)),
            full(length, HEAD), full(length, HEAD),
        ] + [pl.BlockSpec(memory_space=pl.ANY)] * len(deps),
        out_specs=[pl.BlockSpec((4, model, wide), lambda g: (0, 0, g)), full(length, model)],
        out_shape=[
            jax.ShapeDtypeStruct((4, model, local), BF16),
            jax.ShapeDtypeStruct((length, model), BF16),
        ],
        scratch_shapes=[pltpu.VMEM((length, model), F32)],
        compiler_params=params(),
        cost_estimate=cost(2 * length * model * local * 8 + 10 * length * length * local,
                           2 * (4 * length * model + 8 * model * local), length * length * local_heads),
        name="attend_back",
    )(ga, normed, qkv, lse, mixed, w_out, w3, cos, sin, *deps)


def own_grad_kernel(sent_ref, cot_ref, bucket_ref, gate_ref, unsort_ref, up_ref, down_ref, *rest, row_bounds, deps):
    mine_ref, other_ref, act_ref, acc_ref = rest[deps:]
    level = pl.program_id(0)
    for q, rows in enumerate(row_bounds):
        @pl.when(level == q)
        def _(q=q, rows=rows):
            keep = bucket_ref[:rows, :1] >= q
            pre = dot(sent_ref[:rows], up_ref[0])
            active = jnp.where(keep, jnp.maximum(pre, 0.0), 0.0)
            act_ref[0, :rows] = (active * active).astype(BF16)
            gact = dot(cot_ref[:rows], down_ref[0], NT)
            gpre = (gact * (2.0 * gate_ref[:rows, :1]) * active).astype(BF16)
            s = dot(gpre, up_ref[0], NT)
            if q == 0:
                acc_ref[...] = s
            else:
                acc_ref[:rows] += s
            if q == len(row_bounds) - 1:
                half = mine_ref.shape[0]
                total = acc_ref[...].astype(BF16)
                other_ref[...] = dot(unsort_ref[half:], total).astype(BF16)
                mine_ref[...] = dot(unsort_ref[:half], total).astype(BF16)


def own_grad(sent, cot, bucket, gate, unsort, w_up, w_down, row_bounds, deps=()):
    length, model = sent.shape
    levels, _, hidden = w_up.shape
    full = lambda *shape: pl.BlockSpec(shape, lambda q: (0,) * len(shape))
    return pl.pallas_call(
        partial(own_grad_kernel, row_bounds=tuple(row_bounds), deps=len(deps)),
        grid=(levels,),
        in_specs=[
            full(length, model), full(length, model), full(length, 128), full(length, 128), full(length, length),
            pl.BlockSpec((1, model, hidden), lambda q: (q, 0, 0)),
            pl.BlockSpec((1, hidden, model), lambda q: (q, 0, 0)),
        ] + [pl.BlockSpec(memory_space=pl.ANY)] * len(deps),
        out_specs=[full(length // 2, model)] * 2 + [pl.BlockSpec((1, length, hidden), lambda q: (q, 0, 0))],
        out_shape=[jax.ShapeDtypeStruct((length // 2, model), BF16)] * 2
        + [jax.ShapeDtypeStruct((levels, length, hidden), BF16)],
        scratch_shapes=[pltpu.VMEM((length, model), F32)],
        compiler_params=params(),
        cost_estimate=cost(6 * sum(row_bounds) * model * hidden, 4 * levels * model * hidden + 6 * length * model),
        name="own_grad",
    )(sent, cot, bucket, gate, unsort, w_up, w_down, *deps)


def own_forward_kernel(act_ref, cot_ref, unsort_ref, down_ref, *rest, row_bounds, deps):
    ffn_ref, ggate_ref, acc_ref = rest[deps:]
    level = pl.program_id(0)
    for q, rows in enumerate(row_bounds):
        @pl.when(level == q)
        def _(q=q, rows=rows):
            f = dot(act_ref[0, :rows], down_ref[0])
            if q == 0:
                acc_ref[...] = f
            else:
                acc_ref[:rows] += f
            if q == len(row_bounds) - 1:
                total = acc_ref[...]
                ggate = jnp.sum(total * cot_ref[...].astype(F32), -1, keepdims=True)
                ggate_ref[...] = jnp.broadcast_to(ggate, ggate_ref.shape)
                ffn_ref[...] = dot(unsort_ref[...], total.astype(BF16)).astype(BF16)


def own_forward(act, cot, unsort, w_down, row_bounds, deps=()):
    length, model = cot.shape
    levels, hidden, _ = w_down.shape
    full = lambda *shape: pl.BlockSpec(shape, lambda q: (0,) * len(shape))
    return pl.pallas_call(
        partial(own_forward_kernel, row_bounds=tuple(row_bounds), deps=len(deps)),
        grid=(levels,),
        in_specs=[
            pl.BlockSpec((1, length, hidden), lambda q: (q, 0, 0)),
            full(length, model), full(length, length),
            pl.BlockSpec((1, hidden, model), lambda q: (q, 0, 0)),
        ] + [pl.BlockSpec(memory_space=pl.ANY)] * len(deps),
        out_specs=[full(length, model), full(length, 128)],
        out_shape=[jax.ShapeDtypeStruct((length, model), BF16), jax.ShapeDtypeStruct((length, 128), F32)],
        scratch_shapes=[pltpu.VMEM((length, model), F32)],
        compiler_params=params(),
        cost_estimate=cost(2 * sum(row_bounds) * model * hidden, 2 * levels * model * hidden + 6 * length * model),
        name="own_forward",
    )(act, cot, unsort, w_down, *deps)


AUX = 16


def gates_and_buckets(aux):
    row = lax.broadcasted_iota(jnp.int32, (AUX, 128), 0)
    gates = dot(aux, (row < 3).astype(BF16), TN)
    buckets = dot(aux, (row == 3).astype(BF16), TN)
    return gates, buckets


def weight_kernel(*refs, level, rows, group, offsets, fresh, carried, deps):
    count = len(offsets)
    pieces, refs = refs[:4 * count], refs[4 * count:]
    up_ref, down_ref = refs[:2]
    sums = refs[2:2 + carried]
    gup_ref, gdown_ref, up_buf, down_buf, s_buf, aux_buf, c_buf, gup, gdown, sems = refs[2 + carried + deps:]
    b = pl.program_id(0)
    steps = count // group
    core = lax.rem(lax.axis_index("mp"), 2)
    length, part = aux_buf.shape[3], s_buf.shape[2] // 2
    columns = lambda c: pl.ds(pl.multiple_of(c * part, part), part)
    slot = lax.rem(b, 2)

    def tokens_of(step):
        out = []
        for j in range(group):
            k = step * group + j
            to = pl.ds(j * rows, rows)
            mine, other = pieces[4 * k + 2], pieces[4 * k + 3]
            at = offsets[k]
            out += [
                (mine.at[pl.ds(at[2], rows)], s_buf.at[step % 2, to, columns(core)]),
                (other.at[pl.ds(at[3], rows)], s_buf.at[step % 2, to, columns(1 - core)]),
                (mine.at[pl.ds(at[2] + length, AUX), pl.ds(0, length)], aux_buf.at[step % 2, j]),
            ]
        return [pltpu.make_async_copy(x, y, sems.at[step % 2, i]) for i, (x, y) in enumerate(out)]

    def cots_of(step):
        out = []
        for j in range(group):
            k = step * group + j
            to = pl.ds(j * rows, rows)
            at = offsets[k]
            out += [
                (pieces[4 * k].at[pl.ds(at[0], rows)], c_buf.at[step % 2, to, columns(core)]),
                (pieces[4 * k + 1].at[pl.ds(at[1], rows)], c_buf.at[step % 2, to, columns(1 - core)]),
            ]
        return [pltpu.make_async_copy(x, y, sems.at[2 + step % 2, i]) for i, (x, y) in enumerate(out)]

    up_copy = pltpu.make_async_copy(up_ref.at[level], up_buf, sems.at[4, 0])
    down_copy = pltpu.make_async_copy(down_ref.at[level], down_buf, sems.at[4, 1])
    ends = [pltpu.make_async_copy(gup, gup_ref.at[level], sems.at[4, 2]),
            pltpu.make_async_copy(gdown, gdown_ref.at[level], sems.at[4, 3])]
    begins = [] if fresh else [
        pltpu.make_async_copy(sums[0].at[level], gup, sems.at[5, 0]),
        pltpu.make_async_copy(sums[1].at[level], gdown, sems.at[5, 1])]

    @pl.when(b == 0)
    def _():
        for c in [up_copy] + tokens_of(0) + [down_copy] + cots_of(0) + begins:
            c.start()

    for step in range(1, steps):
        @pl.when(b == step - 1)
        def _(step=step):
            for c in tokens_of(step) + cots_of(step):
                c.start()

    @pl.when(b == 0)
    def _():
        up_copy.wait()

    for step in range(steps):
        @pl.when(b == step)
        def _(step=step):
            for c in tokens_of(step):
                c.wait()

    columns_of = [gates_and_buckets(aux_buf[slot, j]) for j in range(group)]
    gate = jnp.concatenate([g[:rows, :1] for g, _ in columns_of], 0)
    keep = jnp.concatenate([k[:rows, :1] for _, k in columns_of], 0) >= level
    pre = dot(s_buf[slot], up_buf[...])
    active = jnp.where(keep, jnp.maximum(pre, 0.0), 0.0)
    act = (active * active * gate).astype(BF16)

    @pl.when(b == 0)
    def _():
        down_copy.wait()

    for step in range(steps):
        @pl.when(b == step)
        def _(step=step):
            for c in cots_of(step):
                c.wait()

    gact = dot(c_buf[slot], down_buf[...], NT)
    gpre = (gact * (2.0 * gate) * active).astype(BF16)

    @pl.when(b == 0)
    def _():
        if fresh:
            gup[...] = dot(s_buf[slot], gpre, TN)
            gdown[...] = dot(act, c_buf[slot], TN)
        else:
            for c in begins:
                c.wait()
            gup[...] += dot(s_buf[slot], gpre, TN)
            gdown[...] += dot(act, c_buf[slot], TN)

    if steps > 2:
        @pl.when(jnp.logical_and(b > 0, b < steps - 1))
        def _():
            gup[...] += dot(s_buf[slot], gpre, TN)
            gdown[...] += dot(act, c_buf[slot], TN)

    @pl.when(b == steps - 1)
    def _():
        gup[...] += dot(s_buf[slot], gpre, TN)
        ends[0].start()
        gdown[...] += dot(act, c_buf[slot], TN)
        ends[1].start()
        for c in ends:
            c.wait()


def weight_gradients(level, rows, length, blocks, w_up, w_down, carried, fresh, deps=()):
    levels, model, hidden = w_up.shape
    count = len(blocks)
    group = 2
    anywhere = pl.BlockSpec(memory_space=pl.ANY)
    arrays = [x for block in blocks for x, _ in block]
    offsets = tuple(tuple(at for _, at in block) for block in blocks)
    first = len(arrays) + 2
    return pl.pallas_call(
        partial(weight_kernel, level=level, rows=rows, group=group, offsets=offsets, fresh=fresh, carried=len(carried),
                deps=len(deps)),
        grid=(count // group,),
        in_specs=[anywhere] * (first + len(carried) + len(deps)),
        out_specs=[anywhere] * 2,
        out_shape=[jax.ShapeDtypeStruct((levels, model, hidden), F32), jax.ShapeDtypeStruct((levels, hidden, model), F32)],
        input_output_aliases={first: 0, first + 1: 1} if carried else {},
        scratch_shapes=[
            pltpu.VMEM((model, hidden), BF16), pltpu.VMEM((hidden, model), BF16),
            pltpu.VMEM((2, group * rows, model), BF16), pltpu.VMEM((2, group, AUX, length), BF16),
            pltpu.VMEM((2, group * rows, model), BF16),
            pltpu.VMEM((model, hidden), F32), pltpu.VMEM((hidden, model), F32),
            pltpu.SemaphoreType.DMA((6, 3 * group)),
        ],
        compiler_params=params(),
        cost_estimate=cost(8 * count * rows * model * hidden, 4 * count * rows * model + 16 * model * hidden),
        name=f"weight_gradients_{level}" + ("" if fresh else "_more"),
    )(*arrays, w_up, w_down, *carried, *deps)


def unpack_kernel(order_ref, *refs, count, carried):
    chunk_refs = refs[:count]
    qkv_ref, out_ref = refs[count + carried:]
    size = qkv_ref.shape[1]
    for k in range(count):
        @pl.when(pl.program_id(0) == k)
        def _(k=k):
            for c in range(3):
                qkv_ref[c] = chunk_refs[k][c * size:(c + 1) * size].astype(F32)
            out_ref[...] = chunk_refs[k][3 * size:4 * size].astype(F32).T


def unpack(order, chunks, size, total, carried=()):
    height, local = chunks[0].shape
    anywhere = pl.BlockSpec(memory_space=pl.ANY)
    count = len(chunks)
    return pl.pallas_call(
        partial(unpack_kernel, count=count, carried=len(carried)),
        grid_spec=pltpu.PrefetchScalarGridSpec(
            num_scalar_prefetch=1,
            grid=(count,),
            in_specs=[pl.BlockSpec((height, local), lambda b, o: (0, 0), pipeline_mode=pl.Buffered(1))] * count
            + [anywhere] * len(carried),
            out_specs=[
                pl.BlockSpec((3, size, local), lambda b, o: (0, o[b], 0)),
                pl.BlockSpec((local, size), lambda b, o: (0, o[b])),
            ],
        ),
        out_shape=[
            jax.ShapeDtypeStruct((3, total * size, local), F32),
            jax.ShapeDtypeStruct((local, total * size), F32),
        ],
        input_output_aliases={count + 1: 0, count + 2: 1} if carried else {},
        compiler_params=params(),
        cost_estimate=cost(0, 24 * count * size * local),
        name="unpack_some" if not carried else "unpack_rest",
    )(order, *chunks, *carried)


def add_kernel(*refs, count):
    total = refs[0][...].astype(F32)
    for ref in refs[1:count]:
        total = total + ref[...].astype(F32)
    refs[-1][...] = total.astype(BF16)


def add_rows(parts, deps=()):
    rows, columns = parts[0].shape
    block = pl.BlockSpec((rows // 4, columns), lambda i: (i, 0))
    return pl.pallas_call(
        partial(add_kernel, count=len(parts)),
        grid=(4,),
        in_specs=[block] * len(parts) + [pl.BlockSpec(memory_space=pl.ANY)] * len(deps),
        out_specs=block,
        out_shape=jax.ShapeDtypeStruct((rows, columns), BF16),
        compiler_params=params(),
        cost_estimate=cost(rows * columns, 6 * rows * columns),
        name="add_rows",
    )(*parts, *deps)


def pass_kernel(*refs):
    pass


def after(arrays, deps):
    anywhere = pl.BlockSpec(memory_space=pl.ANY)
    return pl.pallas_call(
        pass_kernel,
        in_specs=[anywhere] * (len(arrays) + len(deps)),
        out_specs=[anywhere] * len(arrays),
        out_shape=[jax.ShapeDtypeStruct(x.shape, x.dtype) for x in arrays],
        input_output_aliases={i: i for i in range(len(arrays))},
        compiler_params=params(),
        cost_estimate=cost(0, 0),
        name="after",
    )(*arrays, *deps)


def join_kernel(index_ref, right_local, left_local, right_ref, left_ref, *rest, cut, deps):
    right_out, left_out = rest[deps:]
    size = right_local.shape[1]
    if right_ref.shape[1] == size:
        right_out[0] = (right_local[0].astype(F32) + right_ref[0].astype(F32)).astype(BF16)
        left_out[0] = (left_local[0].astype(F32) + left_ref[0].astype(F32)).astype(BF16)
    else:
        right_out[0, :cut] = (right_local[0, :cut].astype(F32) + right_ref[0].astype(F32)).astype(BF16)
        right_out[0, cut:] = right_local[0, cut:]
        left_out[0, :cut] = left_local[0, :cut]
        left_out[0, cut:] = (left_local[0, cut:].astype(F32) + left_ref[0].astype(F32)).astype(BF16)


def join(grads, indices, right, left, size, deps=()):
    kinds, _, local = grads.shape
    arrived = right.shape[1]
    out = pl.BlockSpec((1, size, local), lambda i, o: (i, 0, 0))
    return pl.pallas_call(
        partial(join_kernel, cut=size // 2, deps=len(deps)),
        grid_spec=pltpu.PrefetchScalarGridSpec(
            num_scalar_prefetch=1,
            grid=(kinds,),
            in_specs=[
                pl.BlockSpec((1, size, local), lambda i, o: (i, o[0], 0)),
                pl.BlockSpec((1, size, local), lambda i, o: (i, o[1], 0)),
                pl.BlockSpec((1, arrived, local), lambda i, o: (i, 0, 0)),
                pl.BlockSpec((1, arrived, local), lambda i, o: (i, 0, 0)),
            ] + [pl.BlockSpec(memory_space=pl.ANY)] * len(deps),
            out_specs=[out, out],
        ),
        out_shape=[jax.ShapeDtypeStruct((kinds, size, local), BF16)] * 2,
        compiler_params=params(),
        cost_estimate=cost(2 * kinds * size * local, 12 * kinds * size * local),
        name="join",
    )(indices, grads, grads, right, left, *deps)


def join_own_kernel(index_ref, local_ref, right_ref, left_ref, extra_ref, *rest):
    kinds, size, _ = right_ref.shape
    for c in range(kinds):
        total = local_ref[c].astype(F32) + right_ref[c].astype(F32) + left_ref[c].astype(F32)
        rest[-1][c * size:(c + 1) * size] = total.astype(BF16)
    rest[-1][kinds * size:] = extra_ref[...]


def join_own(grads, indices, right, left, extra, deps=()):
    kinds, size, local = right.shape
    block = pl.BlockSpec((kinds, size, local), lambda i, o: (0, 0, 0))
    height = kinds * size + extra.shape[0]
    return pl.pallas_call(
        join_own_kernel,
        grid_spec=pltpu.PrefetchScalarGridSpec(
            num_scalar_prefetch=1,
            grid=(1,),
            in_specs=[pl.BlockSpec((kinds, size, local), lambda i, o: (0, o[0], 0)), block, block,
                      pl.BlockSpec(extra.shape, lambda i, o: (0, 0))]
            + [pl.BlockSpec(memory_space=pl.ANY)] * len(deps),
            out_specs=pl.BlockSpec((height, local), lambda i, o: (0, 0)),
        ),
        out_shape=jax.ShapeDtypeStruct((height, local), BF16),
        compiler_params=params(),
        cost_estimate=cost(2 * kinds * size * local, 8 * kinds * size * local),
        name="join_own",
    )(indices, grads, right, left, extra, *deps)


def ring_order(count):
    nz = 4 if count % 4 == 0 else 1
    ny = count // nz
    if nz == 1 or ny % 2:
        return list(range(count))
    order = [(z, 0) for z in range(nz)]
    for y in range(1, ny):
        line = list(range(1, nz))
        order += [(z, y) for z in (reversed(line) if y % 2 else line)]
    order += [(0, y) for y in range(ny - 1, 0, -1)]
    return [z * ny + y for z, y in order]


class Ring:
    def __init__(self):
        self.log = []
        self.count = lax.axis_size("dp")
        self.order = ring_order(self.count)
        n = self.count
        place = [0] * n
        for p, d in enumerate(self.order):
            place[d] = p
        self.position = jnp.array(place, jnp.int32)[lax.axis_index("dp")]
        self.right = [(self.order[p], self.order[(p + 1) % n]) for p in range(n)]
        self.left = [(self.order[(p + 1) % n], self.order[p]) for p in range(n)]

    def to_right(self, x):
        out = lax.ppermute(x, "dp", self.right)
        self.log.append(out)
        return out

    def to_left(self, x):
        out = lax.ppermute(x, "dp", self.left)
        self.log.append(out)
        return out

    def logged(self, f, *args):
        self.log = []
        out = f(*args)
        pairs = [tuple(self.log[i:i + 2]) for i in range(0, len(self.log), 2)]
        self.log = []
        return out, pairs

    def gather(self, x, axis):
        out = [x]
        r = l = x
        for _ in range(self.count // 2 - 1):
            r, l = self.to_right(r), self.to_left(l)
            out += [r, l]
        size = x.shape[axis]
        cut = size // 32 * 16
        first = self.to_right(lax.slice_in_dim(r, 0, cut, axis=axis))
        second = self.to_left(lax.slice_in_dim(l, cut, size, axis=axis))
        out.append(jnp.concatenate([first, second], axis))
        return out

    def offsets(self):
        out = [0]
        for k in range(1, self.count // 2):
            out += [-k, k]
        return out + [self.count // 2]

    def indices(self):
        return [(self.position + k) % self.count for k in self.offsets()]

    def reduce_start(self, x):
        size = x.shape[1] // self.count
        cut = size // 2
        far = self.count // 2
        at = ((self.position + far) % self.count) * size
        r = lax.dynamic_slice_in_dim(x, at, cut, axis=1)
        l = lax.dynamic_slice_in_dim(x, at + cut, cut, axis=1)
        return (self.to_right(r), self.to_left(l)), (r, l)

    def reduce_step(self, x, arrived, k, deps=()):
        indices = jnp.stack([(self.position + k) % self.count, (self.position - k) % self.count]).astype(jnp.int32)
        r, l = join(x, indices, *arrived, x.shape[1] // self.count, deps)
        return (self.to_right(r), self.to_left(l)), (r, l)

    def reduce_end(self, x, arrived, extra, deps=()):
        return join_own(x, self.position[None].astype(jnp.int32), *arrived, extra, deps)


def core_swap(x):
    n = lax.axis_size("mp")
    return lax.ppermute(x, "mp", [(i, i ^ 1) for i in range(n)])


def sum_over_x(x, deps=()):
    n = lax.axis_size("mp") // 2
    index = lax.axis_index("mp")
    parts = [x] + [
        lax.ppermute(x, "mp", [(i, (i + 2 * k) % (2 * n)) for i in range(2 * n)]) for k in range(1, n)
    ]
    if n == 1:
        return x.astype(F32)
    if deps:
        parts[1:] = after(parts[1:], deps)
    if n == 2:
        return parts[0].astype(F32) + parts[1].astype(F32)
    stacked = jnp.stack(parts)
    total = None
    for j in range(n):
        term = lax.dynamic_index_in_dim(stacked, (index // 2 - j) % n, 0, keepdims=False).astype(F32)
        total = term if total is None else total + term
    return total


def on_device(tokens, gain_first, w_qkv, w_out, gain_second, router, w_up, w_down, slot, cotangent):
    length, model = tokens.shape
    buckets = w_up.shape[0]
    devices_dp = lax.axis_size("dp")
    groups = devices_dp // buckets
    capacity = length * 5 // (4 * devices_dp)
    row_bounds = [min(length, (buckets - level) * groups * capacity) for level in range(buckets)]
    ring = Ring()
    core = lax.axis_index("mp") % 2
    half = length // 2

    bucket_ids = slot // capacity // groups
    places = jnp.arange(length, dtype=jnp.int32)
    key = (buckets - 1 - bucket_ids) * length + places
    rank = jnp.sum((key[None, :] < key[:, None]).astype(jnp.int32), 1)
    rank_here = jnp.roll(rank, -core * half)
    sort_rows = places[:, None] == rank[None, :]
    sort_here = places[:, None] == rank_here[None, :]
    sort_low = sort_here.astype(BF16)
    unsort_low = (rank_here[:, None] == places[None, :]).astype(BF16)
    bucket_sorted = jnp.sum(jnp.where(sort_rows, bucket_ids[None, :], 0), 1)

    def part_of(x, c, axis=0):
        size = x.shape[axis] // 2
        return lax.dynamic_slice_in_dim(x, c * size, size, axis=axis)

    def own_rows(x):
        return part_of(x, core)

    def other_rows(x):
        return part_of(x, 1 - core)

    def joined(mine, other):
        return jnp.concatenate([jnp.where(core == 0, mine, other), jnp.where(core == 0, other, mine)], 0)

    cot_sorted = dot(sort_rows.astype(BF16), cotangent).astype(BF16)

    cot_own = part_of(cot_sorted, core, 1)
    cot_first = ring.to_right(cot_own), ring.to_left(cot_own)

    w3 = jnp.transpose(w_qkv, (1, 0, 2))
    cos, sin = rotary_table(length, HEAD)
    part_mine, part_other, normed_low, qkv, lse, mixed = attend(tokens, gain_first[None, :], w3, cos, sin, w_out)
    attn_rows = add_rows([part_mine, core_swap(part_other)])
    attn = sum_over_x(attn_rows)

    resid = own_rows(tokens).astype(F32) + attn
    inv = lax.rsqrt(jnp.mean(resid * resid, -1, keepdims=True) + EPSILON)
    xhat = resid * inv
    normed_second = xhat * gain_second
    logits = jnp.dot(normed_second, router, precision=HIGHEST)
    prob = jax.nn.softmax(logits, axis=-1)
    onehot = (own_rows(bucket_ids)[:, None] == jnp.arange(buckets)[None, :]).astype(F32)
    gate = buckets * jnp.sum(prob * onehot, -1)
    sent_half = normed_second.astype(BF16)
    sent_both = jnp.concatenate([sent_half, core_swap(sent_half)], 0)
    gate_both = jnp.concatenate([gate, core_swap(gate)], 0)
    gate_sorted = jnp.sum(jnp.where(sort_here, gate_both[None, :], 0.0), 1)

    sent_sorted = dot(sort_low, sent_both).astype(BF16)

    gate_1 = low(gate_sorted)
    gate_2 = low(gate_sorted - gate_1.astype(F32))
    gate_3 = low(gate_sorted - gate_1.astype(F32) - gate_2.astype(F32))
    aux = jnp.stack([gate_1, gate_2, gate_3, bucket_sorted.astype(BF16)] + [jnp.zeros_like(gate_1)] * (AUX - 4))
    aux = jnp.pad(aux, ((0, 0), (0, model // 2 - length)))
    sent_own = jnp.concatenate([part_of(sent_sorted, core, 1), aux], 0)
    height = length
    blocks = [((cot_own, 0), (part_of(cot_sorted, 1 - core, 1), 0), (sent_own, 0), (part_of(sent_sorted, 1 - core, 1), 0))]

    def block(mine, other):
        return (mine, 0), (other, 0), (mine, height), (other, height)

    sent_first = ring.to_right(sent_own), ring.to_left(sent_own)

    wide = lambda x: jnp.broadcast_to(x[:, None], (length, 128))
    gsent_mine, gsent_other, act = own_grad(
        sent_sorted, cot_sorted, wide(bucket_sorted), wide(gate_sorted), unsort_low, w_up, w_down, row_bounds,
        cot_first + (sent_own,))
    gsent_rows = add_rows([gsent_mine, core_swap(gsent_other)])
    grad_sent = sum_over_x(gsent_rows).astype(BF16).astype(F32)
    far = devices_dp // 2
    met = []

    def forward(arrived, deps):
        if len(arrived) == 4:
            cot_r, cot_l, sent_r, sent_l = after(arrived, deps)
            r, l = jnp.concatenate([cot_r, sent_r], 0), jnp.concatenate([cot_l, sent_l], 0)
        else:
            r, l = after(arrived, deps)
        if len(met) < far:
            met.extend([(r, core_swap(r)), (l, core_swap(l))])
        else:
            met.extend([(r, None), (l, None)])
        if len(met) < 2 * far - 2:
            return ring.to_right(r), ring.to_left(l)
        return ring.to_right(r[:height]), ring.to_left(l[height:])

    r, l = forward(cot_first + sent_first, (gsent_rows,))
    ffn_part, ggate_part = own_forward(
        act, cot_sorted, sort_rows.astype(BF16).T, w_down, row_bounds, (gsent_rows, met[0][0], met[1][0]))
    ggate_part = jnp.sum(jnp.where(sort_rows, ggate_part[:, :1], 0.0), 0)
    grad_gate = ggate_part + core_swap(ggate_part)
    grad_gate = sum_over_x(own_rows(grad_gate))

    grad_output = own_rows(cotangent).astype(F32)
    grad_prob = buckets * grad_gate[:, None] * onehot
    grad_logits = prob * (grad_prob - jnp.sum(grad_prob * prob, -1, keepdims=True))
    grad_router = jnp.dot(normed_second.T, grad_logits, precision=HIGHEST)
    grad_second = grad_sent + jnp.dot(grad_logits, router.T, precision=HIGHEST)
    grad_gain_second = jnp.sum(grad_second * xhat, 0)
    scaled = grad_second * gain_second
    grad_resid = grad_output + inv * (scaled - xhat * jnp.mean(scaled * xhat, -1, keepdims=True))
    ga_half = low(grad_resid)
    grad_attn = joined(ga_half, core_swap(ga_half))

    grads, first_part = attend_back(
        grad_attn, normed_low, qkv, lse, mixed, w_out, w3, cos, sin, met[0] + met[1])

    ffn_other, = after([other_rows(ffn_part)], (grads,))
    ffn_sum = add_rows([own_rows(ffn_part), core_swap(ffn_other)])

    carried = ()
    arrived, sending = ring.reduce_start(grads)
    chunks = None
    step = 0

    def advance(step, arrived, deps):
        nonlocal chunks
        if step < far - 1:
            return ring.reduce_step(grads, arrived, far - 1 - step, deps)
        if step == far - 1:
            chunks = [ring.reduce_end(grads, arrived, extra, deps)]
            r = l = chunks[0]
        else:
            r, l = after(arrived, deps) if deps else arrived
            chunks.extend([r, l])
        if step < 2 * far - 2:
            sending = (r, l)
            r, l = ring.to_right(r), ring.to_left(l)
        else:
            cut = r.shape[0] // 32 * 16
            sending = (r[:cut], l[cut:])
            r, l = ring.to_right(sending[0]), ring.to_left(sending[1])
            chunks.append(jnp.concatenate([r, l], 0))
        return (r, l), sending

    steps = 2 * far - 1
    while len(met) < far:
        r, l = forward((r, l), (grads, ffn_sum))
    near = len(met)
    sending = sending + met[-2] + met[-1]
    blocks += [block(*x) for x in met[:far - 1]]
    carried = ()
    calls = [(level, rows, True) for level, rows in enumerate(row_bounds)]
    later = [block(*x) for x in met[far - 1:]]
    extra = None
    slots = list(range(buckets))
    for slot_at, level in enumerate(slots):
        rows = row_bounds[level]
        carried = weight_gradients(level, rows, length, blocks, w_up, w_down, tuple(carried), True, sending)
        if slot_at == 0:
            ffn_rows = sum_over_x(ffn_sum, (carried[0],)).astype(BF16).astype(F32)
            output_half = (resid + gate[:, None] * ffn_rows).astype(BF16)
            first_other, = after([other_rows(first_part)], (carried[0], output_half))
            first_other = core_swap(first_other)
        if slot_at == 1:
            first_rows = add_rows([own_rows(first_part), first_other], (carried[0],))
        if slot_at == 2:
            grad_first = sum_over_x(first_rows, (carried[0],)).astype(BF16).astype(F32)
            source = own_rows(tokens).astype(F32)
            inv_first = lax.rsqrt(jnp.mean(source * source, -1, keepdims=True) + EPSILON)
            xhat_first = source * inv_first
            grad_gain_first = jnp.sum(grad_first * xhat_first, 0)
            scaled_first = grad_first * gain_first
            grad_source = inv_first * (
                scaled_first - xhat_first * jnp.mean(scaled_first * xhat_first, -1, keepdims=True))
            tokens_half = (grad_source + grad_resid).astype(BF16)
            small = jnp.concatenate([grad_router.T, grad_gain_second[None], grad_gain_first[None]], 0)
            small = jnp.pad(small, ((0, -small.shape[0] % 8), (0, 0)))
            small_other = core_swap(small)
        if slot_at == 3:
            small_other, = after([small_other], (carried[0],))
            extra = low(small + small_other).reshape(-1, w3.shape[2])
        arrived, sending = advance(step, arrived, (carried[0],))
        step += 1
        if slot_at == 3:
            r, l, *held = after([r, l] + [x for x, _ in met[far:]], (carried[0], sending[0]))
        if slot_at == 1:
            sending = sending + (output_half,)
        if slot_at == 2:
            sending = sending + (tokens_half, small)
            while len(met) < 2 * far - 2:
                r, l = forward((r, l), (carried[0],))
            sending = sending + tuple(pair[0] for pair in met[far:])
    later += [block(x, core_swap(x)) for x in held]
    later.append(((r, 0), (core_swap(r), 0), (l, 0), (core_swap(l), 0)))
    steps = 2 * far - 1
    for level, rows in enumerate(row_bounds):
        if level == buckets - 1 and step == steps:
            order = jnp.stack(ring.indices()).astype(jnp.int32)
            size = model // devices_dp
            unpacked = unpack(order[:-1], chunks[:-1], size, devices_dp)
            sending = sending + (unpacked[0],)
        carried = weight_gradients(level, rows, length, later, w_up, w_down, tuple(carried), False, sending)
        ready = ()
        if level == 0:
            others = [core_swap(x) for x in after([tokens_half, output_half], (carried[0],))]
        if level == 1:
            others = after(others, (carried[0],))
            grad_tokens = joined(tokens_half, others[0])
            output = joined(output_half, others[1])
            ready = (grad_tokens, output)
        sending = ()
        if step < steps:
            arrived, sending = advance(step, arrived, (carried[0],))
            step += 1
        sending = sending + ready
    while step < steps:
        arrived, sending = advance(step, arrived, ())
        step += 1
    grad_up, grad_down = carried
    order = jnp.stack(ring.indices()).astype(jnp.int32)
    size = model // devices_dp
    if devices_dp != 8:
        unpacked = unpack(order[:-1], chunks[:-1], size, devices_dp)
    grad_wqkv, grad_wout = unpack(order[-1:], chunks[-1:], size, devices_dp, unpacked)
    terms = jnp.stack([x[4 * size:] for x in chunks])
    by_place = jnp.zeros((devices_dp,), jnp.int32).at[order].set(jnp.arange(devices_dp, dtype=jnp.int32))
    small = jnp.sum(terms[by_place].astype(F32), 0).reshape(small.shape)

    return (
        output,
        grad_tokens,
        small[buckets + 1],
        jnp.transpose(grad_wqkv, (1, 0, 2)),
        grad_wout,
        small[buckets],
        small[:buckets].T,
        grad_up,
        grad_down,
    )


def solution(mesh):
    placed = (
        P("dp", None),
        P(),
        P(None, None, "mp"),
        P("mp", None),
        P(),
        P(),
        P(None, None, "mp"),
        P(None, "mp", None),
        P("dp"),
        P("dp", None),
    )
    return jax.shard_map(
        on_device,
        mesh=mesh,
        in_specs=placed,
        out_specs=(
            P("dp", None),
            P("dp", None),
            P(),
            P(None, None, "mp"),
            P("mp", None),
            P(),
            P(),
            P(None, None, "mp"),
            P(None, "mp", None),
        ),
        check_vma=False,
    )
```

```python
from functools import partial

import jax
import jax.numpy as jnp
from jax import lax
from jax.experimental import pallas as pl
from jax.experimental.pallas import tpu as pltpu
from jax.sharding import PartitionSpec as P

HEAD = 128
HIGHEST = lax.Precision.HIGHEST
EPSILON = 1e-05
F32 = jnp.float32
BF16 = jnp.bfloat16
VMEM_LIMIT = 56 * 1024 * 1024
COST = 4
NN = (((1,), (0,)), ((), ()))
NT = (((1,), (1,)), ((), ()))
TN = (((0,), (0,)), ((), ()))


def dot(a, b, dims=NN):
    return lax.dot_general(a, b, dims, preferred_element_type=F32)


def low(x):
    return lax.reduce_precision(x, 8, 7).astype(BF16)


def params():
    return pltpu.CompilerParams(vmem_limit_bytes=VMEM_LIMIT)


def cost(flops, nbytes, transcendentals=0):
    return pl.CostEstimate(flops=flops // COST, bytes_accessed=nbytes // COST, transcendentals=transcendentals // COST)


def rotary_table(length, head_size):
    position = jnp.arange(length, dtype=F32)
    inverse = 10000.0 ** (-jnp.arange(0, head_size, 2, dtype=F32) / head_size)
    angles = position[:, None] * inverse[None, :]
    angles = jnp.concatenate([angles, angles], -1)
    sign = jnp.where(jnp.arange(head_size) < head_size // 2, -1.0, 1.0)
    return jnp.cos(angles), jnp.sin(angles) * sign


def attend_kernel(x_ref, gain_ref, w_ref, cos_ref, sin_ref, wout_ref,
                  mine_ref, other_ref, normed_ref, qkv_ref, lse_ref, mixed_ref, *, heads, steps):
    g = pl.program_id(0)
    length = x_ref.shape[0]
    half = length // 2
    scale = HEAD ** -0.5

    @pl.when(g == 0)
    def _():
        values = x_ref[...].astype(F32)
        inv = lax.rsqrt(jnp.mean(values * values, -1, keepdims=True) + EPSILON)
        normed_ref[...] = (values * inv * gain_ref[...]).astype(BF16)

    normed = normed_ref[...]
    cos, sin = cos_ref[...], sin_ref[...]
    projected = [dot(normed, w_ref[c]) for c in range(3)]
    for h in range(heads):
        cols = slice(h * HEAD, (h + 1) * HEAD)
        q, k, v = (p[:, cols] for p in projected)
        q = (q * cos + pltpu.roll(q, HEAD // 2, 1) * sin).astype(BF16)
        k = (k * cos + pltpu.roll(k, HEAD // 2, 1) * sin).astype(BF16)
        v = v.astype(BF16)
        qkv_ref[0, :, cols] = q
        qkv_ref[1, :, cols] = k
        qkv_ref[2, :, cols] = v
        for b in range(2):
            rows = slice(b * half, (b + 1) * half)
            keys = (b + 1) * half
            scores = dot(q[rows], k[:keys], NT) * scale
            at = lax.broadcasted_iota(jnp.int32, scores.shape, 0) + b * half
            to = lax.broadcasted_iota(jnp.int32, scores.shape, 1)
            scores = jnp.where(at >= to, scores, -1000000000.0)
            top = jnp.max(scores, -1, keepdims=True)
            weights = jnp.exp(scores - top)
            total = jnp.sum(weights, -1, keepdims=True)
            lse_ref[h, rows, :] = jnp.broadcast_to(top + jnp.log(total), (half, HEAD))
            low = (weights * (1.0 / total)).astype(BF16)
            mixed_ref[rows, pl.ds(pl.multiple_of((g * heads + h) * HEAD, HEAD), HEAD)] = dot(low, v[:keys]).astype(BF16)

    @pl.when(g == steps - 1)
    def _():
        core = lax.rem(lax.axis_index("mp"), 2)
        for ref, c in ((other_ref, 1 - core), (mine_ref, core)):
            rows = pl.ds(pl.multiple_of(c * half, half), half)
            ref[...] = dot(mixed_ref[rows, :], wout_ref[...]).astype(BF16)


def attend(tokens, gain, w3, cos, sin, w_out):
    length, model = tokens.shape
    local = w3.shape[2]
    local_heads = local // HEAD
    heads = 2 if local_heads % 2 == 0 else 1
    steps = local_heads // heads
    wide = heads * HEAD
    full = lambda *shape: pl.BlockSpec(shape, lambda g: (0,) * len(shape))
    return pl.pallas_call(
        partial(attend_kernel, heads=heads, steps=steps),
        grid=(steps,),
        in_specs=[
            full(length, model), full(1, model),
            pl.BlockSpec((3, model, wide), lambda g: (0, 0, g)),
            full(length, HEAD), full(length, HEAD), full(local, model),
        ],
        out_specs=[
            full(length // 2, model), full(length // 2, model), full(length, model),
            pl.BlockSpec((3, length, wide), lambda g: (0, 0, g)),
            pl.BlockSpec((heads, length, HEAD), lambda g: (g, 0, 0)),
            full(length, local),
        ],
        out_shape=[
            jax.ShapeDtypeStruct((length // 2, model), BF16),
            jax.ShapeDtypeStruct((length // 2, model), BF16),
            jax.ShapeDtypeStruct((length, model), BF16),
            jax.ShapeDtypeStruct((3, length, local), BF16),
            jax.ShapeDtypeStruct((local_heads, length, HEAD), F32),
            jax.ShapeDtypeStruct((length, local), BF16),
        ],
        compiler_params=params(),
        cost_estimate=cost(2 * length * model * local * 4 + 4 * length * length * local,
                           2 * (2 * length * model + 4 * model * local), length * length * local_heads),
        name="attend",
    )(tokens, gain, w3, cos, sin, w_out)


def attend_back_kernel(ga_ref, normed_ref, qkv_ref, lse_ref, mixed_ref, wout_ref, w_ref, cos_ref, sin_ref,
                       *rest, heads, steps, deps):
    grad_ref, first_ref, acc_ref = rest[deps:]
    g = pl.program_id(0)
    length = ga_ref.shape[0]
    half = length // 2
    scale = HEAD ** -0.5
    cos, sin = cos_ref[...], sin_ref[...]
    ga = ga_ref[...]
    gmixed = dot(ga, wout_ref[...], NT).astype(BF16)
    gproj = [[], [], []]
    for h in range(heads):
        cols = slice(h * HEAD, (h + 1) * HEAD)
        q, k, v = (qkv_ref[c, :, cols] for c in range(3))
        gm = gmixed[:, cols]
        gq, gk, gv = [], [None, None], [None, None]
        for b in range(2):
            rows = slice(b * half, (b + 1) * half)
            keys = (b + 1) * half
            scores = dot(q[rows], k[:keys], NT) * scale
            at = lax.broadcasted_iota(jnp.int32, scores.shape, 0) + b * half
            to = lax.broadcasted_iota(jnp.int32, scores.shape, 1)
            probs = jnp.where(at >= to, jnp.exp(scores - lse_ref[h, rows, :1]), 0.0)
            gprobs = dot(gm[rows], v[:keys], NT)
            gscores = probs * (gprobs - jnp.sum(gprobs * probs, -1, keepdims=True))
            gs = gscores.astype(BF16)
            low_probs = probs.astype(BF16)
            gq.append(dot(gs, k[:keys]) * scale)
            for j in range(b + 1):
                part = slice(j * half, (j + 1) * half)
                a = dot(gs[:, part], q[rows], TN) * scale
                c = dot(low_probs[:, part], gm[rows], TN)
                gk[j] = a if gk[j] is None else gk[j] + a
                gv[j] = c if gv[j] is None else gv[j] + c
        gq = jnp.concatenate(gq, 0)
        gk = jnp.concatenate(gk, 0)
        gv = jnp.concatenate(gv, 0)
        gproj[0].append((gq * cos - pltpu.roll(gq, HEAD // 2, 1) * sin).astype(BF16))
        gproj[1].append((gk * cos - pltpu.roll(gk, HEAD // 2, 1) * sin).astype(BF16))
        gproj[2].append(gv.astype(BF16))
    gproj = [jnp.concatenate(p, 1) for p in gproj]

    @pl.when(g == 0)
    def _():
        acc_ref[...] = jnp.zeros_like(acc_ref)

    grad_ref[3] = dot(ga, mixed_ref[...], TN).astype(BF16)
    for c in range(3):
        grad_ref[c] = dot(normed_ref[...], gproj[c], TN).astype(BF16)
        acc_ref[...] += dot(gproj[c], w_ref[c], NT)

    @pl.when(g == steps - 1)
    def _():
        first_ref[...] = acc_ref[...].astype(BF16)


def attend_back(ga, normed, qkv, lse, mixed, w_out, w3, cos, sin, deps=()):
    length, model = ga.shape
    local = w3.shape[2]
    local_heads = local // HEAD
    heads = 2 if local_heads % 2 == 0 else 1
    steps = local_heads // heads
    wide = heads * HEAD
    full = lambda *shape: pl.BlockSpec(shape, lambda g: (0,) * len(shape))
    return pl.pallas_call(
        partial(attend_back_kernel, heads=heads, steps=steps, deps=len(deps)),
        grid=(steps,),
        in_specs=[
            full(length, model), full(length, model),
            pl.BlockSpec((3, length, wide), lambda g: (0, 0, g)),
            pl.BlockSpec((heads, length, HEAD), lambda g: (g, 0, 0)),
            pl.BlockSpec((length, wide), lambda g: (0, g)),
            pl.BlockSpec((wide, model), lambda g: (g, 0)),
            pl.BlockSpec((3, model, wide), lambda g: (0, 0, g)),
            full(length, HEAD), full(length, HEAD),
        ] + [pl.BlockSpec(memory_space=pl.ANY)] * len(deps),
        out_specs=[pl.BlockSpec((4, model, wide), lambda g: (0, 0, g)), full(length, model)],
        out_shape=[
            jax.ShapeDtypeStruct((4, model, local), BF16),
            jax.ShapeDtypeStruct((length, model), BF16),
        ],
        scratch_shapes=[pltpu.VMEM((length, model), F32)],
        compiler_params=params(),
        cost_estimate=cost(2 * length * model * local * 8 + 10 * length * length * local,
                           2 * (4 * length * model + 8 * model * local), length * length * local_heads),
        name="attend_back",
    )(ga, normed, qkv, lse, mixed, w_out, w3, cos, sin, *deps)


def own_grad_kernel(sent_ref, cot_ref, bucket_ref, gate_ref, unsort_ref, up_ref, down_ref, *rest, row_bounds, deps):
    mine_ref, other_ref, act_ref, acc_ref = rest[deps:]
    level = pl.program_id(0)
    for q, rows in enumerate(row_bounds):
        @pl.when(level == q)
        def _(q=q, rows=rows):
            keep = bucket_ref[:rows, :1] >= q
            pre = dot(sent_ref[:rows], up_ref[0])
            active = jnp.where(keep, jnp.maximum(pre, 0.0), 0.0)
            act_ref[0, :rows] = (active * active).astype(BF16)
            gact = dot(cot_ref[:rows], down_ref[0], NT)
            gpre = (gact * (2.0 * gate_ref[:rows, :1]) * active).astype(BF16)
            s = dot(gpre, up_ref[0], NT)
            if q == 0:
                acc_ref[...] = s
            else:
                acc_ref[:rows] += s
            if q == len(row_bounds) - 1:
                half = mine_ref.shape[0]
                total = acc_ref[...].astype(BF16)
                other_ref[...] = dot(unsort_ref[half:], total).astype(BF16)
                mine_ref[...] = dot(unsort_ref[:half], total).astype(BF16)


def own_grad(sent, cot, bucket, gate, unsort, w_up, w_down, row_bounds, deps=()):
    length, model = sent.shape
    levels, _, hidden = w_up.shape
    full = lambda *shape: pl.BlockSpec(shape, lambda q: (0,) * len(shape))
    return pl.pallas_call(
        partial(own_grad_kernel, row_bounds=tuple(row_bounds), deps=len(deps)),
        grid=(levels,),
        in_specs=[
            full(length, model), full(length, model), full(length, 128), full(length, 128), full(length, length),
            pl.BlockSpec((1, model, hidden), lambda q: (q, 0, 0)),
            pl.BlockSpec((1, hidden, model), lambda q: (q, 0, 0)),
        ] + [pl.BlockSpec(memory_space=pl.ANY)] * len(deps),
        out_specs=[full(length // 2, model)] * 2 + [pl.BlockSpec((1, length, hidden), lambda q: (q, 0, 0))],
        out_shape=[jax.ShapeDtypeStruct((length // 2, model), BF16)] * 2
        + [jax.ShapeDtypeStruct((levels, length, hidden), BF16)],
        scratch_shapes=[pltpu.VMEM((length, model), F32)],
        compiler_params=params(),
        cost_estimate=cost(6 * sum(row_bounds) * model * hidden, 4 * levels * model * hidden + 6 * length * model),
        name="own_grad",
    )(sent, cot, bucket, gate, unsort, w_up, w_down, *deps)


def own_forward_kernel(act_ref, cot_ref, unsort_ref, down_ref, *rest, row_bounds, deps):
    ffn_ref, ggate_ref, acc_ref = rest[deps:]
    level = pl.program_id(0)
    for q, rows in enumerate(row_bounds):
        @pl.when(level == q)
        def _(q=q, rows=rows):
            f = dot(act_ref[0, :rows], down_ref[0])
            if q == 0:
                acc_ref[...] = f
            else:
                acc_ref[:rows] += f
            if q == len(row_bounds) - 1:
                total = acc_ref[...]
                ggate = jnp.sum(total * cot_ref[...].astype(F32), -1, keepdims=True)
                ggate_ref[...] = jnp.broadcast_to(ggate, ggate_ref.shape)
                ffn_ref[...] = dot(unsort_ref[...], total.astype(BF16)).astype(BF16)


def own_forward(act, cot, unsort, w_down, row_bounds, deps=()):
    length, model = cot.shape
    levels, hidden, _ = w_down.shape
    full = lambda *shape: pl.BlockSpec(shape, lambda q: (0,) * len(shape))
    return pl.pallas_call(
        partial(own_forward_kernel, row_bounds=tuple(row_bounds), deps=len(deps)),
        grid=(levels,),
        in_specs=[
            pl.BlockSpec((1, length, hidden), lambda q: (q, 0, 0)),
            full(length, model), full(length, length),
            pl.BlockSpec((1, hidden, model), lambda q: (q, 0, 0)),
        ] + [pl.BlockSpec(memory_space=pl.ANY)] * len(deps),
        out_specs=[full(length, model), full(length, 128)],
        out_shape=[jax.ShapeDtypeStruct((length, model), BF16), jax.ShapeDtypeStruct((length, 128), F32)],
        scratch_shapes=[pltpu.VMEM((length, model), F32)],
        compiler_params=params(),
        cost_estimate=cost(2 * sum(row_bounds) * model * hidden, 2 * levels * model * hidden + 6 * length * model),
        name="own_forward",
    )(act, cot, unsort, w_down, *deps)


AUX = 16


def gates_and_buckets(aux):
    row = lax.broadcasted_iota(jnp.int32, (AUX, 128), 0)
    gates = dot(aux, (row < 3).astype(BF16), TN)
    buckets = dot(aux, (row == 3).astype(BF16), TN)
    return gates, buckets


def weight_kernel(*refs, level, rows, group, offsets, fresh, carried, deps):
    count = len(offsets)
    pieces, refs = refs[:4 * count], refs[4 * count:]
    up_ref, down_ref = refs[:2]
    sums = refs[2:2 + carried]
    gup_ref, gdown_ref, up_buf, down_buf, s_buf, aux_buf, c_buf, gup, gdown, sems = refs[2 + carried + deps:]
    b = pl.program_id(0)
    steps = count // group
    core = lax.rem(lax.axis_index("mp"), 2)
    length, part = aux_buf.shape[3], s_buf.shape[2] // 2
    columns = lambda c: pl.ds(pl.multiple_of(c * part, part), part)
    slot = lax.rem(b, 2)

    def tokens_of(step):
        out = []
        for j in range(group):
            k = step * group + j
            to = pl.ds(j * rows, rows)
            mine, other = pieces[4 * k + 2], pieces[4 * k + 3]
            at = offsets[k]
            out += [
                (mine.at[pl.ds(at[2], rows)], s_buf.at[step % 2, to, columns(core)]),
                (other.at[pl.ds(at[3], rows)], s_buf.at[step % 2, to, columns(1 - core)]),
                (mine.at[pl.ds(at[2] + length, AUX), pl.ds(0, length)], aux_buf.at[step % 2, j]),
            ]
        return [pltpu.make_async_copy(x, y, sems.at[step % 2, i]) for i, (x, y) in enumerate(out)]

    def cots_of(step):
        out = []
        for j in range(group):
            k = step * group + j
            to = pl.ds(j * rows, rows)
            at = offsets[k]
            out += [
                (pieces[4 * k].at[pl.ds(at[0], rows)], c_buf.at[step % 2, to, columns(core)]),
                (pieces[4 * k + 1].at[pl.ds(at[1], rows)], c_buf.at[step % 2, to, columns(1 - core)]),
            ]
        return [pltpu.make_async_copy(x, y, sems.at[2 + step % 2, i]) for i, (x, y) in enumerate(out)]

    up_copy = pltpu.make_async_copy(up_ref.at[level], up_buf, sems.at[4, 0])
    down_copy = pltpu.make_async_copy(down_ref.at[level], down_buf, sems.at[4, 1])
    ends = [pltpu.make_async_copy(gup, gup_ref.at[level], sems.at[4, 2]),
            pltpu.make_async_copy(gdown, gdown_ref.at[level], sems.at[4, 3])]
    begins = [] if fresh else [
        pltpu.make_async_copy(sums[0].at[level], gup, sems.at[5, 0]),
        pltpu.make_async_copy(sums[1].at[level], gdown, sems.at[5, 1])]

    @pl.when(b == 0)
    def _():
        for c in [up_copy] + tokens_of(0) + [down_copy] + cots_of(0) + begins:
            c.start()

    for step in range(1, steps):
        @pl.when(b == step - 1)
        def _(step=step):
            for c in tokens_of(step) + cots_of(step):
                c.start()

    @pl.when(b == 0)
    def _():
        up_copy.wait()

    for step in range(steps):
        @pl.when(b == step)
        def _(step=step):
            for c in tokens_of(step):
                c.wait()

    columns_of = [gates_and_buckets(aux_buf[slot, j]) for j in range(group)]
    gate = jnp.concatenate([g[:rows, :1] for g, _ in columns_of], 0)
    keep = jnp.concatenate([k[:rows, :1] for _, k in columns_of], 0) >= level
    pre = dot(s_buf[slot], up_buf[...])
    active = jnp.where(keep, jnp.maximum(pre, 0.0), 0.0)
    act = (active * active * gate).astype(BF16)

    @pl.when(b == 0)
    def _():
        down_copy.wait()

    for step in range(steps):
        @pl.when(b == step)
        def _(step=step):
            for c in cots_of(step):
                c.wait()

    gact = dot(c_buf[slot], down_buf[...], NT)
    gpre = (gact * (2.0 * gate) * active).astype(BF16)

    @pl.when(b == 0)
    def _():
        if fresh:
            gup[...] = dot(s_buf[slot], gpre, TN)
            gdown[...] = dot(act, c_buf[slot], TN)
        else:
            for c in begins:
                c.wait()
            gup[...] += dot(s_buf[slot], gpre, TN)
            gdown[...] += dot(act, c_buf[slot], TN)

    if steps > 2:
        @pl.when(jnp.logical_and(b > 0, b < steps - 1))
        def _():
            gup[...] += dot(s_buf[slot], gpre, TN)
            gdown[...] += dot(act, c_buf[slot], TN)

    @pl.when(b == steps - 1)
    def _():
        gup[...] += dot(s_buf[slot], gpre, TN)
        ends[0].start()
        gdown[...] += dot(act, c_buf[slot], TN)
        ends[1].start()
        for c in ends:
            c.wait()


def weight_gradients(level, rows, length, blocks, w_up, w_down, carried, fresh, deps=()):
    levels, model, hidden = w_up.shape
    count = len(blocks)
    group = 2
    anywhere = pl.BlockSpec(memory_space=pl.ANY)
    arrays = [x for block in blocks for x, _ in block]
    offsets = tuple(tuple(at for _, at in block) for block in blocks)
    first = len(arrays) + 2
    return pl.pallas_call(
        partial(weight_kernel, level=level, rows=rows, group=group, offsets=offsets, fresh=fresh, carried=len(carried),
                deps=len(deps)),
        grid=(count // group,),
        in_specs=[anywhere] * (first + len(carried) + len(deps)),
        out_specs=[anywhere] * 2,
        out_shape=[jax.ShapeDtypeStruct((levels, model, hidden), F32), jax.ShapeDtypeStruct((levels, hidden, model), F32)],
        input_output_aliases={first: 0, first + 1: 1} if carried else {},
        scratch_shapes=[
            pltpu.VMEM((model, hidden), BF16), pltpu.VMEM((hidden, model), BF16),
            pltpu.VMEM((2, group * rows, model), BF16), pltpu.VMEM((2, group, AUX, length), BF16),
            pltpu.VMEM((2, group * rows, model), BF16),
            pltpu.VMEM((model, hidden), F32), pltpu.VMEM((hidden, model), F32),
            pltpu.SemaphoreType.DMA((6, 3 * group)),
        ],
        compiler_params=params(),
        cost_estimate=cost(8 * count * rows * model * hidden, 4 * count * rows * model + 16 * model * hidden),
        name=f"weight_gradients_{level}" + ("" if fresh else "_more"),
    )(*arrays, w_up, w_down, *carried, *deps)


def unpack_kernel(order_ref, *refs, count, carried):
    chunk_refs = refs[:count]
    qkv_ref, out_ref = refs[count + carried:]
    size = qkv_ref.shape[1]
    for k in range(count):
        @pl.when(pl.program_id(0) == k)
        def _(k=k):
            for c in range(3):
                qkv_ref[c] = chunk_refs[k][c * size:(c + 1) * size].astype(F32)
            out_ref[...] = chunk_refs[k][3 * size:4 * size].astype(F32).T


def unpack(order, chunks, size, total, carried=()):
    height, local = chunks[0].shape
    anywhere = pl.BlockSpec(memory_space=pl.ANY)
    count = len(chunks)
    return pl.pallas_call(
        partial(unpack_kernel, count=count, carried=len(carried)),
        grid_spec=pltpu.PrefetchScalarGridSpec(
            num_scalar_prefetch=1,
            grid=(count,),
            in_specs=[pl.BlockSpec((height, local), lambda b, o: (0, 0), pipeline_mode=pl.Buffered(1))] * count
            + [anywhere] * len(carried),
            out_specs=[
                pl.BlockSpec((3, size, local), lambda b, o: (0, o[b], 0)),
                pl.BlockSpec((local, size), lambda b, o: (0, o[b])),
            ],
        ),
        out_shape=[
            jax.ShapeDtypeStruct((3, total * size, local), F32),
            jax.ShapeDtypeStruct((local, total * size), F32),
        ],
        input_output_aliases={count + 1: 0, count + 2: 1} if carried else {},
        compiler_params=params(),
        cost_estimate=cost(0, 24 * count * size * local),
        name="unpack_some" if not carried else "unpack_rest",
    )(order, *chunks, *carried)


def add_kernel(*refs, count):
    total = refs[0][...].astype(F32)
    for ref in refs[1:count]:
        total = total + ref[...].astype(F32)
    refs[-1][...] = total.astype(BF16)


def add_rows(parts, deps=()):
    rows, columns = parts[0].shape
    block = pl.BlockSpec((rows // 4, columns), lambda i: (i, 0))
    return pl.pallas_call(
        partial(add_kernel, count=len(parts)),
        grid=(4,),
        in_specs=[block] * len(parts) + [pl.BlockSpec(memory_space=pl.ANY)] * len(deps),
        out_specs=block,
        out_shape=jax.ShapeDtypeStruct((rows, columns), BF16),
        compiler_params=params(),
        cost_estimate=cost(rows * columns, 6 * rows * columns),
        name="add_rows",
    )(*parts, *deps)


def pass_kernel(*refs):
    pass


def after(arrays, deps):
    anywhere = pl.BlockSpec(memory_space=pl.ANY)
    return pl.pallas_call(
        pass_kernel,
        in_specs=[anywhere] * (len(arrays) + len(deps)),
        out_specs=[anywhere] * len(arrays),
        out_shape=[jax.ShapeDtypeStruct(x.shape, x.dtype) for x in arrays],
        input_output_aliases={i: i for i in range(len(arrays))},
        compiler_params=params(),
        cost_estimate=cost(0, 0),
        name="after",
    )(*arrays, *deps)


def join_kernel(index_ref, right_local, left_local, right_ref, left_ref, *rest, cut, deps):
    right_out, left_out = rest[deps:]
    size = right_local.shape[1]
    if right_ref.shape[1] == size:
        right_out[0] = (right_local[0].astype(F32) + right_ref[0].astype(F32)).astype(BF16)
        left_out[0] = (left_local[0].astype(F32) + left_ref[0].astype(F32)).astype(BF16)
    else:
        right_out[0, :cut] = (right_local[0, :cut].astype(F32) + right_ref[0].astype(F32)).astype(BF16)
        right_out[0, cut:] = right_local[0, cut:]
        left_out[0, :cut] = left_local[0, :cut]
        left_out[0, cut:] = (left_local[0, cut:].astype(F32) + left_ref[0].astype(F32)).astype(BF16)


def join(grads, indices, right, left, size, deps=()):
    kinds, _, local = grads.shape
    arrived = right.shape[1]
    out = pl.BlockSpec((1, size, local), lambda i, o: (i, 0, 0))
    return pl.pallas_call(
        partial(join_kernel, cut=size // 2, deps=len(deps)),
        grid_spec=pltpu.PrefetchScalarGridSpec(
            num_scalar_prefetch=1,
            grid=(kinds,),
            in_specs=[
                pl.BlockSpec((1, size, local), lambda i, o: (i, o[0], 0)),
                pl.BlockSpec((1, size, local), lambda i, o: (i, o[1], 0)),
                pl.BlockSpec((1, arrived, local), lambda i, o: (i, 0, 0)),
                pl.BlockSpec((1, arrived, local), lambda i, o: (i, 0, 0)),
            ] + [pl.BlockSpec(memory_space=pl.ANY)] * len(deps),
            out_specs=[out, out],
        ),
        out_shape=[jax.ShapeDtypeStruct((kinds, size, local), BF16)] * 2,
        compiler_params=params(),
        cost_estimate=cost(2 * kinds * size * local, 12 * kinds * size * local),
        name="join",
    )(indices, grads, grads, right, left, *deps)


def join_own_kernel(index_ref, local_ref, right_ref, left_ref, extra_ref, *rest):
    kinds, size, _ = right_ref.shape
    for c in range(kinds):
        total = local_ref[c].astype(F32) + right_ref[c].astype(F32) + left_ref[c].astype(F32)
        rest[-1][c * size:(c + 1) * size] = total.astype(BF16)
    rest[-1][kinds * size:] = extra_ref[...]


def join_own(grads, indices, right, left, extra, deps=()):
    kinds, size, local = right.shape
    block = pl.BlockSpec((kinds, size, local), lambda i, o: (0, 0, 0))
    height = kinds * size + extra.shape[0]
    return pl.pallas_call(
        join_own_kernel,
        grid_spec=pltpu.PrefetchScalarGridSpec(
            num_scalar_prefetch=1,
            grid=(1,),
            in_specs=[pl.BlockSpec((kinds, size, local), lambda i, o: (0, o[0], 0)), block, block,
                      pl.BlockSpec(extra.shape, lambda i, o: (0, 0))]
            + [pl.BlockSpec(memory_space=pl.ANY)] * len(deps),
            out_specs=pl.BlockSpec((height, local), lambda i, o: (0, 0)),
        ),
        out_shape=jax.ShapeDtypeStruct((height, local), BF16),
        compiler_params=params(),
        cost_estimate=cost(2 * kinds * size * local, 8 * kinds * size * local),
        name="join_own",
    )(indices, grads, right, left, extra, *deps)


def ring_order(count):
    nz = 4 if count % 4 == 0 else 1
    ny = count // nz
    if nz == 1 or ny % 2:
        return list(range(count))
    order = [(z, 0) for z in range(nz)]
    for y in range(1, ny):
        line = list(range(1, nz))
        order += [(z, y) for z in (reversed(line) if y % 2 else line)]
    order += [(0, y) for y in range(ny - 1, 0, -1)]
    return [z * ny + y for z, y in order]


class Ring:
    def __init__(self):
        self.log = []
        self.count = lax.axis_size("dp")
        self.order = ring_order(self.count)
        n = self.count
        place = [0] * n
        for p, d in enumerate(self.order):
            place[d] = p
        self.position = jnp.array(place, jnp.int32)[lax.axis_index("dp")]
        self.right = [(self.order[p], self.order[(p + 1) % n]) for p in range(n)]
        self.left = [(self.order[(p + 1) % n], self.order[p]) for p in range(n)]

    def to_right(self, x):
        out = lax.ppermute(x, "dp", self.right)
        self.log.append(out)
        return out

    def to_left(self, x):
        out = lax.ppermute(x, "dp", self.left)
        self.log.append(out)
        return out

    def logged(self, f, *args):
        self.log = []
        out = f(*args)
        pairs = [tuple(self.log[i:i + 2]) for i in range(0, len(self.log), 2)]
        self.log = []
        return out, pairs

    def gather(self, x, axis):
        out = [x]
        r = l = x
        for _ in range(self.count // 2 - 1):
            r, l = self.to_right(r), self.to_left(l)
            out += [r, l]
        size = x.shape[axis]
        cut = size // 32 * 16
        first = self.to_right(lax.slice_in_dim(r, 0, cut, axis=axis))
        second = self.to_left(lax.slice_in_dim(l, cut, size, axis=axis))
        out.append(jnp.concatenate([first, second], axis))
        return out

    def offsets(self):
        out = [0]
        for k in range(1, self.count // 2):
            out += [-k, k]
        return out + [self.count // 2]

    def indices(self):
        return [(self.position + k) % self.count for k in self.offsets()]

    def reduce_start(self, x):
        size = x.shape[1] // self.count
        cut = size // 2
        far = self.count // 2
        at = ((self.position + far) % self.count) * size
        r = lax.dynamic_slice_in_dim(x, at, cut, axis=1)
        l = lax.dynamic_slice_in_dim(x, at + cut, cut, axis=1)
        return (self.to_right(r), self.to_left(l)), (r, l)

    def reduce_step(self, x, arrived, k, deps=()):
        indices = jnp.stack([(self.position + k) % self.count, (self.position - k) % self.count]).astype(jnp.int32)
        r, l = join(x, indices, *arrived, x.shape[1] // self.count, deps)
        return (self.to_right(r), self.to_left(l)), (r, l)

    def reduce_end(self, x, arrived, extra, deps=()):
        return join_own(x, self.position[None].astype(jnp.int32), *arrived, extra, deps)


def core_swap(x):
    n = lax.axis_size("mp")
    return lax.ppermute(x, "mp", [(i, i ^ 1) for i in range(n)])


def sum_over_x(x, deps=()):
    n = lax.axis_size("mp") // 2
    index = lax.axis_index("mp")
    parts = [x] + [
        lax.ppermute(x, "mp", [(i, (i + 2 * k) % (2 * n)) for i in range(2 * n)]) for k in range(1, n)
    ]
    if n == 1:
        return x.astype(F32)
    if deps:
        parts[1:] = after(parts[1:], deps)
    if n == 2:
        return parts[0].astype(F32) + parts[1].astype(F32)
    stacked = jnp.stack(parts)
    total = None
    for j in range(n):
        term = lax.dynamic_index_in_dim(stacked, (index // 2 - j) % n, 0, keepdims=False).astype(F32)
        total = term if total is None else total + term
    return total


def on_device(tokens, gain_first, w_qkv, w_out, gain_second, router, w_up, w_down, slot, cotangent):
    length, model = tokens.shape
    buckets = w_up.shape[0]
    devices_dp = lax.axis_size("dp")
    groups = devices_dp // buckets
    capacity = length * 5 // (4 * devices_dp)
    row_bounds = [min(length, (buckets - level) * groups * capacity) for level in range(buckets)]
    ring = Ring()
    core = lax.axis_index("mp") % 2
    half = length // 2

    bucket_ids = slot // capacity // groups
    places = jnp.arange(length, dtype=jnp.int32)
    key = (buckets - 1 - bucket_ids) * length + places
    rank = jnp.sum((key[None, :] < key[:, None]).astype(jnp.int32), 1)
    rank_here = jnp.roll(rank, -core * half)
    sort_rows = places[:, None] == rank[None, :]
    sort_here = places[:, None] == rank_here[None, :]
    sort_low = sort_here.astype(BF16)
    unsort_low = (rank_here[:, None] == places[None, :]).astype(BF16)
    bucket_sorted = jnp.sum(jnp.where(sort_rows, bucket_ids[None, :], 0), 1)

    def part_of(x, c, axis=0):
        size = x.shape[axis] // 2
        return lax.dynamic_slice_in_dim(x, c * size, size, axis=axis)

    def own_rows(x):
        return part_of(x, core)

    def other_rows(x):
        return part_of(x, 1 - core)

    def joined(mine, other):
        return jnp.concatenate([jnp.where(core == 0, mine, other), jnp.where(core == 0, other, mine)], 0)

    cot_sorted = dot(sort_rows.astype(BF16), cotangent).astype(BF16)

    cot_own = part_of(cot_sorted, core, 1)
    cot_first = ring.to_right(cot_own), ring.to_left(cot_own)

    w3 = jnp.transpose(w_qkv, (1, 0, 2))
    cos, sin = rotary_table(length, HEAD)
    part_mine, part_other, normed_low, qkv, lse, mixed = attend(tokens, gain_first[None, :], w3, cos, sin, w_out)
    attn_rows = add_rows([part_mine, core_swap(part_other)])
    attn = sum_over_x(attn_rows)

    resid = own_rows(tokens).astype(F32) + attn
    inv = lax.rsqrt(jnp.mean(resid * resid, -1, keepdims=True) + EPSILON)
    xhat = resid * inv
    normed_second = xhat * gain_second
    logits = jnp.dot(normed_second, router, precision=HIGHEST)
    prob = jax.nn.softmax(logits, axis=-1)
    onehot = (own_rows(bucket_ids)[:, None] == jnp.arange(buckets)[None, :]).astype(F32)
    gate = buckets * jnp.sum(prob * onehot, -1)
    sent_half = normed_second.astype(BF16)
    sent_both = jnp.concatenate([sent_half, core_swap(sent_half)], 0)
    gate_both = jnp.concatenate([gate, core_swap(gate)], 0)
    gate_sorted = jnp.sum(jnp.where(sort_here, gate_both[None, :], 0.0), 1)

    sent_sorted = dot(sort_low, sent_both).astype(BF16)

    gate_1 = low(gate_sorted)
    gate_2 = low(gate_sorted - gate_1.astype(F32))
    gate_3 = low(gate_sorted - gate_1.astype(F32) - gate_2.astype(F32))
    aux = jnp.stack([gate_1, gate_2, gate_3, bucket_sorted.astype(BF16)] + [jnp.zeros_like(gate_1)] * (AUX - 4))
    aux = jnp.pad(aux, ((0, 0), (0, model // 2 - length)))
    sent_own = jnp.concatenate([part_of(sent_sorted, core, 1), aux], 0)
    height = length
    blocks = [((cot_own, 0), (part_of(cot_sorted, 1 - core, 1), 0), (sent_own, 0), (part_of(sent_sorted, 1 - core, 1), 0))]

    def block(mine, other):
        return (mine, 0), (other, 0), (mine, height), (other, height)

    sent_first = ring.to_right(sent_own), ring.to_left(sent_own)

    wide = lambda x: jnp.broadcast_to(x[:, None], (length, 128))
    gsent_mine, gsent_other, act = own_grad(
        sent_sorted, cot_sorted, wide(bucket_sorted), wide(gate_sorted), unsort_low, w_up, w_down, row_bounds,
        cot_first + (sent_own,))
    gsent_rows = add_rows([gsent_mine, core_swap(gsent_other)])
    grad_sent = sum_over_x(gsent_rows).astype(BF16).astype(F32)
    far = devices_dp // 2
    met = []

    def forward(arrived, deps):
        if len(arrived) == 4:
            cot_r, cot_l, sent_r, sent_l = after(arrived, deps)
            r, l = jnp.concatenate([cot_r, sent_r], 0), jnp.concatenate([cot_l, sent_l], 0)
        else:
            r, l = after(arrived, deps)
        if len(met) < far:
            met.extend([(r, core_swap(r)), (l, core_swap(l))])
        else:
            met.extend([(r, None), (l, None)])
        if len(met) < 2 * far - 2:
            return ring.to_right(r), ring.to_left(l)
        return ring.to_right(r[:height]), ring.to_left(l[height:])

    r, l = forward(cot_first + sent_first, (gsent_rows,))
    ffn_part, ggate_part = own_forward(
        act, cot_sorted, sort_rows.astype(BF16).T, w_down, row_bounds, (gsent_rows, met[0][0], met[1][0]))
    ggate_part = jnp.sum(jnp.where(sort_rows, ggate_part[:, :1], 0.0), 0)
    grad_gate = ggate_part + core_swap(ggate_part)
    grad_gate = sum_over_x(own_rows(grad_gate))

    grad_output = own_rows(cotangent).astype(F32)
    grad_prob = buckets * grad_gate[:, None] * onehot
    grad_logits = prob * (grad_prob - jnp.sum(grad_prob * prob, -1, keepdims=True))
    grad_router = jnp.dot(normed_second.T, grad_logits, precision=HIGHEST)
    grad_second = grad_sent + jnp.dot(grad_logits, router.T, precision=HIGHEST)
    grad_gain_second = jnp.sum(grad_second * xhat, 0)
    scaled = grad_second * gain_second
    grad_resid = grad_output + inv * (scaled - xhat * jnp.mean(scaled * xhat, -1, keepdims=True))
    ga_half = low(grad_resid)
    grad_attn = joined(ga_half, core_swap(ga_half))

    grads, first_part = attend_back(
        grad_attn, normed_low, qkv, lse, mixed, w_out, w3, cos, sin, met[0] + met[1])

    ffn_other, = after([other_rows(ffn_part)], (grads,))
    ffn_sum = add_rows([own_rows(ffn_part), core_swap(ffn_other)])

    carried = ()
    arrived, sending = ring.reduce_start(grads)
    chunks = None
    step = 0

    def advance(step, arrived, deps):
        nonlocal chunks
        if step < far - 1:
            return ring.reduce_step(grads, arrived, far - 1 - step, deps)
        if step == far - 1:
            chunks = [ring.reduce_end(grads, arrived, extra, deps)]
            r = l = chunks[0]
        else:
            r, l = after(arrived, deps) if deps else arrived
            chunks.extend([r, l])
        if step < 2 * far - 2:
            sending = (r, l)
            r, l = ring.to_right(r), ring.to_left(l)
        else:
            cut = r.shape[0] // 32 * 16
            sending = (r[:cut], l[cut:])
            r, l = ring.to_right(sending[0]), ring.to_left(sending[1])
            chunks.append(jnp.concatenate([r, l], 0))
        return (r, l), sending

    steps = 2 * far - 1
    while len(met) < far:
        r, l = forward((r, l), (grads, ffn_sum))
    near = len(met)
    sending = sending + met[-2] + met[-1]
    blocks += [block(*x) for x in met[:far - 1]]
    carried = ()
    calls = [(level, rows, True) for level, rows in enumerate(row_bounds)]
    later = [block(*x) for x in met[far - 1:]]
    extra = None
    slots = list(range(buckets))
    for slot_at, level in enumerate(slots):
        rows = row_bounds[level]
        carried = weight_gradients(level, rows, length, blocks, w_up, w_down, tuple(carried), True, sending)
        if slot_at == 0:
            ffn_rows = sum_over_x(ffn_sum, (carried[0],)).astype(BF16).astype(F32)
            output_half = (resid + gate[:, None] * ffn_rows).astype(BF16)
            first_other, = after([other_rows(first_part)], (carried[0], output_half))
            first_other = core_swap(first_other)
        if slot_at == 1:
            first_rows = add_rows([own_rows(first_part), first_other], (carried[0],))
        if slot_at == 2:
            grad_first = sum_over_x(first_rows, (carried[0],)).astype(BF16).astype(F32)
            source = own_rows(tokens).astype(F32)
            inv_first = lax.rsqrt(jnp.mean(source * source, -1, keepdims=True) + EPSILON)
            xhat_first = source * inv_first
            grad_gain_first = jnp.sum(grad_first * xhat_first, 0)
            scaled_first = grad_first * gain_first
            grad_source = inv_first * (
                scaled_first - xhat_first * jnp.mean(scaled_first * xhat_first, -1, keepdims=True))
            tokens_half = (grad_source + grad_resid).astype(BF16)
            small = jnp.concatenate([grad_router.T, grad_gain_second[None], grad_gain_first[None]], 0)
            small = jnp.pad(small, ((0, -small.shape[0] % 8), (0, 0)))
            small_other = core_swap(small)
        if slot_at == 3:
            small_other, = after([small_other], (carried[0],))
            extra = low(small + small_other).reshape(-1, w3.shape[2])
        arrived, sending = advance(step, arrived, (carried[0],))
        step += 1
        if slot_at == 3:
            r, l, *held = after([r, l] + [x for x, _ in met[far:]], (carried[0], sending[0]))
        if slot_at == 1:
            sending = sending + (output_half,)
        if slot_at == 2:
            sending = sending + (tokens_half, small)
            while len(met) < 2 * far - 2:
                r, l = forward((r, l), (carried[0],))
            sending = sending + tuple(pair[0] for pair in met[far:])
    later += [block(x, core_swap(x)) for x in held]
    later.append(((r, 0), (core_swap(r), 0), (l, 0), (core_swap(l), 0)))
    steps = 2 * far - 1
    for level, rows in enumerate(row_bounds):
        carried = weight_gradients(level, rows, length, later, w_up, w_down, tuple(carried), False, sending)
        ready = ()
        if level == 0:
            others = [core_swap(x) for x in after([tokens_half, output_half], (carried[0],))]
        if level == 1:
            others = after(others, (carried[0],))
            grad_tokens = joined(tokens_half, others[0])
            output = joined(output_half, others[1])
            ready = (grad_tokens, output)
        sending = ()
        if step < steps:
            arrived, sending = advance(step, arrived, (carried[0],))
            step += 1
        sending = sending + ready
    while step < steps:
        arrived, sending = advance(step, arrived, ())
        step += 1
    grad_up, grad_down = carried
    order = jnp.stack(ring.indices()).astype(jnp.int32)
    size = model // devices_dp
    grad_wqkv, grad_wout = unpack(order, chunks, size, devices_dp)
    terms = jnp.stack([x[4 * size:] for x in chunks])
    by_place = jnp.zeros((devices_dp,), jnp.int32).at[order].set(jnp.arange(devices_dp, dtype=jnp.int32))
    small = jnp.sum(terms[by_place].astype(F32), 0).reshape(small.shape)

    return (
        output,
        grad_tokens,
        small[buckets + 1],
        jnp.transpose(grad_wqkv, (1, 0, 2)),
        grad_wout,
        small[buckets],
        small[:buckets].T,
        grad_up,
        grad_down,
    )


def solution(mesh):
    placed = (
        P("dp", None),
        P(),
        P(None, None, "mp"),
        P("mp", None),
        P(),
        P(),
        P(None, None, "mp"),
        P(None, "mp", None),
        P("dp"),
        P("dp", None),
    )
    return jax.shard_map(
        on_device,
        mesh=mesh,
        in_specs=placed,
        out_specs=(
            P("dp", None),
            P("dp", None),
            P(),
            P(None, None, "mp"),
            P("mp", None),
            P(),
            P(),
            P(None, None, "mp"),
            P(None, "mp", None),
        ),
        check_vma=False,
    )
```

```python
from functools import partial

import jax
import jax.numpy as jnp
from jax import lax
from jax.experimental import pallas as pl
from jax.experimental.pallas import tpu as pltpu
from jax.sharding import PartitionSpec as P

HEAD = 128
HIGHEST = lax.Precision.HIGHEST
EPSILON = 1e-05
F32 = jnp.float32
BF16 = jnp.bfloat16
VMEM_LIMIT = 56 * 1024 * 1024
COST = 4
NN = (((1,), (0,)), ((), ()))
NT = (((1,), (1,)), ((), ()))
TN = (((0,), (0,)), ((), ()))


def dot(a, b, dims=NN):
    return lax.dot_general(a, b, dims, preferred_element_type=F32)


def low(x):
    return lax.reduce_precision(x, 8, 7).astype(BF16)


def params():
    return pltpu.CompilerParams(vmem_limit_bytes=VMEM_LIMIT)


def cost(flops, nbytes, transcendentals=0):
    return pl.CostEstimate(flops=flops // COST, bytes_accessed=nbytes // COST, transcendentals=transcendentals // COST)


def rotary_table(length, head_size):
    position = jnp.arange(length, dtype=F32)
    inverse = 10000.0 ** (-jnp.arange(0, head_size, 2, dtype=F32) / head_size)
    angles = position[:, None] * inverse[None, :]
    angles = jnp.concatenate([angles, angles], -1)
    sign = jnp.where(jnp.arange(head_size) < head_size // 2, -1.0, 1.0)
    return jnp.cos(angles), jnp.sin(angles) * sign


def attend_kernel(x_ref, gain_ref, w_ref, cos_ref, sin_ref, wout_ref,
                  mine_ref, other_ref, normed_ref, qkv_ref, lse_ref, mixed_ref, *, heads, steps):
    g = pl.program_id(0)
    length = x_ref.shape[0]
    half = length // 2
    scale = HEAD ** -0.5

    @pl.when(g == 0)
    def _():
        values = x_ref[...].astype(F32)
        inv = lax.rsqrt(jnp.mean(values * values, -1, keepdims=True) + EPSILON)
        normed_ref[...] = (values * inv * gain_ref[...]).astype(BF16)

    normed = normed_ref[...]
    cos, sin = cos_ref[...], sin_ref[...]
    projected = [dot(normed, w_ref[c]) for c in range(3)]
    for h in range(heads):
        cols = slice(h * HEAD, (h + 1) * HEAD)
        q, k, v = (p[:, cols] for p in projected)
        q = (q * cos + pltpu.roll(q, HEAD // 2, 1) * sin).astype(BF16)
        k = (k * cos + pltpu.roll(k, HEAD // 2, 1) * sin).astype(BF16)
        v = v.astype(BF16)
        qkv_ref[0, :, cols] = q
        qkv_ref[1, :, cols] = k
        qkv_ref[2, :, cols] = v
        for b in range(2):
            rows = slice(b * half, (b + 1) * half)
            keys = (b + 1) * half
            scores = dot(q[rows], k[:keys], NT) * scale
            at = lax.broadcasted_iota(jnp.int32, scores.shape, 0) + b * half
            to = lax.broadcasted_iota(jnp.int32, scores.shape, 1)
            scores = jnp.where(at >= to, scores, -1000000000.0)
            top = jnp.max(scores, -1, keepdims=True)
            weights = jnp.exp(scores - top)
            total = jnp.sum(weights, -1, keepdims=True)
            lse_ref[h, rows, :] = jnp.broadcast_to(top + jnp.log(total), (half, HEAD))
            low = (weights * (1.0 / total)).astype(BF16)
            mixed_ref[rows, pl.ds(pl.multiple_of((g * heads + h) * HEAD, HEAD), HEAD)] = dot(low, v[:keys]).astype(BF16)

    @pl.when(g == steps - 1)
    def _():
        core = lax.rem(lax.axis_index("mp"), 2)
        for ref, c in ((other_ref, 1 - core), (mine_ref, core)):
            rows = pl.ds(pl.multiple_of(c * half, half), half)
            ref[...] = dot(mixed_ref[rows, :], wout_ref[...]).astype(BF16)


def attend(tokens, gain, w3, cos, sin, w_out):
    length, model = tokens.shape
    local = w3.shape[2]
    local_heads = local // HEAD
    heads = 2 if local_heads % 2 == 0 else 1
    steps = local_heads // heads
    wide = heads * HEAD
    full = lambda *shape: pl.BlockSpec(shape, lambda g: (0,) * len(shape))
    return pl.pallas_call(
        partial(attend_kernel, heads=heads, steps=steps),
        grid=(steps,),
        in_specs=[
            full(length, model), full(1, model),
            pl.BlockSpec((3, model, wide), lambda g: (0, 0, g)),
            full(length, HEAD), full(length, HEAD), full(local, model),
        ],
        out_specs=[
            full(length // 2, model), full(length // 2, model), full(length, model),
            pl.BlockSpec((3, length, wide), lambda g: (0, 0, g)),
            pl.BlockSpec((heads, length, HEAD), lambda g: (g, 0, 0)),
            full(length, local),
        ],
        out_shape=[
            jax.ShapeDtypeStruct((length // 2, model), BF16),
            jax.ShapeDtypeStruct((length // 2, model), BF16),
            jax.ShapeDtypeStruct((length, model), BF16),
            jax.ShapeDtypeStruct((3, length, local), BF16),
            jax.ShapeDtypeStruct((local_heads, length, HEAD), F32),
            jax.ShapeDtypeStruct((length, local), BF16),
        ],
        compiler_params=params(),
        cost_estimate=cost(2 * length * model * local * 4 + 4 * length * length * local,
                           2 * (2 * length * model + 4 * model * local), length * length * local_heads),
        name="attend",
    )(tokens, gain, w3, cos, sin, w_out)


def attend_back_kernel(ga_ref, normed_ref, qkv_ref, lse_ref, mixed_ref, wout_ref, w_ref, cos_ref, sin_ref,
                       *rest, heads, steps, deps):
    grad_ref, first_ref, acc_ref = rest[deps:]
    g = pl.program_id(0)
    length = ga_ref.shape[0]
    half = length // 2
    scale = HEAD ** -0.5
    cos, sin = cos_ref[...], sin_ref[...]
    ga = ga_ref[...]
    gmixed = dot(ga, wout_ref[...], NT).astype(BF16)
    gproj = [[], [], []]
    for h in range(heads):
        cols = slice(h * HEAD, (h + 1) * HEAD)
        q, k, v = (qkv_ref[c, :, cols] for c in range(3))
        gm = gmixed[:, cols]
        gq, gk, gv = [], [None, None], [None, None]
        for b in range(2):
            rows = slice(b * half, (b + 1) * half)
            keys = (b + 1) * half
            scores = dot(q[rows], k[:keys], NT) * scale
            at = lax.broadcasted_iota(jnp.int32, scores.shape, 0) + b * half
            to = lax.broadcasted_iota(jnp.int32, scores.shape, 1)
            probs = jnp.where(at >= to, jnp.exp(scores - lse_ref[h, rows, :1]), 0.0)
            gprobs = dot(gm[rows], v[:keys], NT)
            gscores = probs * (gprobs - jnp.sum(gprobs * probs, -1, keepdims=True))
            gs = gscores.astype(BF16)
            low_probs = probs.astype(BF16)
            gq.append(dot(gs, k[:keys]) * scale)
            for j in range(b + 1):
                part = slice(j * half, (j + 1) * half)
                a = dot(gs[:, part], q[rows], TN) * scale
                c = dot(low_probs[:, part], gm[rows], TN)
                gk[j] = a if gk[j] is None else gk[j] + a
                gv[j] = c if gv[j] is None else gv[j] + c
        gq = jnp.concatenate(gq, 0)
        gk = jnp.concatenate(gk, 0)
        gv = jnp.concatenate(gv, 0)
        gproj[0].append((gq * cos - pltpu.roll(gq, HEAD // 2, 1) * sin).astype(BF16))
        gproj[1].append((gk * cos - pltpu.roll(gk, HEAD // 2, 1) * sin).astype(BF16))
        gproj[2].append(gv.astype(BF16))
    gproj = [jnp.concatenate(p, 1) for p in gproj]

    @pl.when(g == 0)
    def _():
        acc_ref[...] = jnp.zeros_like(acc_ref)

    grad_ref[3] = dot(ga, mixed_ref[...], TN).astype(BF16)
    for c in range(3):
        grad_ref[c] = dot(normed_ref[...], gproj[c], TN).astype(BF16)
        acc_ref[...] += dot(gproj[c], w_ref[c], NT)

    @pl.when(g == steps - 1)
    def _():
        first_ref[...] = acc_ref[...].astype(BF16)


def attend_back(ga, normed, qkv, lse, mixed, w_out, w3, cos, sin, deps=()):
    length, model = ga.shape
    local = w3.shape[2]
    local_heads = local // HEAD
    heads = 2 if local_heads % 2 == 0 else 1
    steps = local_heads // heads
    wide = heads * HEAD
    full = lambda *shape: pl.BlockSpec(shape, lambda g: (0,) * len(shape))
    return pl.pallas_call(
        partial(attend_back_kernel, heads=heads, steps=steps, deps=len(deps)),
        grid=(steps,),
        in_specs=[
            full(length, model), full(length, model),
            pl.BlockSpec((3, length, wide), lambda g: (0, 0, g)),
            pl.BlockSpec((heads, length, HEAD), lambda g: (g, 0, 0)),
            pl.BlockSpec((length, wide), lambda g: (0, g)),
            pl.BlockSpec((wide, model), lambda g: (g, 0)),
            pl.BlockSpec((3, model, wide), lambda g: (0, 0, g)),
            full(length, HEAD), full(length, HEAD),
        ] + [pl.BlockSpec(memory_space=pl.ANY)] * len(deps),
        out_specs=[pl.BlockSpec((4, model, wide), lambda g: (0, 0, g)), full(length, model)],
        out_shape=[
            jax.ShapeDtypeStruct((4, model, local), BF16),
            jax.ShapeDtypeStruct((length, model), BF16),
        ],
        scratch_shapes=[pltpu.VMEM((length, model), F32)],
        compiler_params=params(),
        cost_estimate=cost(2 * length * model * local * 8 + 10 * length * length * local,
                           2 * (4 * length * model + 8 * model * local), length * length * local_heads),
        name="attend_back",
    )(ga, normed, qkv, lse, mixed, w_out, w3, cos, sin, *deps)


def own_grad_kernel(sent_ref, cot_ref, bucket_ref, gate_ref, unsort_ref, up_ref, down_ref, *rest, row_bounds, deps):
    mine_ref, other_ref, act_ref, acc_ref = rest[deps:]
    level = pl.program_id(0)
    for q, rows in enumerate(row_bounds):
        @pl.when(level == q)
        def _(q=q, rows=rows):
            keep = bucket_ref[:rows, :1] >= q
            pre = dot(sent_ref[:rows], up_ref[0])
            active = jnp.where(keep, jnp.maximum(pre, 0.0), 0.0)
            act_ref[0, :rows] = (active * active).astype(BF16)
            gact = dot(cot_ref[:rows], down_ref[0], NT)
            gpre = (gact * (2.0 * gate_ref[:rows, :1]) * active).astype(BF16)
            s = dot(gpre, up_ref[0], NT)
            if q == 0:
                acc_ref[...] = s
            else:
                acc_ref[:rows] += s
            if q == len(row_bounds) - 1:
                half = mine_ref.shape[0]
                total = acc_ref[...].astype(BF16)
                other_ref[...] = dot(unsort_ref[half:], total).astype(BF16)
                mine_ref[...] = dot(unsort_ref[:half], total).astype(BF16)


def own_grad(sent, cot, bucket, gate, unsort, w_up, w_down, row_bounds, deps=()):
    length, model = sent.shape
    levels, _, hidden = w_up.shape
    full = lambda *shape: pl.BlockSpec(shape, lambda q: (0,) * len(shape))
    return pl.pallas_call(
        partial(own_grad_kernel, row_bounds=tuple(row_bounds), deps=len(deps)),
        grid=(levels,),
        in_specs=[
            full(length, model), full(length, model), full(length, 128), full(length, 128), full(length, length),
            pl.BlockSpec((1, model, hidden), lambda q: (q, 0, 0)),
            pl.BlockSpec((1, hidden, model), lambda q: (q, 0, 0)),
        ] + [pl.BlockSpec(memory_space=pl.ANY)] * len(deps),
        out_specs=[full(length // 2, model)] * 2 + [pl.BlockSpec((1, length, hidden), lambda q: (q, 0, 0))],
        out_shape=[jax.ShapeDtypeStruct((length // 2, model), BF16)] * 2
        + [jax.ShapeDtypeStruct((levels, length, hidden), BF16)],
        scratch_shapes=[pltpu.VMEM((length, model), F32)],
        compiler_params=params(),
        cost_estimate=cost(6 * sum(row_bounds) * model * hidden, 4 * levels * model * hidden + 6 * length * model),
        name="own_grad",
    )(sent, cot, bucket, gate, unsort, w_up, w_down, *deps)


def own_forward_kernel(act_ref, cot_ref, unsort_ref, down_ref, *rest, row_bounds, deps):
    ffn_ref, ggate_ref, acc_ref = rest[deps:]
    level = pl.program_id(0)
    for q, rows in enumerate(row_bounds):
        @pl.when(level == q)
        def _(q=q, rows=rows):
            f = dot(act_ref[0, :rows], down_ref[0])
            if q == 0:
                acc_ref[...] = f
            else:
                acc_ref[:rows] += f
            if q == len(row_bounds) - 1:
                total = acc_ref[...]
                ggate = jnp.sum(total * cot_ref[...].astype(F32), -1, keepdims=True)
                ggate_ref[...] = jnp.broadcast_to(ggate, ggate_ref.shape)
                ffn_ref[...] = dot(unsort_ref[...], total.astype(BF16)).astype(BF16)


def own_forward(act, cot, unsort, w_down, row_bounds, deps=()):
    length, model = cot.shape
    levels, hidden, _ = w_down.shape
    full = lambda *shape: pl.BlockSpec(shape, lambda q: (0,) * len(shape))
    return pl.pallas_call(
        partial(own_forward_kernel, row_bounds=tuple(row_bounds), deps=len(deps)),
        grid=(levels,),
        in_specs=[
            pl.BlockSpec((1, length, hidden), lambda q: (q, 0, 0)),
            full(length, model), full(length, length),
            pl.BlockSpec((1, hidden, model), lambda q: (q, 0, 0)),
        ] + [pl.BlockSpec(memory_space=pl.ANY)] * len(deps),
        out_specs=[full(length, model), full(length, 128)],
        out_shape=[jax.ShapeDtypeStruct((length, model), BF16), jax.ShapeDtypeStruct((length, 128), F32)],
        scratch_shapes=[pltpu.VMEM((length, model), F32)],
        compiler_params=params(),
        cost_estimate=cost(2 * sum(row_bounds) * model * hidden, 2 * levels * model * hidden + 6 * length * model),
        name="own_forward",
    )(act, cot, unsort, w_down, *deps)


AUX = 16


def gates_and_buckets(aux):
    row = lax.broadcasted_iota(jnp.int32, (AUX, 128), 0)
    gates = dot(aux, (row < 3).astype(BF16), TN)
    buckets = dot(aux, (row == 3).astype(BF16), TN)
    return gates, buckets


def weight_kernel(*refs, level, rows, group, offsets, fresh, carried, deps):
    count = len(offsets)
    pieces, refs = refs[:4 * count], refs[4 * count:]
    up_ref, down_ref = refs[:2]
    sums = refs[2:2 + carried]
    gup_ref, gdown_ref, up_buf, down_buf, s_buf, aux_buf, c_buf, gup, gdown, sems = refs[2 + carried + deps:]
    b = pl.program_id(0)
    steps = count // group
    core = lax.rem(lax.axis_index("mp"), 2)
    length, part = aux_buf.shape[3], s_buf.shape[2] // 2
    columns = lambda c: pl.ds(pl.multiple_of(c * part, part), part)
    slot = lax.rem(b, 2)

    def tokens_of(step):
        out = []
        for j in range(group):
            k = step * group + j
            to = pl.ds(j * rows, rows)
            mine, other = pieces[4 * k + 2], pieces[4 * k + 3]
            at = offsets[k]
            out += [
                (mine.at[pl.ds(at[2], rows)], s_buf.at[step % 2, to, columns(core)]),
                (other.at[pl.ds(at[3], rows)], s_buf.at[step % 2, to, columns(1 - core)]),
                (mine.at[pl.ds(at[2] + length, AUX), pl.ds(0, length)], aux_buf.at[step % 2, j]),
            ]
        return [pltpu.make_async_copy(x, y, sems.at[step % 2, i]) for i, (x, y) in enumerate(out)]

    def cots_of(step):
        out = []
        for j in range(group):
            k = step * group + j
            to = pl.ds(j * rows, rows)
            at = offsets[k]
            out += [
                (pieces[4 * k].at[pl.ds(at[0], rows)], c_buf.at[step % 2, to, columns(core)]),
                (pieces[4 * k + 1].at[pl.ds(at[1], rows)], c_buf.at[step % 2, to, columns(1 - core)]),
            ]
        return [pltpu.make_async_copy(x, y, sems.at[2 + step % 2, i]) for i, (x, y) in enumerate(out)]

    up_copy = pltpu.make_async_copy(up_ref.at[level], up_buf, sems.at[4, 0])
    down_copy = pltpu.make_async_copy(down_ref.at[level], down_buf, sems.at[4, 1])
    ends = [pltpu.make_async_copy(gup, gup_ref.at[level], sems.at[4, 2]),
            pltpu.make_async_copy(gdown, gdown_ref.at[level], sems.at[4, 3])]
    begins = [] if fresh else [
        pltpu.make_async_copy(sums[0].at[level], gup, sems.at[5, 0]),
        pltpu.make_async_copy(sums[1].at[level], gdown, sems.at[5, 1])]

    @pl.when(b == 0)
    def _():
        for c in [up_copy] + tokens_of(0) + [down_copy] + cots_of(0) + begins:
            c.start()

    for step in range(1, steps):
        @pl.when(b == step - 1)
        def _(step=step):
            for c in tokens_of(step) + cots_of(step):
                c.start()

    @pl.when(b == 0)
    def _():
        up_copy.wait()

    for step in range(steps):
        @pl.when(b == step)
        def _(step=step):
            for c in tokens_of(step):
                c.wait()

    columns_of = [gates_and_buckets(aux_buf[slot, j]) for j in range(group)]
    gate = jnp.concatenate([g[:rows, :1] for g, _ in columns_of], 0)
    keep = jnp.concatenate([k[:rows, :1] for _, k in columns_of], 0) >= level
    pre = dot(s_buf[slot], up_buf[...])
    active = jnp.where(keep, jnp.maximum(pre, 0.0), 0.0)
    act = (active * active * gate).astype(BF16)

    @pl.when(b == 0)
    def _():
        down_copy.wait()

    for step in range(steps):
        @pl.when(b == step)
        def _(step=step):
            for c in cots_of(step):
                c.wait()

    gact = dot(c_buf[slot], down_buf[...], NT)
    gpre = (gact * (2.0 * gate) * active).astype(BF16)

    @pl.when(b == 0)
    def _():
        if fresh:
            gup[...] = dot(s_buf[slot], gpre, TN)
            gdown[...] = dot(act, c_buf[slot], TN)
        else:
            for c in begins:
                c.wait()
            gup[...] += dot(s_buf[slot], gpre, TN)
            gdown[...] += dot(act, c_buf[slot], TN)

    if steps > 2:
        @pl.when(jnp.logical_and(b > 0, b < steps - 1))
        def _():
            gup[...] += dot(s_buf[slot], gpre, TN)
            gdown[...] += dot(act, c_buf[slot], TN)

    @pl.when(b == steps - 1)
    def _():
        gup[...] += dot(s_buf[slot], gpre, TN)
        ends[0].start()
        gdown[...] += dot(act, c_buf[slot], TN)
        ends[1].start()
        for c in ends:
            c.wait()


def weight_gradients(level, rows, length, blocks, w_up, w_down, carried, fresh, deps=()):
    levels, model, hidden = w_up.shape
    count = len(blocks)
    group = 2
    anywhere = pl.BlockSpec(memory_space=pl.ANY)
    arrays = [x for block in blocks for x, _ in block]
    offsets = tuple(tuple(at for _, at in block) for block in blocks)
    first = len(arrays) + 2
    return pl.pallas_call(
        partial(weight_kernel, level=level, rows=rows, group=group, offsets=offsets, fresh=fresh, carried=len(carried),
                deps=len(deps)),
        grid=(count // group,),
        in_specs=[anywhere] * (first + len(carried) + len(deps)),
        out_specs=[anywhere] * 2,
        out_shape=[jax.ShapeDtypeStruct((levels, model, hidden), F32), jax.ShapeDtypeStruct((levels, hidden, model), F32)],
        input_output_aliases={first: 0, first + 1: 1} if carried else {},
        scratch_shapes=[
            pltpu.VMEM((model, hidden), BF16), pltpu.VMEM((hidden, model), BF16),
            pltpu.VMEM((2, group * rows, model), BF16), pltpu.VMEM((2, group, AUX, length), BF16),
            pltpu.VMEM((2, group * rows, model), BF16),
            pltpu.VMEM((model, hidden), F32), pltpu.VMEM((hidden, model), F32),
            pltpu.SemaphoreType.DMA((6, 3 * group)),
        ],
        compiler_params=params(),
        cost_estimate=cost(8 * count * rows * model * hidden, 4 * count * rows * model + 16 * model * hidden),
        name=f"weight_gradients_{level}" + ("" if fresh else "_more"),
    )(*arrays, w_up, w_down, *carried, *deps)


def unpack_kernel(order_ref, *refs, count, carried):
    chunk_refs = refs[:count]
    qkv_ref, out_ref = refs[count + carried:]
    size = qkv_ref.shape[1]
    for k in range(count):
        @pl.when(pl.program_id(0) == k)
        def _(k=k):
            for c in range(3):
                qkv_ref[c] = chunk_refs[k][c * size:(c + 1) * size].astype(F32)
            out_ref[...] = chunk_refs[k][3 * size:4 * size].astype(F32).T


def unpack(order, chunks, size, total, carried=()):
    height, local = chunks[0].shape
    anywhere = pl.BlockSpec(memory_space=pl.ANY)
    count = len(chunks)
    return pl.pallas_call(
        partial(unpack_kernel, count=count, carried=len(carried)),
        grid_spec=pltpu.PrefetchScalarGridSpec(
            num_scalar_prefetch=1,
            grid=(count,),
            in_specs=[pl.BlockSpec((height, local), lambda b, o: (0, 0), pipeline_mode=pl.Buffered(1))] * count
            + [anywhere] * len(carried),
            out_specs=[
                pl.BlockSpec((3, size, local), lambda b, o: (0, o[b], 0)),
                pl.BlockSpec((local, size), lambda b, o: (0, o[b])),
            ],
        ),
        out_shape=[
            jax.ShapeDtypeStruct((3, total * size, local), F32),
            jax.ShapeDtypeStruct((local, total * size), F32),
        ],
        input_output_aliases={count + 1: 0, count + 2: 1} if carried else {},
        compiler_params=params(),
        cost_estimate=cost(0, 24 * count * size * local),
        name="unpack_some" if not carried else "unpack_rest",
    )(order, *chunks, *carried)


def add_kernel(*refs, count):
    total = refs[0][...].astype(F32)
    for ref in refs[1:count]:
        total = total + ref[...].astype(F32)
    refs[-1][...] = total.astype(BF16)


def add_rows(parts, deps=()):
    rows, columns = parts[0].shape
    block = pl.BlockSpec((rows // 4, columns), lambda i: (i, 0))
    return pl.pallas_call(
        partial(add_kernel, count=len(parts)),
        grid=(4,),
        in_specs=[block] * len(parts) + [pl.BlockSpec(memory_space=pl.ANY)] * len(deps),
        out_specs=block,
        out_shape=jax.ShapeDtypeStruct((rows, columns), BF16),
        compiler_params=params(),
        cost_estimate=cost(rows * columns, 6 * rows * columns),
        name="add_rows",
    )(*parts, *deps)


def pass_kernel(*refs):
    pass


def after(arrays, deps):
    anywhere = pl.BlockSpec(memory_space=pl.ANY)
    return pl.pallas_call(
        pass_kernel,
        in_specs=[anywhere] * (len(arrays) + len(deps)),
        out_specs=[anywhere] * len(arrays),
        out_shape=[jax.ShapeDtypeStruct(x.shape, x.dtype) for x in arrays],
        input_output_aliases={i: i for i in range(len(arrays))},
        compiler_params=params(),
        cost_estimate=cost(0, 0),
        name="after",
    )(*arrays, *deps)


def join_kernel(index_ref, right_local, left_local, right_ref, left_ref, *rest, cut, deps):
    right_out, left_out = rest[deps:]
    size = right_local.shape[1]
    if right_ref.shape[1] == size:
        right_out[0] = (right_local[0].astype(F32) + right_ref[0].astype(F32)).astype(BF16)
        left_out[0] = (left_local[0].astype(F32) + left_ref[0].astype(F32)).astype(BF16)
    else:
        right_out[0, :cut] = (right_local[0, :cut].astype(F32) + right_ref[0].astype(F32)).astype(BF16)
        right_out[0, cut:] = right_local[0, cut:]
        left_out[0, :cut] = left_local[0, :cut]
        left_out[0, cut:] = (left_local[0, cut:].astype(F32) + left_ref[0].astype(F32)).astype(BF16)


def join(grads, indices, right, left, size, deps=()):
    kinds, _, local = grads.shape
    arrived = right.shape[1]
    out = pl.BlockSpec((1, size, local), lambda i, o: (i, 0, 0))
    return pl.pallas_call(
        partial(join_kernel, cut=size // 2, deps=len(deps)),
        grid_spec=pltpu.PrefetchScalarGridSpec(
            num_scalar_prefetch=1,
            grid=(kinds,),
            in_specs=[
                pl.BlockSpec((1, size, local), lambda i, o: (i, o[0], 0)),
                pl.BlockSpec((1, size, local), lambda i, o: (i, o[1], 0)),
                pl.BlockSpec((1, arrived, local), lambda i, o: (i, 0, 0)),
                pl.BlockSpec((1, arrived, local), lambda i, o: (i, 0, 0)),
            ] + [pl.BlockSpec(memory_space=pl.ANY)] * len(deps),
            out_specs=[out, out],
        ),
        out_shape=[jax.ShapeDtypeStruct((kinds, size, local), BF16)] * 2,
        compiler_params=params(),
        cost_estimate=cost(2 * kinds * size * local, 12 * kinds * size * local),
        name="join",
    )(indices, grads, grads, right, left, *deps)


def join_own_kernel(index_ref, local_ref, right_ref, left_ref, extra_ref, *rest):
    kinds, size, _ = right_ref.shape
    for c in range(kinds):
        total = local_ref[c].astype(F32) + right_ref[c].astype(F32) + left_ref[c].astype(F32)
        rest[-1][c * size:(c + 1) * size] = total.astype(BF16)
    rest[-1][kinds * size:] = extra_ref[...]


def join_own(grads, indices, right, left, extra, deps=()):
    kinds, size, local = right.shape
    block = pl.BlockSpec((kinds, size, local), lambda i, o: (0, 0, 0))
    height = kinds * size + extra.shape[0]
    return pl.pallas_call(
        join_own_kernel,
        grid_spec=pltpu.PrefetchScalarGridSpec(
            num_scalar_prefetch=1,
            grid=(1,),
            in_specs=[pl.BlockSpec((kinds, size, local), lambda i, o: (0, o[0], 0)), block, block,
                      pl.BlockSpec(extra.shape, lambda i, o: (0, 0))]
            + [pl.BlockSpec(memory_space=pl.ANY)] * len(deps),
            out_specs=pl.BlockSpec((height, local), lambda i, o: (0, 0)),
        ),
        out_shape=jax.ShapeDtypeStruct((height, local), BF16),
        compiler_params=params(),
        cost_estimate=cost(2 * kinds * size * local, 8 * kinds * size * local),
        name="join_own",
    )(indices, grads, right, left, extra, *deps)


def ring_order(count):
    nz = 4 if count % 4 == 0 else 1
    ny = count // nz
    if nz == 1 or ny % 2:
        return list(range(count))
    order = [(z, 0) for z in range(nz)]
    for y in range(1, ny):
        line = list(range(1, nz))
        order += [(z, y) for z in (reversed(line) if y % 2 else line)]
    order += [(0, y) for y in range(ny - 1, 0, -1)]
    return [z * ny + y for z, y in order]


class Ring:
    def __init__(self):
        self.log = []
        self.count = lax.axis_size("dp")
        self.order = ring_order(self.count)
        n = self.count
        place = [0] * n
        for p, d in enumerate(self.order):
            place[d] = p
        self.position = jnp.array(place, jnp.int32)[lax.axis_index("dp")]
        self.right = [(self.order[p], self.order[(p + 1) % n]) for p in range(n)]
        self.left = [(self.order[(p + 1) % n], self.order[p]) for p in range(n)]

    def to_right(self, x):
        out = lax.ppermute(x, "dp", self.right)
        self.log.append(out)
        return out

    def to_left(self, x):
        out = lax.ppermute(x, "dp", self.left)
        self.log.append(out)
        return out

    def logged(self, f, *args):
        self.log = []
        out = f(*args)
        pairs = [tuple(self.log[i:i + 2]) for i in range(0, len(self.log), 2)]
        self.log = []
        return out, pairs

    def gather(self, x, axis):
        out = [x]
        r = l = x
        for _ in range(self.count // 2 - 1):
            r, l = self.to_right(r), self.to_left(l)
            out += [r, l]
        size = x.shape[axis]
        cut = size // 32 * 16
        first = self.to_right(lax.slice_in_dim(r, 0, cut, axis=axis))
        second = self.to_left(lax.slice_in_dim(l, cut, size, axis=axis))
        out.append(jnp.concatenate([first, second], axis))
        return out

    def offsets(self):
        out = [0]
        for k in range(1, self.count // 2):
            out += [-k, k]
        return out + [self.count // 2]

    def indices(self):
        return [(self.position + k) % self.count for k in self.offsets()]

    def reduce_start(self, x):
        size = x.shape[1] // self.count
        cut = size // 2
        far = self.count // 2
        at = ((self.position + far) % self.count) * size
        r = lax.dynamic_slice_in_dim(x, at, cut, axis=1)
        l = lax.dynamic_slice_in_dim(x, at + cut, cut, axis=1)
        return (self.to_right(r), self.to_left(l)), (r, l)

    def reduce_step(self, x, arrived, k, deps=()):
        indices = jnp.stack([(self.position + k) % self.count, (self.position - k) % self.count]).astype(jnp.int32)
        r, l = join(x, indices, *arrived, x.shape[1] // self.count, deps)
        return (self.to_right(r), self.to_left(l)), (r, l)

    def reduce_end(self, x, arrived, extra, deps=()):
        return join_own(x, self.position[None].astype(jnp.int32), *arrived, extra, deps)


def core_swap(x):
    n = lax.axis_size("mp")
    return lax.ppermute(x, "mp", [(i, i ^ 1) for i in range(n)])


def sum_over_x(x, deps=()):
    n = lax.axis_size("mp") // 2
    index = lax.axis_index("mp")
    parts = [x] + [
        lax.ppermute(x, "mp", [(i, (i + 2 * k) % (2 * n)) for i in range(2 * n)]) for k in range(1, n)
    ]
    if n == 1:
        return x.astype(F32)
    if deps:
        parts[1:] = after(parts[1:], deps)
    if n == 2:
        return parts[0].astype(F32) + parts[1].astype(F32)
    stacked = jnp.stack(parts)
    total = None
    for j in range(n):
        term = lax.dynamic_index_in_dim(stacked, (index // 2 - j) % n, 0, keepdims=False).astype(F32)
        total = term if total is None else total + term
    return total


def on_device(tokens, gain_first, w_qkv, w_out, gain_second, router, w_up, w_down, slot, cotangent):
    length, model = tokens.shape
    buckets = w_up.shape[0]
    devices_dp = lax.axis_size("dp")
    groups = devices_dp // buckets
    capacity = length * 5 // (4 * devices_dp)
    row_bounds = [min(length, (buckets - level) * groups * capacity) for level in range(buckets)]
    ring = Ring()
    core = lax.axis_index("mp") % 2
    half = length // 2

    bucket_ids = slot // capacity // groups
    places = jnp.arange(length, dtype=jnp.int32)
    key = (buckets - 1 - bucket_ids) * length + places
    rank = jnp.sum((key[None, :] < key[:, None]).astype(jnp.int32), 1)
    rank_here = jnp.roll(rank, -core * half)
    sort_rows = places[:, None] == rank[None, :]
    sort_here = places[:, None] == rank_here[None, :]
    sort_low = sort_here.astype(BF16)
    unsort_low = (rank_here[:, None] == places[None, :]).astype(BF16)
    bucket_sorted = jnp.sum(jnp.where(sort_rows, bucket_ids[None, :], 0), 1)

    def part_of(x, c, axis=0):
        size = x.shape[axis] // 2
        return lax.dynamic_slice_in_dim(x, c * size, size, axis=axis)

    def own_rows(x):
        return part_of(x, core)

    def other_rows(x):
        return part_of(x, 1 - core)

    def joined(mine, other):
        return jnp.concatenate([jnp.where(core == 0, mine, other), jnp.where(core == 0, other, mine)], 0)

    cot_sorted = dot(sort_rows.astype(BF16), cotangent).astype(BF16)

    cot_own = part_of(cot_sorted, core, 1)
    cot_first = ring.to_right(cot_own), ring.to_left(cot_own)

    w3 = jnp.transpose(w_qkv, (1, 0, 2))
    cos, sin = rotary_table(length, HEAD)
    part_mine, part_other, normed_low, qkv, lse, mixed = attend(tokens, gain_first[None, :], w3, cos, sin, w_out)
    attn_rows = add_rows([part_mine, core_swap(part_other)])
    attn = sum_over_x(attn_rows)

    resid = own_rows(tokens).astype(F32) + attn
    inv = lax.rsqrt(jnp.mean(resid * resid, -1, keepdims=True) + EPSILON)
    xhat = resid * inv
    normed_second = xhat * gain_second
    logits = jnp.dot(normed_second, router, precision=HIGHEST)
    prob = jax.nn.softmax(logits, axis=-1)
    onehot = (own_rows(bucket_ids)[:, None] == jnp.arange(buckets)[None, :]).astype(F32)
    gate = buckets * jnp.sum(prob * onehot, -1)
    sent_half = normed_second.astype(BF16)
    sent_both = jnp.concatenate([sent_half, core_swap(sent_half)], 0)
    gate_both = jnp.concatenate([gate, core_swap(gate)], 0)
    gate_sorted = jnp.sum(jnp.where(sort_here, gate_both[None, :], 0.0), 1)

    sent_sorted = dot(sort_low, sent_both).astype(BF16)

    gate_1 = low(gate_sorted)
    gate_2 = low(gate_sorted - gate_1.astype(F32))
    gate_3 = low(gate_sorted - gate_1.astype(F32) - gate_2.astype(F32))
    aux = jnp.stack([gate_1, gate_2, gate_3, bucket_sorted.astype(BF16)] + [jnp.zeros_like(gate_1)] * (AUX - 4))
    aux = jnp.pad(aux, ((0, 0), (0, model // 2 - length)))
    sent_own = jnp.concatenate([part_of(sent_sorted, core, 1), aux], 0)
    height = length
    blocks = [((cot_own, 0), (part_of(cot_sorted, 1 - core, 1), 0), (sent_own, 0), (part_of(sent_sorted, 1 - core, 1), 0))]

    def block(mine, other):
        return (mine, 0), (other, 0), (mine, height), (other, height)

    sent_first = ring.to_right(sent_own), ring.to_left(sent_own)

    wide = lambda x: jnp.broadcast_to(x[:, None], (length, 128))
    gsent_mine, gsent_other, act = own_grad(
        sent_sorted, cot_sorted, wide(bucket_sorted), wide(gate_sorted), unsort_low, w_up, w_down, row_bounds,
        cot_first + (sent_own,))
    gsent_rows = add_rows([gsent_mine, core_swap(gsent_other)])
    grad_sent = sum_over_x(gsent_rows).astype(BF16).astype(F32)
    far = devices_dp // 2
    met = []

    def forward(arrived, deps):
        if len(arrived) == 4:
            cot_r, cot_l, sent_r, sent_l = after(arrived, deps)
            r, l = jnp.concatenate([cot_r, sent_r], 0), jnp.concatenate([cot_l, sent_l], 0)
        else:
            r, l = after(arrived, deps)
        if len(met) < far:
            met.extend([(r, core_swap(r)), (l, core_swap(l))])
        else:
            met.extend([(r, None), (l, None)])
        if len(met) < 2 * far - 2:
            return ring.to_right(r), ring.to_left(l)
        return ring.to_right(r[:height]), ring.to_left(l[height:])

    r, l = forward(cot_first + sent_first, (gsent_rows,))
    ffn_part, ggate_part = own_forward(
        act, cot_sorted, sort_rows.astype(BF16).T, w_down, row_bounds, (gsent_rows, met[0][0], met[1][0]))
    ggate_part = jnp.sum(jnp.where(sort_rows, ggate_part[:, :1], 0.0), 0)
    grad_gate = ggate_part + core_swap(ggate_part)
    grad_gate = sum_over_x(own_rows(grad_gate))

    grad_output = own_rows(cotangent).astype(F32)
    grad_prob = buckets * grad_gate[:, None] * onehot
    grad_logits = prob * (grad_prob - jnp.sum(grad_prob * prob, -1, keepdims=True))
    grad_router = jnp.dot(normed_second.T, grad_logits, precision=HIGHEST)
    grad_second = grad_sent + jnp.dot(grad_logits, router.T, precision=HIGHEST)
    grad_gain_second = jnp.sum(grad_second * xhat, 0)
    scaled = grad_second * gain_second
    grad_resid = grad_output + inv * (scaled - xhat * jnp.mean(scaled * xhat, -1, keepdims=True))
    ga_half = low(grad_resid)
    grad_attn = joined(ga_half, core_swap(ga_half))

    grads, first_part = attend_back(
        grad_attn, normed_low, qkv, lse, mixed, w_out, w3, cos, sin, met[0] + met[1])

    ffn_other, = after([other_rows(ffn_part)], (grads,))
    ffn_sum = add_rows([own_rows(ffn_part), core_swap(ffn_other)])

    carried = ()
    arrived, sending = ring.reduce_start(grads)
    chunks = None
    step = 0

    def advance(step, arrived, deps):
        nonlocal chunks
        if step < far - 1:
            return ring.reduce_step(grads, arrived, far - 1 - step, deps)
        if step == far - 1:
            chunks = [ring.reduce_end(grads, arrived, extra, deps)]
            r = l = chunks[0]
        else:
            r, l = after(arrived, deps) if deps else arrived
            chunks.extend([r, l])
        if step < 2 * far - 2:
            sending = (r, l)
            r, l = ring.to_right(r), ring.to_left(l)
        else:
            cut = r.shape[0] // 32 * 16
            sending = (r[:cut], l[cut:])
            r, l = ring.to_right(sending[0]), ring.to_left(sending[1])
            chunks.append(jnp.concatenate([r, l], 0))
        return (r, l), sending

    steps = 2 * far - 1
    while len(met) < far:
        r, l = forward((r, l), (grads, ffn_sum))
    near = len(met)
    sending = sending + met[-2] + met[-1]
    blocks += [block(*x) for x in met[:far - 1]]
    carried = ()
    calls = [(level, rows, True) for level, rows in enumerate(row_bounds)]
    later = [block(*x) for x in met[far - 1:]]
    extra = None
    slots = list(range(buckets))
    for slot_at, level in enumerate(slots):
        rows = row_bounds[level]
        carried = weight_gradients(level, rows, length, blocks, w_up, w_down, tuple(carried), True, sending)
        if slot_at == 0:
            ffn_rows = sum_over_x(ffn_sum, (carried[0],)).astype(BF16).astype(F32)
            output_half = (resid + gate[:, None] * ffn_rows).astype(BF16)
            first_other, = after([other_rows(first_part)], (carried[0], output_half))
            first_other = core_swap(first_other)
        if slot_at == 1:
            first_rows = add_rows([own_rows(first_part), first_other], (carried[0],))
        if slot_at == 2:
            grad_first = sum_over_x(first_rows, (carried[0],)).astype(BF16).astype(F32)
            source = own_rows(tokens).astype(F32)
            inv_first = lax.rsqrt(jnp.mean(source * source, -1, keepdims=True) + EPSILON)
            xhat_first = source * inv_first
            grad_gain_first = jnp.sum(grad_first * xhat_first, 0)
            scaled_first = grad_first * gain_first
            grad_source = inv_first * (
                scaled_first - xhat_first * jnp.mean(scaled_first * xhat_first, -1, keepdims=True))
            tokens_half = (grad_source + grad_resid).astype(BF16)
            small = jnp.concatenate([grad_router.T, grad_gain_second[None], grad_gain_first[None]], 0)
            small = jnp.pad(small, ((0, -small.shape[0] % 8), (0, 0)))
            small_other = core_swap(small)
        if slot_at == 3:
            small_other, = after([small_other], (carried[0],))
            extra = low(small + small_other).reshape(-1, w3.shape[2])
        arrived, sending = advance(step, arrived, (carried[0],))
        step += 1
        if slot_at == 3:
            held = after([x for x, _ in met[far:]], (carried[0],))
            held = [(x, core_swap(x)) for x in held]
            r, l = after((r, l), (carried[0], sending[0]))
        if slot_at == 1:
            sending = sending + (output_half,)
        if slot_at == 2:
            sending = sending + (tokens_half, small)
            while len(met) < 2 * far - 2:
                r, l = forward((r, l), (carried[0],))
            sending = sending + tuple(pair[0] for pair in met[far:])
    later += [block(*x) for x in held]
    later.append(((r, 0), (core_swap(r), 0), (l, 0), (core_swap(l), 0)))
    steps = 2 * far - 1
    for level, rows in enumerate(row_bounds):
        carried = weight_gradients(level, rows, length, later, w_up, w_down, tuple(carried), False, sending)
        ready = ()
        if level == 0:
            others = [core_swap(x) for x in after([tokens_half, output_half], (carried[0],))]
        if level == 1:
            others = after(others, (carried[0],))
            grad_tokens = joined(tokens_half, others[0])
            output = joined(output_half, others[1])
            ready = (grad_tokens, output)
        sending = ()
        if step < steps:
            arrived, sending = advance(step, arrived, (carried[0],))
            step += 1
        sending = sending + ready
    while step < steps:
        arrived, sending = advance(step, arrived, ())
        step += 1
    grad_up, grad_down = carried
    order = jnp.stack(ring.indices()).astype(jnp.int32)
    size = model // devices_dp
    grad_wqkv, grad_wout = unpack(order, chunks, size, devices_dp)
    terms = jnp.stack([x[4 * size:] for x in chunks])
    by_place = jnp.zeros((devices_dp,), jnp.int32).at[order].set(jnp.arange(devices_dp, dtype=jnp.int32))
    small = jnp.sum(terms[by_place].astype(F32), 0).reshape(small.shape)

    return (
        output,
        grad_tokens,
        small[buckets + 1],
        jnp.transpose(grad_wqkv, (1, 0, 2)),
        grad_wout,
        small[buckets],
        small[:buckets].T,
        grad_up,
        grad_down,
    )


def solution(mesh):
    placed = (
        P("dp", None),
        P(),
        P(None, None, "mp"),
        P("mp", None),
        P(),
        P(),
        P(None, None, "mp"),
        P(None, "mp", None),
        P("dp"),
        P("dp", None),
    )
    return jax.shard_map(
        on_device,
        mesh=mesh,
        in_specs=placed,
        out_specs=(
            P("dp", None),
            P("dp", None),
            P(),
            P(None, None, "mp"),
            P("mp", None),
            P(),
            P(),
            P(None, None, "mp"),
            P(None, "mp", None),
        ),
        check_vma=False,
    )
```

```python
from functools import partial

import jax
import jax.numpy as jnp
from jax import lax
from jax.experimental import pallas as pl
from jax.experimental.pallas import tpu as pltpu
from jax.sharding import PartitionSpec as P

HEAD = 128
HIGHEST = lax.Precision.HIGHEST
EPSILON = 1e-05
F32 = jnp.float32
BF16 = jnp.bfloat16
VMEM_LIMIT = 56 * 1024 * 1024
COST = 4
NN = (((1,), (0,)), ((), ()))
NT = (((1,), (1,)), ((), ()))
TN = (((0,), (0,)), ((), ()))


def dot(a, b, dims=NN):
    return lax.dot_general(a, b, dims, preferred_element_type=F32)


def low(x):
    return lax.reduce_precision(x, 8, 7).astype(BF16)


def params():
    return pltpu.CompilerParams(vmem_limit_bytes=VMEM_LIMIT)


def cost(flops, nbytes, transcendentals=0):
    return pl.CostEstimate(flops=flops // COST, bytes_accessed=nbytes // COST, transcendentals=transcendentals // COST)


def rotary_table(length, head_size):
    position = jnp.arange(length, dtype=F32)
    inverse = 10000.0 ** (-jnp.arange(0, head_size, 2, dtype=F32) / head_size)
    angles = position[:, None] * inverse[None, :]
    angles = jnp.concatenate([angles, angles], -1)
    sign = jnp.where(jnp.arange(head_size) < head_size // 2, -1.0, 1.0)
    return jnp.cos(angles), jnp.sin(angles) * sign


def attend_kernel(x_ref, gain_ref, w_ref, cos_ref, sin_ref, wout_ref,
                  mine_ref, other_ref, normed_ref, qkv_ref, lse_ref, mixed_ref, *, heads, steps):
    g = pl.program_id(0)
    length = x_ref.shape[0]
    half = length // 2
    scale = HEAD ** -0.5

    @pl.when(g == 0)
    def _():
        values = x_ref[...].astype(F32)
        inv = lax.rsqrt(jnp.mean(values * values, -1, keepdims=True) + EPSILON)
        normed_ref[...] = (values * inv * gain_ref[...]).astype(BF16)

    normed = normed_ref[...]
    cos, sin = cos_ref[...], sin_ref[...]
    projected = [dot(normed, w_ref[c]) for c in range(3)]
    for h in range(heads):
        cols = slice(h * HEAD, (h + 1) * HEAD)
        q, k, v = (p[:, cols] for p in projected)
        q = (q * cos + pltpu.roll(q, HEAD // 2, 1) * sin).astype(BF16)
        k = (k * cos + pltpu.roll(k, HEAD // 2, 1) * sin).astype(BF16)
        v = v.astype(BF16)
        qkv_ref[0, :, cols] = q
        qkv_ref[1, :, cols] = k
        qkv_ref[2, :, cols] = v
        for b in range(2):
            rows = slice(b * half, (b + 1) * half)
            keys = (b + 1) * half
            scores = dot(q[rows], k[:keys], NT) * scale
            at = lax.broadcasted_iota(jnp.int32, scores.shape, 0) + b * half
            to = lax.broadcasted_iota(jnp.int32, scores.shape, 1)
            scores = jnp.where(at >= to, scores, -1000000000.0)
            top = jnp.max(scores, -1, keepdims=True)
            weights = jnp.exp(scores - top)
            total = jnp.sum(weights, -1, keepdims=True)
            lse_ref[h, rows, :] = jnp.broadcast_to(top + jnp.log(total), (half, HEAD))
            low = (weights * (1.0 / total)).astype(BF16)
            mixed_ref[rows, pl.ds(pl.multiple_of((g * heads + h) * HEAD, HEAD), HEAD)] = dot(low, v[:keys]).astype(BF16)

    @pl.when(g == steps - 1)
    def _():
        core = lax.rem(lax.axis_index("mp"), 2)
        for ref, c in ((other_ref, 1 - core), (mine_ref, core)):
            rows = pl.ds(pl.multiple_of(c * half, half), half)
            ref[...] = dot(mixed_ref[rows, :], wout_ref[...]).astype(BF16)


def attend(tokens, gain, w3, cos, sin, w_out):
    length, model = tokens.shape
    local = w3.shape[2]
    local_heads = local // HEAD
    heads = 2 if local_heads % 2 == 0 else 1
    steps = local_heads // heads
    wide = heads * HEAD
    full = lambda *shape: pl.BlockSpec(shape, lambda g: (0,) * len(shape))
    return pl.pallas_call(
        partial(attend_kernel, heads=heads, steps=steps),
        grid=(steps,),
        in_specs=[
            full(length, model), full(1, model),
            pl.BlockSpec((3, model, wide), lambda g: (0, 0, g)),
            full(length, HEAD), full(length, HEAD), full(local, model),
        ],
        out_specs=[
            full(length // 2, model), full(length // 2, model), full(length, model),
            pl.BlockSpec((3, length, wide), lambda g: (0, 0, g)),
            pl.BlockSpec((heads, length, HEAD), lambda g: (g, 0, 0)),
            full(length, local),
        ],
        out_shape=[
            jax.ShapeDtypeStruct((length // 2, model), BF16),
            jax.ShapeDtypeStruct((length // 2, model), BF16),
            jax.ShapeDtypeStruct((length, model), BF16),
            jax.ShapeDtypeStruct((3, length, local), BF16),
            jax.ShapeDtypeStruct((local_heads, length, HEAD), F32),
            jax.ShapeDtypeStruct((length, local), BF16),
        ],
        compiler_params=params(),
        cost_estimate=cost(2 * length * model * local * 4 + 4 * length * length * local,
                           2 * (2 * length * model + 4 * model * local), length * length * local_heads),
        name="attend",
    )(tokens, gain, w3, cos, sin, w_out)


def attend_back_kernel(ga_ref, normed_ref, qkv_ref, lse_ref, mixed_ref, wout_ref, w_ref, cos_ref, sin_ref,
                       *rest, heads, steps, deps):
    grad_ref, first_ref, acc_ref = rest[deps:]
    g = pl.program_id(0)
    length = ga_ref.shape[0]
    half = length // 2
    scale = HEAD ** -0.5
    cos, sin = cos_ref[...], sin_ref[...]
    ga = ga_ref[...]
    gmixed = dot(ga, wout_ref[...], NT).astype(BF16)
    gproj = [[], [], []]
    for h in range(heads):
        cols = slice(h * HEAD, (h + 1) * HEAD)
        q, k, v = (qkv_ref[c, :, cols] for c in range(3))
        gm = gmixed[:, cols]
        gq, gk, gv = [], [None, None], [None, None]
        for b in range(2):
            rows = slice(b * half, (b + 1) * half)
            keys = (b + 1) * half
            scores = dot(q[rows], k[:keys], NT) * scale
            at = lax.broadcasted_iota(jnp.int32, scores.shape, 0) + b * half
            to = lax.broadcasted_iota(jnp.int32, scores.shape, 1)
            probs = jnp.where(at >= to, jnp.exp(scores - lse_ref[h, rows, :1]), 0.0)
            gprobs = dot(gm[rows], v[:keys], NT)
            gscores = probs * (gprobs - jnp.sum(gprobs * probs, -1, keepdims=True))
            gs = gscores.astype(BF16)
            low_probs = probs.astype(BF16)
            gq.append(dot(gs, k[:keys]) * scale)
            for j in range(b + 1):
                part = slice(j * half, (j + 1) * half)
                a = dot(gs[:, part], q[rows], TN) * scale
                c = dot(low_probs[:, part], gm[rows], TN)
                gk[j] = a if gk[j] is None else gk[j] + a
                gv[j] = c if gv[j] is None else gv[j] + c
        gq = jnp.concatenate(gq, 0)
        gk = jnp.concatenate(gk, 0)
        gv = jnp.concatenate(gv, 0)
        gproj[0].append((gq * cos - pltpu.roll(gq, HEAD // 2, 1) * sin).astype(BF16))
        gproj[1].append((gk * cos - pltpu.roll(gk, HEAD // 2, 1) * sin).astype(BF16))
        gproj[2].append(gv.astype(BF16))
    gproj = [jnp.concatenate(p, 1) for p in gproj]

    @pl.when(g == 0)
    def _():
        acc_ref[...] = jnp.zeros_like(acc_ref)

    grad_ref[3] = dot(ga, mixed_ref[...], TN).astype(BF16)
    for c in range(3):
        grad_ref[c] = dot(normed_ref[...], gproj[c], TN).astype(BF16)
        acc_ref[...] += dot(gproj[c], w_ref[c], NT)

    @pl.when(g == steps - 1)
    def _():
        first_ref[...] = acc_ref[...].astype(BF16)


def attend_back(ga, normed, qkv, lse, mixed, w_out, w3, cos, sin, deps=()):
    length, model = ga.shape
    local = w3.shape[2]
    local_heads = local // HEAD
    heads = 2 if local_heads % 2 == 0 else 1
    steps = local_heads // heads
    wide = heads * HEAD
    full = lambda *shape: pl.BlockSpec(shape, lambda g: (0,) * len(shape))
    return pl.pallas_call(
        partial(attend_back_kernel, heads=heads, steps=steps, deps=len(deps)),
        grid=(steps,),
        in_specs=[
            full(length, model), full(length, model),
            pl.BlockSpec((3, length, wide), lambda g: (0, 0, g)),
            pl.BlockSpec((heads, length, HEAD), lambda g: (g, 0, 0)),
            pl.BlockSpec((length, wide), lambda g: (0, g)),
            pl.BlockSpec((wide, model), lambda g: (g, 0)),
            pl.BlockSpec((3, model, wide), lambda g: (0, 0, g)),
            full(length, HEAD), full(length, HEAD),
        ] + [pl.BlockSpec(memory_space=pl.ANY)] * len(deps),
        out_specs=[pl.BlockSpec((4, model, wide), lambda g: (0, 0, g)), full(length, model)],
        out_shape=[
            jax.ShapeDtypeStruct((4, model, local), BF16),
            jax.ShapeDtypeStruct((length, model), BF16),
        ],
        scratch_shapes=[pltpu.VMEM((length, model), F32)],
        compiler_params=params(),
        cost_estimate=cost(2 * length * model * local * 8 + 10 * length * length * local,
                           2 * (4 * length * model + 8 * model * local), length * length * local_heads),
        name="attend_back",
    )(ga, normed, qkv, lse, mixed, w_out, w3, cos, sin, *deps)


def own_grad_kernel(sent_ref, cot_ref, bucket_ref, gate_ref, unsort_ref, up_ref, down_ref, *rest, row_bounds, deps):
    mine_ref, other_ref, act_ref, acc_ref = rest[deps:]
    level = pl.program_id(0)
    for q, rows in enumerate(row_bounds):
        @pl.when(level == q)
        def _(q=q, rows=rows):
            keep = bucket_ref[:rows, :1] >= q
            pre = dot(sent_ref[:rows], up_ref[0])
            active = jnp.where(keep, jnp.maximum(pre, 0.0), 0.0)
            act_ref[0, :rows] = (active * active).astype(BF16)
            gact = dot(cot_ref[:rows], down_ref[0], NT)
            gpre = (gact * (2.0 * gate_ref[:rows, :1]) * active).astype(BF16)
            s = dot(gpre, up_ref[0], NT)
            if q == 0:
                acc_ref[...] = s
            else:
                acc_ref[:rows] += s
            if q == len(row_bounds) - 1:
                half = mine_ref.shape[0]
                total = acc_ref[...].astype(BF16)
                other_ref[...] = dot(unsort_ref[half:], total).astype(BF16)
                mine_ref[...] = dot(unsort_ref[:half], total).astype(BF16)


def own_grad(sent, cot, bucket, gate, unsort, w_up, w_down, row_bounds, deps=()):
    length, model = sent.shape
    levels, _, hidden = w_up.shape
    full = lambda *shape: pl.BlockSpec(shape, lambda q: (0,) * len(shape))
    return pl.pallas_call(
        partial(own_grad_kernel, row_bounds=tuple(row_bounds), deps=len(deps)),
        grid=(levels,),
        in_specs=[
            full(length, model), full(length, model), full(length, 128), full(length, 128), full(length, length),
            pl.BlockSpec((1, model, hidden), lambda q: (q, 0, 0)),
            pl.BlockSpec((1, hidden, model), lambda q: (q, 0, 0)),
        ] + [pl.BlockSpec(memory_space=pl.ANY)] * len(deps),
        out_specs=[full(length // 2, model)] * 2 + [pl.BlockSpec((1, length, hidden), lambda q: (q, 0, 0))],
        out_shape=[jax.ShapeDtypeStruct((length // 2, model), BF16)] * 2
        + [jax.ShapeDtypeStruct((levels, length, hidden), BF16)],
        scratch_shapes=[pltpu.VMEM((length, model), F32)],
        compiler_params=params(),
        cost_estimate=cost(6 * sum(row_bounds) * model * hidden, 4 * levels * model * hidden + 6 * length * model),
        name="own_grad",
    )(sent, cot, bucket, gate, unsort, w_up, w_down, *deps)


def own_forward_kernel(act_ref, cot_ref, unsort_ref, down_ref, *rest, row_bounds, deps):
    ffn_ref, ggate_ref, acc_ref = rest[deps:]
    level = pl.program_id(0)
    for q, rows in enumerate(row_bounds):
        @pl.when(level == q)
        def _(q=q, rows=rows):
            f = dot(act_ref[0, :rows], down_ref[0])
            if q == 0:
                acc_ref[...] = f
            else:
                acc_ref[:rows] += f
            if q == len(row_bounds) - 1:
                total = acc_ref[...]
                ggate = jnp.sum(total * cot_ref[...].astype(F32), -1, keepdims=True)
                ggate_ref[...] = jnp.broadcast_to(ggate, ggate_ref.shape)
                ffn_ref[...] = dot(unsort_ref[...], total.astype(BF16)).astype(BF16)


def own_forward(act, cot, unsort, w_down, row_bounds, deps=()):
    length, model = cot.shape
    levels, hidden, _ = w_down.shape
    full = lambda *shape: pl.BlockSpec(shape, lambda q: (0,) * len(shape))
    return pl.pallas_call(
        partial(own_forward_kernel, row_bounds=tuple(row_bounds), deps=len(deps)),
        grid=(levels,),
        in_specs=[
            pl.BlockSpec((1, length, hidden), lambda q: (q, 0, 0)),
            full(length, model), full(length, length),
            pl.BlockSpec((1, hidden, model), lambda q: (q, 0, 0)),
        ] + [pl.BlockSpec(memory_space=pl.ANY)] * len(deps),
        out_specs=[full(length, model), full(length, 128)],
        out_shape=[jax.ShapeDtypeStruct((length, model), BF16), jax.ShapeDtypeStruct((length, 128), F32)],
        scratch_shapes=[pltpu.VMEM((length, model), F32)],
        compiler_params=params(),
        cost_estimate=cost(2 * sum(row_bounds) * model * hidden, 2 * levels * model * hidden + 6 * length * model),
        name="own_forward",
    )(act, cot, unsort, w_down, *deps)


AUX = 16


def gates_and_buckets(aux):
    row = lax.broadcasted_iota(jnp.int32, (AUX, 128), 0)
    gates = dot(aux, (row < 3).astype(BF16), TN)
    buckets = dot(aux, (row == 3).astype(BF16), TN)
    return gates, buckets


def weight_kernel(*refs, level, rows, group, offsets, fresh, carried, deps):
    count = len(offsets)
    pieces, refs = refs[:4 * count], refs[4 * count:]
    up_ref, down_ref = refs[:2]
    sums = refs[2:2 + carried]
    gup_ref, gdown_ref, up_buf, down_buf, s_buf, aux_buf, c_buf, gup, gdown, sems = refs[2 + carried + deps:]
    b = pl.program_id(0)
    steps = count // group
    core = lax.rem(lax.axis_index("mp"), 2)
    length, part = aux_buf.shape[3], s_buf.shape[2] // 2
    columns = lambda c: pl.ds(pl.multiple_of(c * part, part), part)
    slot = lax.rem(b, 2)

    def tokens_of(step):
        out = []
        for j in range(group):
            k = step * group + j
            to = pl.ds(j * rows, rows)
            mine, other = pieces[4 * k + 2], pieces[4 * k + 3]
            at = offsets[k]
            out += [
                (mine.at[pl.ds(at[2], rows)], s_buf.at[step % 2, to, columns(core)]),
                (other.at[pl.ds(at[3], rows)], s_buf.at[step % 2, to, columns(1 - core)]),
                (mine.at[pl.ds(at[2] + length, AUX), pl.ds(0, length)], aux_buf.at[step % 2, j]),
            ]
        return [pltpu.make_async_copy(x, y, sems.at[step % 2, i]) for i, (x, y) in enumerate(out)]

    def cots_of(step):
        out = []
        for j in range(group):
            k = step * group + j
            to = pl.ds(j * rows, rows)
            at = offsets[k]
            out += [
                (pieces[4 * k].at[pl.ds(at[0], rows)], c_buf.at[step % 2, to, columns(core)]),
                (pieces[4 * k + 1].at[pl.ds(at[1], rows)], c_buf.at[step % 2, to, columns(1 - core)]),
            ]
        return [pltpu.make_async_copy(x, y, sems.at[2 + step % 2, i]) for i, (x, y) in enumerate(out)]

    up_copy = pltpu.make_async_copy(up_ref.at[level], up_buf, sems.at[4, 0])
    down_copy = pltpu.make_async_copy(down_ref.at[level], down_buf, sems.at[4, 1])
    ends = [pltpu.make_async_copy(gup, gup_ref.at[level], sems.at[4, 2]),
            pltpu.make_async_copy(gdown, gdown_ref.at[level], sems.at[4, 3])]
    begins = [] if fresh else [
        pltpu.make_async_copy(sums[0].at[level], gup, sems.at[5, 0]),
        pltpu.make_async_copy(sums[1].at[level], gdown, sems.at[5, 1])]

    @pl.when(b == 0)
    def _():
        for c in [up_copy] + tokens_of(0) + [down_copy] + cots_of(0) + begins:
            c.start()

    for step in range(1, steps):
        @pl.when(b == step - 1)
        def _(step=step):
            for c in tokens_of(step) + cots_of(step):
                c.start()

    @pl.when(b == 0)
    def _():
        up_copy.wait()

    for step in range(steps):
        @pl.when(b == step)
        def _(step=step):
            for c in tokens_of(step):
                c.wait()

    columns_of = [gates_and_buckets(aux_buf[slot, j]) for j in range(group)]
    gate = jnp.concatenate([g[:rows, :1] for g, _ in columns_of], 0)
    keep = jnp.concatenate([k[:rows, :1] for _, k in columns_of], 0) >= level
    pre = dot(s_buf[slot], up_buf[...])
    active = jnp.where(keep, jnp.maximum(pre, 0.0), 0.0)
    act = (active * active * gate).astype(BF16)

    @pl.when(b == 0)
    def _():
        down_copy.wait()

    for step in range(steps):
        @pl.when(b == step)
        def _(step=step):
            for c in cots_of(step):
                c.wait()

    gact = dot(c_buf[slot], down_buf[...], NT)
    gpre = (gact * (2.0 * gate) * active).astype(BF16)

    @pl.when(b == 0)
    def _():
        if fresh:
            gup[...] = dot(s_buf[slot], gpre, TN)
            gdown[...] = dot(act, c_buf[slot], TN)
        else:
            for c in begins:
                c.wait()
            gup[...] += dot(s_buf[slot], gpre, TN)
            gdown[...] += dot(act, c_buf[slot], TN)

    if steps > 2:
        @pl.when(jnp.logical_and(b > 0, b < steps - 1))
        def _():
            gup[...] += dot(s_buf[slot], gpre, TN)
            gdown[...] += dot(act, c_buf[slot], TN)

    @pl.when(b == steps - 1)
    def _():
        gup[...] += dot(s_buf[slot], gpre, TN)
        ends[0].start()
        gdown[...] += dot(act, c_buf[slot], TN)
        ends[1].start()
        for c in ends:
            c.wait()


def weight_gradients(level, rows, length, blocks, w_up, w_down, carried, fresh, deps=()):
    levels, model, hidden = w_up.shape
    count = len(blocks)
    group = 2
    anywhere = pl.BlockSpec(memory_space=pl.ANY)
    arrays = [x for block in blocks for x, _ in block]
    offsets = tuple(tuple(at for _, at in block) for block in blocks)
    first = len(arrays) + 2
    return pl.pallas_call(
        partial(weight_kernel, level=level, rows=rows, group=group, offsets=offsets, fresh=fresh, carried=len(carried),
                deps=len(deps)),
        grid=(count // group,),
        in_specs=[anywhere] * (first + len(carried) + len(deps)),
        out_specs=[anywhere] * 2,
        out_shape=[jax.ShapeDtypeStruct((levels, model, hidden), F32), jax.ShapeDtypeStruct((levels, hidden, model), F32)],
        input_output_aliases={first: 0, first + 1: 1} if carried else {},
        scratch_shapes=[
            pltpu.VMEM((model, hidden), BF16), pltpu.VMEM((hidden, model), BF16),
            pltpu.VMEM((2, group * rows, model), BF16), pltpu.VMEM((2, group, AUX, length), BF16),
            pltpu.VMEM((2, group * rows, model), BF16),
            pltpu.VMEM((model, hidden), F32), pltpu.VMEM((hidden, model), F32),
            pltpu.SemaphoreType.DMA((6, 3 * group)),
        ],
        compiler_params=params(),
        cost_estimate=cost(8 * count * rows * model * hidden, 4 * count * rows * model + 16 * model * hidden),
        name=f"weight_gradients_{level}" + ("" if fresh else "_more"),
    )(*arrays, w_up, w_down, *carried, *deps)


def unpack_kernel(order_ref, *refs, count, carried):
    chunk_refs = refs[:count]
    qkv_ref, out_ref = refs[count + carried:]
    size = qkv_ref.shape[1]
    for k in range(count):
        @pl.when(pl.program_id(0) == k)
        def _(k=k):
            for c in range(3):
                qkv_ref[c] = chunk_refs[k][c * size:(c + 1) * size].astype(F32)
            out_ref[...] = chunk_refs[k][3 * size:4 * size].astype(F32).T


def unpack(order, chunks, size, total, carried=()):
    height, local = chunks[0].shape
    anywhere = pl.BlockSpec(memory_space=pl.ANY)
    count = len(chunks)
    return pl.pallas_call(
        partial(unpack_kernel, count=count, carried=len(carried)),
        grid_spec=pltpu.PrefetchScalarGridSpec(
            num_scalar_prefetch=1,
            grid=(count,),
            in_specs=[pl.BlockSpec((height, local), lambda b, o: (0, 0), pipeline_mode=pl.Buffered(1))] * count
            + [anywhere] * len(carried),
            out_specs=[
                pl.BlockSpec((3, size, local), lambda b, o: (0, o[b], 0)),
                pl.BlockSpec((local, size), lambda b, o: (0, o[b])),
            ],
        ),
        out_shape=[
            jax.ShapeDtypeStruct((3, total * size, local), F32),
            jax.ShapeDtypeStruct((local, total * size), F32),
        ],
        input_output_aliases={count + 1: 0, count + 2: 1} if carried else {},
        compiler_params=params(),
        cost_estimate=cost(0, 24 * count * size * local),
        name="unpack_some" if not carried else "unpack_rest",
    )(order, *chunks, *carried)


def add_kernel(*refs, count):
    total = refs[0][...].astype(F32)
    for ref in refs[1:count]:
        total = total + ref[...].astype(F32)
    refs[-1][...] = total.astype(BF16)


def add_rows(parts, deps=()):
    rows, columns = parts[0].shape
    block = pl.BlockSpec((rows // 2, columns), lambda i: (i, 0))
    return pl.pallas_call(
        partial(add_kernel, count=len(parts)),
        grid=(2,),
        in_specs=[block] * len(parts) + [pl.BlockSpec(memory_space=pl.ANY)] * len(deps),
        out_specs=block,
        out_shape=jax.ShapeDtypeStruct((rows, columns), BF16),
        compiler_params=params(),
        cost_estimate=cost(rows * columns, 6 * rows * columns),
        name="add_rows",
    )(*parts, *deps)


def pass_kernel(*refs):
    pass


def after(arrays, deps):
    anywhere = pl.BlockSpec(memory_space=pl.ANY)
    return pl.pallas_call(
        pass_kernel,
        in_specs=[anywhere] * (len(arrays) + len(deps)),
        out_specs=[anywhere] * len(arrays),
        out_shape=[jax.ShapeDtypeStruct(x.shape, x.dtype) for x in arrays],
        input_output_aliases={i: i for i in range(len(arrays))},
        compiler_params=params(),
        cost_estimate=cost(0, 0),
        name="after",
    )(*arrays, *deps)


def join_kernel(index_ref, right_local, left_local, right_ref, left_ref, *rest, cut, deps):
    right_out, left_out = rest[deps:]
    size = right_local.shape[1]
    if right_ref.shape[1] == size:
        right_out[0] = (right_local[0].astype(F32) + right_ref[0].astype(F32)).astype(BF16)
        left_out[0] = (left_local[0].astype(F32) + left_ref[0].astype(F32)).astype(BF16)
    else:
        right_out[0, :cut] = (right_local[0, :cut].astype(F32) + right_ref[0].astype(F32)).astype(BF16)
        right_out[0, cut:] = right_local[0, cut:]
        left_out[0, :cut] = left_local[0, :cut]
        left_out[0, cut:] = (left_local[0, cut:].astype(F32) + left_ref[0].astype(F32)).astype(BF16)


def join(grads, indices, right, left, size, deps=()):
    kinds, _, local = grads.shape
    arrived = right.shape[1]
    out = pl.BlockSpec((1, size, local), lambda i, o: (i, 0, 0))
    return pl.pallas_call(
        partial(join_kernel, cut=size // 2, deps=len(deps)),
        grid_spec=pltpu.PrefetchScalarGridSpec(
            num_scalar_prefetch=1,
            grid=(kinds,),
            in_specs=[
                pl.BlockSpec((1, size, local), lambda i, o: (i, o[0], 0)),
                pl.BlockSpec((1, size, local), lambda i, o: (i, o[1], 0)),
                pl.BlockSpec((1, arrived, local), lambda i, o: (i, 0, 0)),
                pl.BlockSpec((1, arrived, local), lambda i, o: (i, 0, 0)),
            ] + [pl.BlockSpec(memory_space=pl.ANY)] * len(deps),
            out_specs=[out, out],
        ),
        out_shape=[jax.ShapeDtypeStruct((kinds, size, local), BF16)] * 2,
        compiler_params=params(),
        cost_estimate=cost(2 * kinds * size * local, 12 * kinds * size * local),
        name="join",
    )(indices, grads, grads, right, left, *deps)


def join_own_kernel(index_ref, local_ref, right_ref, left_ref, extra_ref, *rest):
    kinds, size, _ = right_ref.shape
    for c in range(kinds):
        total = local_ref[c].astype(F32) + right_ref[c].astype(F32) + left_ref[c].astype(F32)
        rest[-1][c * size:(c + 1) * size] = total.astype(BF16)
    rest[-1][kinds * size:] = extra_ref[...]


def join_own(grads, indices, right, left, extra, deps=()):
    kinds, size, local = right.shape
    block = pl.BlockSpec((kinds, size, local), lambda i, o: (0, 0, 0))
    height = kinds * size + extra.shape[0]
    return pl.pallas_call(
        join_own_kernel,
        grid_spec=pltpu.PrefetchScalarGridSpec(
            num_scalar_prefetch=1,
            grid=(1,),
            in_specs=[pl.BlockSpec((kinds, size, local), lambda i, o: (0, o[0], 0)), block, block,
                      pl.BlockSpec(extra.shape, lambda i, o: (0, 0))]
            + [pl.BlockSpec(memory_space=pl.ANY)] * len(deps),
            out_specs=pl.BlockSpec((height, local), lambda i, o: (0, 0)),
        ),
        out_shape=jax.ShapeDtypeStruct((height, local), BF16),
        compiler_params=params(),
        cost_estimate=cost(2 * kinds * size * local, 8 * kinds * size * local),
        name="join_own",
    )(indices, grads, right, left, extra, *deps)


def ring_order(count):
    nz = 4 if count % 4 == 0 else 1
    ny = count // nz
    if nz == 1 or ny % 2:
        return list(range(count))
    order = [(z, 0) for z in range(nz)]
    for y in range(1, ny):
        line = list(range(1, nz))
        order += [(z, y) for z in (reversed(line) if y % 2 else line)]
    order += [(0, y) for y in range(ny - 1, 0, -1)]
    return [z * ny + y for z, y in order]


class Ring:
    def __init__(self):
        self.log = []
        self.count = lax.axis_size("dp")
        self.order = ring_order(self.count)
        n = self.count
        place = [0] * n
        for p, d in enumerate(self.order):
            place[d] = p
        self.position = jnp.array(place, jnp.int32)[lax.axis_index("dp")]
        self.right = [(self.order[p], self.order[(p + 1) % n]) for p in range(n)]
        self.left = [(self.order[(p + 1) % n], self.order[p]) for p in range(n)]

    def to_right(self, x):
        out = lax.ppermute(x, "dp", self.right)
        self.log.append(out)
        return out

    def to_left(self, x):
        out = lax.ppermute(x, "dp", self.left)
        self.log.append(out)
        return out

    def logged(self, f, *args):
        self.log = []
        out = f(*args)
        pairs = [tuple(self.log[i:i + 2]) for i in range(0, len(self.log), 2)]
        self.log = []
        return out, pairs

    def gather(self, x, axis):
        out = [x]
        r = l = x
        for _ in range(self.count // 2 - 1):
            r, l = self.to_right(r), self.to_left(l)
            out += [r, l]
        size = x.shape[axis]
        cut = size // 32 * 16
        first = self.to_right(lax.slice_in_dim(r, 0, cut, axis=axis))
        second = self.to_left(lax.slice_in_dim(l, cut, size, axis=axis))
        out.append(jnp.concatenate([first, second], axis))
        return out

    def offsets(self):
        out = [0]
        for k in range(1, self.count // 2):
            out += [-k, k]
        return out + [self.count // 2]

    def indices(self):
        return [(self.position + k) % self.count for k in self.offsets()]

    def reduce_start(self, x):
        size = x.shape[1] // self.count
        cut = size // 2
        far = self.count // 2
        at = ((self.position + far) % self.count) * size
        r = lax.dynamic_slice_in_dim(x, at, cut, axis=1)
        l = lax.dynamic_slice_in_dim(x, at + cut, cut, axis=1)
        return (self.to_right(r), self.to_left(l)), (r, l)

    def reduce_step(self, x, arrived, k, deps=()):
        indices = jnp.stack([(self.position + k) % self.count, (self.position - k) % self.count]).astype(jnp.int32)
        r, l = join(x, indices, *arrived, x.shape[1] // self.count, deps)
        return (self.to_right(r), self.to_left(l)), (r, l)

    def reduce_end(self, x, arrived, extra, deps=()):
        return join_own(x, self.position[None].astype(jnp.int32), *arrived, extra, deps)


def core_swap(x):
    n = lax.axis_size("mp")
    return lax.ppermute(x, "mp", [(i, i ^ 1) for i in range(n)])


def sum_over_x(x, deps=()):
    n = lax.axis_size("mp") // 2
    index = lax.axis_index("mp")
    parts = [x] + [
        lax.ppermute(x, "mp", [(i, (i + 2 * k) % (2 * n)) for i in range(2 * n)]) for k in range(1, n)
    ]
    if n == 1:
        return x.astype(F32)
    if deps:
        parts[1:] = after(parts[1:], deps)
    if n == 2:
        return parts[0].astype(F32) + parts[1].astype(F32)
    stacked = jnp.stack(parts)
    total = None
    for j in range(n):
        term = lax.dynamic_index_in_dim(stacked, (index // 2 - j) % n, 0, keepdims=False).astype(F32)
        total = term if total is None else total + term
    return total


def on_device(tokens, gain_first, w_qkv, w_out, gain_second, router, w_up, w_down, slot, cotangent):
    length, model = tokens.shape
    buckets = w_up.shape[0]
    devices_dp = lax.axis_size("dp")
    groups = devices_dp // buckets
    capacity = length * 5 // (4 * devices_dp)
    row_bounds = [min(length, (buckets - level) * groups * capacity) for level in range(buckets)]
    ring = Ring()
    core = lax.axis_index("mp") % 2
    half = length // 2

    bucket_ids = slot // capacity // groups
    places = jnp.arange(length, dtype=jnp.int32)
    key = (buckets - 1 - bucket_ids) * length + places
    rank = jnp.sum((key[None, :] < key[:, None]).astype(jnp.int32), 1)
    rank_here = jnp.roll(rank, -core * half)
    sort_rows = places[:, None] == rank[None, :]
    sort_here = places[:, None] == rank_here[None, :]
    sort_low = sort_here.astype(BF16)
    unsort_low = (rank_here[:, None] == places[None, :]).astype(BF16)
    bucket_sorted = jnp.sum(jnp.where(sort_rows, bucket_ids[None, :], 0), 1)

    def part_of(x, c, axis=0):
        size = x.shape[axis] // 2
        return lax.dynamic_slice_in_dim(x, c * size, size, axis=axis)

    def own_rows(x):
        return part_of(x, core)

    def other_rows(x):
        return part_of(x, 1 - core)

    def joined(mine, other):
        return jnp.concatenate([jnp.where(core == 0, mine, other), jnp.where(core == 0, other, mine)], 0)

    cot_sorted = dot(sort_rows.astype(BF16), cotangent).astype(BF16)

    cot_own = part_of(cot_sorted, core, 1)
    cot_first = ring.to_right(cot_own), ring.to_left(cot_own)

    w3 = jnp.transpose(w_qkv, (1, 0, 2))
    cos, sin = rotary_table(length, HEAD)
    part_mine, part_other, normed_low, qkv, lse, mixed = attend(tokens, gain_first[None, :], w3, cos, sin, w_out)
    attn_rows = add_rows([part_mine, core_swap(part_other)])
    attn = sum_over_x(attn_rows)

    resid = own_rows(tokens).astype(F32) + attn
    inv = lax.rsqrt(jnp.mean(resid * resid, -1, keepdims=True) + EPSILON)
    xhat = resid * inv
    normed_second = xhat * gain_second
    logits = jnp.dot(normed_second, router, precision=HIGHEST)
    prob = jax.nn.softmax(logits, axis=-1)
    onehot = (own_rows(bucket_ids)[:, None] == jnp.arange(buckets)[None, :]).astype(F32)
    gate = buckets * jnp.sum(prob * onehot, -1)
    sent_half = normed_second.astype(BF16)
    sent_both = jnp.concatenate([sent_half, core_swap(sent_half)], 0)
    gate_both = jnp.concatenate([gate, core_swap(gate)], 0)
    gate_sorted = jnp.sum(jnp.where(sort_here, gate_both[None, :], 0.0), 1)

    sent_sorted = dot(sort_low, sent_both).astype(BF16)

    gate_1 = low(gate_sorted)
    gate_2 = low(gate_sorted - gate_1.astype(F32))
    gate_3 = low(gate_sorted - gate_1.astype(F32) - gate_2.astype(F32))
    aux = jnp.stack([gate_1, gate_2, gate_3, bucket_sorted.astype(BF16)] + [jnp.zeros_like(gate_1)] * (AUX - 4))
    aux = jnp.pad(aux, ((0, 0), (0, model // 2 - length)))
    sent_own = jnp.concatenate([part_of(sent_sorted, core, 1), aux], 0)
    height = length
    blocks = [((cot_own, 0), (part_of(cot_sorted, 1 - core, 1), 0), (sent_own, 0), (part_of(sent_sorted, 1 - core, 1), 0))]

    def block(mine, other):
        return (mine, 0), (other, 0), (mine, height), (other, height)

    sent_first = ring.to_right(sent_own), ring.to_left(sent_own)

    wide = lambda x: jnp.broadcast_to(x[:, None], (length, 128))
    gsent_mine, gsent_other, act = own_grad(
        sent_sorted, cot_sorted, wide(bucket_sorted), wide(gate_sorted), unsort_low, w_up, w_down, row_bounds,
        cot_first + (sent_own,))
    gsent_rows = add_rows([gsent_mine, core_swap(gsent_other)])
    grad_sent = sum_over_x(gsent_rows).astype(BF16).astype(F32)
    far = devices_dp // 2
    met = []

    def forward(arrived, deps):
        if len(arrived) == 4:
            cot_r, cot_l, sent_r, sent_l = after(arrived, deps)
            r, l = jnp.concatenate([cot_r, sent_r], 0), jnp.concatenate([cot_l, sent_l], 0)
        else:
            r, l = after(arrived, deps)
        if len(met) < far:
            met.extend([(r, core_swap(r)), (l, core_swap(l))])
        else:
            met.extend([(r, None), (l, None)])
        if len(met) < 2 * far - 2:
            return ring.to_right(r), ring.to_left(l)
        return ring.to_right(r[:height]), ring.to_left(l[height:])

    r, l = forward(cot_first + sent_first, (gsent_rows,))
    ffn_part, ggate_part = own_forward(
        act, cot_sorted, sort_rows.astype(BF16).T, w_down, row_bounds, (gsent_rows, met[0][0], met[1][0]))
    ggate_part = jnp.sum(jnp.where(sort_rows, ggate_part[:, :1], 0.0), 0)
    grad_gate = ggate_part + core_swap(ggate_part)
    grad_gate = sum_over_x(own_rows(grad_gate))

    grad_output = own_rows(cotangent).astype(F32)
    grad_prob = buckets * grad_gate[:, None] * onehot
    grad_logits = prob * (grad_prob - jnp.sum(grad_prob * prob, -1, keepdims=True))
    grad_router = jnp.dot(normed_second.T, grad_logits, precision=HIGHEST)
    grad_second = grad_sent + jnp.dot(grad_logits, router.T, precision=HIGHEST)
    grad_gain_second = jnp.sum(grad_second * xhat, 0)
    scaled = grad_second * gain_second
    grad_resid = grad_output + inv * (scaled - xhat * jnp.mean(scaled * xhat, -1, keepdims=True))
    ga_half = low(grad_resid)
    grad_attn = joined(ga_half, core_swap(ga_half))

    grads, first_part = attend_back(
        grad_attn, normed_low, qkv, lse, mixed, w_out, w3, cos, sin, met[0] + met[1])

    ffn_other, = after([other_rows(ffn_part)], (grads,))
    ffn_sum = add_rows([own_rows(ffn_part), core_swap(ffn_other)])

    carried = ()
    arrived, sending = ring.reduce_start(grads)
    chunks = None
    step = 0

    def advance(step, arrived, deps):
        nonlocal chunks
        if step < far - 1:
            return ring.reduce_step(grads, arrived, far - 1 - step, deps)
        if step == far - 1:
            chunks = [ring.reduce_end(grads, arrived, extra, deps)]
            r = l = chunks[0]
        else:
            r, l = after(arrived, deps) if deps else arrived
            chunks.extend([r, l])
        if step < 2 * far - 2:
            sending = (r, l)
            r, l = ring.to_right(r), ring.to_left(l)
        else:
            cut = r.shape[0] // 32 * 16
            sending = (r[:cut], l[cut:])
            r, l = ring.to_right(sending[0]), ring.to_left(sending[1])
            chunks.append(jnp.concatenate([r, l], 0))
        return (r, l), sending

    steps = 2 * far - 1
    while len(met) < far:
        r, l = forward((r, l), (grads, ffn_sum))
    near = len(met)
    sending = sending + met[-2] + met[-1]
    blocks += [block(*x) for x in met[:far - 1]]
    carried = ()
    calls = [(level, rows, True) for level, rows in enumerate(row_bounds)]
    later = [block(*x) for x in met[far - 1:]]
    extra = None
    slots = list(range(buckets))
    for slot_at, level in enumerate(slots):
        rows = row_bounds[level]
        carried = weight_gradients(level, rows, length, blocks, w_up, w_down, tuple(carried), True, sending)
        if slot_at == 0:
            ffn_rows = sum_over_x(ffn_sum, (carried[0],)).astype(BF16).astype(F32)
            output_half = (resid + gate[:, None] * ffn_rows).astype(BF16)
            first_other, = after([other_rows(first_part)], (carried[0], output_half))
            first_other = core_swap(first_other)
        if slot_at == 1:
            first_rows = add_rows([own_rows(first_part), first_other], (carried[0],))
        if slot_at == 2:
            grad_first = sum_over_x(first_rows, (carried[0],)).astype(BF16).astype(F32)
            source = own_rows(tokens).astype(F32)
            inv_first = lax.rsqrt(jnp.mean(source * source, -1, keepdims=True) + EPSILON)
            xhat_first = source * inv_first
            grad_gain_first = jnp.sum(grad_first * xhat_first, 0)
            scaled_first = grad_first * gain_first
            grad_source = inv_first * (
                scaled_first - xhat_first * jnp.mean(scaled_first * xhat_first, -1, keepdims=True))
            tokens_half = (grad_source + grad_resid).astype(BF16)
            small = jnp.concatenate([grad_router.T, grad_gain_second[None], grad_gain_first[None]], 0)
            small = jnp.pad(small, ((0, -small.shape[0] % 8), (0, 0)))
            small_other = core_swap(small)
        if slot_at == 3:
            small_other, = after([small_other], (carried[0],))
            extra = low(small + small_other).reshape(-1, w3.shape[2])
        arrived, sending = advance(step, arrived, (carried[0],))
        step += 1
        if slot_at == 3:
            r, l, *held = after([r, l] + [x for x, _ in met[far:]], (carried[0], sending[0]))
        if slot_at == 1:
            sending = sending + (output_half,)
        if slot_at == 2:
            sending = sending + (tokens_half, small)
            while len(met) < 2 * far - 2:
                r, l = forward((r, l), (carried[0],))
            sending = sending + tuple(pair[0] for pair in met[far:])
    later += [block(x, core_swap(x)) for x in held]
    later.append(((r, 0), (core_swap(r), 0), (l, 0), (core_swap(l), 0)))
    steps = 2 * far - 1
    for level, rows in enumerate(row_bounds):
        carried = weight_gradients(level, rows, length, later, w_up, w_down, tuple(carried), False, sending)
        ready = ()
        if level == 0:
            others = [core_swap(x) for x in after([tokens_half, output_half], (carried[0],))]
        if level == 1:
            others = after(others, (carried[0],))
            grad_tokens = joined(tokens_half, others[0])
            output = joined(output_half, others[1])
            ready = (grad_tokens, output)
        sending = ()
        if step < steps:
            arrived, sending = advance(step, arrived, (carried[0],))
            step += 1
        sending = sending + ready
    while step < steps:
        arrived, sending = advance(step, arrived, ())
        step += 1
    grad_up, grad_down = carried
    order = jnp.stack(ring.indices()).astype(jnp.int32)
    size = model // devices_dp
    grad_wqkv, grad_wout = unpack(order, chunks, size, devices_dp)
    terms = jnp.stack([x[4 * size:] for x in chunks])
    by_place = jnp.zeros((devices_dp,), jnp.int32).at[order].set(jnp.arange(devices_dp, dtype=jnp.int32))
    small = jnp.sum(terms[by_place].astype(F32), 0).reshape(small.shape)

    return (
        output,
        grad_tokens,
        small[buckets + 1],
        jnp.transpose(grad_wqkv, (1, 0, 2)),
        grad_wout,
        small[buckets],
        small[:buckets].T,
        grad_up,
        grad_down,
    )


def solution(mesh):
    placed = (
        P("dp", None),
        P(),
        P(None, None, "mp"),
        P("mp", None),
        P(),
        P(),
        P(None, None, "mp"),
        P(None, "mp", None),
        P("dp"),
        P("dp", None),
    )
    return jax.shard_map(
        on_device,
        mesh=mesh,
        in_specs=placed,
        out_specs=(
            P("dp", None),
            P("dp", None),
            P(),
            P(None, None, "mp"),
            P("mp", None),
            P(),
            P(),
            P(None, None, "mp"),
            P(None, "mp", None),
        ),
        check_vma=False,
    )
```
